32 devices in a mesh: dp: 8 (over z, y), mp: 4 (over x, core).
Axes of the slice: x: 2, y: 2, z: 4, core: 2. Of those that a mesh axis runs over, the one named last changes fastest.
Arguments:
- tokens: bfloat16 [2, 8192, 768], P(None, 'dp'), may hold values from -6 to 6
- cotangent: bfloat16 [2, 8192, 768], P(None, 'dp'), may hold values from -6 to 6
- segments: int32 [8192], replicated, may hold values from 0 to 1, as said below
- route_query: int32 [2, 1024], P(None, 'dp'), may hold values from 0 to 1023, as said below
- route_key: int32 [2, 1024], replicated, may hold values from 0 to 1023, as said below
- route_ffn: int32 [2, 1024], P(None, 'dp'), may hold values from 0 to 1023, as said below
- attn_in: float32 [6, 768, 768], P(None, 'dp', 'mp'), may hold values from -0.21875 to 0.21875
- attn_out: float32 [2, 768, 768], P(None, ('mp', 'dp')), may hold values from -1.25 to 1.25
- light_in: float32 [2, 768, 1024], P(None, 'dp', 'mp'), may hold values from -0.21875 to 0.21875
- light_out: float32 [1024, 768], P(('mp', 'dp')), may hold values from -0.1875 to 0.1875
- heavy_in: float32 [2, 768, 4096], P(None, 'dp', 'mp'), may hold values from -0.21875 to 0.21875
- heavy_out: float32 [4096, 768], P(('mp', 'dp')), may hold values from -0.09375 to 0.09375
- gains: float32 [2, 768], P(None, 'dp'), may hold values from 0.4 to 3
- router: float32 [3, 768], P(None, 'dp'), may hold values from -0.21875 to 0.21875
- row_attn_in: float32 [6, 768], replicated, may hold values from 163.84 to 2621.44
- col_attn_in: float32 [6, 768], replicated, may hold values from 163.84 to 2621.44
- row_attn_out: float32 [2, 768], replicated, may hold values from 819.2 to 13107.2
- col_attn_out: float32 [2, 768], replicated, may hold values from 819.2 to 13107.2
- row_light_in: float32 [2, 768], replicated, may hold values from 819.2 to 13107.2
- col_light_in: float32 [2, 1024], replicated, may hold values from 819.2 to 13107.2
- row_light_out: float32 [1024], replicated, may hold values from 1638.4 to 26214.4
- col_light_out: float32 [768], replicated, may hold values from 1638.4 to 26214.4
- row_heavy_in: float32 [2, 768], replicated, may hold values from 81.92 to 1310.72
- col_heavy_in: float32 [2, 4096], replicated, may hold values from 81.92 to 1310.72
- row_heavy_out: float32 [4096], replicated, may hold values from 163.84 to 2621.44
- col_heavy_out: float32 [768], replicated, may hold values from 163.84 to 2621.44
- second_gains: float32 [2, 768], P(None, 'dp'), may hold values from 1638.4 to 26214.4
- second_router: float32 [3, 768], P(None, 'dp'), may hold values from 16384 to 262144
Outputs:
- mixed: bfloat16 [2, 8192, 768], P(None, 'dp')
- grad_tokens: float32 [2, 8192, 768], P(None, 'dp')
- grad_attn_in: float32 [6, 768, 768], P(None, 'dp', 'mp')
- rows_attn_in: float32 [6, 768], replicated
- cols_attn_in: float32 [6, 768], replicated
- new_attn_in: float32 [6, 768, 768], P(None, 'dp', 'mp')
- grad_attn_out: float32 [2, 768, 768], P(None, ('mp', 'dp'))
- rows_attn_out: float32 [2, 768], replicated
- cols_attn_out: float32 [2, 768], replicated
- new_attn_out: float32 [2, 768, 768], P(None, ('mp', 'dp'))
- grad_light_in: float32 [2, 768, 1024], P(None, 'dp', 'mp')
- rows_light_in: float32 [2, 768], replicated
- cols_light_in: float32 [2, 1024], replicated
- new_light_in: float32 [2, 768, 1024], P(None, 'dp', 'mp')
- grad_light_out: float32 [1024, 768], P(('mp', 'dp'))
- rows_light_out: float32 [1024], replicated
- cols_light_out: float32 [768], replicated
- new_light_out: float32 [1024, 768], P(('mp', 'dp'))
- grad_heavy_in: float32 [2, 768, 4096], P(None, 'dp', 'mp')
- rows_heavy_in: float32 [2, 768], replicated
- cols_heavy_in: float32 [2, 4096], replicated
- new_heavy_in: float32 [2, 768, 4096], P(None, 'dp', 'mp')
- grad_heavy_out: float32 [4096, 768], P(('mp', 'dp'))
- rows_heavy_out: float32 [4096], replicated
- cols_heavy_out: float32 [768], replicated
- new_heavy_out: float32 [4096, 768], P(('mp', 'dp'))
- grad_gains: float32 [2, 768], P(None, 'dp')
- moment_gains: float32 [2, 768], P(None, 'dp')
- new_gains: float32 [2, 768], P(None, 'dp')
- grad_router: float32 [3, 768], P(None, 'dp')
- moment_router: float32 [3, 768], P(None, 'dp')
- new_router: float32 [3, 768], P(None, 'dp')
The draws below stay inside these ranges and needn't reach their ends.
Inputs may be any that keep to these rules, and one draw needn't show every extreme that they name: `segments`: ids never fall; every run of one id is 2048 tokens or longer. `route_query`: entries k * 128 to (k + 1) * 128 - 1 of a row are distinct rising token positions within the k-th block of 1024 tokens, counted from the block's start; in one block of each row the first and the last position are both among them. `route_key`: entries k * 128 to (k + 1) * 128 - 1 of a row are distinct rising token positions within the k-th block of 1024 tokens, counted from the block's start; in one block of each row the first and the last position are both among them. `route_ffn`: entries k * 128 to (k + 1) * 128 - 1 of a row are distinct rising token positions within the k-th block of 1024 tokens, counted from the block's start; in one block of each row the first and the last position are both among them.
All inputs are finite; a program needn't handle non-finite values.
Results may differ from the reference program's by a relative error of at most 0.024.
The reference program's roundings to bfloat16 on the way count: a program that leaves them out, or rounds other values in their place, can miss the bound.
Values may be sent and summed in bfloat16 or wider, within the bound.
No kernel may reach another device: no remote copies, remote signals or barrier semaphores. Data moves between devices by JAX's collectives and lax.ppermute only.
A program may use at most 256 MiB of HBM per device.

```python
import math
import jax
import jax.numpy as jnp
from jax import lax

D = 768
LH = 8
LDH = 96
HH = 12
HDH = 64
LF = 1024
HF = 4096
WIN = 128
TOK_DEV = 1024
MICRO = 2
STEP = 10
R_DEV = 128
TOKENS = 8192
ROUTED = 1024
DOCS = 2


def routed_slots(key):
    blocks = TOKENS // TOK_DEV
    row_keys = jax.random.split(key, MICRO)

    def one_row(row_key):
        pick_key, edge_key = jax.random.split(row_key)
        keys = jax.random.split(pick_key, blocks)
        drawn = jax.vmap(lambda one_key: jnp.sort(jax.random.permutation(one_key, TOK_DEV)[:R_DEV]))(keys)
        inner = jax.random.permutation(jax.random.fold_in(edge_key, 5), TOK_DEV - 2)[:R_DEV - 2] + 1
        edged = jnp.sort(jnp.concatenate([jnp.array([0, TOK_DEV - 1], jnp.int32), inner.astype(jnp.int32)]))
        chosen = jax.random.randint(edge_key, (), 0, blocks)
        flags = (jnp.arange(blocks) == chosen)[:, None]
        return jnp.where(flags, edged[None, :], drawn).reshape(ROUTED)
    return jax.vmap(one_row)(row_keys).astype(jnp.int32)


def draw_route_query(key, part):
    key = jax.random.fold_in(key, 21)
    return routed_slots(key)


def draw_route_key(key, part):
    key = jax.random.fold_in(key, 22)
    return routed_slots(key)


def draw_route_ffn(key, part):
    key = jax.random.fold_in(key, 23)
    return routed_slots(key)


def draw_segments(key, part):
    key = jax.random.fold_in(key, 31)
    shares = jax.random.randint(key, (DOCS,), 1, 64)
    spare = TOKENS - 2 * TOK_DEV * DOCS
    extra = shares * spare // jnp.sum(shares)
    extra = extra.at[DOCS - 1].add(spare - jnp.sum(extra))
    lengths = 2 * TOK_DEV + extra
    starts = jnp.cumsum(lengths) - lengths
    position = jnp.arange(TOKENS, dtype=jnp.int32)
    return jnp.sum((position[:, None] >= starts[None, 1:]).astype(jnp.int32), axis=1).astype(jnp.int32)


def draw_gains(key, part):
    key = jax.random.fold_in(key, 41)
    noise = 0.08 * jnp.clip(jax.random.normal(key, (2, D), jnp.float32), -3.0, 3.0)
    ramp = 0.6 + 1.2 * jnp.arange(D, dtype=jnp.float32) / (D - 1)
    return (ramp[None, :] * (1.0 + noise)).astype(jnp.float32)


def shard_levels(stream_key, shape, pieces, low, largest):
    def one(dim, shards_of):
        steps = jax.random.uniform(jax.random.fold_in(jax.random.fold_in(stream_key, 6), dim), (shards_of,), jnp.float32, low / len(pieces), largest / len(pieces))
        return jnp.repeat(jnp.exp(steps), shape[dim] // shards_of).reshape((-1,) + (1,) * (len(shape) - dim - 1))

    loudness = one(*pieces[0])
    for cut in pieces[1:]:
        loudness = loudness * one(*cut)
    return loudness


def gaussian(stream_key, shape, deviation, reach, pieces=(), held_as=jnp.bfloat16):
    loudness = shard_levels(stream_key, shape, pieces, -0.22, 0.18) if pieces else 1.0
    values = jax.random.normal(stream_key, shape, jnp.float32) * deviation * loudness
    return jnp.minimum(jnp.maximum(values, -reach), reach).astype(held_as)


def setup_inputs(seed: int = 0) -> dict:
    streams_of = jax.random.split(jax.random.key(seed), 29)
    tokens = gaussian(streams_of[0], (MICRO, TOKENS, D), 1.0, 6.0, ((1, 8),))
    cotangent = gaussian(streams_of[1], (MICRO, TOKENS, D), 1.0, 6.0, ((1, 8),))
    segments = draw_segments(jax.random.fold_in(streams_of[28], 71), 0)
    route_query = draw_route_query(jax.random.fold_in(streams_of[28], 71), 0)
    route_key = draw_route_key(jax.random.fold_in(streams_of[28], 71), 0)
    route_ffn = draw_route_ffn(jax.random.fold_in(streams_of[28], 71), 0)
    attn_in = gaussian(streams_of[6], (6, D, D), D ** -0.5, 0.21875, ((1, 8), (2, 4)), jnp.float32)
    attn_out = gaussian(streams_of[7], (2, D, D), (D // 32) ** -0.5, 1.25, ((1, 32),), jnp.float32)
    light_in = gaussian(streams_of[8], (2, D, LF), D ** -0.5, 0.21875, ((1, 8), (2, 4)), jnp.float32)
    light_out = gaussian(streams_of[9], (LF, D), LF ** -0.5, 0.1875, ((0, 32),), jnp.float32)
    heavy_in = gaussian(streams_of[10], (2, D, HF), D ** -0.5, 0.21875, ((1, 8), (2, 4)), jnp.float32)
    heavy_out = gaussian(streams_of[11], (HF, D), HF ** -0.5, 0.09375, ((0, 32),), jnp.float32)
    gains = draw_gains(jax.random.fold_in(streams_of[28], 71), 0)
    router = gaussian(streams_of[13], (3, D), D ** -0.5, 0.21875, ((1, 8),), jnp.float32)
    row_attn_in = jnp.clip(jnp.exp(jax.random.uniform(streams_of[14], (6, D), jnp.float32, math.log(163.84), math.log(2621.44))), 163.84, 2621.44)
    col_attn_in = jnp.clip(jnp.exp(jax.random.uniform(streams_of[15], (6, D), jnp.float32, math.log(163.84), math.log(2621.44))), 163.84, 2621.44)
    row_attn_out = jnp.clip(jnp.exp(jax.random.uniform(streams_of[16], (2, D), jnp.float32, math.log(819.2), math.log(13107.2))), 819.2, 13107.2)
    col_attn_out = jnp.clip(jnp.exp(jax.random.uniform(streams_of[17], (2, D), jnp.float32, math.log(819.2), math.log(13107.2))), 819.2, 13107.2)
    row_light_in = jnp.clip(jnp.exp(jax.random.uniform(streams_of[18], (2, D), jnp.float32, math.log(819.2), math.log(13107.2))), 819.2, 13107.2)
    col_light_in = jnp.clip(jnp.exp(jax.random.uniform(streams_of[19], (2, LF), jnp.float32, math.log(819.2), math.log(13107.2))), 819.2, 13107.2)
    row_light_out = jnp.clip(jnp.exp(jax.random.uniform(streams_of[20], (LF,), jnp.float32, math.log(1638.4), math.log(26214.4))), 1638.4, 26214.4)
    col_light_out = jnp.clip(jnp.exp(jax.random.uniform(streams_of[21], (D,), jnp.float32, math.log(1638.4), math.log(26214.4))), 1638.4, 26214.4)
    row_heavy_in = jnp.clip(jnp.exp(jax.random.uniform(streams_of[22], (2, D), jnp.float32, math.log(81.92), math.log(1310.72))), 81.92, 1310.72)
    col_heavy_in = jnp.clip(jnp.exp(jax.random.uniform(streams_of[23], (2, HF), jnp.float32, math.log(81.92), math.log(1310.72))), 81.92, 1310.72)
    row_heavy_out = jnp.clip(jnp.exp(jax.random.uniform(streams_of[24], (HF,), jnp.float32, math.log(163.84), math.log(2621.44))), 163.84, 2621.44)
    col_heavy_out = jnp.clip(jnp.exp(jax.random.uniform(streams_of[25], (D,), jnp.float32, math.log(163.84), math.log(2621.44))), 163.84, 2621.44)
    second_gains = jnp.clip(jnp.exp(math.log(26214.4) - 2.7725887 * jax.random.uniform(streams_of[26], (2, D), jnp.float32) ** shard_levels(streams_of[26], (2, D), ((1, 8),), -0.2, 0.2)), 1638.4, 26214.4)
    second_router = jnp.clip(jnp.exp(math.log(262144.0) - 2.7725887 * jax.random.uniform(streams_of[27], (3, D), jnp.float32) ** shard_levels(streams_of[27], (3, D), ((1, 8),), -0.2, 0.2)), 16384.0, 262144.0)
    return {"tokens": tokens, "cotangent": cotangent, "segments": segments, "route_query": route_query, "route_key": route_key, "route_ffn": route_ffn, "attn_in": attn_in, "attn_out": attn_out, "light_in": light_in, "light_out": light_out, "heavy_in": heavy_in, "heavy_out": heavy_out, "gains": gains, "router": router, "row_attn_in": row_attn_in, "col_attn_in": col_attn_in, "row_attn_out": row_attn_out, "col_attn_out": col_attn_out, "row_light_in": row_light_in, "col_light_in": col_light_in, "row_light_out": row_light_out, "col_light_out": col_light_out, "row_heavy_in": row_heavy_in, "col_heavy_in": col_heavy_in, "row_heavy_out": row_heavy_out, "col_heavy_out": col_heavy_out, "second_gains": second_gains, "second_router": second_router}


highest = lax.Precision.HIGHEST
norm_eps = 1e-06
tiny_square = 1e-30
scale_floor = 0.001
clip_level = 1.0
step_rate = 0.5
masked_score = -1e+30

@jax.custom_vjp
def low(v):
    return lax.optimization_barrier(v.astype(jnp.bfloat16)).astype(jnp.float32)

@jax.custom_vjp
def low_back(v):
    return v

def low_keep(v):
    return (low(v), None)

def low_pass(kept, grad):
    return (grad,)

def back_keep(v):
    return (v, None)

def back_low(kept, grad):
    return (low(grad),)
low.defvjp(low_keep, low_pass)
low_back.defvjp(back_keep, back_low)

def both_round(values):
    return low_back(low(values))

def matmul(left, right):
    return jnp.dot(left, right, precision=highest)

def rms_norm(values, gain_row):
    return values * lax.rsqrt(lax.optimization_barrier(jnp.mean(values * values, axis=-1, keepdims=True)) + norm_eps) * gain_row

def attend(scores, allowed, value_heads):
    masked = jnp.where(allowed[None], scores, masked_score)
    top_score = lax.optimization_barrier(jnp.max(masked, axis=-1, keepdims=True))
    exp_scores = jnp.exp(masked - top_score)
    probs_low = low(exp_scores / lax.optimization_barrier(jnp.sum(exp_scores, axis=-1, keepdims=True)))
    return jnp.einsum('hqk,khd->qhd', probs_low, value_heads, precision=highest)

def light_attention(queries, keys, values, segment_ids):
    radius = WIN // 2
    key_span = TOK_DEV + 2 * radius
    query_heads = queries.reshape(TOKENS, LH, LDH)
    key_pad = jnp.pad(keys.reshape(TOKENS, LH, LDH), ((radius, radius), (0, 0), (0, 0)))
    value_pad = jnp.pad(values.reshape(TOKENS, LH, LDH), ((radius, radius), (0, 0), (0, 0)))
    seg_pad = jnp.pad(segment_ids, (radius, radius), constant_values=-1)
    offset = jnp.arange(TOK_DEV)[:, None] - jnp.arange(key_span)[None, :] + radius
    nearby = jnp.abs(offset) <= radius

    def one_block(block_start):
        query_block = lax.dynamic_slice_in_dim(query_heads, block_start, TOK_DEV, 0)
        key_block = lax.dynamic_slice_in_dim(key_pad, block_start, key_span, 0)
        value_block = lax.dynamic_slice_in_dim(value_pad, block_start, key_span, 0)
        seg_query = lax.dynamic_slice_in_dim(segment_ids, block_start, TOK_DEV, 0)
        seg_key = lax.dynamic_slice_in_dim(seg_pad, block_start, key_span, 0)
        allowed = nearby & (seg_query[:, None] == seg_key[None, :])
        scores = low_back(jnp.einsum('qhd,khd->hqk', query_block, key_block, precision=highest) / math.sqrt(LDH))
        return attend(scores, allowed, value_block)
    starts = (jnp.arange(TOKENS // TOK_DEV) * TOK_DEV).astype(jnp.int32)
    return lax.map(jax.checkpoint(one_block), starts).reshape(TOKENS, LH * LDH)

def heavy_attention(queries, keys, values, seg_query, seg_key):
    query_heads = queries.reshape(ROUTED, HH, HDH)
    key_heads = keys.reshape(ROUTED, HH, HDH)
    value_heads = values.reshape(ROUTED, HH, HDH)

    def one_block(block_start):
        query_block = lax.dynamic_slice_in_dim(query_heads, block_start, R_DEV, 0)
        seg_block = lax.dynamic_slice_in_dim(seg_query, block_start, R_DEV, 0)
        allowed = seg_block[:, None] == seg_key[None, :]
        scores = low_back(jnp.einsum('qhd,khd->hqk', query_block, key_heads, precision=highest) / math.sqrt(HDH))
        return attend(scores, allowed, value_heads)
    starts = (jnp.arange(ROUTED // R_DEV) * R_DEV).astype(jnp.int32)
    return lax.map(jax.checkpoint(one_block), starts).reshape(ROUTED, HH * HDH)

def global_rows(local_rows):
    return (local_rows + jnp.arange(ROUTED) // R_DEV * TOK_DEV).astype(jnp.int32)

def layer(inputs_all, params, segments, route_query, route_key, route_ffn):
    attn_w, attn_out_w, light_in_w, light_out_w, heavy_in_w, heavy_out_w, gain_w, router_w = [low(weight) for weight in params]
    results = []
    for micro_index in range(MICRO):
        segment_ids = segments * (micro_index % 2)
        inputs = inputs_all[micro_index]
        normed = rms_norm(inputs, gain_w[0])
        normed_low = low(normed)
        light_query = both_round(matmul(normed_low, attn_w[0]))
        light_key = both_round(matmul(normed_low, attn_w[1]))
        light_value = both_round(matmul(normed_low, attn_w[2]))
        light_mix = both_round(light_attention(light_query, light_key, light_value, segment_ids))
        query_rows = global_rows(route_query[micro_index])
        key_rows = global_rows(route_key[micro_index])
        query_score = jax.nn.sigmoid(lax.optimization_barrier(jnp.sum(normed[query_rows] * router_w[0], axis=-1)))
        key_score = jax.nn.sigmoid(lax.optimization_barrier(jnp.sum(normed[key_rows] * router_w[1], axis=-1)))
        heavy_query = both_round(matmul(normed_low[query_rows], attn_w[3]))
        heavy_key = both_round(matmul(normed_low[key_rows], attn_w[4]))
        raw_value = low_back(matmul(normed_low[key_rows], attn_w[5]))
        heavy_value = both_round(raw_value * key_score[:, None])
        heavy_mix = both_round(heavy_attention(heavy_query, heavy_key, heavy_value, segment_ids[query_rows], segment_ids[key_rows]))
        heavy_proj = low_back(matmul(heavy_mix, attn_out_w[1]))
        attn_total = matmul(light_mix, attn_out_w[0]).at[query_rows].add(query_score[:, None] * heavy_proj)
        middle = inputs + low_back(attn_total)
        normed_two = rms_norm(middle, gain_w[1])
        low_two = low(normed_two)
        light_gate = low_back(matmul(low_two, light_in_w[0]))
        light_up = low_back(matmul(low_two, light_in_w[1]))
        hidden = low(jax.nn.gelu(light_gate) * light_up)
        ffn_rows = global_rows(route_ffn[micro_index])
        ffn_score = jax.nn.sigmoid(lax.optimization_barrier(jnp.sum(normed_two[ffn_rows] * router_w[2], axis=-1)))
        rows_low = low_two[ffn_rows]
        heavy_gate = low_back(matmul(rows_low, heavy_in_w[0]))
        heavy_up = low_back(matmul(rows_low, heavy_in_w[1]))
        heavy_hidden = low(jax.nn.gelu(heavy_gate) * heavy_up)
        heavy_ffn = low_back(matmul(heavy_hidden, heavy_out_w))
        ffn_total = matmul(hidden, light_out_w).at[ffn_rows].add(ffn_score[:, None] * heavy_ffn)
        results.append(middle + ffn_total)
    return jnp.stack(results)

def finish_update(weight, update, axes):
    rms_update = jnp.sqrt(lax.optimization_barrier(jnp.mean(update * update, axis=axes, keepdims=True)))
    rms_weight = jnp.sqrt(lax.optimization_barrier(jnp.mean(weight * weight, axis=axes, keepdims=True)))
    step_size = step_rate * jnp.maximum(scale_floor, rms_weight) / jnp.maximum(1.0, rms_update / clip_level)
    return weight - step_size * update

def factored_update(weight, gradient, row_old, col_old):
    decay_rate = 1.0 - STEP ** (-0.8)
    square = gradient * gradient + tiny_square
    row_new = decay_rate * row_old + (1.0 - decay_rate) * lax.optimization_barrier(jnp.mean(square, axis=-1))
    col_new = decay_rate * col_old + (1.0 - decay_rate) * lax.optimization_barrier(jnp.mean(square, axis=-2))
    row_mean = lax.optimization_barrier(jnp.mean(row_new, axis=-1))[..., None, None]
    update = gradient * lax.rsqrt(row_new[..., :, None] * col_new[..., None, :] / row_mean)
    return (finish_update(weight, update, (-2, -1)), row_new, col_new)

def vector_update(weight, gradient, second_old):
    decay_rate = 1.0 - STEP ** (-0.8)
    second_new = decay_rate * second_old + (1.0 - decay_rate) * (gradient * gradient + tiny_square)
    update = gradient * lax.rsqrt(second_new)
    return (finish_update(weight, update, (-1,)), second_new)

def reference(tokens, cotangent, segments, route_query, route_key, route_ffn, attn_in, attn_out, light_in, light_out, heavy_in, heavy_out, gains, router, row_attn_in, col_attn_in, row_attn_out, col_attn_out, row_light_in, col_light_in, row_light_out, col_light_out, row_heavy_in, col_heavy_in, row_heavy_out, col_heavy_out, second_gains, second_router):
    params = (attn_in, attn_out, light_in, light_out, heavy_in, heavy_out, gains, router)

    def forward(inputs_all, weights):
        return layer(inputs_all, weights, segments, route_query, route_key, route_ffn)
    result, pullback = jax.vjp(forward, tokens.astype(jnp.float32), params)
    grad_tokens, gradients = pullback(cotangent.astype(jnp.float32))
    grad_attn_in, grad_attn_out, grad_light_in, grad_light_out, grad_heavy_in, grad_heavy_out, grad_gains, grad_router = gradients
    new_attn_in, rows_attn_in, cols_attn_in = factored_update(attn_in, grad_attn_in, row_attn_in, col_attn_in)
    new_attn_out, rows_attn_out, cols_attn_out = factored_update(attn_out, grad_attn_out, row_attn_out, col_attn_out)
    new_light_in, rows_light_in, cols_light_in = factored_update(light_in, grad_light_in, row_light_in, col_light_in)
    new_light_out, rows_light_out, cols_light_out = factored_update(light_out, grad_light_out, row_light_out, col_light_out)
    new_heavy_in, rows_heavy_in, cols_heavy_in = factored_update(heavy_in, grad_heavy_in, row_heavy_in, col_heavy_in)
    new_heavy_out, rows_heavy_out, cols_heavy_out = factored_update(heavy_out, grad_heavy_out, row_heavy_out, col_heavy_out)
    new_gains, moment_gains = vector_update(gains, grad_gains, second_gains)
    new_router, moment_router = vector_update(router, grad_router, second_router)
    return (result.astype(jnp.bfloat16), grad_tokens, grad_attn_in, rows_attn_in, cols_attn_in, new_attn_in, grad_attn_out, rows_attn_out, cols_attn_out, new_attn_out, grad_light_in, rows_light_in, cols_light_in, new_light_in, grad_light_out, rows_light_out, cols_light_out, new_light_out, grad_heavy_in, rows_heavy_in, cols_heavy_in, new_heavy_in, grad_heavy_out, rows_heavy_out, cols_heavy_out, new_heavy_out, grad_gains, moment_gains, new_gains, grad_router, moment_router, new_router)
```

```python
import functools
import math

import jax
import jax.numpy as jnp
from jax import lax
from jax.experimental import pallas as pl
from jax.experimental.pallas import tpu as pltpu
from jax.sharding import PartitionSpec as P

D = 768
LH = 8
LDH = 96
HH = 12
HDH = 64
WIN = 128
STEP = 10

norm_eps = 1e-06
tiny_square = 1e-30
scale_floor = 0.001
clip_level = 1.0
step_rate = 0.5
masked_score = -1e30
gelu_scale = math.sqrt(2.0 / math.pi)
gelu_cubic = 0.044715

low = jnp.bfloat16
wide = jnp.float32
CHUNK = 256
BLOCK = 128
RADIUS = WIN // 2
KEYS = 1024
VMEM_BYTES = 60 * 1024 * 1024


def nn(left, right):
    return lax.dot_general(left, right, (((1,), (0,)), ((), ())), preferred_element_type=wide)


def nt(left, right):
    return lax.dot_general(left, right, (((1,), (1,)), ((), ())), preferred_element_type=wide)


def tn(left, right):
    return lax.dot_general(left, right, (((0,), (0,)), ((), ())), preferred_element_type=wide)


def sigmoid(logit):
    return 1.0 / (1.0 + jnp.exp(-logit))


def gelu_pair(gate):
    squared = gate * gate
    bent = jnp.tanh(gelu_scale * gate * (1.0 + gelu_cubic * squared))
    half = 0.5 * (1.0 + bent)
    value = gate * half
    slope = half + 0.5 * gate * (1.0 - bent * bent) * gelu_scale * (1.0 + 3.0 * gelu_cubic * squared)
    return value, slope


def picks_rows(idx_col, count):
    spots = lax.broadcasted_iota(jnp.int32, (idx_col.shape[0], count), 1)
    return (spots == idx_col).astype(low)


def picks_cols(idx_row, start, count):
    spots = lax.broadcasted_iota(jnp.int32, (count, idx_row.shape[1]), 0) + start
    return (spots == idx_row).astype(low)


def head_mask(width, size, head):
    spot = lax.broadcasted_iota(jnp.int32, (1, width), 1)
    return ((spot >= head * size) & (spot < (head + 1) * size)).astype(low)


def softmax_parts(scores, allowed):
    masked = jnp.where(allowed, scores, masked_score)
    top = jnp.max(masked, axis=-1, keepdims=True)
    grown = jnp.exp(masked - top)
    return grown * (1.0 / jnp.sum(grown, axis=-1, keepdims=True))


def inverse_rms(values):
    return lax.rsqrt(jnp.mean(values * values, axis=-1, keepdims=True) + norm_eps)


def norm_back(values, gain_row, upstream):
    inverse = inverse_rms(values)
    unit = values * inverse
    scaled = upstream * gain_row
    pulled = inverse * (scaled - unit * jnp.mean(scaled * unit, axis=-1, keepdims=True))
    return pulled, jnp.sum(upstream * unit, axis=0, keepdims=True)


def in_vmem(shape, dtype):
    return jax.ShapeDtypeStruct(shape, dtype)


def kernel_call(body, outs, scratch, args, scalars=0, flops=0):
    vmem = pl.BlockSpec(memory_space=pltpu.VMEM)
    smem = pl.BlockSpec(memory_space=pltpu.SMEM)
    moved = sum(a.size * a.dtype.itemsize for a in args) + sum(
        math.prod(o.shape) * jnp.dtype(o.dtype).itemsize for o in outs
    )
    return pl.pallas_call(
        body,
        out_shape=outs,
        in_specs=[smem] * scalars + [vmem] * (len(args) - scalars),
        out_specs=[vmem] * len(outs),
        scratch_shapes=scratch,
        compiler_params=pltpu.CompilerParams(vmem_limit_bytes=VMEM_BYTES),
        cost_estimate=pl.CostEstimate(flops=flops, bytes_accessed=moved, transcendentals=0),
    )(*args)


def mp_total(core, first_ref, second_ref, near_ref, far_ref, chunk, per_half):
    rows = pl.ds(pl.multiple_of(chunk * CHUNK, CHUNK), CHUNK)
    mine = (first_ref[rows, :].astype(wide) + second_ref[rows, :].astype(wide)).astype(low)
    inner = pl.ds(pl.multiple_of((chunk % per_half) * CHUNK, CHUNK), CHUNK)
    flag = ((chunk // per_half) == core).astype(wide)
    other = near_ref[inner, :].astype(wide) * flag + far_ref[inner, :].astype(wide) * (1.0 - flag)
    return mine.astype(wide) + other


def unpack_body(got_ref, w_in_ref, w_out_ref, key_ref, vec_ref):
    count, _, lane = got_ref.shape
    in_rows = w_in_ref.shape[1] // count
    head_cols = w_in_ref.shape[2]
    for j in range(3):
        pair = got_ref[:, j * in_rows : (j + 1) * in_rows, :].reshape(count * in_rows, lane)
        w_in_ref[2 * j] = pair[:, :head_cols]
        w_in_ref[2 * j + 1] = pair[:, head_cols:]
    base = 3 * in_rows
    out_rows = w_out_ref.shape[1] // count
    sides = w_out_ref.shape[2] // lane
    for j in range(sides):
        cols = slice(j * lane, (j + 1) * lane)
        blocks = [
            got_ref[d, base + j * 2 * out_rows : base + (j + 1) * 2 * out_rows, :].astype(wide)
            for d in range(count)
        ]
        for s in range(2):
            w_out_ref[s, :, cols] = jnp.concatenate(
                [b[s * out_rows : (s + 1) * out_rows] for b in blocks], axis=0
            ).astype(low)
    base = base + 2 * out_rows * sides
    _, micros, quarter, _ = key_ref.shape
    for j in range(sides):
        cols = slice(j * lane, (j + 1) * lane)
        for m in range(micros):
            at = base + (j * micros + m) * quarter
            key_ref[:, m, :, cols] = got_ref[:, at : at + quarter, :]
    base = base + sides * micros * quarter
    vec_ref[...] = jnp.concatenate(
        [got_ref[d, base : base + 16, :].astype(wide)[:8, :in_rows] for d in range(count)], axis=1
    )


def block_of(ref, base, index, full):
    count = ref.shape[0]
    rows = full // count
    at = base // count + index * rows
    return ref[:, at : at + rows, :].reshape(full, CHUNK)


def part_of(ref, base, index, full, piece):
    count = ref.shape[0]
    rows = full // count
    at = base // count + index * rows
    if rows <= CHUNK:
        span = CHUNK // rows
        return ref[piece * span : (piece + 1) * span, at : at + rows, :].reshape(CHUNK, CHUNK)
    return ref[0, at + piece * CHUNK : at + (piece + 1) * CHUNK, :]


def ffn_bases(width, light, heavy):
    sides = width // CHUNK
    light_in = 2 * (light // CHUNK) * width
    light_out = sides * light
    heavy_in = 2 * (heavy // CHUNK) * width
    bases = [0, light_in, light_in + light_out, light_in + light_out + heavy_in]
    return bases, bases[3] + sides * heavy


def project_body(
    tok_ref, vec_ref, w_ref, qcol_ref, kcol_ref,
    n1b_ref, q_ref, k_ref, v_ref, hq_ref, sq_ref, nq_ref, nk_ref,
    qrows_ref, low_ref,
):
    count = tok_ref.shape[1]
    micros = tok_ref.shape[0]
    for m in range(micros):

        def step(c, carry):
            rows = pl.ds(pl.multiple_of(c * CHUNK, CHUNK), CHUNK)
            values = tok_ref[m, rows, :].astype(wide)
            normed = values * inverse_rms(values) * vec_ref[0:1, :]
            high = normed.astype(low)
            n1b_ref[m, rows, :] = high
            low_ref[rows, :] = (normed - high.astype(wide)).astype(low)
            q_ref[m, rows, :] = nn(high, w_ref[0]).astype(low)
            k_ref[m, rows, :] = nn(high, w_ref[1]).astype(low)
            v_ref[m, rows, :] = nn(high, w_ref[2]).astype(low)
            return carry

        lax.fori_loop(0, count // CHUNK, step, 0)
        picks = picks_rows(qcol_ref[m], count)
        query_rows = nn(picks, n1b_ref[m])
        query_wide = query_rows + nn(picks, low_ref[...])
        qrows_ref[m] = query_rows.astype(low)
        nq_ref[m] = query_wide
        hq_ref[m] = nn(query_rows.astype(low), w_ref[3]).astype(low)
        sq_ref[m] = sigmoid(jnp.sum(query_wide * vec_ref[2:3, :], axis=-1, keepdims=True))
        picks = picks_rows(kcol_ref[m], count)
        nk_ref[m] = nn(picks, n1b_ref[m]) + nn(picks, low_ref[...])


def keys_body(o_ref, a_ref, b_ref, c_ref, vec_ref, w_ref, n_ref, k_ref, v_ref, sk_ref):
    blocks, _, part, width = o_ref.shape
    for p, ref in enumerate((o_ref, a_ref, b_ref, c_ref)):
        values = ref[:, 0].reshape(blocks * part, width).astype(wide)
        normed = values * inverse_rms(values) * vec_ref[0:1, :]
        high = normed.astype(low)
        score = sigmoid(jnp.sum(normed * vec_ref[3:4, :], axis=-1, keepdims=True))
        n_ref[0, :, p] = high.reshape(blocks, part, width)
        sk_ref[0, :, p] = score.reshape(blocks, part, 1)
        k_ref[0, :, p] = nn(high, w_ref[4]).astype(low).reshape(blocks, part, -1)
        v_ref[0, :, p] = (nn(high, w_ref[5]) * score).astype(low).reshape(blocks, part, -1)


def fill_extended(ext_ref, prev, inner, after):
    count = inner.shape[0]
    ext_ref[0:RADIUS, :] = prev
    ext_ref[RADIUS : RADIUS + count, :] = inner
    ext_ref[RADIUS + count :, :] = after


def near_mask(seg_q, seg_k):
    shape = (BLOCK, 2 * BLOCK)
    gap = lax.broadcasted_iota(jnp.int32, shape, 1) - lax.broadcasted_iota(jnp.int32, shape, 0)
    return (gap >= 0) & (gap <= 2 * RADIUS) & (seg_q == seg_k)


def attend_body(
    q_ref, k_ref, v_ref, prev_ref, after_ref, hq_ref, hk_ref, hv_ref, sq_ref, wo_ref,
    qrow_ref, segq_ref, segk_ref, hsegq_ref, hsegk_ref,
    part_ref, lmix_ref, hmix_ref, hproj_ref,
    kx_ref, vx_ref, rows_ref,
):
    count, width = q_ref.shape
    light_heads = width // LDH
    heavy_heads = width // HDH
    fill_extended(kx_ref, prev_ref[0], k_ref[...], after_ref[0])
    fill_extended(vx_ref, prev_ref[1], v_ref[...], after_ref[1])
    allowed = hsegq_ref[...] == hsegk_ref[...]
    mix = jnp.zeros((hq_ref.shape[0], width), wide)
    for h in range(heavy_heads):
        mask = head_mask(width, HDH, h)
        probs = softmax_parts(nt(hq_ref[...], hk_ref[...] * mask) * (1.0 / math.sqrt(HDH)), allowed)
        mix = mix + nn(probs.astype(low), hv_ref[...] * mask)
    mix_low = mix.astype(low)
    hmix_ref[...] = mix_low
    proj = nn(mix_low, wo_ref[1])
    hproj_ref[...] = proj
    rows_ref[...] = (sq_ref[...] * proj).astype(low)

    def step(b, carry):
        rows = pl.ds(pl.multiple_of(b * BLOCK, BLOCK), BLOCK)
        keys = pl.ds(pl.multiple_of(b * BLOCK, BLOCK), 2 * BLOCK)
        seg_k = jnp.concatenate([segk_ref[b], segk_ref[b + 1]], axis=1)
        near = near_mask(segq_ref[rows, :], seg_k)
        queries = q_ref[rows, :]
        block_keys = kx_ref[keys, :]
        block_values = vx_ref[keys, :]
        total = jnp.zeros((BLOCK, width), wide)
        for h in range(light_heads):
            mask = head_mask(width, LDH, h)
            probs = softmax_parts(nt(queries, block_keys * mask) * (1.0 / math.sqrt(LDH)), near)
            total = total + nn(probs.astype(low), block_values * mask)
        total_low = total.astype(low)
        lmix_ref[rows, :] = total_low
        spread = picks_cols(qrow_ref[...], b * BLOCK, BLOCK)
        part_ref[rows, :] = (nn(total_low, wo_ref[0]) + nn(spread, rows_ref[...])).astype(low)
        return carry

    lax.fori_loop(0, count // BLOCK, step, 0)


def ffn_body(
    core_ref, first_ref, second_ref, near_ref, far_ref, tok_ref, cot_ref, vec_ref,
    fcol_ref, frow_ref, w_ref,
    middle_ref, y_ref, g_ref, n2b_ref, hidden_ref, dgu_ref, frows_ref, hhid_ref, dhgu_ref, dhout_ref,
    router_ref,
    low_ref, out_rows_ref, grad_rows_ref,
):
    count, width = tok_ref.shape
    chunks = count // CHUNK
    core = core_ref[0]
    light = hidden_ref.shape[1]
    heavy = hhid_ref.shape[1]
    sides = width // CHUNK
    bases, _ = ffn_bases(width, light, heavy)

    def heavy_in(s, j):
        return block_of(w_ref, bases[2], s * (heavy // CHUNK) + j, width)

    def heavy_out(t, j):
        return part_of(w_ref, bases[3], t, heavy, j)

    def light_in(s):
        return block_of(w_ref, bases[0], s, width)

    def light_out(t):
        return block_of(w_ref, bases[1], t, light)

    def enter(c, carry):
        rows = pl.ds(pl.multiple_of(c * CHUNK, CHUNK), CHUNK)
        middle = tok_ref[rows, :].astype(wide) + mp_total(
            core, first_ref, second_ref, near_ref, far_ref, c, chunks // 2
        )
        middle_ref[rows, :] = middle
        normed = middle * inverse_rms(middle) * vec_ref[1:2, :]
        high = normed.astype(low)
        n2b_ref[rows, :] = high
        low_ref[rows, :] = (normed - high.astype(wide)).astype(low)
        return carry

    lax.fori_loop(0, chunks, enter, 0)
    picks = picks_rows(fcol_ref[...], count)
    rows_high = nn(picks, n2b_ref[...])
    rows_wide = rows_high + nn(picks, low_ref[...])
    rows_low = rows_high.astype(low)
    frows_ref[...] = rows_low
    score = sigmoid(jnp.sum(rows_wide * vec_ref[4:5, :], axis=-1, keepdims=True))
    cot_rows = nn(picks, cot_ref[...])
    grad_out = (score * cot_rows).astype(low)
    dhout_ref[...] = grad_out
    out_rows = [jnp.zeros((rows_low.shape[0], CHUNK), wide) for _ in range(sides)]
    grad_rows = jnp.zeros(rows_low.shape, wide)
    for j in range(heavy // CHUNK):
        cols = slice(j * CHUNK, (j + 1) * CHUNK)
        gate = nn(rows_low, heavy_in(0, j))
        up = nn(rows_low, heavy_in(1, j))
        value, slope = gelu_pair(gate)
        hid = (value * up).astype(low)
        hhid_ref[:, cols] = hid
        grad_hid = jnp.zeros_like(gate)
        for t in range(sides):
            piece = heavy_out(t, j)
            out_rows[t] = out_rows[t] + nn(hid, piece)
            grad_hid = grad_hid + nt(grad_out[:, t * CHUNK : (t + 1) * CHUNK], piece)
        grad_gate = (grad_hid * up * slope).astype(low)
        grad_up = (grad_hid * value).astype(low)
        dhgu_ref[0, :, cols] = grad_gate
        dhgu_ref[1, :, cols] = grad_up
        grad_rows = grad_rows + nt(grad_gate, heavy_in(0, j)) + nt(grad_up, heavy_in(1, j))
    out_rows = jnp.concatenate(out_rows, axis=1)
    logit = jnp.sum(cot_rows * out_rows, axis=-1, keepdims=True) * score * (1.0 - score)
    router_ref[...] = jnp.sum(logit * rows_wide, axis=0, keepdims=True)
    out_rows_ref[...] = (score * out_rows).astype(low)
    grad_rows_ref[...] = (grad_rows + logit * vec_ref[4:5, :]).astype(low)

    def light_rows(c, carry):
        rows = pl.ds(pl.multiple_of(c * CHUNK, CHUNK), CHUNK)
        normed = n2b_ref[rows, :]
        gate = nn(normed, light_in(0))
        up = nn(normed, light_in(1))
        value, slope = gelu_pair(gate)
        hid = (value * up).astype(low)
        hidden_ref[rows, :] = hid
        spread = picks_cols(frow_ref[...], c * CHUNK, CHUNK)
        spread_out = nn(spread, out_rows_ref[...])
        grad_hid = jnp.zeros_like(gate)
        for t in range(sides):
            cols = slice(t * CHUNK, (t + 1) * CHUNK)
            y_ref[rows, cols] = (nn(hid, light_out(t)) + spread_out[:, cols]).astype(low)
            grad_hid = grad_hid + nt(cot_ref[rows, cols], light_out(t))
        grad_gate = (grad_hid * up * slope).astype(low)
        grad_up = (grad_hid * value).astype(low)
        dgu_ref[0, rows, :] = grad_gate
        dgu_ref[1, rows, :] = grad_up
        g_ref[rows, :] = (
            nt(grad_gate, light_in(0)) + nt(grad_up, light_in(1)) + nn(spread, grad_rows_ref[...])
        ).astype(low)
        return carry

    lax.fori_loop(0, chunks, light_rows, 0)


def ffn_grads_body(cot_ref, *refs):
    out_ref, turned_ref, rows_ref = refs[-3:]
    micros, tokens, width = cot_ref.shape
    groups = [refs[7 * m : 7 * m + 7] for m in range(micros)]
    count = out_ref.shape[0]
    light = groups[0][1].shape[1]
    heavy = groups[0][4].shape[1]
    routed = groups[0][3].shape[0]
    sides = width // CHUNK
    bases, _ = ffn_bases(width, light, heavy)

    def put(base, index, value):
        rows = value.shape[0] // count
        at = base // count + index * rows
        out_ref[:, at : at + rows, :] = value.astype(low).reshape(count, rows, CHUNK)

    light_out = jnp.zeros((light, width), wide)
    for m, group in enumerate(groups):
        turned_ref[:, m * tokens : (m + 1) * tokens] = group[0][...].T
        rows_ref[:, m * routed : (m + 1) * routed] = group[3][...].T
        light_out = light_out + tn(group[1][...], cot_ref[m])
    for t in range(sides):
        put(bases[1], t, light_out[:, t * CHUNK : (t + 1) * CHUNK])
    for s in range(2):
        total = jnp.zeros((width, CHUNK), wide)
        for m, group in enumerate(groups):
            total = total + nn(turned_ref[:, m * tokens : (m + 1) * tokens], group[2][s])
        put(bases[0], s, total)
    pieces = heavy // CHUNK
    for s in range(2):
        for j in range(pieces):
            total = jnp.zeros((width, CHUNK), wide)
            for m, group in enumerate(groups):
                total = total + nn(
                    rows_ref[:, m * routed : (m + 1) * routed],
                    group[5][s, :, j * CHUNK : (j + 1) * CHUNK],
                )
            put(bases[2], s * pieces + j, total)
    for t in range(sides):
        cols = slice(t * CHUNK, (t + 1) * CHUNK)
        total = jnp.zeros((heavy, CHUNK), wide)
        for m, group in enumerate(groups):
            total = total + tn(group[4][...], group[6][:, cols])
        put(bases[3], t, total)


def attend_back_body(
    core_ref, first_ref, second_ref, near_ref, far_ref, middle_ref, cot_ref, vec_ref,
    q_ref, k_ref, v_ref, prev_ref, after_ref, hq_ref, hk_ref, hv_ref, sk_ref, sq_ref, hproj_ref, wo_ref,
    qcol_ref, segq_ref, segk_ref, hsegq_ref, hsegk_ref,
    gmid_ref, agl_ref, gain_ref, dq_ref, inner_ref, edges_ref, dhq_ref, dhk_ref, dhv_ref, draw_ref,
    dproj_ref, logit_ref,
    kx_ref, vx_ref, dmix_ref, dkx_ref, dvx_ref,
):
    count, width = q_ref.shape
    chunks = count // CHUNK
    light_heads = width // LDH
    heavy_heads = width // HDH
    core = core_ref[0]
    fill_extended(kx_ref, prev_ref[0], k_ref[...], after_ref[0])
    fill_extended(vx_ref, prev_ref[1], v_ref[...], after_ref[1])
    gain_ref[...] = jnp.zeros_like(gain_ref)

    def enter(c, carry):
        rows = pl.ds(pl.multiple_of(c * CHUNK, CHUNK), CHUNK)
        upstream = mp_total(core, first_ref, second_ref, near_ref, far_ref, c, chunks // 2)
        pulled, gain = norm_back(middle_ref[rows, :], vec_ref[1:2, :], upstream)
        gain_ref[...] += gain
        grad_middle = cot_ref[rows, :].astype(wide) + pulled
        gmid_ref[rows, :] = grad_middle
        grad_low = grad_middle.astype(low)
        agl_ref[rows, :] = grad_low
        dmix_ref[rows, :] = nt(grad_low, wo_ref[0]).astype(low)
        return carry

    lax.fori_loop(0, chunks, enter, 0)

    picks = picks_rows(qcol_ref[...], count)
    grad_rows = nn(picks, agl_ref[...])
    score = sq_ref[...]
    dproj = (score * grad_rows).astype(low)
    dproj_ref[...] = dproj
    logit_ref[...] = (
        jnp.sum(grad_rows * hproj_ref[...], axis=-1, keepdims=True) * score * (1.0 - score)
    )
    dmix = nt(dproj, wo_ref[1]).astype(low)
    scale = 1.0 / math.sqrt(HDH)
    key_count = hk_ref.shape[0]
    if key_count <= KEYS:
        allowed = hsegq_ref[...] == hsegk_ref[...]
        dq = jnp.zeros((hq_ref.shape[0], width), wide)
        dk = jnp.zeros((key_count, width), wide)
        dv = jnp.zeros((key_count, width), wide)
        for h in range(heavy_heads):
            mask = head_mask(width, HDH, h)
            keys = hk_ref[...] * mask
            probs = softmax_parts(nt(hq_ref[...], keys) * scale, allowed)
            grad_soft = nt(dmix, hv_ref[...] * mask)
            centre = jnp.sum(probs * grad_soft, axis=-1, keepdims=True)
            grad_scores = (probs * (grad_soft - centre)).astype(low)
            dq = dq + nn(grad_scores, keys)
            dk = dk + tn(grad_scores, hq_ref[...] * mask)
            dv = dv + tn(probs.astype(low), dmix * mask)
        dhk_ref[...] = (dk * scale).astype(low)
        dhv_ref[...] = dv.astype(low)
        draw_ref[...] = (dv * sk_ref[...]).astype(low)
    else:
        pieces = key_count // KEYS

        def piece_of(c, mask):
            spots = pl.ds(pl.multiple_of(c * KEYS, KEYS), KEYS)
            allowed = hsegq_ref[...] == hsegk_ref[:, spots]
            keys = hk_ref[spots, :] * mask
            scores = jnp.where(allowed, nt(hq_ref[...], keys) * scale, masked_score)
            return spots, keys, scores, nt(dmix, hv_ref[spots, :] * mask)

        blank = jnp.zeros((hq_ref.shape[0], 1), wide)
        stats = []
        for h in range(heavy_heads):
            mask = head_mask(width, HDH, h)

            def find_top(c, top):
                return jnp.maximum(top, jnp.max(piece_of(c, mask)[2], axis=-1, keepdims=True))

            top = lax.fori_loop(0, pieces, find_top, blank + masked_score)

            def add_up(c, sums):
                _, _, scores, grad_soft = piece_of(c, mask)
                grown = jnp.exp(scores - top)
                return (
                    sums[0] + jnp.sum(grown, axis=-1, keepdims=True),
                    sums[1] + jnp.sum(grown * grad_soft, axis=-1, keepdims=True),
                )

            total, moment = lax.fori_loop(0, pieces, add_up, (blank, blank))
            stats.append((mask, top, 1.0 / total, moment / total))

        def pull(c, dq):
            dk = jnp.zeros((KEYS, width), wide)
            dv = jnp.zeros((KEYS, width), wide)
            for mask, top, inverse, centre in stats:
                spots, keys, scores, grad_soft = piece_of(c, mask)
                probs = jnp.exp(scores - top) * inverse
                grad_scores = (probs * (grad_soft - centre)).astype(low)
                dq = dq + nn(grad_scores, keys)
                dk = dk + tn(grad_scores, hq_ref[...] * mask)
                dv = dv + tn(probs.astype(low), dmix * mask)
            dhk_ref[spots, :] = (dk * scale).astype(low)
            dhv_ref[spots, :] = dv.astype(low)
            draw_ref[spots, :] = (dv * sk_ref[spots, :]).astype(low)
            return dq

        dq = lax.fori_loop(0, pieces, pull, jnp.zeros((hq_ref.shape[0], width), wide))
    dhq_ref[...] = (dq * scale).astype(low)

    dkx_ref[...] = jnp.zeros_like(dkx_ref)
    dvx_ref[...] = jnp.zeros_like(dvx_ref)
    light_scale = 1.0 / math.sqrt(LDH)

    def step(b, carry):
        rows = pl.ds(pl.multiple_of(b * BLOCK, BLOCK), BLOCK)
        spans = pl.ds(pl.multiple_of(b * BLOCK, BLOCK), 2 * BLOCK)
        seg_k = jnp.concatenate([segk_ref[b], segk_ref[b + 1]], axis=1)
        near = near_mask(segq_ref[rows, :], seg_k)
        queries = q_ref[rows, :]
        block_keys = kx_ref[spans, :]
        block_values = vx_ref[spans, :]
        mix = dmix_ref[rows, :]
        grad_q = jnp.zeros((BLOCK, width), wide)
        grad_k = jnp.zeros((2 * BLOCK, width), wide)
        grad_v = jnp.zeros((2 * BLOCK, width), wide)
        for h in range(light_heads):
            mask = head_mask(width, LDH, h)
            keys = block_keys * mask
            probs = softmax_parts(nt(queries, keys) * light_scale, near)
            grad_soft = nt(mix, block_values * mask)
            centre = jnp.sum(probs * grad_soft, axis=-1, keepdims=True)
            grad_scores = (probs * (grad_soft - centre)).astype(low)
            grad_q = grad_q + nn(grad_scores, keys)
            grad_k = grad_k + tn(grad_scores, queries * mask)
            grad_v = grad_v + tn(probs.astype(low), mix * mask)
        dq_ref[rows, :] = (grad_q * light_scale).astype(low)
        dkx_ref[spans, :] += grad_k * light_scale
        dvx_ref[spans, :] += grad_v
        return carry

    lax.fori_loop(0, count // BLOCK, step, 0)
    for s, ref in enumerate((dkx_ref, dvx_ref)):
        inner_ref[s] = ref[RADIUS : RADIUS + count, :]
        edges_ref[0, s] = ref[RADIUS + count :, :].astype(low)
        edges_ref[1, s] = ref[:RADIUS, :].astype(low)


def project_back_body(
    dq_ref, inner_ref, prev_ref, after_ref, dhq_ref, logit_ref, owned_ref, nq_ref, nk_ref, vec_ref, w_ref,
    qrow_ref, krow_ref,
    part_ref, dkv_ref, router_ref,
    rows_ref,
):
    count, width = dq_ref.shape
    routed = dhq_ref.shape[0]
    sources = owned_ref.shape[0]
    for s in range(2):
        dkv_ref[s, RADIUS : count - RADIUS, :] = inner_ref[s, RADIUS : count - RADIUS, :].astype(low)
        dkv_ref[s, :RADIUS, :] = (inner_ref[s, :RADIUS, :] + prev_ref[s].astype(wide)).astype(low)
        dkv_ref[s, count - RADIUS :, :] = (
            inner_ref[s, count - RADIUS :, :] + after_ref[s].astype(wide)
        ).astype(low)
    owned = owned_ref[0].astype(wide)
    for s in range(1, sources):
        owned = owned + owned_ref[s].astype(wide)
    grad_k = owned[:, :width]
    grad_v = owned[:, width:]
    grad_v = grad_v.astype(low).astype(wide)
    key_wide = nk_ref[...]
    raw = nn(key_wide.astype(low), w_ref[5])
    score = sigmoid(jnp.sum(key_wide * vec_ref[3:4, :], axis=-1, keepdims=True))
    key_logit = jnp.sum(grad_v * raw, axis=-1, keepdims=True) * score * (1.0 - score)
    grad_raw = (grad_v * score).astype(low)
    query_logit = logit_ref[...]
    router_ref[0:1, :] = jnp.sum(query_logit * nq_ref[...], axis=0, keepdims=True)
    router_ref[1:2, :] = jnp.sum(key_logit * key_wide, axis=0, keepdims=True)
    rows_ref[0:routed, :] = (nt(dhq_ref[...], w_ref[3]) + query_logit * vec_ref[2:3, :]).astype(low)
    rows_ref[routed:, :] = (
        nt(grad_k.astype(low), w_ref[4]) + nt(grad_raw, w_ref[5]) + key_logit * vec_ref[3:4, :]
    ).astype(low)

    def step(c, carry):
        rows = pl.ds(pl.multiple_of(c * CHUNK, CHUNK), CHUNK)
        spread = jnp.concatenate(
            [picks_cols(qrow_ref[...], c * CHUNK, CHUNK), picks_cols(krow_ref[...], c * CHUNK, CHUNK)],
            axis=1,
        )
        part_ref[rows, :] = (
            nt(dq_ref[rows, :], w_ref[0])
            + nt(dkv_ref[0, rows, :], w_ref[1])
            + nt(dkv_ref[1, rows, :], w_ref[2])
            + nn(spread, rows_ref[...])
        ).astype(low)
        return carry

    lax.fori_loop(0, count // CHUNK, step, 0)


def finish_body(core_ref, *refs):
    micros = (len(refs) - 4) // 5
    pieces = refs[: 4 * micros]
    grads = refs[4 * micros : 5 * micros]
    tok_ref, vec_ref, out_ref, gain_ref = refs[5 * micros :]
    chunks = tok_ref.shape[1] // CHUNK
    core = core_ref[0]
    gain_ref[...] = jnp.zeros_like(gain_ref)
    for m in range(micros):
        first_ref, second_ref, near_ref, far_ref = pieces[4 * m : 4 * m + 4]

        def step(c, carry):
            rows = pl.ds(pl.multiple_of(c * CHUNK, CHUNK), CHUNK)
            upstream = mp_total(core, first_ref, second_ref, near_ref, far_ref, c, chunks // 2)
            pulled, gain = norm_back(tok_ref[m, rows, :].astype(wide), vec_ref[0:1, :], upstream)
            gain_ref[...] += gain
            out_ref[m, rows, :] = grads[m][rows, :] + pulled
            return carry

        lax.fori_loop(0, chunks, step, 0)


def join_body(core_ref, *refs):
    out_ref = refs[-1]
    micros = out_ref.shape[0]
    chunks = out_ref.shape[1] // CHUNK
    core = core_ref[0]
    for m in range(micros):
        middle_ref, first_ref, second_ref, near_ref, far_ref = refs[5 * m : 5 * m + 5]

        def step(c, carry):
            rows = pl.ds(pl.multiple_of(c * CHUNK, CHUNK), CHUNK)
            total = mp_total(core, first_ref, second_ref, near_ref, far_ref, c, chunks // 2)
            out_ref[m, rows, :] = (middle_ref[rows, :] + total).astype(low)
            return carry

        lax.fori_loop(0, chunks, step, 0)


def attn_grads_body(normed_ref, query_ref, key_ref, *refs):
    micros, tokens, width = normed_ref.shape
    outs = refs[9 * micros : -2]
    turned_ref, other_ref = refs[-2:]
    groups = [refs[9 * m : 9 * m + 9] for m in range(micros)]
    keys = key_ref.shape[1]
    grads = []
    for m in range(micros):
        turned_ref[:, m * tokens : (m + 1) * tokens] = normed_ref[m].T
    for s in range(3):
        total = 0.0
        for m, group in enumerate(groups):
            grad = group[0][...] if s == 0 else group[1][s - 1]
            total = total + nn(turned_ref[:, m * tokens : (m + 1) * tokens], grad)
        grads.append(total)
    total = 0.0
    for m, group in enumerate(groups):
        total = total + tn(query_ref[m], group[2][...])
    grads.append(total)
    for m in range(micros):
        other_ref[:, m * keys : (m + 1) * keys] = key_ref[m].T
    for s in (3, 4):
        total = 0.0
        for m, group in enumerate(groups):
            total = total + nn(other_ref[:, m * keys : (m + 1) * keys], group[s][...])
        grads.append(total)
    out_grads = []
    for mix, grad in ((5, 6), (7, 8)):
        total = 0.0
        for group in groups:
            total = total + tn(group[mix][...], group[grad][...])
        out_grads.append(total)
    (out_ref,) = outs
    count, _, lane = out_ref.shape
    in_rows = width // count
    for j in range(3):
        pair = jnp.concatenate([grads[2 * j], grads[2 * j + 1]], axis=1).astype(low)
        out_ref[:, j * in_rows : (j + 1) * in_rows, :] = pair.reshape(count, in_rows, lane)
    out_rows = out_grads[0].shape[0] // count
    for d in range(count):
        rows = slice(d * out_rows, (d + 1) * out_rows)
        both = jnp.concatenate([g[rows] for g in out_grads], axis=0).astype(low)
        for j in range(width // lane):
            at = 3 * in_rows + j * 2 * out_rows
            out_ref[d, at : at + 2 * out_rows, :] = both[:, j * lane : (j + 1) * lane]


def scaled_step(weight, update, weight_sum, update_sum, count_all, lead_shape):
    rms_weight = jnp.sqrt(weight_sum / count_all).reshape(lead_shape)
    rms_update = jnp.sqrt(update_sum / count_all).reshape(lead_shape)
    step_size = (
        step_rate * jnp.maximum(scale_floor, rms_weight) / jnp.maximum(1.0, rms_update / clip_level)
    )
    return weight - step_size * update


def after(value, *others):
    return lax.optimization_barrier((value,) + others)[0]


def shards(
    tokens,
    cotangent,
    segments,
    route_query,
    route_key,
    route_ffn,
    attn_in,
    attn_out,
    light_in,
    light_out,
    heavy_in,
    heavy_out,
    gains,
    router,
    row_attn_in,
    col_attn_in,
    row_attn_out,
    col_attn_out,
    row_light_in,
    col_light_in,
    row_light_out,
    col_light_out,
    row_heavy_in,
    col_heavy_in,
    row_heavy_out,
    col_heavy_out,
    second_gains,
    second_router,
):
    data_size = lax.axis_size("dp")
    model_size = lax.axis_size("mp")
    data_index = lax.axis_index("dp")
    model_index = lax.axis_index("mp")
    core = model_index % 2
    core_flag = core.astype(jnp.int32).reshape(1)
    core_pairs = [(i, i ^ 1) for i in range(model_size)]
    far_pairs = [(i, i ^ 2) for i in range(model_size)]
    micro_count, tok_local, width = tokens.shape
    routed_local = route_query.shape[1]
    routed_all = route_key.shape[1]
    quarter = routed_local // model_size
    head_cols = attn_in.shape[2]
    in_rows = attn_in.shape[1]

    order = jnp.arange(model_size) ^ model_index
    key_blocks = route_key.reshape(micro_count, data_size, model_size, quarter)
    key_blocks = jnp.take(key_blocks, order, axis=2)
    key_local = lax.dynamic_slice_in_dim(key_blocks, data_index, 1, axis=1)[:, 0]
    my_quarter = key_local[:, 0]
    picks = (my_quarter[:, :, None] == jnp.arange(tok_local)[None, None, :]).astype(low)
    my_rows = jnp.einsum("mrt,mtd->mrd", picks, tokens, preferred_element_type=wide).astype(low)

    lane = 2 * head_cols
    sides = width // lane
    out_rows = attn_out.shape[1]
    small = jnp.concatenate([gains, router], axis=0).astype(low)
    small_block = jnp.pad(small, ((0, 16 - small.shape[0]), (0, lane - in_rows)))
    in_block = (
        attn_in.astype(low).reshape(3, 2, in_rows, head_cols).transpose(0, 2, 1, 3).reshape(3 * in_rows, lane)
    )

    def sideways(rows):
        return rows.reshape(-1, sides, lane).transpose(1, 0, 2).reshape(-1, lane)

    out_block = sideways(attn_out.astype(low).reshape(2 * out_rows, width))
    key_block = sideways(my_rows.reshape(-1, width))
    pack_one = jnp.concatenate([in_block, out_block, key_block, small_block], axis=0)
    got_one = lax.all_gather(pack_one, "dp", axis=0, tiled=False)
    aligned = in_rows % 16 == 0 and out_rows % 8 == 0 and light_out.shape[0] % 16 == 0
    if aligned:
        w_in, w_out, key_rows, vectors = kernel_call(
            unpack_body,
            [
                in_vmem((6, width, head_cols), low),
                in_vmem((2, data_size * out_rows, width), low),
                in_vmem((data_size, micro_count, quarter, width), low),
                in_vmem((8, width), wide),
            ],
            [],
            (got_one,),
        )
    else:
        w_in = (
            got_one[:, : 3 * in_rows]
            .reshape(data_size, 3, in_rows, 2, head_cols)
            .transpose(1, 3, 0, 2, 4)
            .reshape(6, width, head_cols)
        )
        at = 3 * in_rows
        w_out = (
            got_one[:, at : at + out_block.shape[0]]
            .reshape(data_size, sides, 2, out_rows, lane)
            .transpose(2, 0, 3, 1, 4)
            .reshape(2, data_size * out_rows, width)
        )
        at = at + out_block.shape[0]
        key_rows = (
            got_one[:, at : at + key_block.shape[0]]
            .reshape(data_size, sides, micro_count, quarter, lane)
            .transpose(0, 2, 3, 1, 4)
            .reshape(data_size, micro_count, quarter, width)
        )
        at = at + key_block.shape[0]
        vectors = got_one[:, at : at + 8, :in_rows].transpose(1, 0, 2).reshape(8, width).astype(wide)

    def blocked(weight):
        lead, rows, cols = weight.shape
        return weight.reshape(lead, rows, cols // CHUNK, CHUNK).transpose(0, 2, 1, 3).reshape(-1, rows, CHUNK)

    def unblocked(blocks, lead):
        count, rows, _ = blocks.shape
        return blocks.reshape(lead, count // lead, rows, CHUNK).transpose(0, 2, 1, 3).reshape(lead, rows, -1)

    light_hidden = light_in.shape[2]
    heavy_hidden = heavy_in.shape[2]
    blocks = [blocked(w.astype(low)) for w in (light_in, light_out[None], heavy_in, heavy_out[None])]
    block_rows = [b.shape[0] * b.shape[1] for b in blocks]
    pack_two = jnp.concatenate([b.reshape(-1, CHUNK) for b in blocks], axis=0)
    pack_two = after(pack_two, got_one)
    w_ffn = lax.all_gather(pack_two, "dp", axis=0, tiled=False)
    if not aligned:
        pieces = []
        at = 0
        for block in blocks:
            size = block.shape[0] * block.shape[1]
            pieces.append(
                w_ffn[:, at : at + size]
                .reshape((data_size,) + block.shape)
                .transpose(1, 0, 2, 3)
                .reshape(-1, CHUNK)
            )
            at = at + size
        w_ffn = jnp.concatenate(pieces, axis=0)[None]

    turns = (jnp.arange(micro_count) % 2)[:, None]
    segment_ids = segments[None, :] * turns
    seg_padded = jnp.pad(segment_ids, ((0, 0), (RADIUS, RADIUS)), constant_values=-1)
    seg_local = lax.dynamic_slice_in_dim(segment_ids, data_index * tok_local, tok_local, axis=1)
    seg_extended = lax.dynamic_slice_in_dim(
        seg_padded, data_index * tok_local, tok_local + 2 * RADIUS, axis=1
    ).reshape(micro_count, -1, 1, BLOCK)

    def picked(ids, spots):
        hit = spots[..., :, None] == jnp.arange(tok_local)
        return jnp.sum(jnp.where(hit, ids[..., None, :], 0), axis=-1)

    key_seg = picked(
        segment_ids.reshape(micro_count, data_size, tok_local),
        key_blocks.reshape(micro_count, data_size, routed_local),
    ).reshape(micro_count, -1)
    query_seg = picked(seg_local, route_query)
    key_list = key_local.reshape(micro_count, -1)

    project_outs = [
        in_vmem((micro_count, tok_local, width), low),
        in_vmem((micro_count, tok_local, head_cols), low),
        in_vmem((micro_count, tok_local, head_cols), low),
        in_vmem((micro_count, tok_local, head_cols), low),
        in_vmem((micro_count, routed_local, head_cols), low),
        in_vmem((micro_count, routed_local, 1), wide),
        in_vmem((micro_count, routed_local, width), wide),
        in_vmem((micro_count, routed_local, width), wide),
        in_vmem((micro_count, routed_local, width), low),
    ]
    normed_low, light_q, light_k, light_v, heavy_q, score_q, rows_q, rows_k, rows_q_low = kernel_call(
        project_body,
        project_outs,
        [pltpu.VMEM((tok_local, width), low)],
        (tokens, vectors, w_in, route_query[:, :, None], key_list[:, :, None]),
        flops=5_000_000_000,
    )

    up = [(i, i + 1) for i in range(data_size - 1)]
    down = [(i + 1, i) for i in range(data_size - 1)]
    light_kv = (light_k, light_v)
    tails = jnp.stack([a[:, tok_local - RADIUS :] for a in light_kv], axis=1)
    heads = jnp.stack([a[:, :RADIUS] for a in light_kv], axis=1)
    halo_prev = lax.ppermute(tails, "dp", up)
    halo_next = lax.ppermute(heads, "dp", down)

    rows_core = lax.ppermute(key_rows, "mp", core_pairs)
    rows_far = lax.ppermute(key_rows, "mp", far_pairs)
    rows_both = lax.ppermute(rows_far, "mp", core_pairs)
    split = (micro_count, data_size, model_size, quarter)
    span = min(data_size, 8)
    row_spec = pl.BlockSpec((span, 1, quarter, width), lambda m, i: (i, m, 0, 0))

    def split_spec(cols):
        return pl.BlockSpec((1, span, model_size, quarter, cols), lambda m, i: (m, i, 0, 0, 0))

    key_normed, heavy_k, heavy_v, score_k = pl.pallas_call(
        keys_body,
        grid=(micro_count, data_size // span),
        out_shape=[
            in_vmem(split + (width,), low),
            in_vmem(split + (head_cols,), low),
            in_vmem(split + (head_cols,), low),
            in_vmem(split + (1,), wide),
        ],
        in_specs=[row_spec] * 4
        + [
            pl.BlockSpec((8, width), lambda m, i: (0, 0)),
            pl.BlockSpec((6, width, head_cols), lambda m, i: (0, 0, 0)),
        ],
        out_specs=[split_spec(width), split_spec(head_cols), split_spec(head_cols), split_spec(1)],
        compiler_params=pltpu.CompilerParams(vmem_limit_bytes=VMEM_BYTES),
        cost_estimate=pl.CostEstimate(flops=10_000_000_000, bytes_accessed=10_000_000, transcendentals=0),
    )(key_rows, rows_core, rows_far, rows_both, vectors, w_in)
    key_normed = key_normed.reshape(micro_count, routed_all, width)
    heavy_k = heavy_k.reshape(micro_count, routed_all, head_cols)
    heavy_v = heavy_v.reshape(micro_count, routed_all, head_cols)
    score_k = score_k.reshape(micro_count, routed_all, 1)

    half_rows = tok_local // 2

    def mp_sum(part):
        second = lax.ppermute(part, "mp", core_pairs)
        mine = lax.dynamic_slice_in_dim(part, core * half_rows, half_rows, 0).astype(wide)
        theirs = lax.dynamic_slice_in_dim(second, core * half_rows, half_rows, 0).astype(wide)
        near = lax.ppermute((mine + theirs).astype(low), "mp", far_pairs)
        far = lax.ppermute(near, "mp", core_pairs)
        return part, second, near, far

    extended = pltpu.VMEM((tok_local + 2 * RADIUS, head_cols), low)
    row_shape = (tok_local, width)
    attended = []
    for m in range(micro_count):
        segs = (
            seg_local[m][:, None],
            seg_extended[m],
            query_seg[m][:, None],
            key_seg[m][None, :],
        )
        part, light_mix, heavy_mix, heavy_proj = kernel_call(
            attend_body,
            [
                in_vmem(row_shape, low),
                in_vmem((tok_local, head_cols), low),
                in_vmem((routed_local, head_cols), low),
                in_vmem((routed_local, width), wide),
            ],
            [extended, extended, pltpu.VMEM((routed_local, width), low)],
            (
                light_q[m], light_k[m], light_v[m], halo_prev[m], halo_next[m], heavy_q[m], heavy_k[m],
                heavy_v[m], score_q[m], w_out, route_query[m][None, :],
            )
            + segs,
            flops=4_000_000_000,
        )
        attended.append((segs, light_mix, heavy_mix, heavy_proj, mp_sum(part)))

    fed = []
    for m in range(micro_count):
        outs = kernel_call(
            ffn_body,
            [
                in_vmem(row_shape, wide),
                in_vmem(row_shape, low),
                in_vmem(row_shape, low),
                in_vmem(row_shape, low),
                in_vmem((tok_local, light_hidden), low),
                in_vmem((2, tok_local, light_hidden), low),
                in_vmem((routed_local, width), low),
                in_vmem((routed_local, heavy_hidden), low),
                in_vmem((2, routed_local, heavy_hidden), low),
                in_vmem((routed_local, width), low),
                in_vmem((1, width), wide),
            ],
            [
                pltpu.VMEM(row_shape, low),
                pltpu.VMEM((routed_local, width), low),
                pltpu.VMEM((routed_local, width), low),
            ],
            (core_flag,)
            + attended[m][4]
            + (
                tokens[m], cotangent[m], vectors, route_ffn[m][:, None], route_ffn[m][None, :], w_ffn,
            ),
            scalars=1,
            flops=6_000_000_000,
        )
        fed.append(tuple(outs) + (mp_sum(outs[2]),))

    grad_args = (cotangent,)
    for m in range(micro_count):
        grad_args = grad_args + tuple(fed[m][3:10])
    total_rows = ffn_bases(width, light_hidden, heavy_hidden)[1]
    split = data_size if aligned else 1
    (pack_ffn,) = kernel_call(
        ffn_grads_body,
        [in_vmem((split, total_rows // split, CHUNK), low)],
        [
            pltpu.VMEM((width, micro_count * tok_local), low),
            pltpu.VMEM((width, micro_count * routed_local), low),
        ],
        grad_args,
        flops=4_000_000_000,
    )
    if not aligned:
        pieces = []
        at = 0
        for block in blocks:
            size = block.shape[0] * block.shape[1] * data_size
            pieces.append(
                pack_ffn[0, at : at + size]
                .reshape(block.shape[0], data_size, block.shape[1], CHUNK)
                .transpose(1, 0, 2, 3)
                .reshape(data_size, -1, CHUNK)
            )
            at = at + size
        pack_ffn = jnp.concatenate(pieces, axis=1)
    sum_ffn = lax.psum_scatter(pack_ffn.reshape(-1, CHUNK), "dp", scatter_dimension=0, tiled=True)
    y_moved = []
    held = fed[-1][11][2]
    for m in range(micro_count):
        moved = mp_sum(after(fed[m][1], held))
        held = moved[2]
        y_moved.append(moved)

    backs = []
    for m in range(micro_count):
        segs, light_mix, heavy_mix, heavy_proj, _ = attended[m]
        outs = kernel_call(
            attend_back_body,
            [
                in_vmem(row_shape, wide),
                in_vmem(row_shape, low),
                in_vmem((1, width), wide),
                in_vmem((tok_local, head_cols), low),
                in_vmem((2, tok_local, head_cols), wide),
                in_vmem((2, 2, RADIUS, head_cols), low),
                in_vmem((routed_local, head_cols), low),
                in_vmem((routed_all, head_cols), low),
                in_vmem((routed_all, head_cols), low),
                in_vmem((routed_all, head_cols), low),
                in_vmem((routed_local, width), low),
                in_vmem((routed_local, 1), wide),
            ],
            [
                extended,
                extended,
                pltpu.VMEM((tok_local, head_cols), low),
                pltpu.VMEM((tok_local + 2 * RADIUS, head_cols), wide),
                pltpu.VMEM((tok_local + 2 * RADIUS, head_cols), wide),
            ],
            (core_flag,)
            + fed[m][11]
            + (
                fed[m][0], cotangent[m], vectors, light_q[m], light_k[m], light_v[m], halo_prev[m],
                halo_next[m], heavy_q[m], heavy_k[m], heavy_v[m], score_k[m], score_q[m], heavy_proj,
                w_out, route_query[m][:, None],
            )
            + segs,
            scalars=1,
            flops=8_000_000_000,
        )
        spread = jnp.concatenate([outs[7], outs[8]], axis=1).reshape(data_size, routed_local, 2 * head_cols)
        owned = lax.all_to_all(spread, "dp", 0, 0, tiled=True)
        backs.append((outs, owned))
    edges = jnp.stack([backs[m][0][5] for m in range(micro_count)], axis=1)
    from_prev = lax.ppermute(edges[0], "dp", up)
    from_next = lax.ppermute(edges[1], "dp", down)

    last = []
    for m in range(micro_count):
        outs, owned = backs[m]
        part, grads_kv, router_part = kernel_call(
            project_back_body,
            [
                in_vmem(row_shape, low),
                in_vmem((2, tok_local, head_cols), low),
                in_vmem((2, width), wide),
            ],
            [pltpu.VMEM((2 * routed_local, width), low)],
            (
                outs[3], outs[4], from_prev[m], from_next[m], outs[6], outs[11], owned, rows_q[m], rows_k[m],
                vectors, w_in, route_query[m][None, :], key_list[m][None, :],
            ),
            flops=3_000_000_000,
        )
        last.append((mp_sum(part), grads_kv, router_part))

    attn_rows = 3 * in_rows + 2 * out_rows * sides
    groups = []
    for m in range(micro_count):
        outs = backs[m][0]
        groups.append(
            (outs[3], last[m][1], outs[6], outs[7], outs[9], attended[m][1], outs[1], attended[m][2], outs[10])
        )
    if aligned:
        (pack_attn,) = kernel_call(
            attn_grads_body,
            [in_vmem((data_size, attn_rows, lane), low)],
            [
                pltpu.VMEM((width, micro_count * tok_local), low),
                pltpu.VMEM((width, micro_count * routed_all), low),
            ],
            (normed_low, rows_q_low, key_normed) + sum(groups, ()),
            flops=4_000_000_000,
        )
    else:
        totals = [0.0] * 8
        for m, group in enumerate(groups):
            pairs = (
                (normed_low[m], group[0]), (normed_low[m], group[1][0]), (normed_low[m], group[1][1]),
                (rows_q_low[m], group[2]), (key_normed[m], group[3]), (key_normed[m], group[4]),
                (group[5], group[6]), (group[7], group[8]),
            )
            totals = [total + tn(left, right) for total, (left, right) in zip(totals, pairs)]
        grad_in = jnp.stack(totals[:6]).astype(low)
        grad_out = jnp.stack(totals[6:]).astype(low)
        pack_attn = jnp.concatenate(
            [
                grad_in.reshape(3, 2, data_size, in_rows, head_cols)
                .transpose(2, 0, 3, 1, 4)
                .reshape(data_size, 3 * in_rows, lane),
                grad_out.reshape(2, data_size, out_rows, sides, lane)
                .transpose(1, 3, 0, 2, 4)
                .reshape(data_size, -1, lane),
            ],
            axis=1,
        )
    pack_attn = after(pack_attn.reshape(-1, lane), sum_ffn)
    sum_attn = lax.psum_scatter(pack_attn, "dp", scatter_dimension=0, tiled=True)

    join_args = ()
    for m in range(micro_count):
        join_args = join_args + (fed[m][0],) + y_moved[m]
    (mixed,) = kernel_call(
        join_body, [in_vmem(tokens.shape, low)], [], (core_flag,) + join_args, scalars=1
    )
    pieces = ()
    for m in range(micro_count):
        pieces = pieces + last[m][0]
    grad_tokens, gain_one = kernel_call(
        finish_body,
        [in_vmem(tokens.shape, wide), in_vmem((1, width), wide)],
        [],
        (core_flag,) + pieces + tuple(backs[m][0][0] for m in range(micro_count)) + (tokens, vectors),
        scalars=1,
    )
    gain_two = sum(backs[m][0][2] for m in range(micro_count))
    router_low = sum(last[m][2] for m in range(micro_count))
    router_ffn = sum(fed[m][10] for m in range(micro_count))
    vector_grads = jnp.concatenate(
        [gain_one / model_size, gain_two / model_size, router_low, router_ffn], axis=0
    )

    grad_attn_in = (
        sum_attn[: 3 * in_rows]
        .reshape(3, in_rows, 2, head_cols)
        .transpose(0, 2, 1, 3)
        .reshape(6, in_rows, head_cols)
        .astype(wide)
    )
    grad_attn_out = (
        sum_attn[3 * in_rows :]
        .reshape(sides, 2, out_rows, lane)
        .transpose(1, 2, 0, 3)
        .reshape(2, out_rows, width)
        .astype(wide)
    )
    ffn_grads = []
    at = 0
    for weight, block, size in zip((light_in, light_out, heavy_in, heavy_out), blocks, block_rows):
        lead = weight.size // (weight.shape[-1] * weight.shape[-2])
        ffn_grads.append(
            unblocked(sum_ffn[at : at + size].reshape(block.shape), lead).reshape(weight.shape).astype(wide)
        )
        at = at + size
    reduced = [grad_attn_in, grad_attn_out] + ffn_grads

    device_count = data_size * model_size

    def all_parts(values):
        sent = jnp.broadcast_to(values[None, :], (device_count, values.shape[0]))
        return lax.all_to_all(sent, ("dp", "mp"), 0, 0, tiled=True)

    local_spot = model_index * data_size + data_index
    specs = (
        (attn_in, reduced[0], row_attn_in, col_attn_in, data_index * attn_in.shape[-2], model_index * attn_in.shape[-1]),
        (attn_out, reduced[1], row_attn_out, col_attn_out, local_spot * attn_out.shape[-2], 0),
        (light_in, reduced[2], row_light_in, col_light_in, data_index * light_in.shape[-2], model_index * light_in.shape[-1]),
        (light_out, reduced[3], row_light_out, col_light_out, local_spot * light_out.shape[-2], 0),
        (heavy_in, reduced[4], row_heavy_in, col_heavy_in, data_index * heavy_in.shape[-2], model_index * heavy_in.shape[-1]),
        (heavy_out, reduced[5], row_heavy_out, col_heavy_out, local_spot * heavy_out.shape[-2], 0),
    )
    tall = (True, False, True, False, True, False)
    decay_rate = 1.0 - STEP ** (-0.8)

    def updated(chosen, vectors_too):
        parts = []
        for index in chosen:
            weight, gradient = specs[index][:2]
            square = gradient * gradient + tiny_square
            parts.append(jnp.sum(square, axis=-1).reshape(-1))
            parts.append(jnp.sum(square, axis=-2).reshape(-1))
            parts.append(jnp.sum(weight * weight, axis=(-2, -1)).reshape(-1))
        if vectors_too:
            parts.append(jnp.sum(gains * gains, axis=-1) / model_size)
            parts.append(jnp.sum(router * router, axis=-1) / model_size)
            parts.append(vector_grads.reshape(-1))
        starts = [0]
        for part in parts:
            starts.append(starts[-1] + part.shape[0])
        packed = jnp.pad(jnp.concatenate(parts), (0, -starts[-1] % 1024))
        gathered = all_parts(packed).reshape(data_size, model_size, -1)

        def section(place):
            return gathered[:, :, starts[place] : starts[place + 1]]

        pending = []
        update_parts = []
        for place, index in enumerate(chosen):
            weight, gradient, row_old, col_old, row_start, col_start = specs[index]
            lead = weight.shape[:-2]
            rows_here = section(3 * place).reshape((data_size, model_size) + lead + (weight.shape[-2],))
            cols_here = section(3 * place + 1).reshape((data_size, model_size) + lead + (weight.shape[-1],))
            weight_sum = jnp.sum(section(3 * place + 2), axis=(0, 1))
            if tall[index]:
                row_sum = jnp.moveaxis(jnp.sum(rows_here, axis=1), 0, -2).reshape(row_old.shape)
                col_sum = jnp.moveaxis(jnp.sum(cols_here, axis=0), 0, -2).reshape(col_old.shape)
            else:
                row_sum = jnp.moveaxis(jnp.swapaxes(rows_here, 0, 1), (0, 1), (-3, -2)).reshape(row_old.shape)
                col_sum = jnp.sum(cols_here, axis=(0, 1))
            row_new = decay_rate * row_old + (1.0 - decay_rate) * row_sum / col_old.shape[-1]
            col_new = decay_rate * col_old + (1.0 - decay_rate) * col_sum / row_old.shape[-1]
            row_mean = jnp.mean(row_new, axis=-1)[..., None, None]
            my_rows = lax.dynamic_slice_in_dim(row_new, row_start, weight.shape[-2], row_new.ndim - 1)
            my_cols = lax.dynamic_slice_in_dim(col_new, col_start, weight.shape[-1], col_new.ndim - 1)
            update = gradient * lax.rsqrt(my_rows[..., :, None] * my_cols[..., None, :] / row_mean)
            update_parts.append(jnp.sum(update * update, axis=(-2, -1)).reshape(-1))
            count_all = row_old.shape[-1] * col_old.shape[-1]
            pending.append(
                (weight, gradient, update, (row_new, col_new), weight_sum, count_all, lead + (1, 1))
            )
        if vectors_too:
            base = 3 * len(chosen)
            vector_sum = jnp.sum(section(base + 2), axis=(0, 1)).reshape(5, width)
            mine = lax.dynamic_slice_in_dim(vector_sum, data_index * gains.shape[1], gains.shape[1], 1)
            for weight, gradient, second_old, place in (
                (gains, mine[:2], second_gains, base),
                (router, mine[2:], second_router, base + 1),
            ):
                second_new = decay_rate * second_old + (1.0 - decay_rate) * (gradient * gradient + tiny_square)
                update = gradient * lax.rsqrt(second_new)
                update_parts.append(jnp.sum(update * update, axis=-1) / model_size)
                weight_sum = jnp.sum(section(place), axis=(0, 1))
                pending.append(
                    (weight, gradient, update, (second_new,), weight_sum, D, (weight.shape[0], 1))
                )
        update_pack = jnp.concatenate(update_parts)
        padding = -update_pack.shape[0] % 128
        update_sums = jnp.sum(all_parts(jnp.pad(update_pack, (0, padding))), axis=0)
        results = []
        at = 0
        for weight, gradient, update, moments, weight_sum, count_all, lead_shape in pending:
            lead_count = weight_sum.shape[0]
            update_sum = update_sums[at : at + lead_count]
            at = at + lead_count
            new_weight = scaled_step(weight, update, weight_sum, update_sum, count_all, lead_shape)
            results.append([gradient, *moments, new_weight])
        return results

    ffn_results = updated((2, 3, 4, 5), False)
    attn_results = updated((0, 1), True)
    results = [mixed, grad_tokens]
    for result in attn_results[:2] + ffn_results + attn_results[2:]:
        results.extend(result)
    return tuple(results)


def solution(mesh):
    placed = (
        P(None, "dp", None),
        P(None, "dp", None),
        P(),
        P(None, "dp"),
        P(),
        P(None, "dp"),
        P(None, "dp", "mp"),
        P(None, ("mp", "dp"), None),
        P(None, "dp", "mp"),
        P(("mp", "dp"), None),
        P(None, "dp", "mp"),
        P(("mp", "dp"), None),
        P(None, "dp"),
        P(None, "dp"),
        P(),
        P(),
        P(),
        P(),
        P(),
        P(),
        P(),
        P(),
        P(),
        P(),
        P(),
        P(),
        P(None, "dp"),
        P(None, "dp"),
    )
    return jax.shard_map(
        shards,
        mesh=mesh,
        in_specs=placed,
        out_specs=(
            P(None, "dp", None),
            P(None, "dp", None),
            P(None, "dp", "mp"),
            P(),
            P(),
            P(None, "dp", "mp"),
            P(None, ("mp", "dp"), None),
            P(),
            P(),
            P(None, ("mp", "dp"), None),
            P(None, "dp", "mp"),
            P(),
            P(),
            P(None, "dp", "mp"),
            P(("mp", "dp"), None),
            P(),
            P(),
            P(("mp", "dp"), None),
            P(None, "dp", "mp"),
            P(),
            P(),
            P(None, "dp", "mp"),
            P(("mp", "dp"), None),
            P(),
            P(),
            P(("mp", "dp"), None),
            P(None, "dp"),
            P(None, "dp"),
            P(None, "dp"),
            P(None, "dp"),
            P(None, "dp"),
            P(None, "dp"),
        ),
        check_vma=False,
    )
```

```python
import functools
import math

import jax
import jax.numpy as jnp
from jax import lax
from jax.experimental import pallas as pl
from jax.experimental.pallas import tpu as pltpu
from jax.sharding import PartitionSpec as P

D = 768
LH = 8
LDH = 96
HH = 12
HDH = 64
WIN = 128
STEP = 10

norm_eps = 1e-06
tiny_square = 1e-30
scale_floor = 0.001
clip_level = 1.0
step_rate = 0.5
masked_score = -1e30
gelu_scale = math.sqrt(2.0 / math.pi)
gelu_cubic = 0.044715

low = jnp.bfloat16
wide = jnp.float32
CHUNK = 256
BLOCK = 128
RADIUS = WIN // 2
KEYS = 1024
VMEM_BYTES = 60 * 1024 * 1024
LARGE = 200 * 1024


def nn(left, right):
    return lax.dot_general(left, right, (((1,), (0,)), ((), ())), preferred_element_type=wide)


def nt(left, right):
    return lax.dot_general(left, right, (((1,), (1,)), ((), ())), preferred_element_type=wide)


def tn(left, right):
    return lax.dot_general(left, right, (((0,), (0,)), ((), ())), preferred_element_type=wide)


def sigmoid(logit):
    return 1.0 / (1.0 + jnp.exp(-logit))


def gelu_pair(gate):
    squared = gate * gate
    bent = jnp.tanh(gelu_scale * gate * (1.0 + gelu_cubic * squared))
    half = 0.5 * (1.0 + bent)
    value = gate * half
    slope = half + 0.5 * gate * (1.0 - bent * bent) * gelu_scale * (1.0 + 3.0 * gelu_cubic * squared)
    return value, slope


def picks_rows(idx_col, count):
    spots = lax.broadcasted_iota(jnp.int32, (idx_col.shape[0], count), 1)
    return (spots == idx_col).astype(low)


def picks_cols(idx_row, start, count):
    spots = lax.broadcasted_iota(jnp.int32, (count, idx_row.shape[1]), 0) + start
    return (spots == idx_row).astype(low)


def head_mask(width, size, head):
    spot = lax.broadcasted_iota(jnp.int32, (1, width), 1)
    return ((spot >= head * size) & (spot < (head + 1) * size)).astype(low)


def softmax_parts(scores, allowed):
    masked = jnp.where(allowed, scores, masked_score)
    top = jnp.max(masked, axis=-1, keepdims=True)
    grown = jnp.exp(masked - top)
    return grown * (1.0 / jnp.sum(grown, axis=-1, keepdims=True))


def inverse_rms(values):
    return lax.rsqrt(jnp.mean(values * values, axis=-1, keepdims=True) + norm_eps)


def norm_back(values, gain_row, upstream):
    inverse = inverse_rms(values)
    unit = values * inverse
    scaled = upstream * gain_row
    pulled = inverse * (scaled - unit * jnp.mean(scaled * unit, axis=-1, keepdims=True))
    return pulled, jnp.sum(upstream * unit, axis=0, keepdims=True)


def in_vmem(shape, dtype):
    return jax.ShapeDtypeStruct(shape, dtype)


def vmem_bytes(shape, dtype):
    size = jnp.dtype(dtype).itemsize
    shape = (1,) * (2 - len(shape)) + tuple(shape)
    rows, cols = -(-shape[-2] // (32 // size)) * (32 // size), -(-shape[-1] // 128) * 128
    return math.prod(shape[:-2]) * rows * cols * size


class Transfers:
    def __init__(self, ins, outs, sems):
        self.ins = {id(held): (far, held) for far, held in ins}
        self.outs = {id(held): (far, held) for far, held in outs}
        self.sems, self.used = sems, 0
        self.begun, self.finished, self.going = {}, set(), []

    def copy(self, source, target):
        made = pltpu.make_async_copy(source, target, self.sems.at[self.used])
        self.used += 1
        made.start()
        return made

    def begin(self, *refs):
        for ref in refs:
            if id(ref) in self.ins and id(ref) not in self.begun:
                self.begun[id(ref)] = self.copy(*self.ins[id(ref)])

    def need(self, *refs):
        self.begin(*refs)
        for ref in refs:
            if id(ref) in self.ins and id(ref) not in self.finished:
                self.begun[id(ref)].wait()
                self.finished.add(id(ref))

    def done(self, ref, part=None):
        if id(ref) not in self.outs:
            return
        far, held = self.outs[id(ref)]
        self.finished.add(id(ref))
        if part is None:
            self.going.append(self.copy(held, far))
        else:
            self.going.append(self.copy(held.at[part], far.at[part]))

    def close(self):
        for far, held in self.ins.values():
            self.need(held)
        for far, held in self.outs.values():
            if id(held) not in self.finished:
                self.done(held)
        for made in self.going:
            made.wait()


class Pick:
    def __init__(self, array, index):
        self.array, self.index = array, index
        self.shape, self.dtype = array.shape[1:], array.dtype


def kernel_call(body, outs, scratch, args, scalars=0, weight=10, managed=False, parts=4):
    vmem = pl.BlockSpec(memory_space=pltpu.VMEM)
    smem = pl.BlockSpec(memory_space=pltpu.SMEM)
    far = pl.BlockSpec(memory_space=pl.ANY)

    def large(x):
        return managed and vmem_bytes(x.shape, x.dtype) >= LARGE

    picked = {i: arg.index for i, arg in enumerate(args) if isinstance(arg, Pick)}
    ins = [i for i in range(scalars, len(args)) if large(args[i])]
    assert all(i in ins for i in picked)
    ends = [i for i in range(len(outs)) if large(outs[i])]
    held = [pltpu.VMEM(args[i].shape, args[i].dtype) for i in ins]
    held = held + [pltpu.VMEM(outs[i].shape, outs[i].dtype) for i in ends]
    sems = [pltpu.SemaphoreType.DMA((len(held) + parts,))] if managed else []

    def run(*refs):
        refs = list(refs)
        count = len(args) + len(outs)
        operands, results = refs[: len(args)], refs[len(args) : count]
        kept = refs[count : count + len(held)]
        rest = refs[count + len(held) :]
        if managed:
            rest, sem = rest[:-1], rest[-1]
            pairs_in, pairs_out = [], []
            for i, ref in zip(ins, kept):
                pairs_in.append((operands[i].at[picked[i]] if i in picked else operands[i], ref))
                operands[i] = ref
            for i, ref in zip(ends, kept[len(ins) :]):
                pairs_out.append((results[i], ref))
                results[i] = ref
            moves = Transfers(pairs_in, pairs_out, sem)
            body(moves, *operands, *results, *rest)
            moves.close()
        else:
            body(*operands, *results, *rest)

    return pl.pallas_call(
        run,
        out_shape=outs,
        in_specs=[smem] * scalars + [far if large(x) else vmem for x in args[scalars:]],
        out_specs=[far if large(x) else vmem for x in outs],
        scratch_shapes=held + list(scratch) + sems,
        compiler_params=pltpu.CompilerParams(vmem_limit_bytes=VMEM_BYTES),
        cost_estimate=pl.CostEstimate(
            flops=weight * 1_150_000_000, bytes_accessed=1_000_000, transcendentals=0
        ),
    )(*(arg.array if isinstance(arg, Pick) else arg for arg in args))


def mp_total(core, mine_ref, other_ref, chunk, per_half, size=CHUNK):
    rows = pl.ds(pl.multiple_of((chunk % per_half) * size, size), size)
    flag = ((chunk // per_half) == core).astype(wide)
    return mine_ref[rows, :].astype(wide) * flag + other_ref[rows, :].astype(wide) * (1.0 - flag)


def mp_store(core, keep_ref, send_ref, chunk, per_half, size, value):
    rows = pl.ds(pl.multiple_of((chunk % per_half) * size, size), size)
    kept = (chunk // per_half) == core

    @pl.when(kept)
    def _():
        keep_ref[rows, :] = value

    @pl.when(jnp.logical_not(kept))
    def _():
        send_ref[rows, :] = value


def unpack_body(got_ref, w_in_ref, w_out_ref, vec_ref):
    count, _, lane = got_ref.shape
    in_rows = w_in_ref.shape[1] // count
    head_cols = w_in_ref.shape[2]
    for j in range(3):
        pair = got_ref[:, j * in_rows : (j + 1) * in_rows, :].reshape(count * in_rows, lane)
        w_in_ref[2 * j] = pair[:, :head_cols]
        w_in_ref[2 * j + 1] = pair[:, head_cols:]
    base = 3 * in_rows
    out_rows = w_out_ref.shape[1] // count
    sides = w_out_ref.shape[2] // lane
    for j in range(sides):
        cols = slice(j * lane, (j + 1) * lane)
        blocks = [
            got_ref[d, base + j * 2 * out_rows : base + (j + 1) * 2 * out_rows, :].astype(wide)
            for d in range(count)
        ]
        for s in range(2):
            w_out_ref[s, :, cols] = jnp.concatenate(
                [b[s * out_rows : (s + 1) * out_rows] for b in blocks], axis=0
            ).astype(low)
    base = base + 2 * out_rows * sides
    vec_ref[...] = jnp.concatenate(
        [got_ref[d, base : base + 16, :].astype(wide)[:8, :in_rows] for d in range(count)], axis=1
    )


def block_of(ref, base, index, full):
    count = ref.shape[0]
    rows = full // count
    at = base // count + index * rows
    return ref[:, at : at + rows, :].reshape(full, CHUNK)


def part_of(ref, base, index, full, piece):
    count = ref.shape[0]
    rows = full // count
    at = base // count + index * rows
    if rows <= CHUNK:
        span = CHUNK // rows
        return ref[piece * span : (piece + 1) * span, at : at + rows, :].reshape(CHUNK, CHUNK)
    return ref[0, at + piece * CHUNK : at + (piece + 1) * CHUNK, :]


def ffn_bases(width, light, heavy):
    sides = width // CHUNK
    light_in = 2 * (light // CHUNK) * width
    light_out = sides * light
    heavy_in = 2 * (heavy // CHUNK) * width
    bases = [0, light_in, light_in + light_out, light_in + light_out + heavy_in]
    return bases, bases[3] + sides * heavy


def project_body(moves, vec_ref, w_ref, *refs):
    low_ref = refs[-1]
    micros = (len(refs) - 1) // 12
    inputs, outputs = refs[: 3 * micros], refs[3 * micros : -1]
    for m in range(micros):
        moves.begin(inputs[3 * m])
        moves.begin(w_ref)
    for m in range(micros):
        tok_ref, qcol_ref, kcol_ref = inputs[3 * m : 3 * m + 3]
        n1b_ref, q_ref, k_ref, v_ref, hq_ref, sq_ref, nq_ref, nk_ref, qrows_ref = outputs[9 * m : 9 * m + 9]
        count = tok_ref.shape[0]
        moves.need(tok_ref, w_ref)

        def step(c, carry):
            rows = pl.ds(pl.multiple_of(c * CHUNK, CHUNK), CHUNK)
            values = tok_ref[rows, :].astype(wide)
            normed = values * inverse_rms(values) * vec_ref[0:1, :]
            high = normed.astype(low)
            n1b_ref[rows, :] = high
            low_ref[rows, :] = (normed - high.astype(wide)).astype(low)
            q_ref[rows, :] = nn(high, w_ref[0]).astype(low)
            k_ref[rows, :] = nn(high, w_ref[1]).astype(low)
            v_ref[rows, :] = nn(high, w_ref[2]).astype(low)
            return carry

        lax.fori_loop(0, count // CHUNK, step, 0)
        for ref in (k_ref, v_ref, q_ref, n1b_ref):
            moves.done(ref)
        picks = picks_rows(qcol_ref[...], count)
        query_rows = nn(picks, n1b_ref[...])
        query_wide = query_rows + nn(picks, low_ref[...])
        qrows_ref[...] = query_rows.astype(low)
        nq_ref[...] = query_wide
        hq_ref[...] = nn(query_rows.astype(low), w_ref[3]).astype(low)
        sq_ref[...] = sigmoid(jnp.sum(query_wide * vec_ref[2:3, :], axis=-1, keepdims=True))
        picks = picks_rows(kcol_ref[...], count)
        nk_ref[...] = nn(picks, n1b_ref[...]) + nn(picks, low_ref[...])
        for ref in (qrows_ref, nq_ref, nk_ref):
            moves.done(ref)


def keys_body(o_ref, a_ref, b_ref, c_ref, vec_ref, w_ref, *outs):
    blocks, micros, part, width = o_ref.shape
    for m in range(micros):
        n_ref, k_ref, v_ref, sk_ref = outs[4 * m : 4 * m + 4]
        for p, ref in enumerate((o_ref, a_ref, b_ref, c_ref)):
            values = ref[:, m].reshape(blocks * part, width).astype(wide)
            normed = values * inverse_rms(values) * vec_ref[0:1, :]
            high = normed.astype(low)
            score = sigmoid(jnp.sum(normed * vec_ref[3:4, :], axis=-1, keepdims=True))
            n_ref[:, p] = high.reshape(blocks, part, width)
            sk_ref[:, p] = score.reshape(blocks, part, 1)
            k_ref[:, p] = nn(high, w_ref[4]).astype(low).reshape(blocks, part, -1)
            v_ref[:, p] = (nn(high, w_ref[5]) * score).astype(low).reshape(blocks, part, -1)


def fill_extended(ext_ref, prev, inner, after):
    count = inner.shape[0]
    ext_ref[0:RADIUS, :] = prev
    ext_ref[RADIUS : RADIUS + count, :] = inner
    ext_ref[RADIUS + count :, :] = after


def near_mask(seg_q, seg_k):
    shape = (BLOCK, 2 * BLOCK)
    gap = lax.broadcasted_iota(jnp.int32, shape, 1) - lax.broadcasted_iota(jnp.int32, shape, 0)
    return (gap >= 0) & (gap <= 2 * RADIUS) & (seg_q == seg_k)


def attend_body(
    core_ref, q_ref, k_ref, v_ref, prev_ref, after_ref, hq_ref, hk_ref, hv_ref, sq_ref, wo_ref,
    qrow_ref, segq_ref, segk_ref, hsegq_ref, hsegk_ref,
    keep_ref, send_ref, lmix_ref, hmix_ref, hproj_ref,
    kx_ref, vx_ref, rows_ref,
):
    count, width = q_ref.shape
    light_heads = width // LDH
    heavy_heads = width // HDH
    allowed = hsegq_ref[...] == hsegk_ref[...]
    mix = jnp.zeros((hq_ref.shape[0], width), wide)
    for h in range(heavy_heads):
        mask = head_mask(width, HDH, h)
        probs = softmax_parts(nt(hq_ref[...], hk_ref[...] * mask) * (1.0 / math.sqrt(HDH)), allowed)
        mix = mix + nn(probs.astype(low), hv_ref[...] * mask)
    mix_low = mix.astype(low)
    hmix_ref[...] = mix_low
    proj = nn(mix_low, wo_ref[1])
    hproj_ref[...] = proj
    rows_ref[...] = (sq_ref[...] * proj).astype(low)
    fill_extended(kx_ref, prev_ref[0], k_ref[...], after_ref[0])
    fill_extended(vx_ref, prev_ref[1], v_ref[...], after_ref[1])

    def step(b, carry):
        rows = pl.ds(pl.multiple_of(b * BLOCK, BLOCK), BLOCK)
        keys = pl.ds(pl.multiple_of(b * BLOCK, BLOCK), 2 * BLOCK)
        seg_k = jnp.concatenate([segk_ref[b], segk_ref[b + 1]], axis=1)
        near = near_mask(segq_ref[rows, :], seg_k)
        queries = q_ref[rows, :]
        block_keys = kx_ref[keys, :]
        block_values = vx_ref[keys, :]
        total = jnp.zeros((BLOCK, width), wide)
        for h in range(light_heads):
            mask = head_mask(width, LDH, h)
            probs = softmax_parts(nt(queries, block_keys * mask) * (1.0 / math.sqrt(LDH)), near)
            total = total + nn(probs.astype(low), block_values * mask)
        total_low = total.astype(low)
        lmix_ref[rows, :] = total_low
        spread = picks_cols(qrow_ref[...], b * BLOCK, BLOCK)
        part = (nn(total_low, wo_ref[0]) + nn(spread, rows_ref[...])).astype(low)
        mp_store(core_ref[0], keep_ref, send_ref, b, count // BLOCK // 2, BLOCK, part)
        return carry

    lax.fori_loop(0, count // BLOCK, step, 0)


def ffn_body(last, *refs):
    moves, core_ref, mine_ref, other_ref, tok_ref, cot_ref, vec_ref, fcol_ref, frow_ref, w_ref = refs[:10]
    low_ref, out_rows_ref, grad_rows_ref = refs[-3:]
    if last:
        earlier = [refs[10 + 8 * m : 18 + 8 * m] for m in range(last)]
        middle_ref, ykeep_ref, ysend_ref, gkeep_ref, gsend_ref, router_ref, pack_ref = refs[10 + 8 * last : 17 + 8 * last]
        own = refs[17 + 8 * last : 24 + 8 * last]
        turned_ref, turned_rows_ref = refs[24 + 8 * last : 26 + 8 * last]
    else:
        earlier = []
        middle_ref, ykeep_ref, ysend_ref, gkeep_ref, gsend_ref, router_ref = refs[10:16]
        own = refs[16:23]
    n2b_ref, hidden_ref, dgu_ref, frows_ref, hhid_ref, dhgu_ref, dhout_ref = own
    count, width = tok_ref.shape
    chunks = count // CHUNK
    core = core_ref[0]
    light = hidden_ref.shape[1]
    heavy = hhid_ref.shape[1]
    sides = width // CHUNK
    bases, _ = ffn_bases(width, light, heavy)
    moves.begin(mine_ref, other_ref, tok_ref)
    moves.begin(w_ref, cot_ref)
    for group in earlier:
        moves.begin(*group)
    moves.need(mine_ref, other_ref, tok_ref)

    def heavy_in(s, j):
        return block_of(w_ref, bases[2], s * (heavy // CHUNK) + j, width)

    def heavy_out(t, j):
        return part_of(w_ref, bases[3], t, heavy, j)

    def light_in(s):
        return block_of(w_ref, bases[0], s, width)

    def light_out(t):
        return block_of(w_ref, bases[1], t, light)

    def enter(c, carry):
        rows = pl.ds(pl.multiple_of(c * CHUNK, CHUNK), CHUNK)
        middle = tok_ref[rows, :].astype(wide) + mp_total(core, mine_ref, other_ref, c, chunks // 2)
        middle_ref[rows, :] = middle.astype(low)
        normed = middle * inverse_rms(middle) * vec_ref[1:2, :]
        high = normed.astype(low)
        n2b_ref[rows, :] = high
        low_ref[rows, :] = (normed - high.astype(wide)).astype(low)
        return carry

    lax.fori_loop(0, chunks, enter, 0)
    moves.done(middle_ref)
    moves.done(n2b_ref)
    moves.need(w_ref, cot_ref)
    picks = picks_rows(fcol_ref[...], count)
    rows_high = nn(picks, n2b_ref[...])
    rows_wide = rows_high + nn(picks, low_ref[...])
    rows_low = rows_high.astype(low)
    frows_ref[...] = rows_low
    score = sigmoid(jnp.sum(rows_wide * vec_ref[4:5, :], axis=-1, keepdims=True))
    cot_rows = nn(picks, cot_ref[...])
    grad_out = (score * cot_rows).astype(low)
    dhout_ref[...] = grad_out
    out_rows = [jnp.zeros((rows_low.shape[0], CHUNK), wide) for _ in range(sides)]
    grad_rows = jnp.zeros(rows_low.shape, wide)
    for j in range(heavy // CHUNK):
        cols = slice(j * CHUNK, (j + 1) * CHUNK)
        gate = nn(rows_low, heavy_in(0, j))
        up = nn(rows_low, heavy_in(1, j))
        value, slope = gelu_pair(gate)
        hid = (value * up).astype(low)
        hhid_ref[:, cols] = hid
        grad_hid = jnp.zeros_like(gate)
        for t in range(sides):
            piece = heavy_out(t, j)
            out_rows[t] = out_rows[t] + nn(hid, piece)
            grad_hid = grad_hid + nt(grad_out[:, t * CHUNK : (t + 1) * CHUNK], piece)
        grad_gate = (grad_hid * up * slope).astype(low)
        grad_up = (grad_hid * value).astype(low)
        dhgu_ref[0, :, cols] = grad_gate
        dhgu_ref[1, :, cols] = grad_up
        grad_rows = grad_rows + nt(grad_gate, heavy_in(0, j)) + nt(grad_up, heavy_in(1, j))
    out_rows = jnp.concatenate(out_rows, axis=1)
    logit = jnp.sum(cot_rows * out_rows, axis=-1, keepdims=True) * score * (1.0 - score)
    router_ref[...] = jnp.sum(logit * rows_wide, axis=0, keepdims=True)
    out_rows_ref[...] = (score * out_rows).astype(low)
    grad_rows_ref[...] = (grad_rows + logit * vec_ref[4:5, :]).astype(low)
    for ref in (frows_ref, hhid_ref, dhgu_ref, dhout_ref):
        moves.done(ref)

    def light_rows(c, carry):
        rows = pl.ds(pl.multiple_of(c * CHUNK, CHUNK), CHUNK)
        normed = n2b_ref[rows, :]
        gate = nn(normed, light_in(0))
        up = nn(normed, light_in(1))
        value, slope = gelu_pair(gate)
        hid = (value * up).astype(low)
        hidden_ref[rows, :] = hid
        spread = picks_cols(frow_ref[...], c * CHUNK, CHUNK)
        spread_out = nn(spread, out_rows_ref[...])
        grad_hid = jnp.zeros_like(gate)
        outs = []
        for t in range(sides):
            cols = slice(t * CHUNK, (t + 1) * CHUNK)
            outs.append((nn(hid, light_out(t)) + spread_out[:, cols]).astype(low))
            grad_hid = grad_hid + nt(cot_ref[rows, cols], light_out(t))
        grad_gate = (grad_hid * up * slope).astype(low)
        grad_up = (grad_hid * value).astype(low)
        dgu_ref[0, rows, :] = grad_gate
        dgu_ref[1, rows, :] = grad_up
        grad = nt(grad_gate, light_in(0)) + nt(grad_up, light_in(1)) + nn(spread, grad_rows_ref[...])
        mp_store(core, ykeep_ref, ysend_ref, c, chunks // 2, CHUNK, jnp.concatenate(outs, axis=1))
        mp_store(core, gkeep_ref, gsend_ref, c, chunks // 2, CHUNK, grad.astype(low))
        return carry

    lax.fori_loop(0, chunks, light_rows, 0)
    for ref in (gsend_ref, gkeep_ref, ysend_ref, ykeep_ref):
        moves.done(ref)
    if not last:
        return

    split = pack_ref.shape[0]

    def put(base, index, value):
        rows = value.shape[0] // split
        at = base // split + index * rows
        pack_ref[:, at : at + rows, :] = value.astype(low).reshape(split, rows, CHUNK)

    def sent(base, end):
        moves.done(pack_ref, (slice(None), slice(base // split, end // split)))

    for group in earlier:
        moves.need(*group)
    groups = earlier + [own + (cot_ref,)]
    routed = frows_ref.shape[0]
    for m, group in enumerate(groups):
        turned_ref[:, m * count : (m + 1) * count] = group[0][...].T
        turned_rows_ref[:, m * routed : (m + 1) * routed] = group[3][...].T
    pieces = heavy // CHUNK
    for s in range(2):
        for j in range(pieces):
            total = jnp.zeros((width, CHUNK), wide)
            for m, group in enumerate(groups):
                total = total + nn(
                    turned_rows_ref[:, m * routed : (m + 1) * routed],
                    group[5][s, :, j * CHUNK : (j + 1) * CHUNK],
                )
            put(bases[2], s * pieces + j, total)
    sent(bases[2], bases[3])
    for t in range(sides):
        cols = slice(t * CHUNK, (t + 1) * CHUNK)
        total = jnp.zeros((heavy, CHUNK), wide)
        for group in groups:
            total = total + tn(group[4][...], group[6][:, cols])
        put(bases[3], t, total)
    sent(bases[3], split * pack_ref.shape[1])
    for s in range(2):
        total = jnp.zeros((width, CHUNK), wide)
        for m, group in enumerate(groups):
            total = total + nn(turned_ref[:, m * count : (m + 1) * count], group[2][s])
        put(bases[0], s, total)
    total = jnp.zeros((light, width), wide)
    for group in groups:
        total = total + tn(group[1][...], group[7][...])
    for t in range(sides):
        put(bases[1], t, total[:, t * CHUNK : (t + 1) * CHUNK])
    sent(0, bases[2])


def attend_back_body(
    mine, moves, core_ref, mine_ref, other_ref, middle_ref, cot_ref, vec_ref,
    q_ref, k_ref, v_ref, prev_ref, after_ref, hq_ref, hk_ref, hv_ref, sk_ref, sq_ref, hproj_ref, wo_ref,
    qcol_ref, segq_ref, segk_ref, hsegq_ref, hsegk_ref, earlier_edges_ref,
    agl_ref, gain_ref, dq_ref, inner_ref, rims_ref, edges_ref, dhq_ref, spread_ref, draw_ref,
    dproj_ref, logit_ref,
    kx_ref, vx_ref, dmix_ref, dkx_ref, dvx_ref,
):
    count, width = q_ref.shape
    chunks = count // CHUNK
    light_heads = width // LDH
    heavy_heads = width // HDH
    core = core_ref[0]
    moves.begin(mine_ref, other_ref, middle_ref, cot_ref, wo_ref)
    moves.begin(hk_ref, hv_ref, sk_ref, hproj_ref, k_ref, v_ref, q_ref, segq_ref)
    moves.need(mine_ref, other_ref, middle_ref, cot_ref, wo_ref)
    gain_ref[...] = jnp.zeros_like(gain_ref)

    def enter(c, carry):
        rows = pl.ds(pl.multiple_of(c * CHUNK, CHUNK), CHUNK)
        upstream = mp_total(core, mine_ref, other_ref, c, chunks // 2)
        pulled, gain = norm_back(middle_ref[rows, :].astype(wide), vec_ref[1:2, :], upstream)
        gain_ref[...] += gain
        grad_low = (cot_ref[rows, :].astype(wide) + pulled).astype(low)
        agl_ref[rows, :] = grad_low
        dmix_ref[rows, :] = nt(grad_low, wo_ref[0]).astype(low)
        return carry

    lax.fori_loop(0, chunks, enter, 0)

    moves.done(agl_ref)
    moves.need(hk_ref, hv_ref, sk_ref, hproj_ref)
    picks = picks_rows(qcol_ref[...], count)
    grad_rows = nn(picks, agl_ref[...])
    score = sq_ref[...]
    dproj = (score * grad_rows).astype(low)
    dproj_ref[...] = dproj
    logit_ref[...] = (
        jnp.sum(grad_rows * hproj_ref[...], axis=-1, keepdims=True) * score * (1.0 - score)
    )
    dmix = nt(dproj, wo_ref[1]).astype(low)
    scale = 1.0 / math.sqrt(HDH)
    key_count = hk_ref.shape[0]
    if key_count <= KEYS:
        allowed = hsegq_ref[...] == hsegk_ref[...]
        dq = jnp.zeros((hq_ref.shape[0], width), wide)
        dk = jnp.zeros((key_count, width), wide)
        dv = jnp.zeros((key_count, width), wide)
        for h in range(heavy_heads):
            mask = head_mask(width, HDH, h)
            keys = hk_ref[...] * mask
            probs = softmax_parts(nt(hq_ref[...], keys) * scale, allowed)
            grad_soft = nt(dmix, hv_ref[...] * mask)
            centre = jnp.sum(probs * grad_soft, axis=-1, keepdims=True)
            grad_scores = (probs * (grad_soft - centre)).astype(low)
            dq = dq + nn(grad_scores, keys)
            dk = dk + tn(grad_scores, hq_ref[...] * mask)
            dv = dv + tn(probs.astype(low), dmix * mask)
        both = jnp.concatenate([(dk * scale).astype(low), dv.astype(low)], axis=1)
        spread_ref[...] = both.reshape(spread_ref.shape)
        draw_ref[...] = (dv * sk_ref[...]).astype(low)
    else:
        pieces = key_count // KEYS

        def piece_of(c, mask):
            spots = pl.ds(pl.multiple_of(c * KEYS, KEYS), KEYS)
            allowed = hsegq_ref[...] == hsegk_ref[:, spots]
            keys = hk_ref[spots, :] * mask
            scores = jnp.where(allowed, nt(hq_ref[...], keys) * scale, masked_score)
            return spots, keys, scores, nt(dmix, hv_ref[spots, :] * mask)

        blank = jnp.zeros((hq_ref.shape[0], 1), wide)
        stats = []
        for h in range(heavy_heads):
            mask = head_mask(width, HDH, h)

            def find_top(c, top):
                return jnp.maximum(top, jnp.max(piece_of(c, mask)[2], axis=-1, keepdims=True))

            top = lax.fori_loop(0, pieces, find_top, blank + masked_score)

            def add_up(c, sums):
                _, _, scores, grad_soft = piece_of(c, mask)
                grown = jnp.exp(scores - top)
                return (
                    sums[0] + jnp.sum(grown, axis=-1, keepdims=True),
                    sums[1] + jnp.sum(grown * grad_soft, axis=-1, keepdims=True),
                )

            total, moment = lax.fori_loop(0, pieces, add_up, (blank, blank))
            stats.append((mask, top, 1.0 / total, moment / total))

        def pull(c, dq):
            dk = jnp.zeros((KEYS, width), wide)
            dv = jnp.zeros((KEYS, width), wide)
            for mask, top, inverse, centre in stats:
                spots, keys, scores, grad_soft = piece_of(c, mask)
                probs = jnp.exp(scores - top) * inverse
                grad_scores = (probs * (grad_soft - centre)).astype(low)
                dq = dq + nn(grad_scores, keys)
                dk = dk + tn(grad_scores, hq_ref[...] * mask)
                dv = dv + tn(probs.astype(low), dmix * mask)
            owners = KEYS // spread_ref.shape[1]
            both = jnp.concatenate([(dk * scale).astype(low), dv.astype(low)], axis=1)
            spread_ref[pl.ds(c * owners, owners)] = both.reshape((owners,) + spread_ref.shape[1:])
            draw_ref[spots, :] = (dv * sk_ref[spots, :]).astype(low)
            return dq

        dq = lax.fori_loop(0, pieces, pull, jnp.zeros((hq_ref.shape[0], width), wide))
    dhq_ref[...] = (dq * scale).astype(low)
    moves.need(k_ref, v_ref, q_ref, segq_ref)
    if mine > 0:
        edges_ref[:, :mine] = earlier_edges_ref[...]
    for ref in (spread_ref, draw_ref, dproj_ref):
        moves.done(ref)
    fill_extended(kx_ref, prev_ref[0], k_ref[...], after_ref[0])
    fill_extended(vx_ref, prev_ref[1], v_ref[...], after_ref[1])
    dkx_ref[...] = jnp.zeros_like(dkx_ref)
    dvx_ref[...] = jnp.zeros_like(dvx_ref)
    light_scale = 1.0 / math.sqrt(LDH)

    def step(b, carry):
        rows = pl.ds(pl.multiple_of(b * BLOCK, BLOCK), BLOCK)
        spans = pl.ds(pl.multiple_of(b * BLOCK, BLOCK), 2 * BLOCK)
        seg_k = jnp.concatenate([segk_ref[b], segk_ref[b + 1]], axis=1)
        near = near_mask(segq_ref[rows, :], seg_k)
        queries = q_ref[rows, :]
        block_keys = kx_ref[spans, :]
        block_values = vx_ref[spans, :]
        mix = dmix_ref[rows, :]
        grad_q = jnp.zeros((BLOCK, width), wide)
        grad_k = jnp.zeros((2 * BLOCK, width), wide)
        grad_v = jnp.zeros((2 * BLOCK, width), wide)
        for h in range(light_heads):
            mask = head_mask(width, LDH, h)
            keys = block_keys * mask
            probs = softmax_parts(nt(queries, keys) * light_scale, near)
            grad_soft = nt(mix, block_values * mask)
            centre = jnp.sum(probs * grad_soft, axis=-1, keepdims=True)
            grad_scores = (probs * (grad_soft - centre)).astype(low)
            grad_q = grad_q + nn(grad_scores, keys)
            grad_k = grad_k + tn(grad_scores, queries * mask)
            grad_v = grad_v + tn(probs.astype(low), mix * mask)
        dq_ref[rows, :] = (grad_q * light_scale).astype(low)
        dkx_ref[spans, :] += grad_k * light_scale
        dvx_ref[spans, :] += grad_v
        return carry

    lax.fori_loop(0, count // BLOCK, step, 0)
    for s, ref in enumerate((dkx_ref, dvx_ref)):
        inner_ref[s] = ref[RADIUS : RADIUS + count, :].astype(low)
        rims_ref[s, :RADIUS, :] = ref[RADIUS : 2 * RADIUS, :]
        rims_ref[s, RADIUS:, :] = ref[count : RADIUS + count, :]
        edges_ref[0, mine, s] = ref[RADIUS + count :, :].astype(low)
        edges_ref[1, mine, s] = ref[:RADIUS, :].astype(low)


def project_back_body(
    core_ref, dq_ref, inner_ref, rims_ref, prev_ref, after_ref, dhq_ref, logit_ref, nq_ref, vec_ref, w_ref, qrow_ref,
    normed_ref,
    keep_ref, send_ref, dkv_ref, router_ref, gain_ref,
    rows_ref,
):
    count, width = dq_ref.shape
    for s in range(2):
        dkv_ref[s, RADIUS : count - RADIUS, :] = inner_ref[s, RADIUS : count - RADIUS, :]
        dkv_ref[s, :RADIUS, :] = (rims_ref[s, :RADIUS, :] + prev_ref[s].astype(wide)).astype(low)
        dkv_ref[s, count - RADIUS :, :] = (rims_ref[s, RADIUS:, :] + after_ref[s].astype(wide)).astype(low)
    query_logit = logit_ref[...]
    router_ref[...] = jnp.sum(query_logit * nq_ref[...], axis=0, keepdims=True)
    rows_ref[...] = (nt(dhq_ref[...], w_ref[3]) + query_logit * vec_ref[2:3, :]).astype(low)

    def step(c, carry):
        rows = pl.ds(pl.multiple_of(c * CHUNK, CHUNK), CHUNK)
        part = (
            nt(dq_ref[rows, :], w_ref[0])
            + nt(dkv_ref[0, rows, :], w_ref[1])
            + nt(dkv_ref[1, rows, :], w_ref[2])
            + nn(picks_cols(qrow_ref[...], c * CHUNK, CHUNK), rows_ref[...])
        )
        gain_ref[...] += jnp.sum(part * normed_ref[rows, :].astype(wide), axis=0, keepdims=True)
        mp_store(core_ref[0], keep_ref, send_ref, c, count // CHUNK // 2, CHUNK, part.astype(low))
        return carry

    gain_ref[...] = jnp.zeros_like(gain_ref)
    lax.fori_loop(0, count // CHUNK, step, 0)
    gain_ref[...] = gain_ref[...] / vec_ref[0:1, :]


def keys_back_body(micros, place_ref, owned_ref, vec_ref, w_ref, *refs):
    keep_ref, send_ref, split_ref, turn_ref, rows_ref = refs[-5:]
    nk_refs, vectors = refs[:micros], refs[micros:-5]
    gain_ones, gain_twos, queries, ffns = (vectors[i * micros : (i + 1) * micros] for i in range(4))
    routed = nk_refs[0].shape[0]
    width = w_ref.shape[2]
    parts = place_ref.shape[0] - 1
    part = routed // parts
    inverse_gain = 1.0 / vec_ref[0:1, :]
    router_key = jnp.zeros((1, vec_ref.shape[1]), wide)
    gain_one = jnp.zeros((1, vec_ref.shape[1]), wide)
    for m in range(micros):
        owned = owned_ref[m * routed : (m + 1) * routed, :]
        grad_k = owned[:, :width]
        grad_v = owned[:, width:].astype(wide)
        key_wide = nk_refs[m][...]
        raw = nn(key_wide.astype(low), w_ref[5])
        score = sigmoid(jnp.sum(key_wide * vec_ref[3:4, :], axis=-1, keepdims=True))
        logit = jnp.sum(grad_v * raw, axis=-1, keepdims=True) * score * (1.0 - score)
        router_key = router_key + jnp.sum(logit * key_wide, axis=0, keepdims=True)
        rows = nt(grad_k, w_ref[4]) + nt((grad_v * score).astype(low), w_ref[5]) + logit * vec_ref[3:4, :]
        gain_one = gain_one + jnp.sum(rows * key_wide, axis=0, keepdims=True) * inverse_gain
        turn_ref[...] = rows.astype(low)
        for p in range(parts):
            spot = pl.multiple_of(place_ref[1 + p] * part, part)
            rows_ref[m * routed + p * part : m * routed + (p + 1) * part, :] = turn_ref[pl.ds(spot, part), :]
    half = rows_ref.shape[0] // 2
    for c in range(2):
        mp_store(place_ref[0], keep_ref, send_ref, c, 1, half, rows_ref[c * half : (c + 1) * half, :])

    def added(refs):
        total = refs[0][...]
        for ref in refs[1:]:
            total = total + ref[...]
        return total

    gain_one = gain_one + added(gain_ones)
    lines = (gain_one, added(gain_twos) * (1.0 / parts), added(queries), router_key, added(ffns))
    split_ref[...] = jnp.zeros_like(split_ref)
    count = split_ref.shape[0]
    size = gain_one.shape[1] // count
    for d in range(count):
        for i, line in enumerate(lines):
            split_ref[d, i : i + 1, :size] = line[:, d * size : (d + 1) * size]


def finish_body(chunks, core_ref, kmine_ref, kother_ref, vec_ref, *refs):
    micros = (len(refs) - 3) // 4
    groups = [refs[4 * m : 4 * m + 4] for m in range(micros)]
    tok_ref, out_ref, keys_ref = refs[4 * micros :]
    routed = groups[0][3].shape[1]
    core = core_ref[0]
    chunk = pl.program_id(0)

    @pl.when(chunk == 0)
    def _():
        half = keys_ref.shape[0] // 2
        for c in range(2):
            keys_ref[c * half : (c + 1) * half, :] = mp_total(core, kmine_ref, kother_ref, c, 1, half).astype(low)

    flag = (chunk // (chunks // 2) == core).astype(wide)
    for m in range(micros):
        mine_ref, other_ref, grad_ref, krow_ref = groups[m]
        upstream = mine_ref[...].astype(wide) * flag + other_ref[...].astype(wide) * (1.0 - flag)
        spread = picks_cols(krow_ref[...], chunk * CHUNK, CHUNK)
        upstream = upstream + nn(spread, keys_ref[m * routed : (m + 1) * routed, :])
        pulled, _ = norm_back(tok_ref[m].astype(wide), vec_ref[0:1, :], upstream)
        out_ref[m] = grad_ref[...].astype(wide) + pulled


def join_body(chunks, core_ref, *refs):
    out_ref = refs[-1]
    flag = (pl.program_id(0) // (chunks // 2) == core_ref[0]).astype(wide)
    for m in range(out_ref.shape[0]):
        middle_ref, mine_ref, other_ref = refs[3 * m : 3 * m + 3]
        total = mine_ref[...].astype(wide) * flag + other_ref[...].astype(wide) * (1.0 - flag)
        out_ref[m] = (middle_ref[...].astype(wide) + total).astype(low)


def attn_grads_body(moves, *refs):
    out_ref, turned_ref, other_ref = refs[-3:]
    micros = len(refs) // 12
    groups = [refs[12 * m : 12 * m + 12] for m in range(micros)]
    tokens, width = groups[0][9].shape
    keys = groups[0][11].shape[0]
    for group in groups:
        moves.begin(group[9], group[0], group[1], group[10])
    for group in groups:
        moves.begin(group[11], group[3], group[4], group[5], group[6], group[7], group[8])
    for group in groups:
        moves.need(group[9], group[0], group[1], group[10])
    grads = []
    for m in range(micros):
        turned_ref[:, m * tokens : (m + 1) * tokens] = groups[m][9][...].T
    for s in range(3):
        total = 0.0
        for m, group in enumerate(groups):
            grad = group[0][...] if s == 0 else group[1][s - 1]
            total = total + nn(turned_ref[:, m * tokens : (m + 1) * tokens], grad)
        grads.append(total)
    total = 0.0
    for m, group in enumerate(groups):
        total = total + tn(group[10][...], group[2][...])
    grads.append(total)
    for group in groups:
        moves.need(*group)
    for m in range(micros):
        other_ref[:, m * keys : (m + 1) * keys] = groups[m][11][...].T
    for s in (3, 4):
        total = 0.0
        for m, group in enumerate(groups):
            if s == 3:
                grad = group[s][...].reshape(keys, -1)[:, : group[4].shape[1]]
            else:
                grad = group[s][...]
            total = total + nn(other_ref[:, m * keys : (m + 1) * keys], grad)
        grads.append(total)
    out_grads = []
    for mix, grad in ((5, 6), (7, 8)):
        total = 0.0
        for group in groups:
            total = total + tn(group[mix][...], group[grad][...])
        out_grads.append(total)
    count, _, lane = out_ref.shape
    in_rows = width // count
    for j in range(3):
        pair = jnp.concatenate([grads[2 * j], grads[2 * j + 1]], axis=1).astype(low)
        out_ref[:, j * in_rows : (j + 1) * in_rows, :] = pair.reshape(count, in_rows, lane)
    out_rows = out_grads[0].shape[0] // count
    own = groups[0][3].shape[1]
    for m, group in enumerate(groups):
        at = out_ref.shape[1] - (micros - m) * own
        out_ref[:, at : at + own, :] = group[3][...]
    for d in range(count):
        rows = slice(d * out_rows, (d + 1) * out_rows)
        both = jnp.concatenate([g[rows] for g in out_grads], axis=0).astype(low)
        for j in range(width // lane):
            at = 3 * in_rows + j * 2 * out_rows
            out_ref[d, at : at + 2 * out_rows, :] = both[:, j * lane : (j + 1) * lane]


class Matrix:
    def __init__(self, array, lead, tall, cols_at, rows_at, weight_at):
        self.array, self.lead, self.tall = array, lead, tall
        self.cols_at, self.rows_at, self.weight_at = cols_at, rows_at, weight_at

    def read(self, refs):
        ref = refs[self.array]
        return ref[...] if self.lead is None else ref[self.lead]

    def write(self, refs, value):
        if self.lead is None:
            refs[self.array][...] = value
        else:
            refs[self.array][self.lead] = value

    def line(self):
        lead = 0 if self.lead is None else self.lead
        return slice(lead, lead + 1)


def ffn_matrices(light, heavy, width):
    return [
        Matrix(0, 0, True, [(0, 0, light)], (4, 0), (4, 768)),
        Matrix(0, 1, True, [(1, 0, light)], (4, 128), (4, 769)),
        Matrix(1, None, False, [(0, light, width)], (4, 256), (4, 770)),
        Matrix(2, 0, True, [(2, 0, heavy)], (4, 384), (4, 771)),
        Matrix(2, 1, True, [(3, 0, heavy)], (4, 512), (4, 772)),
        Matrix(3, None, False, [(1, light, width)], (4, 640), (4, 773)),
    ]


def attn_matrices(cols, width):
    listed = [
        Matrix(0, i, True, [(i, 0, cols)], (6 + i // 4, 128 * (i % 4)), (i, 224)) for i in range(6)
    ]
    piece = width // 3
    for s in range(2):
        spots = [(3 * s + j, 256, piece) for j in range(3)]
        listed.append(Matrix(1, s, False, spots, (7, 256 + 128 * s), (s, 232)))
    return listed


def total_of(values):
    return jnp.sum(jnp.sum(values, axis=1, keepdims=True), axis=0, keepdims=True)


def sums_body(matrices, unpack, array_count, *refs):
    weights = refs[-2 * array_count - 1 : -array_count - 1]
    grads, sums_ref = refs[-array_count - 1 : -1], refs[-1]
    unpack(refs[: -2 * array_count - 1], grads)
    sums_ref[...] = jnp.zeros_like(sums_ref)
    for matrix in matrices:
        square = matrix.read(grads)
        square = square * square + tiny_square
        cols = jnp.sum(square, axis=0, keepdims=True)
        at = 0
        for row, lane, size in matrix.cols_at:
            sums_ref[row : row + 1, lane : lane + size] = cols[:, at : at + size]
            at = at + size
        rows = lax.dot_general(
            jnp.ones((8, square.shape[1]), wide),
            square,
            (((1,), (1,)), ((), ())),
            precision=lax.Precision.HIGHEST,
            preferred_element_type=wide,
        )
        row, lane = matrix.rows_at
        sums_ref[row : row + 1, lane : lane + square.shape[0]] = rows[0:1]
        weight = matrix.read(weights)
        row, lane = matrix.weight_at
        sums_ref[row : row + 1, lane : lane + 1] = total_of(weight * weight)


def lane_row(values):
    spots = lax.broadcasted_iota(jnp.int32, (1, 128), 1)
    row = jnp.zeros((1, 128), wide)
    for place, value in enumerate(values):
        row = row + jnp.where(spots == place, value, 0.0)
    return row


def moments_body(matrices, array_count, vector_count, data_size, model_size, place_ref, parts_ref, *refs):
    keep = 1.0 - STEP ** (-0.8)
    n = array_count
    grads, row_old, col_old, row_mine, col_mine = (refs[i * n : (i + 1) * n] for i in range(5))
    at = 5 * n
    vector_in = refs[at : at + 3 * vector_count]
    at = at + 3 * vector_count
    updates, row_new, col_new = (refs[at + i * n : at + (i + 1) * n] for i in range(3))
    at = at + 3 * n
    vector_out = refs[at : at + 2 * vector_count]
    aux_ref = refs[-1]
    d, k = place_ref[0], place_ref[1]
    devices = data_size * model_size
    whole = parts_ref[0]
    for i in range(1, devices):
        whole = whole + parts_ref[i]
    by_model = []
    for j in range(model_size):
        total = parts_ref[j]
        for i in range(1, data_size):
            total = total + parts_ref[i * model_size + j]
        by_model.append(total)
    by_data = []
    for i in range(data_size):
        total = parts_ref[i * model_size]
        for j in range(1, model_size):
            total = total + parts_ref[i * model_size + j]
        by_data.append(total)
    my_cols = parts_ref[k]
    for i in range(1, data_size):
        my_cols = my_cols + parts_ref[i * model_size + k]
    my_rows = parts_ref[d * model_size]
    for j in range(1, model_size):
        my_rows = my_rows + parts_ref[d * model_size + j]
    mine = parts_ref[d * model_size + k]

    def cols_of(sums, matrix):
        pieces = [sums[row : row + 1, lane : lane + size] for row, lane, size in matrix.cols_at]
        return pieces[0] if len(pieces) == 1 else jnp.concatenate(pieces, axis=1)

    lines, extents = [], []
    for matrix in matrices:
        grad_rows, grad_cols = matrix.read(grads).shape
        row_total = grad_rows * data_size * (1 if matrix.tall else model_size)
        col_total = grad_cols * (model_size if matrix.tall else 1)
        extents.append((row_total, col_total))
        row, lane = matrix.rows_at
        source = my_rows if matrix.tall else mine
        old = row_mine[matrix.array][matrix.line(), :]
        lines.append(keep * old + (1.0 - keep) / col_total * source[row : row + 1, lane : lane + 128])
    while len(lines) < 8:
        lines.append(jnp.zeros((1, 128), wide))
    columns = jnp.concatenate(lines, axis=0).T
    update_sums, weight_sums = [], []
    for place, (matrix, (row_total, col_total)) in enumerate(zip(matrices, extents)):
        grad = matrix.read(grads)
        row, lane = matrix.rows_at
        size = grad.shape[0]
        old_rows = row_old[matrix.array][matrix.line(), :]
        old_cols = col_old[matrix.array][matrix.line(), :]
        mean = keep * jnp.mean(old_rows, axis=1, keepdims=True) + (1.0 - keep) / (
            row_total * col_total
        ) * jnp.sum(whole[row : row + 1, lane : lane + 128], axis=1, keepdims=True)
        if matrix.tall:
            cols = keep * col_mine[matrix.array][matrix.line(), :] + (1.0 - keep) / row_total * cols_of(my_cols, matrix)
            all_cols = jnp.concatenate([cols_of(sums, matrix) for sums in by_model], axis=1)
            all_rows = jnp.concatenate([sums[row : row + 1, lane : lane + size] for sums in by_data], axis=1)
            new_cols = keep * old_cols + (1.0 - keep) / row_total * all_cols
        else:
            cols = keep * old_cols + (1.0 - keep) / row_total * cols_of(whole, matrix)
            all_rows = jnp.concatenate(
                [
                    parts_ref[i * model_size + j, row : row + 1, lane : lane + size]
                    for j in range(model_size)
                    for i in range(data_size)
                ],
                axis=1,
            )
            new_cols = cols
        row_new[matrix.array][matrix.line(), :] = keep * old_rows + (1.0 - keep) / col_total * all_rows
        col_new[matrix.array][matrix.line(), :] = new_cols
        update = grad * lax.rsqrt(columns[:size, place : place + 1] * (cols / mean))
        matrix.write(updates, update)
        update_sums.append(total_of(update * update))
        row, lane = matrix.weight_at
        weight_sums.append(whole[row : row + 1, lane : lane + 1] * (1.0 / devices))
    for i in range(vector_count):
        grad_ref, old_ref, weight_ref = vector_in[3 * i : 3 * i + 3]
        grad = grad_ref[...]
        moment = keep * old_ref[...] + (1.0 - keep) * (grad * grad + tiny_square)
        update = grad * lax.rsqrt(moment)
        vector_out[2 * i][...] = moment
        vector_out[2 * i + 1][...] = update
        for r in range(grad.shape[0]):
            line = update[r : r + 1]
            update_sums.append(total_of(line * line) * (1.0 / model_size))
            line = weight_ref[r : r + 1, :]
            weight_sums.append(total_of(line * line) * (1.0 / model_size))
    aux_ref[...] = jnp.zeros_like(aux_ref)
    aux_ref[0:1, :] = lane_row(update_sums)
    aux_ref[1:2, :] = lane_row(weight_sums)


def step_size(update_sum, weight_sum, count):
    rms_weight = jnp.sqrt(weight_sum * (1.0 / count))
    rms_update = jnp.sqrt(update_sum * (1.0 / count))
    return step_rate * jnp.maximum(scale_floor, rms_weight) / jnp.maximum(1.0, rms_update / clip_level)


def weights_body(matrices, counts, array_count, vector_count, aux_ref, *refs):
    n = array_count + vector_count
    weights, updates, news = refs[:n], refs[n : 2 * n], refs[2 * n :]
    sums = aux_ref[0]
    for i in range(1, aux_ref.shape[0]):
        sums = sums + aux_ref[i]

    def step(place):
        spot = slice(place, place + 1)
        return step_size(sums[0:1, spot], sums[1:2, spot], counts[place])

    for place, matrix in enumerate(matrices):
        matrix.write(news, matrix.read(weights) - step(place) * matrix.read(updates))
    place = len(matrices)
    for i in range(array_count, n):
        for r in range(weights[i].shape[0]):
            row = slice(r, r + 1)
            news[i][row, :] = weights[i][row, :] - step(place) * updates[i][row, :]
            place = place + 1


def after(value, *others):
    return lax.optimization_barrier((value,) + others)[0]


def shards(
    tokens,
    cotangent,
    segments,
    route_query,
    route_key,
    route_ffn,
    attn_in,
    attn_out,
    light_in,
    light_out,
    heavy_in,
    heavy_out,
    gains,
    router,
    row_attn_in,
    col_attn_in,
    row_attn_out,
    col_attn_out,
    row_light_in,
    col_light_in,
    row_light_out,
    col_light_out,
    row_heavy_in,
    col_heavy_in,
    row_heavy_out,
    col_heavy_out,
    second_gains,
    second_router,
):
    data_size = lax.axis_size("dp")
    model_size = lax.axis_size("mp")
    data_index = lax.axis_index("dp")
    model_index = lax.axis_index("mp")
    core = model_index % 2
    order = jnp.arange(model_size) ^ model_index
    core_flag = jnp.concatenate([core.reshape(1), order]).astype(jnp.int32)
    core_pairs = [(i, i ^ 1) for i in range(model_size)]
    far_pairs = [(i, i ^ 2) for i in range(model_size)]
    micro_count, tok_local, width = tokens.shape
    routed_local = route_query.shape[1]
    routed_all = route_key.shape[1]
    quarter = routed_local // model_size
    head_cols = attn_in.shape[2]
    in_rows = attn_in.shape[1]

    key_blocks = route_key.reshape(micro_count, data_size, model_size, quarter)
    own_keys = lax.dynamic_slice_in_dim(key_blocks, data_index, 1, axis=1)
    key_blocks = jnp.take(key_blocks, order, axis=2)
    key_local = lax.dynamic_slice_in_dim(key_blocks, data_index, 1, axis=1)[:, 0]
    my_quarter = key_local[:, 0]
    picks = (my_quarter[:, :, None] == jnp.arange(tok_local)[None, None, :]).astype(low)
    my_rows = jnp.einsum("mrt,mtd->mrd", picks, tokens, preferred_element_type=wide).astype(low)

    def to_all(rows):
        sent = jnp.broadcast_to(rows[None], (data_size,) + rows.shape)
        return lax.all_to_all(sent, "dp", 0, 0, tiled=True)

    key_rows = to_all(my_rows).reshape(data_size, micro_count, quarter, width)
    rows_core = lax.ppermute(key_rows, "mp", core_pairs)
    rows_far = lax.ppermute(key_rows, "mp", far_pairs)
    rows_both = lax.ppermute(rows_far, "mp", core_pairs)

    lane = 2 * head_cols
    sides = width // lane
    in_rows = attn_in.shape[1]
    out_rows = attn_out.shape[1]
    small = jnp.concatenate([gains, router], axis=0).astype(low)
    small_block = jnp.pad(small, ((0, 16 - small.shape[0]), (0, lane - in_rows)))
    in_block = (
        attn_in.astype(low).reshape(3, 2, in_rows, head_cols).transpose(0, 2, 1, 3).reshape(3 * in_rows, lane)
    )

    def sideways(rows):
        return rows.reshape(-1, sides, lane).transpose(1, 0, 2).reshape(-1, lane)

    out_block = sideways(attn_out.astype(low).reshape(2 * out_rows, width))
    pack_one = jnp.concatenate([in_block, out_block, small_block], axis=0)
    got_one = lax.all_gather(pack_one, "dp", axis=0, tiled=False)
    aligned = in_rows % 16 == 0 and out_rows % 8 == 0 and light_out.shape[0] % 16 == 0
    if aligned:
        w_in, w_out, vectors = kernel_call(
            unpack_body,
            [
                in_vmem((6, width, head_cols), low),
                in_vmem((2, data_size * out_rows, width), low),
                in_vmem((8, width), wide),
            ],
            [],
            (got_one,),
            weight=5,
        )
    else:
        w_in = (
            got_one[:, : 3 * in_rows]
            .reshape(data_size, 3, in_rows, 2, head_cols)
            .transpose(1, 3, 0, 2, 4)
            .reshape(6, width, head_cols)
        )
        at = 3 * in_rows
        w_out = (
            got_one[:, at : at + out_block.shape[0]]
            .reshape(data_size, sides, 2, out_rows, lane)
            .transpose(2, 0, 3, 1, 4)
            .reshape(2, data_size * out_rows, width)
        )
        at = at + out_block.shape[0]
        vectors = got_one[:, at : at + 8, :in_rows].transpose(1, 0, 2).reshape(8, width).astype(wide)

    def blocked(weight):
        lead, rows, cols = weight.shape
        return weight.reshape(lead, rows, cols // CHUNK, CHUNK).transpose(0, 2, 1, 3).reshape(-1, rows, CHUNK)

    def unblocked(blocks, lead):
        count, rows, _ = blocks.shape
        return blocks.reshape(lead, count // lead, rows, CHUNK).transpose(0, 2, 1, 3).reshape(lead, rows, -1)

    light_hidden = light_in.shape[2]
    heavy_hidden = heavy_in.shape[2]
    blocks = [blocked(w.astype(low)) for w in (light_in, light_out[None], heavy_in, heavy_out[None])]
    block_rows = [b.shape[0] * b.shape[1] for b in blocks]
    pack_two = jnp.concatenate([b.reshape(-1, CHUNK) for b in blocks], axis=0)
    w_ffn = lax.all_gather(after(pack_two, got_one, rows_far), "dp", axis=0, tiled=False)
    if not aligned:
        pieces = []
        at = 0
        for block in blocks:
            size = block.shape[0] * block.shape[1]
            pieces.append(
                w_ffn[:, at : at + size]
                .reshape((data_size,) + block.shape)
                .transpose(1, 0, 2, 3)
                .reshape(-1, CHUNK)
            )
            at = at + size
        w_ffn = jnp.concatenate(pieces, axis=0)[None]

    attn_in, attn_out, light_in, light_out, heavy_in, heavy_out, gains, router = (
        lax.optimization_barrier(
            (got_one, attn_in, attn_out, light_in, light_out, heavy_in, heavy_out, gains, router)
        )[1:]
    )

    local_spot = model_index * data_size + data_index
    ffn_list = ffn_matrices(light_hidden, heavy_hidden, width)
    ffn_weights = (light_in, light_out, heavy_in, heavy_out)
    ffn_moments = (
        (row_light_in, col_light_in),
        (row_light_out, col_light_out),
        (row_heavy_in, col_heavy_in),
        (row_heavy_out, col_heavy_out),
    )
    attn_list = attn_matrices(head_cols, width)
    attn_weights = (attn_in, attn_out)
    attn_moments = ((row_attn_in, col_attn_in), (row_attn_out, col_attn_out))

    def moments_of(matrices, weights, moments):
        row_old, col_old, row_mine, col_mine = [], [], [], []
        for array, weight in enumerate(weights):
            rows, cols = moments[array]
            tall = [m.tall for m in matrices if m.array == array][0]
            lead = rows.size // rows.shape[-1]
            rows, cols = rows.reshape(lead, -1), cols.reshape(lead, -1)
            size, span = weight.shape[-2:]
            spot = data_index if tall else local_spot
            my_rows = lax.dynamic_slice_in_dim(rows, spot * size, size, 1)
            row_mine.append(jnp.pad(my_rows, ((0, 0), (0, 128 - size)), constant_values=1.0))
            col_mine.append(lax.dynamic_slice_in_dim(cols, model_index * span, span, 1) if tall else cols)
            row_old.append(rows)
            col_old.append(cols)
        return row_old, col_old, row_mine, col_mine

    ffn_here, attn_here, w_ffn = lax.optimization_barrier(
        (
            moments_of(ffn_list, ffn_weights, ffn_moments),
            moments_of(attn_list, attn_weights, attn_moments),
            w_ffn,
        )
    )

    turns = (jnp.arange(micro_count) % 2)[:, None]
    segment_ids = segments[None, :] * turns
    seg_padded = jnp.pad(segment_ids, ((0, 0), (RADIUS, RADIUS)), constant_values=-1)
    seg_local = lax.dynamic_slice_in_dim(segment_ids, data_index * tok_local, tok_local, axis=1)
    seg_extended = lax.dynamic_slice_in_dim(
        seg_padded, data_index * tok_local, tok_local + 2 * RADIUS, axis=1
    ).reshape(micro_count, -1, 1, BLOCK)

    def picked(ids, spots):
        hit = spots[..., :, None] == jnp.arange(tok_local)
        return jnp.sum(jnp.where(hit, ids[..., None, :], 0), axis=-1)

    key_seg = picked(
        segment_ids.reshape(micro_count, data_size, tok_local),
        key_blocks.reshape(micro_count, data_size, routed_local),
    ).reshape(micro_count, -1)
    query_seg = picked(seg_local, route_query)
    key_list = key_local.reshape(micro_count, -1)

    query_col, query_row = route_query[:, :, None], route_query[:, None, :]
    key_col, key_row = key_list[:, :, None], own_keys.reshape(micro_count, 1, routed_local)
    ffn_col, ffn_row = route_ffn[:, :, None], route_ffn[:, None, :]
    segs = (seg_local[:, :, None], seg_extended, query_seg[:, :, None], key_seg[:, None, :])

    micros = range(micro_count)
    token_parts = [Pick(tokens, m) for m in micros]
    cot_parts = [Pick(cotangent, m) for m in micros]
    projected = kernel_call(
        project_body,
        [
            in_vmem((tok_local, width), low),
            in_vmem((tok_local, head_cols), low),
            in_vmem((tok_local, head_cols), low),
            in_vmem((tok_local, head_cols), low),
            in_vmem((routed_local, head_cols), low),
            in_vmem((routed_local, 1), wide),
            in_vmem((routed_local, width), wide),
            in_vmem((routed_local, width), wide),
            in_vmem((routed_local, width), low),
        ]
        * micro_count,
        [pltpu.VMEM((tok_local, width), low)],
        (vectors, w_in) + sum(((token_parts[m], query_col[m], key_col[m]) for m in micros), ()),
        managed=True,
            weight=12,
    )
    normed_low, light_q, light_k, light_v, heavy_q, score_q, rows_q, rows_k, rows_q_low = (
        projected[i::9] for i in range(9)
    )

    up = [(i, i + 1) for i in range(data_size - 1)]
    down = [(i + 1, i) for i in range(data_size - 1)]
    tails = jnp.stack([jnp.stack([k[tok_local - RADIUS :], v[tok_local - RADIUS :]]) for k, v in zip(light_k, light_v)])
    heads = jnp.stack([jnp.stack([k[:RADIUS], v[:RADIUS]]) for k, v in zip(light_k, light_v)])
    halo_prev = lax.ppermute(tails, "dp", up)
    halo_next = lax.ppermute(heads, "dp", down)

    split = (data_size, model_size, quarter)
    span = min(data_size, 8)

    def split_spec(cols):
        return pl.BlockSpec((span, model_size, quarter, cols), lambda i: (i, 0, 0, 0))

    keyed = pl.pallas_call(
        keys_body,
        grid=(data_size // span,),
        out_shape=[
            in_vmem(split + (width,), low),
            in_vmem(split + (head_cols,), low),
            in_vmem(split + (head_cols,), low),
            in_vmem(split + (1,), wide),
        ]
        * micro_count,
        in_specs=[pl.BlockSpec((span, micro_count, quarter, width), lambda i: (i, 0, 0, 0))] * 4
        + [
            pl.BlockSpec((8, width), lambda i: (0, 0)),
            pl.BlockSpec((6, width, head_cols), lambda i: (0, 0, 0)),
        ],
        out_specs=[split_spec(width), split_spec(head_cols), split_spec(head_cols), split_spec(1)] * micro_count,
        compiler_params=pltpu.CompilerParams(vmem_limit_bytes=VMEM_BYTES),
        cost_estimate=pl.CostEstimate(flops=6 * 1_150_000_000, bytes_accessed=1_000_000, transcendentals=0),
    )(key_rows, rows_core, rows_far, rows_both, vectors, w_in)
    key_normed, heavy_k, heavy_v, score_k = (
        [a.reshape(routed_all, -1) for a in keyed[i::4]] for i in range(4)
    )

    def mp_first(keep, send, *earlier):
        got = lax.ppermute(after(send, *earlier), "mp", core_pairs)
        return (keep.astype(wide) + got.astype(wide)).astype(low)

    def mp_second(mine):
        return mine, lax.ppermute(mine, "mp", far_pairs)

    def mp_third(moved, *held):
        mine, near = moved
        near = after(near, *held)
        done = (mine.astype(wide) + near.astype(wide)).astype(low)
        return done, lax.ppermute(done, "mp", core_pairs)

    extended = pltpu.VMEM((tok_local + 2 * RADIUS, head_cols), low)
    row_shape = (tok_local, width)
    half_shape = (tok_local // 2, width)

    def all_picks(arrays, m):
        return tuple(a[m] for a in arrays)

    attended = []
    attn_moved = []
    held, earlier = (), ()
    for m in micros:
        outs = kernel_call(
            attend_body,
            [
                in_vmem(half_shape, low),
                in_vmem(half_shape, low),
                in_vmem((tok_local, head_cols), low),
                in_vmem((routed_local, head_cols), low),
                in_vmem((routed_local, width), wide),
            ],
            [extended, extended, pltpu.VMEM((routed_local, width), low)],
            (core_flag,)
            + all_picks((light_q, light_k, light_v, halo_prev, halo_next, heavy_q, heavy_k, heavy_v, score_q), m)
            + (after(w_out, *held),)
            + all_picks((query_row,) + segs, m),
            scalars=1,
            managed=False,
            weight=11,
        )
        attended.append(outs)
        begun = mp_first(outs[0], outs[1], *earlier)
        attn_moved.append(mp_second(begun))
        held, earlier = (begun,), (attn_moved[m][1],)

    fed = []
    grad_moved = []
    split = data_size if aligned else 1
    total_rows = ffn_bases(width, light_hidden, heavy_hidden)[1]
    own = [
        (row_shape, low),
        ((tok_local, light_hidden), low),
        ((2, tok_local, light_hidden), low),
        ((routed_local, width), low),
        ((routed_local, heavy_hidden), low),
        ((2, routed_local, heavy_hidden), low),
        ((routed_local, width), low),
    ]
    for m in micros:
        beside = attended[m + 1][0] if m + 1 < micro_count else fed[m - 1][1]
        ffn_outs = [
            in_vmem(row_shape, low),
            in_vmem(half_shape, low),
            in_vmem(half_shape, low),
            in_vmem(half_shape, low),
            in_vmem(half_shape, low),
            in_vmem((1, width), wide),
        ]
        scratch = [
            pltpu.VMEM(row_shape, low),
            pltpu.VMEM((routed_local, width), low),
            pltpu.VMEM((routed_local, width), low),
        ]
        kept = ()
        if m + 1 < micro_count:
            ffn_outs = ffn_outs + [in_vmem(*o) for o in own]
        else:
            ffn_outs = ffn_outs + [in_vmem((split, total_rows // split, CHUNK), low)]
            scratch = [
                *(pltpu.VMEM(*o) for o in own),
                pltpu.VMEM((width, micro_count * tok_local), low),
                pltpu.VMEM((width, micro_count * routed_local), low),
                *scratch,
            ]
            for i in range(m):
                kept = kept + tuple(fed[i][6:13]) + (cot_parts[i],)
        outs = kernel_call(
            functools.partial(ffn_body, m if m + 1 == micro_count else 0),
            ffn_outs,
            scratch,
            (core_flag,)
            + mp_third(attn_moved[m], beside)
            + (token_parts[m], cot_parts[m], after(vectors, *held), ffn_col[m], ffn_row[m], w_ffn)
            + kept,
            scalars=1,
            managed=True,
            weight=17 if m + 1 < micro_count else 23,
        )
        fed.append(outs)
        begun = mp_first(outs[3], outs[4], *earlier)
        grad_moved.append(mp_second(begun))
        held, earlier = (begun,), (grad_moved[m][1],)
    pack_ffn = fed[-1][6]
    if not aligned:
        pieces = []
        at = 0
        for block in blocks:
            size = block.shape[0] * block.shape[1] * data_size
            pieces.append(
                pack_ffn[0, at : at + size]
                .reshape(block.shape[0], data_size, block.shape[1], CHUNK)
                .transpose(1, 0, 2, 3)
                .reshape(data_size, -1, CHUNK)
            )
            at = at + size
        pack_ffn = jnp.concatenate(pieces, axis=1)
    sum_ffn = lax.psum_scatter(pack_ffn.reshape(-1, CHUNK), "dp", scatter_dimension=0, tiled=True)

    y_moved = []
    backs = []
    edges = jnp.zeros((2, 1, 2, RADIUS, head_cols), low)
    y_begun = [mp_first(fed[m][1], fed[m][2]) for m in micros]
    for m in micros:
        outs = kernel_call(
            functools.partial(attend_back_body, m),
            [
                in_vmem(row_shape, low),
                in_vmem((1, width), wide),
                in_vmem((tok_local, head_cols), low),
                in_vmem((2, tok_local, head_cols), low),
                in_vmem((2, 2 * RADIUS, head_cols), wide),
                in_vmem((2, m + 1, 2, RADIUS, head_cols), low),
                in_vmem((routed_local, head_cols), low),
                in_vmem((data_size, routed_local, 2 * head_cols), low),
                in_vmem((routed_all, head_cols), low),
                in_vmem((routed_local, width), low),
                in_vmem((routed_local, 1), wide),
            ],
            [
                extended,
                extended,
                pltpu.VMEM((tok_local, head_cols), low),
                pltpu.VMEM((tok_local + 2 * RADIUS, head_cols), wide),
                pltpu.VMEM((tok_local + 2 * RADIUS, head_cols), wide),
            ],
            (core_flag,)
            + mp_third(grad_moved[m], pack_ffn if m == 0 else backs[m - 1][0])
            + (fed[m][0], cot_parts[m], after(vectors, pack_ffn, y_begun[m]))
            + all_picks(
                (light_q, light_k, light_v, halo_prev, halo_next, heavy_q, heavy_k, heavy_v, score_k, score_q), m
            )
            + (attended[m][4], w_out)
            + all_picks((query_col,) + segs, m)
            + (edges,),
            scalars=1,
            managed=True,
            weight=22,
        )
        edges = outs[5]
        backs.append(outs)
        y_moved.append(mp_second(after(y_begun[m], outs[0], *earlier)))
        earlier = (y_moved[m][1],)
    held = ()

    from_prev = lax.ppermute(edges[0], "dp", up)
    from_next = lax.ppermute(edges[1], "dp", down)

    last = []
    last_moved = []
    for m in micros:
        outs = backs[m]
        made = kernel_call(
            project_back_body,
            [
                in_vmem(half_shape, low),
                in_vmem(half_shape, low),
                in_vmem((2, tok_local, head_cols), low),
                in_vmem((1, width), wide),
                in_vmem((1, width), wide),
            ],
            [pltpu.VMEM((routed_local, width), low)],
            (core_flag, outs[2], outs[3], outs[4], from_prev[m], from_next[m], outs[6], outs[10], rows_q[m])
            + (after(vectors, *held), w_in, query_row[m], normed_low[m]),
            scalars=1,
            managed=False,
            weight=8,
        )
        last.append(made)
        if m + 1 < micro_count:
            begun = mp_first(made[0], made[1])
            last_moved.append(mp_second(after(begun, *earlier)))
            held, earlier = (), (last_moved[m][1],)

    attn_rows = 3 * in_rows + 2 * out_rows * sides
    groups = []
    for m in micros:
        outs = backs[m]
        groups.append(
            (outs[2], last[m][2], outs[6], outs[7], outs[8], attended[m][2], outs[0], attended[m][3], outs[9])
            + (normed_low[m], rows_q_low[m], key_normed[m])
        )
    if aligned:
        (pack_attn,) = kernel_call(
            attn_grads_body,
            [in_vmem((data_size, attn_rows + micro_count * routed_local, lane), low)],
            [
                pltpu.VMEM((width, micro_count * tok_local), low),
                pltpu.VMEM((width, micro_count * routed_all), low),
            ],
            sum(groups, ()),
            managed=True,
            weight=12,
        )
    else:
        totals = [0.0] * 8
        for m, group in enumerate(groups):
            grad_k = group[3].reshape(routed_all, -1)[:, :head_cols]
            pairs = (
                (normed_low[m], group[0]), (normed_low[m], group[1][0]), (normed_low[m], group[1][1]),
                (rows_q_low[m], group[2]), (key_normed[m], grad_k), (key_normed[m], group[4]),
                (group[5], group[6]), (group[7], group[8]),
            )
            totals = [total + tn(left, right) for total, (left, right) in zip(totals, pairs)]
        grad_in = jnp.stack(totals[:6]).astype(low)
        grad_out = jnp.stack(totals[6:]).astype(low)
        pack_attn = jnp.concatenate(
            [
                grad_in.reshape(3, 2, data_size, in_rows, head_cols)
                .transpose(2, 0, 3, 1, 4)
                .reshape(data_size, 3 * in_rows, lane),
                grad_out.reshape(2, data_size, out_rows, sides, lane)
                .transpose(1, 3, 0, 2, 4)
                .reshape(data_size, -1, lane),
            ]
            + [backs[m][7] for m in micros],
            axis=1,
        )
    sum_attn = lax.psum_scatter(
        after(pack_attn.reshape(-1, lane), sum_ffn), "dp", scatter_dimension=0, tiled=True
    )
    owned = sum_attn[attn_rows:]
    sum_attn = sum_attn[:attn_rows]
    begun = mp_first(last[-1][0], last[-1][1], pack_attn)
    last_moved.append(mp_second(after(begun, *earlier)))
    earlier = (last_moved[-1][1],)

    device_count = data_size * model_size

    def all_parts(values):
        sent = jnp.broadcast_to(values[None], (device_count,) + values.shape)
        return lax.all_to_all(sent, ("dp", "mp"), 0, 0, tiled=True)

    place = jnp.stack([data_index, model_index]).astype(jnp.int32)

    def unpack_ffn(sources, grads):
        if len(sources) > 1:
            for source, grad in zip(sources, grads):
                grad[...] = source[...]
            return
        (ref,) = sources
        at = 0
        for grad, lead in zip(grads, (2, 0, 2, 0)):
            rows, cols = grad.shape[-2:]
            for l in range(max(lead, 1)):
                for j in range(cols // CHUNK):
                    value = ref[at : at + rows, :].astype(wide)
                    spot = slice(j * CHUNK, (j + 1) * CHUNK)
                    if lead:
                        grad[l, :, spot] = value
                    else:
                        grad[:, spot] = value
                    at = at + rows

    def unpack_attn(sources, grads):
        if len(sources) > 1:
            for source, grad in zip(sources, grads):
                grad[...] = source[...]
            return
        (ref,) = sources
        total = ref[...].astype(wide)
        for j in range(3):
            pair = total[j * in_rows : (j + 1) * in_rows]
            grads[0][2 * j] = pair[:, :head_cols]
            grads[0][2 * j + 1] = pair[:, head_cols:]
        for j in range(sides):
            at = 3 * in_rows + 2 * j * out_rows
            for m in range(2):
                grads[1][m, :, j * lane : (j + 1) * lane] = total[at + m * out_rows : at + (m + 1) * out_rows]

    def first_sums(matrices, unpack, sources, sums_shape, weights, blocks=None):
        n = len(weights)
        sums_out = kernel_call(
            functools.partial(sums_body, matrices, unpack, n),
            [in_vmem(w.shape, wide) for w in weights] + [in_vmem(sums_shape, wide)],
            [],
            tuple(sources) + tuple(weights),
            weight=4,
        )
        rows, cols = sums_shape
        size = rows * cols
        sent = jnp.broadcast_to(sums_out[n].reshape(1, 1, size), (device_count, 1, size))
        if blocks is None:
            got = lax.all_to_all(sent, ("dp", "mp"), 0, 0, tiled=True)
            return sums_out, got.reshape(device_count, rows, cols)
        block = blocks.shape[1:]
        own = jnp.broadcast_to(
            blocks.reshape(data_size, 1, 1, -1), (data_size, model_size, 1, math.prod(block))
        ).reshape(device_count, 1, -1)
        got = lax.all_to_all(jnp.concatenate([sent, own], axis=2), ("dp", "mp"), 0, 0, tiled=True)
        parts = got[:, :, :size].reshape(device_count, rows, cols)
        return sums_out, parts, jnp.sum(got[:, 0, size:], axis=0).reshape(block)

    def optimize(matrices, sums_out, parts, weights, moments, moments_here, vectors_in):
        n = len(weights)
        grads = tuple(sums_out[:n])
        row_old, col_old, row_mine, col_mine = moments_here
        vector_count = len(vectors_in)
        made = kernel_call(
            functools.partial(moments_body, matrices, n, vector_count, data_size, model_size),
            [in_vmem(w.shape, wide) for w in weights]
            + [in_vmem(r.shape, wide) for r in row_old]
            + [in_vmem(c.shape, wide) for c in col_old]
            + [in_vmem(v[0].shape, wide) for v in vectors_in for _ in range(2)]
            + [in_vmem((8, 128), wide)],
            [],
            (place, parts)
            + grads
            + tuple(row_old)
            + tuple(col_old)
            + tuple(row_mine)
            + tuple(col_mine)
            + sum(vectors_in, ()),
            scalars=1,
            weight=5,
        )
        updates, row_new, col_new = made[:n], made[n : 2 * n], made[2 * n : 3 * n]
        vector_made = made[3 * n : -1]
        counts = [
            weights[m.array].shape[-2] * weights[m.array].shape[-1] * device_count for m in matrices
        ] + [width for v in vectors_in for _ in range(v[0].shape[0])]
        all_weights = tuple(weights) + tuple(v[2] for v in vectors_in)

        def finish(aux):
            news = kernel_call(
                functools.partial(weights_body, matrices, counts, n, vector_count),
                [in_vmem(w.shape, wide) for w in all_weights],
                [],
                (aux,) + all_weights + tuple(updates) + tuple(vector_made[1::2]),
                weight=4,
            )
            results = []
            for array in range(n):
                rows, cols = moments[array]
                results.append(
                    [grads[array], row_new[array].reshape(rows.shape), col_new[array].reshape(cols.shape), news[array]]
                )
            for i in range(vector_count):
                results.append([vectors_in[i][0], vector_made[2 * i], news[n + i]])
            return results

        return made[-1], finish

    if aligned:
        ffn_sources = (sum_ffn,)
    else:
        ffn_sources = []
        at = 0
        for weight, block, size in zip((light_in, light_out, heavy_in, heavy_out), blocks, block_rows):
            lead = weight.size // (weight.shape[-1] * weight.shape[-2])
            ffn_sources.append(
                unblocked(sum_ffn[at : at + size].reshape(block.shape), lead).reshape(weight.shape).astype(wide)
            )
            at = at + size
    ffn_made, ffn_parts = first_sums(
        ffn_list, unpack_ffn, ffn_sources, (5, light_hidden + width), ffn_weights
    )
    ffn_sums = ffn_made[-1]
    ffn_aux, ffn_finish = optimize(
        ffn_list,
        ffn_made,
        ffn_parts,
        ffn_weights,
        ffn_moments,
        ffn_here,
        (),
    )
    ffn_got = all_parts(ffn_aux)
    ffn_results = ffn_finish(ffn_got)

    key_half = (micro_count * routed_local // 2, width)
    key_keep, key_send, vector_blocks = kernel_call(
        functools.partial(keys_back_body, micro_count),
        [in_vmem(key_half, low), in_vmem(key_half, low), in_vmem((data_size, 8, 128), wide)],
        [pltpu.VMEM((routed_local, width), low), pltpu.VMEM((micro_count * routed_local, width), low)],
        (core_flag, owned, vectors, w_in)
        + tuple(rows_k)
        + tuple(last[m][4] for m in micros)
        + tuple(backs[m][1] for m in micros)
        + tuple(last[m][3] for m in micros)
        + tuple(fed[m][5] for m in micros),
        scalars=1,
        weight=5,
    )
    key_begun = mp_first(key_keep, key_send)
    key_moved = mp_second(key_begun)
    chunks = tok_local // CHUNK
    smem = pl.BlockSpec(memory_space=pltpu.SMEM)
    by_chunk = pl.BlockSpec((CHUNK, width), lambda i: (i, 0))
    by_half = pl.BlockSpec((CHUNK, width), lambda i: (i % (chunks // 2), 0))
    both_out = pl.BlockSpec((micro_count, CHUNK, width), lambda i: (0, i, 0))

    def fixed(shape):
        return pl.BlockSpec(shape, lambda i: (0,) * len(shape))

    def streamed(body, in_specs, out_specs, outs, scratch, args, weight):
        return pl.pallas_call(
            functools.partial(body, chunks),
            grid=(chunks,),
            in_specs=in_specs,
            out_specs=out_specs,
            out_shape=outs,
            scratch_shapes=scratch,
            compiler_params=pltpu.CompilerParams(vmem_limit_bytes=VMEM_BYTES),
            cost_estimate=pl.CostEstimate(flops=weight * 1_150_000_000, bytes_accessed=1_000_000, transcendentals=0),
        )(*args)

    join_args = (core_flag,)
    for m in micros:
        join_args = join_args + (fed[m][0],) + mp_third(y_moved[m], pack_attn)
    (mixed,) = streamed(
        join_body,
        [smem] + [by_chunk, by_half, by_half] * micro_count,
        [both_out],
        [in_vmem(tokens.shape, low)],
        [],
        join_args,
        6,
    )
    pieces = mp_third(key_moved) + (vectors,)
    for m in micros:
        pieces = pieces + mp_third(last_moved[m], pack_attn if m + 1 < micro_count else mixed)
        pieces = pieces + (backs[m][0], key_row[m])
    (grad_tokens,) = streamed(
        finish_body,
        [smem, fixed(key_half), fixed(key_half), fixed((8, width))]
        + [by_half, by_half, by_chunk, fixed((1, routed_local))] * micro_count
        + [both_out],
        [both_out],
        [in_vmem(tokens.shape, wide)],
        [pltpu.VMEM((micro_count * routed_local, width), low)],
        (core_flag,) + pieces + (tokens,),
        8,
    )
    if aligned:
        attn_sources = (sum_attn,)
    else:
        sum_attn = sum_attn.astype(wide)
        attn_sources = (
            sum_attn[: 3 * in_rows]
            .reshape(3, in_rows, 2, head_cols)
            .transpose(0, 2, 1, 3)
            .reshape(6, in_rows, head_cols),
            sum_attn[3 * in_rows :]
            .reshape(sides, 2, out_rows, lane)
            .transpose(1, 2, 0, 3)
            .reshape(2, out_rows, width),
        )
    attn_sums, attn_parts, my_vectors = first_sums(
        attn_list, unpack_attn, attn_sources, (8, 512), attn_weights, vector_blocks
    )
    my_vectors = my_vectors[:, :in_rows]
    attn_aux, attn_finish = optimize(
        attn_list,
        attn_sums,
        attn_parts,
        attn_weights,
        attn_moments,
        attn_here,
        ((my_vectors[:2], second_gains, gains), (my_vectors[2:5], second_router, router)),
    )
    attn_results = attn_finish(all_parts(attn_aux))
    results = [mixed, grad_tokens]
    for result in attn_results[:2] + ffn_results + attn_results[2:]:
        results.extend(result)
    return tuple(results)


def solution(mesh):
    placed = (
        P(None, "dp", None),
        P(None, "dp", None),
        P(),
        P(None, "dp"),
        P(),
        P(None, "dp"),
        P(None, "dp", "mp"),
        P(None, ("mp", "dp"), None),
        P(None, "dp", "mp"),
        P(("mp", "dp"), None),
        P(None, "dp", "mp"),
        P(("mp", "dp"), None),
        P(None, "dp"),
        P(None, "dp"),
        P(),
        P(),
        P(),
        P(),
        P(),
        P(),
        P(),
        P(),
        P(),
        P(),
        P(),
        P(),
        P(None, "dp"),
        P(None, "dp"),
    )
    return jax.shard_map(
        shards,
        mesh=mesh,
        in_specs=placed,
        out_specs=(
            P(None, "dp", None),
            P(None, "dp", None),
            P(None, "dp", "mp"),
            P(),
            P(),
            P(None, "dp", "mp"),
            P(None, ("mp", "dp"), None),
            P(),
            P(),
            P(None, ("mp", "dp"), None),
            P(None, "dp", "mp"),
            P(),
            P(),
            P(None, "dp", "mp"),
            P(("mp", "dp"), None),
            P(),
            P(),
            P(("mp", "dp"), None),
            P(None, "dp", "mp"),
            P(),
            P(),
            P(None, "dp", "mp"),
            P(("mp", "dp"), None),
            P(),
            P(),
            P(("mp", "dp"), None),
            P(None, "dp"),
            P(None, "dp"),
            P(None, "dp"),
            P(None, "dp"),
            P(None, "dp"),
            P(None, "dp"),
        ),
        check_vma=False,
    )
```

```python
import functools
import math

import jax
import jax.numpy as jnp
from jax import lax
from jax.experimental import pallas as pl
from jax.experimental.pallas import tpu as pltpu
from jax.sharding import PartitionSpec as P

D = 768
LH = 8
LDH = 96
HH = 12
HDH = 64
WIN = 128
STEP = 10

norm_eps = 1e-06
tiny_square = 1e-30
scale_floor = 0.001
clip_level = 1.0
step_rate = 0.5
masked_score = -1e30
gelu_scale = math.sqrt(2.0 / math.pi)
gelu_cubic = 0.044715

low = jnp.bfloat16
wide = jnp.float32
CHUNK = 256
BLOCK = 128
RADIUS = WIN // 2
KEYS = 1024
VECTORS_AT = 512
VMEM_BYTES = 60 * 1024 * 1024
LARGE = 200 * 1024


def nn(left, right):
    return lax.dot_general(left, right, (((1,), (0,)), ((), ())), preferred_element_type=wide)


def nt(left, right):
    return lax.dot_general(left, right, (((1,), (1,)), ((), ())), preferred_element_type=wide)


def tn(left, right):
    return lax.dot_general(left, right, (((0,), (0,)), ((), ())), preferred_element_type=wide)


def sigmoid(logit):
    return 1.0 / (1.0 + jnp.exp(-logit))


def gelu_pair(gate):
    squared = gate * gate
    bent = jnp.tanh(gelu_scale * gate * (1.0 + gelu_cubic * squared))
    half = 0.5 * (1.0 + bent)
    value = gate * half
    slope = half + 0.5 * gate * (1.0 - bent * bent) * gelu_scale * (1.0 + 3.0 * gelu_cubic * squared)
    return value, slope


def picks_rows(idx_col, count):
    spots = lax.broadcasted_iota(jnp.int32, (idx_col.shape[0], count), 1)
    return (spots == idx_col).astype(low)


def picks_cols(idx_row, start, count):
    spots = lax.broadcasted_iota(jnp.int32, (count, idx_row.shape[1]), 0) + start
    return (spots == idx_row).astype(low)


def head_mask(width, size, head):
    spot = lax.broadcasted_iota(jnp.int32, (1, width), 1)
    return ((spot >= head * size) & (spot < (head + 1) * size)).astype(low)


def softmax_parts(scores, allowed):
    masked = jnp.where(allowed, scores, masked_score)
    top = jnp.max(masked, axis=-1, keepdims=True)
    grown = jnp.exp(masked - top)
    return grown * (1.0 / jnp.sum(grown, axis=-1, keepdims=True))


def inverse_rms(values):
    return lax.rsqrt(jnp.mean(values * values, axis=-1, keepdims=True) + norm_eps)


def norm_back(values, gain_row, upstream):
    inverse = inverse_rms(values)
    unit = values * inverse
    scaled = upstream * gain_row
    pulled = inverse * (scaled - unit * jnp.mean(scaled * unit, axis=-1, keepdims=True))
    return pulled, jnp.sum(upstream * unit, axis=0, keepdims=True)


def in_vmem(shape, dtype):
    return jax.ShapeDtypeStruct(shape, dtype)


def vmem_bytes(shape, dtype):
    size = jnp.dtype(dtype).itemsize
    shape = (1,) * (2 - len(shape)) + tuple(shape)
    rows, cols = -(-shape[-2] // (32 // size)) * (32 // size), -(-shape[-1] // 128) * 128
    return math.prod(shape[:-2]) * rows * cols * size


class Transfers:
    def __init__(self, ins, outs, sems):
        self.ins = {id(held): (far, held) for far, held in ins}
        self.outs = {id(held): (far, held) for far, held in outs}
        self.sems, self.used = sems, 0
        self.begun, self.finished, self.going = {}, set(), []

    def copy(self, source, target):
        made = pltpu.make_async_copy(source, target, self.sems.at[self.used])
        self.used += 1
        made.start()
        return made

    def begin(self, *refs):
        for ref in refs:
            if id(ref) in self.ins and id(ref) not in self.begun:
                self.begun[id(ref)] = self.copy(*self.ins[id(ref)])

    def need(self, *refs):
        self.begin(*refs)
        for ref in refs:
            if id(ref) in self.ins and id(ref) not in self.finished:
                self.begun[id(ref)].wait()
                self.finished.add(id(ref))

    def done(self, ref, part=None):
        if id(ref) not in self.outs:
            return
        far, held = self.outs[id(ref)]
        self.finished.add(id(ref))
        if part is None:
            self.going.append(self.copy(held, far))
        else:
            self.going.append(self.copy(held.at[part], far.at[part]))

    def close(self):
        for far, held in self.ins.values():
            self.need(held)
        for far, held in self.outs.values():
            if id(held) not in self.finished:
                self.done(held)
        for made in self.going:
            made.wait()


class Pick:
    def __init__(self, array, index):
        self.array, self.index = array, index
        self.shape, self.dtype = array.shape[1:], array.dtype


def kernel_call(body, outs, scratch, args, scalars=0, weight=10, managed=False, parts=4):
    vmem = pl.BlockSpec(memory_space=pltpu.VMEM)
    smem = pl.BlockSpec(memory_space=pltpu.SMEM)
    far = pl.BlockSpec(memory_space=pl.ANY)

    def large(x):
        return managed and vmem_bytes(x.shape, x.dtype) >= LARGE

    picked = {i: arg.index for i, arg in enumerate(args) if isinstance(arg, Pick)}
    ins = [i for i in range(scalars, len(args)) if large(args[i])]
    assert all(i in ins for i in picked)
    ends = [i for i in range(len(outs)) if large(outs[i])]
    held = [pltpu.VMEM(args[i].shape, args[i].dtype) for i in ins]
    held = held + [pltpu.VMEM(outs[i].shape, outs[i].dtype) for i in ends]
    sems = [pltpu.SemaphoreType.DMA((len(held) + parts,))] if managed else []

    def run(*refs):
        refs = list(refs)
        count = len(args) + len(outs)
        operands, results = refs[: len(args)], refs[len(args) : count]
        kept = refs[count : count + len(held)]
        rest = refs[count + len(held) :]
        if managed:
            rest, sem = rest[:-1], rest[-1]
            pairs_in, pairs_out = [], []
            for i, ref in zip(ins, kept):
                pairs_in.append((operands[i].at[picked[i]] if i in picked else operands[i], ref))
                operands[i] = ref
            for i, ref in zip(ends, kept[len(ins) :]):
                pairs_out.append((results[i], ref))
                results[i] = ref
            moves = Transfers(pairs_in, pairs_out, sem)
            body(moves, *operands, *results, *rest)
            moves.close()
        else:
            body(*operands, *results, *rest)

    return pl.pallas_call(
        run,
        out_shape=outs,
        in_specs=[smem] * scalars + [far if large(x) else vmem for x in args[scalars:]],
        out_specs=[far if large(x) else vmem for x in outs],
        scratch_shapes=held + list(scratch) + sems,
        compiler_params=pltpu.CompilerParams(vmem_limit_bytes=VMEM_BYTES),
        cost_estimate=pl.CostEstimate(
            flops=weight * 1_150_000_000, bytes_accessed=1_000_000, transcendentals=0
        ),
    )(*(arg.array if isinstance(arg, Pick) else arg for arg in args))


def mp_total(core, mine_ref, other_ref, chunk, per_half, size=CHUNK):
    rows = pl.ds(pl.multiple_of((chunk % per_half) * size, size), size)
    flag = ((chunk // per_half) == core).astype(wide)
    return mine_ref[rows, :].astype(wide) * flag + other_ref[rows, :].astype(wide) * (1.0 - flag)


def mp_store(core, keep_ref, send_ref, chunk, per_half, size, value):
    rows = pl.ds(pl.multiple_of((chunk % per_half) * size, size), size)
    kept = (chunk // per_half) == core

    @pl.when(kept)
    def _():
        keep_ref[rows, :] = value

    @pl.when(jnp.logical_not(kept))
    def _():
        send_ref[rows, :] = value


def unpack_body(got_ref, w_in_ref, w_out_ref, vec_ref):
    count, _, lane = got_ref.shape
    in_rows = w_in_ref.shape[1] // count
    head_cols = w_in_ref.shape[2]
    for j in range(3):
        pair = got_ref[:, j * in_rows : (j + 1) * in_rows, :].reshape(count * in_rows, lane)
        w_in_ref[2 * j] = pair[:, :head_cols]
        w_in_ref[2 * j + 1] = pair[:, head_cols:]
    base = 3 * in_rows
    out_rows = w_out_ref.shape[1] // count
    sides = w_out_ref.shape[2] // lane
    for j in range(sides):
        cols = slice(j * lane, (j + 1) * lane)
        blocks = [
            got_ref[d, base + j * 2 * out_rows : base + (j + 1) * 2 * out_rows, :].astype(wide)
            for d in range(count)
        ]
        for s in range(2):
            w_out_ref[s, :, cols] = jnp.concatenate(
                [b[s * out_rows : (s + 1) * out_rows] for b in blocks], axis=0
            ).astype(low)
    base = base + 2 * out_rows * sides
    vec_ref[...] = jnp.concatenate(
        [got_ref[d, base : base + 16, :].astype(wide)[:8, :in_rows] for d in range(count)], axis=1
    )


def block_of(ref, base, index, full):
    count = ref.shape[0]
    rows = full // count
    return ref[:, row_span(base // count + index * rows, rows), :].reshape(full, CHUNK)


def row_span(start, size):
    if isinstance(start, int):
        return slice(start, start + size)
    return pl.ds(pl.multiple_of(start, math.gcd(size, 128)), size)


def col_span(index):
    return pl.ds(pl.multiple_of(index * CHUNK, CHUNK), CHUNK)


def part_of(ref, base, index, full, piece):
    count = ref.shape[0]
    rows = full // count
    at = base // count + index * rows
    if rows <= CHUNK:
        span = CHUNK // rows
        return ref[pl.ds(piece * span, span), at : at + rows, :].reshape(CHUNK, CHUNK)
    return ref[0, row_span(at + piece * CHUNK, CHUNK), :]


def ffn_bases(width, light, heavy):
    sides = width // CHUNK
    light_in = 2 * (light // CHUNK) * width
    light_out = sides * light
    heavy_in = 2 * (heavy // CHUNK) * width
    bases = [0, light_in, light_in + light_out, light_in + light_out + heavy_in]
    return bases, bases[3] + sides * heavy


def project_body(moves, vec_ref, w_ref, *refs):
    low_ref = refs[-1]
    micros = (len(refs) - 1) // 12
    inputs, outputs = refs[: 3 * micros], refs[3 * micros : -1]
    for m in range(micros):
        moves.begin(inputs[3 * m])
        moves.begin(w_ref)
    for m in range(micros):
        tok_ref, qcol_ref, kcol_ref = inputs[3 * m : 3 * m + 3]
        n1b_ref, q_ref, k_ref, v_ref, hq_ref, sq_ref, nq_ref, nk_ref, qrows_ref = outputs[9 * m : 9 * m + 9]
        count = tok_ref.shape[0]
        moves.need(tok_ref, w_ref)

        def step(c, carry):
            rows = pl.ds(pl.multiple_of(c * CHUNK, CHUNK), CHUNK)
            values = tok_ref[rows, :].astype(wide)
            normed = values * inverse_rms(values) * vec_ref[0:1, :]
            high = normed.astype(low)
            n1b_ref[rows, :] = high
            low_ref[rows, :] = (normed - high.astype(wide)).astype(low)
            q_ref[rows, :] = nn(high, w_ref[0]).astype(low)
            k_ref[rows, :] = nn(high, w_ref[1]).astype(low)
            v_ref[rows, :] = nn(high, w_ref[2]).astype(low)
            return carry

        lax.fori_loop(0, count // CHUNK, step, 0)
        for ref in (k_ref, v_ref, q_ref, n1b_ref):
            moves.done(ref)
        picks = picks_rows(qcol_ref[...], count)
        query_rows = nn(picks, n1b_ref[...])
        query_wide = query_rows + nn(picks, low_ref[...])
        qrows_ref[...] = query_rows.astype(low)
        nq_ref[...] = query_wide
        hq_ref[...] = nn(query_rows.astype(low), w_ref[3]).astype(low)
        sq_ref[...] = sigmoid(jnp.sum(query_wide * vec_ref[2:3, :], axis=-1, keepdims=True))
        picks = picks_rows(kcol_ref[...], count)
        nk_ref[...] = nn(picks, n1b_ref[...]) + nn(picks, low_ref[...])
        for ref in (qrows_ref, nq_ref, nk_ref):
            moves.done(ref)


def keys_body(o_ref, a_ref, b_ref, c_ref, vec_ref, w_ref, *outs):
    blocks, micros, part, width = o_ref.shape
    for m in range(micros):
        n_ref, k_ref, v_ref, sk_ref = outs[4 * m : 4 * m + 4]
        for p, ref in enumerate((o_ref, a_ref, b_ref, c_ref)):
            values = ref[:, m].reshape(blocks * part, width).astype(wide)
            normed = values * inverse_rms(values) * vec_ref[0:1, :]
            high = normed.astype(low)
            score = sigmoid(jnp.sum(normed * vec_ref[3:4, :], axis=-1, keepdims=True))
            n_ref[:, p] = high.reshape(blocks, part, width)
            sk_ref[:, p] = score.reshape(blocks, part, 1)
            k_ref[:, p] = nn(high, w_ref[4]).astype(low).reshape(blocks, part, -1)
            v_ref[:, p] = (nn(high, w_ref[5]) * score).astype(low).reshape(blocks, part, -1)


def fill_extended(ext_ref, prev, inner, after):
    count = inner.shape[0]
    ext_ref[0:RADIUS, :] = prev
    ext_ref[RADIUS : RADIUS + count, :] = inner
    ext_ref[RADIUS + count :, :] = after


def near_mask(seg_q, seg_k):
    shape = (BLOCK, 2 * BLOCK)
    gap = lax.broadcasted_iota(jnp.int32, shape, 1) - lax.broadcasted_iota(jnp.int32, shape, 0)
    return (gap >= 0) & (gap <= 2 * RADIUS) & (seg_q == seg_k)


def attend_body(
    core_ref, q_ref, k_ref, v_ref, prev_ref, after_ref, hq_ref, hk_ref, hv_ref, sq_ref, wo_ref,
    qrow_ref, segq_ref, segk_ref, hsegq_ref, hsegk_ref,
    keep_ref, send_ref, lmix_ref, hmix_ref, hproj_ref,
    kx_ref, vx_ref, rows_ref,
):
    count, width = q_ref.shape
    light_heads = width // LDH
    heavy_heads = width // HDH
    allowed = hsegq_ref[...] == hsegk_ref[...]
    mix = jnp.zeros((hq_ref.shape[0], width), wide)
    for h in range(heavy_heads):
        mask = head_mask(width, HDH, h)
        probs = softmax_parts(nt(hq_ref[...], hk_ref[...] * mask) * (1.0 / math.sqrt(HDH)), allowed)
        mix = mix + nn(probs.astype(low), hv_ref[...] * mask)
    mix_low = mix.astype(low)
    hmix_ref[...] = mix_low
    proj = nn(mix_low, wo_ref[1])
    hproj_ref[...] = proj
    rows_ref[...] = (sq_ref[...] * proj).astype(low)
    fill_extended(kx_ref, prev_ref[0], k_ref[...], after_ref[0])
    fill_extended(vx_ref, prev_ref[1], v_ref[...], after_ref[1])

    def step(b, carry):
        rows = pl.ds(pl.multiple_of(b * BLOCK, BLOCK), BLOCK)
        keys = pl.ds(pl.multiple_of(b * BLOCK, BLOCK), 2 * BLOCK)
        seg_k = jnp.concatenate([segk_ref[b], segk_ref[b + 1]], axis=1)
        near = near_mask(segq_ref[rows, :], seg_k)
        queries = q_ref[rows, :]
        block_keys = kx_ref[keys, :]
        block_values = vx_ref[keys, :]
        total = jnp.zeros((BLOCK, width), wide)
        for h in range(light_heads):
            mask = head_mask(width, LDH, h)
            probs = softmax_parts(nt(queries, block_keys * mask) * (1.0 / math.sqrt(LDH)), near)
            total = total + nn(probs.astype(low), block_values * mask)
        total_low = total.astype(low)
        lmix_ref[rows, :] = total_low
        spread = picks_cols(qrow_ref[...], b * BLOCK, BLOCK)
        part = (nn(total_low, wo_ref[0]) + nn(spread, rows_ref[...])).astype(low)
        mp_store(core_ref[0], keep_ref, send_ref, b, count // BLOCK // 2, BLOCK, part)
        return carry

    lax.fori_loop(0, count // BLOCK, step, 0)


def ffn_body(last, *refs):
    moves, core_ref, mine_ref, other_ref, tok_ref, cot_ref, vec_ref, fcol_ref, frow_ref, w_ref = refs[:10]
    low_ref, out_rows_ref, grad_rows_ref = refs[-3:]
    if last:
        earlier = [refs[10 + 8 * m : 18 + 8 * m] for m in range(last)]
        middle_ref, ykeep_ref, ysend_ref, gkeep_ref, gsend_ref, router_ref, pack_ref = refs[10 + 8 * last : 17 + 8 * last]
        own = refs[17 + 8 * last : 24 + 8 * last]
        turned_ref, turned_rows_ref = refs[24 + 8 * last : 26 + 8 * last]
    else:
        earlier = []
        middle_ref, ykeep_ref, ysend_ref, gkeep_ref, gsend_ref, router_ref = refs[10:16]
        own = refs[16:23]
    n2b_ref, hidden_ref, dgu_ref, frows_ref, hhid_ref, dhgu_ref, dhout_ref = own
    count, width = tok_ref.shape
    chunks = count // CHUNK
    core = core_ref[0]
    light = hidden_ref.shape[1]
    heavy = hhid_ref.shape[1]
    sides = width // CHUNK
    bases, _ = ffn_bases(width, light, heavy)
    moves.begin(mine_ref, other_ref, tok_ref)
    moves.begin(w_ref, cot_ref)
    for group in earlier:
        moves.begin(*group)
    moves.need(mine_ref, other_ref, tok_ref)

    def heavy_in(s, j):
        return block_of(w_ref, bases[2], s * (heavy // CHUNK) + j, width)

    def heavy_out(t, j):
        return part_of(w_ref, bases[3], t, heavy, j)

    def light_in(s):
        return block_of(w_ref, bases[0], s, width)

    def light_out(t):
        return block_of(w_ref, bases[1], t, light)

    def enter(c, carry):
        rows = pl.ds(pl.multiple_of(c * CHUNK, CHUNK), CHUNK)
        middle = tok_ref[rows, :].astype(wide) + mp_total(core, mine_ref, other_ref, c, chunks // 2)
        middle_ref[rows, :] = middle.astype(low)
        normed = middle * inverse_rms(middle) * vec_ref[1:2, :]
        high = normed.astype(low)
        n2b_ref[rows, :] = high
        low_ref[rows, :] = (normed - high.astype(wide)).astype(low)
        return carry

    lax.fori_loop(0, chunks, enter, 0)
    moves.done(middle_ref)
    moves.done(n2b_ref)
    moves.need(w_ref, cot_ref)
    picks = picks_rows(fcol_ref[...], count)
    rows_high = nn(picks, n2b_ref[...])
    rows_wide = rows_high + nn(picks, low_ref[...])
    rows_low = rows_high.astype(low)
    frows_ref[...] = rows_low
    score = sigmoid(jnp.sum(rows_wide * vec_ref[4:5, :], axis=-1, keepdims=True))
    cot_rows = nn(picks, cot_ref[...])
    grad_out = (score * cot_rows).astype(low)
    dhout_ref[...] = grad_out
    out_rows = [jnp.zeros((rows_low.shape[0], CHUNK), wide) for _ in range(sides)]
    grad_rows = jnp.zeros(rows_low.shape, wide)
    for j in range(heavy // CHUNK):
        cols = slice(j * CHUNK, (j + 1) * CHUNK)
        gate = nn(rows_low, heavy_in(0, j))
        up = nn(rows_low, heavy_in(1, j))
        value, slope = gelu_pair(gate)
        hid = (value * up).astype(low)
        hhid_ref[:, cols] = hid
        grad_hid = jnp.zeros_like(gate)
        for t in range(sides):
            piece = heavy_out(t, j)
            out_rows[t] = out_rows[t] + nn(hid, piece)
            grad_hid = grad_hid + nt(grad_out[:, t * CHUNK : (t + 1) * CHUNK], piece)
        grad_gate = (grad_hid * up * slope).astype(low)
        grad_up = (grad_hid * value).astype(low)
        dhgu_ref[0, :, cols] = grad_gate
        dhgu_ref[1, :, cols] = grad_up
        grad_rows = grad_rows + nt(grad_gate, heavy_in(0, j)) + nt(grad_up, heavy_in(1, j))
    out_rows = jnp.concatenate(out_rows, axis=1)
    logit = jnp.sum(cot_rows * out_rows, axis=-1, keepdims=True) * score * (1.0 - score)
    router_ref[...] = jnp.sum(logit * rows_wide, axis=0, keepdims=True)
    out_rows_ref[...] = (score * out_rows).astype(low)
    grad_rows_ref[...] = (grad_rows + logit * vec_ref[4:5, :]).astype(low)
    for ref in (frows_ref, hhid_ref, dhgu_ref, dhout_ref):
        moves.done(ref)

    def light_rows(c, carry):
        rows = pl.ds(pl.multiple_of(c * CHUNK, CHUNK), CHUNK)
        normed = n2b_ref[rows, :]
        gate = nn(normed, light_in(0))
        up = nn(normed, light_in(1))
        value, slope = gelu_pair(gate)
        hid = (value * up).astype(low)
        hidden_ref[rows, :] = hid
        spread = picks_cols(frow_ref[...], c * CHUNK, CHUNK)
        spread_out = nn(spread, out_rows_ref[...])
        grad_hid = jnp.zeros_like(gate)
        outs = []
        for t in range(sides):
            cols = slice(t * CHUNK, (t + 1) * CHUNK)
            outs.append((nn(hid, light_out(t)) + spread_out[:, cols]).astype(low))
            grad_hid = grad_hid + nt(cot_ref[rows, cols], light_out(t))
        grad_gate = (grad_hid * up * slope).astype(low)
        grad_up = (grad_hid * value).astype(low)
        dgu_ref[0, rows, :] = grad_gate
        dgu_ref[1, rows, :] = grad_up
        grad = nt(grad_gate, light_in(0)) + nt(grad_up, light_in(1)) + nn(spread, grad_rows_ref[...])
        mp_store(core, ykeep_ref, ysend_ref, c, chunks // 2, CHUNK, jnp.concatenate(outs, axis=1))
        mp_store(core, gkeep_ref, gsend_ref, c, chunks // 2, CHUNK, grad.astype(low))
        return carry

    lax.fori_loop(0, chunks, light_rows, 0)
    for ref in (gsend_ref, gkeep_ref, ysend_ref, ykeep_ref):
        moves.done(ref)
    if not last:
        return

    split = pack_ref.shape[0]

    def put(base, index, value):
        rows = value.shape[0] // split
        at = base // split + index * rows
        pack_ref[:, at : at + rows, :] = value.astype(low).reshape(split, rows, CHUNK)

    def sent(base, end):
        moves.done(pack_ref, (slice(None), slice(base // split, end // split)))

    for group in earlier:
        moves.need(*group)
    groups = earlier + [own + (cot_ref,)]
    routed = frows_ref.shape[0]
    for m, group in enumerate(groups):
        turned_ref[:, m * count : (m + 1) * count] = group[0][...].T
        turned_rows_ref[:, m * routed : (m + 1) * routed] = group[3][...].T
    pieces = heavy // CHUNK
    for s in range(2):
        for j in range(pieces):
            total = jnp.zeros((width, CHUNK), wide)
            for m, group in enumerate(groups):
                total = total + nn(
                    turned_rows_ref[:, m * routed : (m + 1) * routed],
                    group[5][s, :, j * CHUNK : (j + 1) * CHUNK],
                )
            put(bases[2], s * pieces + j, total)
    sent(bases[2], bases[3])
    for t in range(sides):
        cols = slice(t * CHUNK, (t + 1) * CHUNK)
        total = jnp.zeros((heavy, CHUNK), wide)
        for group in groups:
            total = total + tn(group[4][...], group[6][:, cols])
        put(bases[3], t, total)
    sent(bases[3], split * pack_ref.shape[1])
    for s in range(2):
        total = jnp.zeros((width, CHUNK), wide)
        for m, group in enumerate(groups):
            total = total + nn(turned_ref[:, m * count : (m + 1) * count], group[2][s])
        put(bases[0], s, total)
    total = jnp.zeros((light, width), wide)
    for group in groups:
        total = total + tn(group[1][...], group[7][...])
    for t in range(sides):
        put(bases[1], t, total[:, t * CHUNK : (t + 1) * CHUNK])
    sent(0, bases[2])


def attend_back_body(
    mine, moves, core_ref, mine_ref, other_ref, middle_ref, cot_ref, vec_ref,
    q_ref, k_ref, v_ref, prev_ref, after_ref, hq_ref, hk_ref, hv_ref, sk_ref, sq_ref, hproj_ref, wo_ref,
    qcol_ref, segq_ref, segk_ref, hsegq_ref, hsegk_ref, earlier_edges_ref,
    agl_ref, gain_ref, dq_ref, inner_ref, rims_ref, edges_ref, dhq_ref, spread_ref, draw_ref,
    dproj_ref, logit_ref,
    kx_ref, vx_ref, dmix_ref, dkx_ref, dvx_ref, dk_ref, dv_ref,
):
    count, width = q_ref.shape
    chunks = count // CHUNK
    light_heads = width // LDH
    heavy_heads = width // HDH
    core = core_ref[0]
    moves.begin(mine_ref, other_ref, middle_ref, cot_ref, wo_ref)
    moves.begin(hk_ref, hv_ref, sk_ref, hproj_ref, k_ref, v_ref, q_ref, segq_ref)
    moves.need(mine_ref, other_ref, middle_ref, cot_ref, wo_ref)
    gain_ref[...] = jnp.zeros_like(gain_ref)

    def enter(c, carry):
        rows = pl.ds(pl.multiple_of(c * CHUNK, CHUNK), CHUNK)
        upstream = mp_total(core, mine_ref, other_ref, c, chunks // 2)
        pulled, gain = norm_back(middle_ref[rows, :].astype(wide), vec_ref[1:2, :], upstream)
        gain_ref[...] += gain
        grad_low = (cot_ref[rows, :].astype(wide) + pulled).astype(low)
        agl_ref[rows, :] = grad_low
        dmix_ref[rows, :] = nt(grad_low, wo_ref[0]).astype(low)
        return carry

    lax.fori_loop(0, chunks, enter, 0)

    moves.done(agl_ref)
    moves.need(hk_ref, hv_ref, sk_ref, hproj_ref)
    picks = picks_rows(qcol_ref[...], count)
    grad_rows = nn(picks, agl_ref[...])
    score = sq_ref[...]
    dproj = (score * grad_rows).astype(low)
    dproj_ref[...] = dproj
    logit_ref[...] = (
        jnp.sum(grad_rows * hproj_ref[...], axis=-1, keepdims=True) * score * (1.0 - score)
    )
    dmix = nt(dproj, wo_ref[1]).astype(low)
    scale = 1.0 / math.sqrt(HDH)
    key_count = hk_ref.shape[0]
    if key_count <= KEYS:
        dk_ref[...] = jnp.zeros_like(dk_ref)
        dv_ref[...] = jnp.zeros_like(dv_ref)

        def one_head(h, dq):
            allowed = hsegq_ref[...] == hsegk_ref[...]
            mask = head_mask(width, HDH, h)
            keys = hk_ref[...] * mask
            probs = softmax_parts(nt(hq_ref[...], keys) * scale, allowed)
            grad_soft = nt(dmix, hv_ref[...] * mask)
            centre = jnp.sum(probs * grad_soft, axis=-1, keepdims=True)
            grad_scores = (probs * (grad_soft - centre)).astype(low)
            dk_ref[...] += tn(grad_scores, hq_ref[...] * mask)
            dv_ref[...] += tn(probs.astype(low), dmix * mask)
            return dq + nn(grad_scores, keys)

        dq = lax.fori_loop(0, heavy_heads, one_head, jnp.zeros((hq_ref.shape[0], width), wide))
        dk, dv = dk_ref[...], dv_ref[...]
        both = jnp.concatenate([(dk * scale).astype(low), dv.astype(low)], axis=1)
        spread_ref[...] = both.reshape(spread_ref.shape)
        draw_ref[...] = (dv * sk_ref[...]).astype(low)
    else:
        pieces = key_count // KEYS

        def piece_of(c, mask):
            spots = pl.ds(pl.multiple_of(c * KEYS, KEYS), KEYS)
            allowed = hsegq_ref[...] == hsegk_ref[:, spots]
            keys = hk_ref[spots, :] * mask
            scores = jnp.where(allowed, nt(hq_ref[...], keys) * scale, masked_score)
            return spots, keys, scores, nt(dmix, hv_ref[spots, :] * mask)

        blank = jnp.zeros((hq_ref.shape[0], 1), wide)
        stats = []
        for h in range(heavy_heads):
            mask = head_mask(width, HDH, h)

            def find_top(c, top):
                return jnp.maximum(top, jnp.max(piece_of(c, mask)[2], axis=-1, keepdims=True))

            top = lax.fori_loop(0, pieces, find_top, blank + masked_score)

            def add_up(c, sums):
                _, _, scores, grad_soft = piece_of(c, mask)
                grown = jnp.exp(scores - top)
                return (
                    sums[0] + jnp.sum(grown, axis=-1, keepdims=True),
                    sums[1] + jnp.sum(grown * grad_soft, axis=-1, keepdims=True),
                )

            total, moment = lax.fori_loop(0, pieces, add_up, (blank, blank))
            stats.append((mask, top, 1.0 / total, moment / total))

        def pull(c, dq):
            dk = jnp.zeros((KEYS, width), wide)
            dv = jnp.zeros((KEYS, width), wide)
            for mask, top, inverse, centre in stats:
                spots, keys, scores, grad_soft = piece_of(c, mask)
                probs = jnp.exp(scores - top) * inverse
                grad_scores = (probs * (grad_soft - centre)).astype(low)
                dq = dq + nn(grad_scores, keys)
                dk = dk + tn(grad_scores, hq_ref[...] * mask)
                dv = dv + tn(probs.astype(low), dmix * mask)
            owners = KEYS // spread_ref.shape[1]
            both = jnp.concatenate([(dk * scale).astype(low), dv.astype(low)], axis=1)
            spread_ref[pl.ds(c * owners, owners)] = both.reshape((owners,) + spread_ref.shape[1:])
            draw_ref[spots, :] = (dv * sk_ref[spots, :]).astype(low)
            return dq

        dq = lax.fori_loop(0, pieces, pull, jnp.zeros((hq_ref.shape[0], width), wide))
    dhq_ref[...] = (dq * scale).astype(low)
    moves.need(k_ref, v_ref, q_ref, segq_ref)
    if mine > 0:
        edges_ref[:, :mine] = earlier_edges_ref[...]
    for ref in (spread_ref, draw_ref, dproj_ref):
        moves.done(ref)
    fill_extended(kx_ref, prev_ref[0], k_ref[...], after_ref[0])
    fill_extended(vx_ref, prev_ref[1], v_ref[...], after_ref[1])
    dkx_ref[...] = jnp.zeros_like(dkx_ref)
    dvx_ref[...] = jnp.zeros_like(dvx_ref)
    light_scale = 1.0 / math.sqrt(LDH)

    def step(b, carry):
        rows = pl.ds(pl.multiple_of(b * BLOCK, BLOCK), BLOCK)
        spans = pl.ds(pl.multiple_of(b * BLOCK, BLOCK), 2 * BLOCK)
        seg_k = jnp.concatenate([segk_ref[b], segk_ref[b + 1]], axis=1)
        near = near_mask(segq_ref[rows, :], seg_k)
        queries = q_ref[rows, :]
        block_keys = kx_ref[spans, :]
        block_values = vx_ref[spans, :]
        mix = dmix_ref[rows, :]
        grad_q = jnp.zeros((BLOCK, width), wide)
        grad_k = jnp.zeros((2 * BLOCK, width), wide)
        grad_v = jnp.zeros((2 * BLOCK, width), wide)
        for h in range(light_heads):
            mask = head_mask(width, LDH, h)
            keys = block_keys * mask
            probs = softmax_parts(nt(queries, keys) * light_scale, near)
            grad_soft = nt(mix, block_values * mask)
            centre = jnp.sum(probs * grad_soft, axis=-1, keepdims=True)
            grad_scores = (probs * (grad_soft - centre)).astype(low)
            grad_q = grad_q + nn(grad_scores, keys)
            grad_k = grad_k + tn(grad_scores, queries * mask)
            grad_v = grad_v + tn(probs.astype(low), mix * mask)
        dq_ref[rows, :] = (grad_q * light_scale).astype(low)
        dkx_ref[spans, :] += grad_k * light_scale
        dvx_ref[spans, :] += grad_v
        return carry

    lax.fori_loop(0, count // BLOCK, step, 0)
    for s, ref in enumerate((dkx_ref, dvx_ref)):
        inner_ref[s] = ref[RADIUS : RADIUS + count, :].astype(low)
        rims_ref[s, :RADIUS, :] = ref[RADIUS : 2 * RADIUS, :]
        rims_ref[s, RADIUS:, :] = ref[count : RADIUS + count, :]
        edges_ref[0, mine, s] = ref[RADIUS + count :, :].astype(low)
        edges_ref[1, mine, s] = ref[:RADIUS, :].astype(low)


def project_back_body(
    core_ref, dq_ref, inner_ref, rims_ref, prev_ref, after_ref, dhq_ref, logit_ref, nq_ref, vec_ref, w_ref, qrow_ref,
    normed_ref,
    keep_ref, send_ref, dkv_ref, router_ref, gain_ref,
    rows_ref,
):
    count, width = dq_ref.shape
    for s in range(2):
        dkv_ref[s, RADIUS : count - RADIUS, :] = inner_ref[s, RADIUS : count - RADIUS, :]
        dkv_ref[s, :RADIUS, :] = (rims_ref[s, :RADIUS, :] + prev_ref[s].astype(wide)).astype(low)
        dkv_ref[s, count - RADIUS :, :] = (rims_ref[s, RADIUS:, :] + after_ref[s].astype(wide)).astype(low)
    query_logit = logit_ref[...]
    router_ref[...] = jnp.sum(query_logit * nq_ref[...], axis=0, keepdims=True)
    rows_ref[...] = (nt(dhq_ref[...], w_ref[3]) + query_logit * vec_ref[2:3, :]).astype(low)

    def step(c, carry):
        rows = pl.ds(pl.multiple_of(c * CHUNK, CHUNK), CHUNK)
        part = (
            nt(dq_ref[rows, :], w_ref[0])
            + nt(dkv_ref[0, rows, :], w_ref[1])
            + nt(dkv_ref[1, rows, :], w_ref[2])
            + nn(picks_cols(qrow_ref[...], c * CHUNK, CHUNK), rows_ref[...])
        )
        gain_ref[...] += jnp.sum(part * normed_ref[rows, :].astype(wide), axis=0, keepdims=True)
        mp_store(core_ref[0], keep_ref, send_ref, c, count // CHUNK // 2, CHUNK, part.astype(low))
        return carry

    gain_ref[...] = jnp.zeros_like(gain_ref)
    lax.fori_loop(0, count // CHUNK, step, 0)
    gain_ref[...] = gain_ref[...] / vec_ref[0:1, :]


def owners_body(micros, matrices, unpack, place_ref, owned_ref, vec_ref, w_ref, *refs):
    at = 5 * micros
    nk_refs, vectors = refs[:micros], refs[micros:at]
    gain_ones, gain_twos, queries = (vectors[i * micros : (i + 1) * micros] for i in range(3))
    ffns = vectors[3 * micros :]
    weights = refs[at : at + 2]
    sources, results, sums_ref = refs[at + 2 : -8], refs[-8:-1], refs[-1]
    keep_ref, send_ref = results[:2]
    grads = results[2:4]
    split_ref, turn_ref, rows_ref = results[4:]
    routed = nk_refs[0].shape[0]
    width = w_ref.shape[2]
    parts = place_ref.shape[0] - 1
    part = routed // parts
    inverse_gain = 1.0 / vec_ref[0:1, :]
    router_key = jnp.zeros((1, vec_ref.shape[1]), wide)
    gain_one = jnp.zeros((1, vec_ref.shape[1]), wide)
    for m in range(micros):
        start = owned_ref.shape[0] - (micros - m) * routed
        owned = owned_ref[start : start + routed, :]
        grad_k = owned[:, :width]
        grad_v = owned[:, width:].astype(wide)
        key_wide = nk_refs[m][...]
        raw = nn(key_wide.astype(low), w_ref[5])
        score = sigmoid(jnp.sum(key_wide * vec_ref[3:4, :], axis=-1, keepdims=True))
        logit = jnp.sum(grad_v * raw, axis=-1, keepdims=True) * score * (1.0 - score)
        router_key = router_key + jnp.sum(logit * key_wide, axis=0, keepdims=True)
        rows = nt(grad_k, w_ref[4]) + nt((grad_v * score).astype(low), w_ref[5]) + logit * vec_ref[3:4, :]
        gain_one = gain_one + jnp.sum(rows * key_wide, axis=0, keepdims=True) * inverse_gain
        turn_ref[...] = rows.astype(low)
        for p in range(parts):
            spot = pl.multiple_of(place_ref[1 + p] * part, part)
            rows_ref[m * routed + p * part : m * routed + (p + 1) * part, :] = turn_ref[pl.ds(spot, part), :]
    half = rows_ref.shape[0] // 2
    for c in range(2):
        mp_store(place_ref[0], keep_ref, send_ref, c, 1, half, rows_ref[c * half : (c + 1) * half, :])

    def added(refs):
        total = refs[0][...]
        for ref in refs[1:]:
            total = total + ref[...]
        return total

    gain_one = gain_one + added(gain_ones)
    lines = (gain_one, added(gain_twos) * (1.0 / parts), added(queries), router_key, added(ffns))
    unpack(sources if sources else (owned_ref,), grads)
    sums_ref[...] = jnp.zeros_like(sums_ref)
    write_sums(matrices, grads, weights, sums_ref)
    count = split_ref.shape[0]
    size = gain_one.shape[1] // count
    for d in range(count):
        for i, line in enumerate(lines):
            sums_ref[i : i + 1, VECTORS_AT : VECTORS_AT + size] = line[:, d * size : (d + 1) * size]
        split_ref[d] = sums_ref[...].astype(low)


def finish_body(chunks, core_ref, kmine_ref, kother_ref, vec_ref, *refs):
    micros = (len(refs) - 3) // 4
    groups = [refs[4 * m : 4 * m + 4] for m in range(micros)]
    tok_ref, out_ref, keys_ref = refs[4 * micros :]
    routed = groups[0][3].shape[1]
    core = core_ref[0]
    chunk = pl.program_id(0)

    @pl.when(chunk == 0)
    def _():
        half = keys_ref.shape[0] // 2
        for c in range(2):
            keys_ref[c * half : (c + 1) * half, :] = mp_total(core, kmine_ref, kother_ref, c, 1, half).astype(low)

    flag = (chunk // (chunks // 2) == core).astype(wide)
    for m in range(micros):
        mine_ref, other_ref, grad_ref, krow_ref = groups[m]
        upstream = mine_ref[...].astype(wide) * flag + other_ref[...].astype(wide) * (1.0 - flag)
        spread = picks_cols(krow_ref[...], chunk * CHUNK, CHUNK)
        upstream = upstream + nn(spread, keys_ref[m * routed : (m + 1) * routed, :])
        pulled, _ = norm_back(tok_ref[m].astype(wide), vec_ref[0:1, :], upstream)
        out_ref[m] = grad_ref[...].astype(wide) + pulled


def join_body(chunks, core_ref, *refs):
    out_ref = refs[-1]
    flag = (pl.program_id(0) // (chunks // 2) == core_ref[0]).astype(wide)
    for m in range(out_ref.shape[0]):
        middle_ref, mine_ref, other_ref = refs[3 * m : 3 * m + 3]
        total = mine_ref[...].astype(wide) * flag + other_ref[...].astype(wide) * (1.0 - flag)
        out_ref[m] = (middle_ref[...].astype(wide) + total).astype(low)


def attn_grads_body(moves, *refs):
    out_ref, turned_ref, other_ref = refs[-3:]
    micros = len(refs) // 12
    groups = [refs[12 * m : 12 * m + 12] for m in range(micros)]
    tokens, width = groups[0][9].shape
    keys = groups[0][11].shape[0]
    for group in groups:
        moves.begin(group[9], group[0], group[1], group[10])
    for group in groups:
        moves.begin(group[11], group[3], group[4], group[5], group[6], group[7], group[8])
    for group in groups:
        moves.need(group[9], group[0], group[1], group[10])
    grads = []
    for m in range(micros):
        turned_ref[:, m * tokens : (m + 1) * tokens] = groups[m][9][...].T
    for s in range(3):
        total = 0.0
        for m, group in enumerate(groups):
            grad = group[0][...] if s == 0 else group[1][s - 1]
            total = total + nn(turned_ref[:, m * tokens : (m + 1) * tokens], grad)
        grads.append(total)
    total = 0.0
    for m, group in enumerate(groups):
        total = total + tn(group[10][...], group[2][...])
    grads.append(total)
    for group in groups:
        moves.need(*group)
    for m in range(micros):
        other_ref[:, m * keys : (m + 1) * keys] = groups[m][11][...].T
    for s in (3, 4):
        total = 0.0
        for m, group in enumerate(groups):
            if s == 3:
                grad = group[s][...].reshape(keys, -1)[:, : group[4].shape[1]]
            else:
                grad = group[s][...]
            total = total + nn(other_ref[:, m * keys : (m + 1) * keys], grad)
        grads.append(total)
    out_grads = []
    for mix, grad in ((5, 6), (7, 8)):
        total = 0.0
        for group in groups:
            total = total + tn(group[mix][...], group[grad][...])
        out_grads.append(total)
    count, _, lane = out_ref.shape
    in_rows = width // count
    for j in range(3):
        pair = jnp.concatenate([grads[2 * j], grads[2 * j + 1]], axis=1).astype(low)
        out_ref[:, j * in_rows : (j + 1) * in_rows, :] = pair.reshape(count, in_rows, lane)
    out_rows = out_grads[0].shape[0] // count
    own = groups[0][3].shape[1]
    for m, group in enumerate(groups):
        at = out_ref.shape[1] - (micros - m) * own
        out_ref[:, at : at + own, :] = group[3][...]
    for d in range(count):
        rows = slice(d * out_rows, (d + 1) * out_rows)
        both = jnp.concatenate([g[rows] for g in out_grads], axis=0).astype(low)
        for j in range(width // lane):
            at = 3 * in_rows + j * 2 * out_rows
            out_ref[d, at : at + 2 * out_rows, :] = both[:, j * lane : (j + 1) * lane]


class Matrix:
    def __init__(self, array, lead, tall, cols_at, rows_at, weight_at):
        self.array, self.lead, self.tall = array, lead, tall
        self.cols_at, self.rows_at, self.weight_at = cols_at, rows_at, weight_at

    def read(self, refs):
        ref = refs[self.array]
        return ref[...] if self.lead is None else ref[self.lead]

    def write(self, refs, value):
        if self.lead is None:
            refs[self.array][...] = value
        else:
            refs[self.array][self.lead] = value

    def line(self):
        lead = 0 if self.lead is None else self.lead
        return slice(lead, lead + 1)


def ffn_matrices(light, heavy, width):
    return [
        Matrix(0, 0, True, [(0, 0, light)], (4, 0), (4, 768)),
        Matrix(0, 1, True, [(1, 0, light)], (4, 128), (4, 769)),
        Matrix(1, None, False, [(0, light, width)], (4, 256), (4, 770)),
        Matrix(2, 0, True, [(2, 0, heavy)], (4, 384), (4, 771)),
        Matrix(2, 1, True, [(3, 0, heavy)], (4, 512), (4, 772)),
        Matrix(3, None, False, [(1, light, width)], (4, 640), (4, 773)),
    ]


def attn_matrices(cols, width):
    listed = [
        Matrix(0, i, True, [(i, 0, cols)], (6 + i // 4, 128 * (i % 4)), (i, 224)) for i in range(6)
    ]
    piece = width // 3
    for s in range(2):
        spots = [(3 * s + j, 256, piece) for j in range(3)]
        listed.append(Matrix(1, s, False, spots, (7, 256 + 128 * s), (s, 232)))
    return listed


def total_of(values):
    return jnp.sum(jnp.sum(values, axis=1, keepdims=True), axis=0, keepdims=True)


def sums_body(matrices, unpack, array_count, *refs):
    weights = refs[-2 * array_count - 1 : -array_count - 1]
    grads, sums_ref = refs[-array_count - 1 : -1], refs[-1]
    unpack(refs[: -2 * array_count - 1], grads)
    sums_ref[...] = jnp.zeros_like(sums_ref)
    write_sums(matrices, grads, weights, sums_ref)


def write_sums(matrices, grads, weights, sums_ref):
    for matrix in matrices:
        square = matrix.read(grads)
        square = square * square + tiny_square
        cols = jnp.sum(square, axis=0, keepdims=True)
        at = 0
        for row, lane, size in matrix.cols_at:
            sums_ref[row : row + 1, lane : lane + size] = cols[:, at : at + size]
            at = at + size
        rows = lax.dot_general(
            jnp.ones((8, square.shape[1]), wide),
            square,
            (((1,), (1,)), ((), ())),
            precision=lax.Precision.HIGHEST,
            preferred_element_type=wide,
        )
        row, lane = matrix.rows_at
        sums_ref[row : row + 1, lane : lane + square.shape[0]] = rows[0:1]
        weight = matrix.read(weights)
        row, lane = matrix.weight_at
        sums_ref[row : row + 1, lane : lane + 1] = total_of(weight * weight)


def lane_row(values):
    spots = lax.broadcasted_iota(jnp.int32, (1, 128), 1)
    row = jnp.zeros((1, 128), wide)
    for place, value in enumerate(values):
        row = row + jnp.where(spots == place, value, 0.0)
    return row


def moments_body(matrices, array_count, vector_count, data_size, model_size, place_ref, parts_ref, *refs):
    keep = 1.0 - STEP ** (-0.8)
    n = array_count
    grads, row_old, col_old, row_mine, col_mine = (refs[i * n : (i + 1) * n] for i in range(5))
    at = 5 * n
    vector_in = refs[at : at + 2 * vector_count]
    at = at + 2 * vector_count
    updates, row_new, col_new = (refs[at + i * n : at + (i + 1) * n] for i in range(3))
    at = at + 3 * n
    vector_out = refs[at : at + 3 * vector_count]
    aux_ref = refs[-1]
    d, k = place_ref[0], place_ref[1]
    devices = data_size * model_size

    def part(index):
        return parts_ref[index].astype(wide)

    whole = part(0)
    for i in range(1, devices):
        whole = whole + part(i)
    by_model = []
    for j in range(model_size):
        total = part(j)
        for i in range(1, data_size):
            total = total + part(i * model_size + j)
        by_model.append(total)
    by_data = []
    for i in range(data_size):
        total = part(i * model_size)
        for j in range(1, model_size):
            total = total + part(i * model_size + j)
        by_data.append(total)
    my_cols = part(k)
    for i in range(1, data_size):
        my_cols = my_cols + part(i * model_size + k)
    my_rows = part(d * model_size)
    for j in range(1, model_size):
        my_rows = my_rows + part(d * model_size + j)
    mine = part(d * model_size + k)

    def cols_of(sums, matrix):
        pieces = [sums[row : row + 1, lane : lane + size] for row, lane, size in matrix.cols_at]
        return pieces[0] if len(pieces) == 1 else jnp.concatenate(pieces, axis=1)

    lines, extents = [], []
    for matrix in matrices:
        grad_rows, grad_cols = matrix.read(grads).shape
        row_total = grad_rows * data_size * (1 if matrix.tall else model_size)
        col_total = grad_cols * (model_size if matrix.tall else 1)
        extents.append((row_total, col_total))
        row, lane = matrix.rows_at
        source = my_rows if matrix.tall else mine
        old = row_mine[matrix.array][matrix.line(), :]
        lines.append(keep * old + (1.0 - keep) / col_total * source[row : row + 1, lane : lane + 128])
    while len(lines) < 8:
        lines.append(jnp.zeros((1, 128), wide))
    columns = jnp.concatenate(lines, axis=0).T
    update_sums, weight_sums = [], []
    for place, (matrix, (row_total, col_total)) in enumerate(zip(matrices, extents)):
        grad = matrix.read(grads)
        row, lane = matrix.rows_at
        size = grad.shape[0]
        old_rows = row_old[matrix.array][matrix.line(), :]
        old_cols = col_old[matrix.array][matrix.line(), :]
        mean = keep * jnp.mean(old_rows, axis=1, keepdims=True) + (1.0 - keep) / (
            row_total * col_total
        ) * jnp.sum(whole[row : row + 1, lane : lane + 128], axis=1, keepdims=True)
        if matrix.tall:
            cols = keep * col_mine[matrix.array][matrix.line(), :] + (1.0 - keep) / row_total * cols_of(my_cols, matrix)
            all_cols = jnp.concatenate([cols_of(sums, matrix) for sums in by_model], axis=1)
            all_rows = jnp.concatenate([sums[row : row + 1, lane : lane + size] for sums in by_data], axis=1)
            new_cols = keep * old_cols + (1.0 - keep) / row_total * all_cols
        else:
            cols = keep * old_cols + (1.0 - keep) / row_total * cols_of(whole, matrix)
            all_rows = jnp.concatenate(
                [
                    part(i * model_size + j)[row : row + 1, lane : lane + size]
                    for j in range(model_size)
                    for i in range(data_size)
                ],
                axis=1,
            )
            new_cols = cols
        row_new[matrix.array][matrix.line(), :] = keep * old_rows + (1.0 - keep) / col_total * all_rows
        col_new[matrix.array][matrix.line(), :] = new_cols
        update = grad * lax.rsqrt(columns[:size, place : place + 1] * (cols / mean))
        matrix.write(updates, update)
        update_sums.append(total_of(update * update))
        row, lane = matrix.weight_at
        weight_sums.append(whole[row : row + 1, lane : lane + 1] * (1.0 / devices))
    line_at = 0
    for i in range(vector_count):
        old_ref, weight_ref = vector_in[2 * i : 2 * i + 2]
        lines, size = old_ref.shape
        grad = whole[line_at : line_at + lines, VECTORS_AT : VECTORS_AT + size]
        line_at = line_at + lines
        vector_out[3 * i + 2][...] = grad
        moment = keep * old_ref[...] + (1.0 - keep) * (grad * grad + tiny_square)
        update = grad * lax.rsqrt(moment)
        vector_out[3 * i][...] = moment
        vector_out[3 * i + 1][...] = update
        for r in range(grad.shape[0]):
            line = update[r : r + 1]
            update_sums.append(total_of(line * line) * (1.0 / model_size))
            line = weight_ref[r : r + 1, :]
            weight_sums.append(total_of(line * line) * (1.0 / model_size))
    aux_ref[...] = jnp.zeros_like(aux_ref)
    aux_ref[0:1, :] = lane_row(update_sums)
    aux_ref[1:2, :] = lane_row(weight_sums)


def step_size(update_sum, weight_sum, count):
    rms_weight = jnp.sqrt(weight_sum * (1.0 / count))
    rms_update = jnp.sqrt(update_sum * (1.0 / count))
    return step_rate * jnp.maximum(scale_floor, rms_weight) / jnp.maximum(1.0, rms_update / clip_level)


def weights_body(matrices, counts, array_count, vector_count, aux_ref, *refs):
    n = array_count + vector_count
    weights, updates, news = refs[:n], refs[n : 2 * n], refs[2 * n :]
    sums = aux_ref[0]
    for i in range(1, aux_ref.shape[0]):
        sums = sums + aux_ref[i]

    def step(place):
        spot = slice(place, place + 1)
        return step_size(sums[0:1, spot], sums[1:2, spot], counts[place])

    for place, matrix in enumerate(matrices):
        matrix.write(news, matrix.read(weights) - step(place) * matrix.read(updates))
    place = len(matrices)
    for i in range(array_count, n):
        for r in range(weights[i].shape[0]):
            row = slice(r, r + 1)
            news[i][row, :] = weights[i][row, :] - step(place) * updates[i][row, :]
            place = place + 1


def after(value, *others):
    return lax.optimization_barrier((value,) + others)[0]


def shards(
    tokens,
    cotangent,
    segments,
    route_query,
    route_key,
    route_ffn,
    attn_in,
    attn_out,
    light_in,
    light_out,
    heavy_in,
    heavy_out,
    gains,
    router,
    row_attn_in,
    col_attn_in,
    row_attn_out,
    col_attn_out,
    row_light_in,
    col_light_in,
    row_light_out,
    col_light_out,
    row_heavy_in,
    col_heavy_in,
    row_heavy_out,
    col_heavy_out,
    second_gains,
    second_router,
):
    data_size = lax.axis_size("dp")
    model_size = lax.axis_size("mp")
    data_index = lax.axis_index("dp")
    model_index = lax.axis_index("mp")
    core = model_index % 2
    order = jnp.arange(model_size) ^ model_index
    core_flag = jnp.concatenate([core.reshape(1), order]).astype(jnp.int32)
    core_pairs = [(i, i ^ 1) for i in range(model_size)]
    far_pairs = [(i, i ^ 2) for i in range(model_size)]
    micro_count, tok_local, width = tokens.shape
    routed_local = route_query.shape[1]
    routed_all = route_key.shape[1]
    quarter = routed_local // model_size
    head_cols = attn_in.shape[2]
    in_rows = attn_in.shape[1]

    key_blocks = route_key.reshape(micro_count, data_size, model_size, quarter)
    own_keys = lax.dynamic_slice_in_dim(key_blocks, data_index, 1, axis=1)
    key_blocks = jnp.take(key_blocks, order, axis=2)
    key_local = lax.dynamic_slice_in_dim(key_blocks, data_index, 1, axis=1)[:, 0]
    my_quarter = key_local[:, 0]
    picks = (my_quarter[:, :, None] == jnp.arange(tok_local)[None, None, :]).astype(low)
    my_rows = jnp.einsum("mrt,mtd->mrd", picks, tokens, preferred_element_type=wide).astype(low)

    def to_all(rows):
        sent = jnp.broadcast_to(rows[None], (data_size,) + rows.shape)
        return lax.all_to_all(sent, "dp", 0, 0, tiled=True)

    key_rows = to_all(my_rows).reshape(data_size, micro_count, quarter, width)
    rows_core = lax.ppermute(key_rows, "mp", core_pairs)
    rows_far = lax.ppermute(key_rows, "mp", far_pairs)
    rows_both = lax.ppermute(rows_far, "mp", core_pairs)

    lane = 2 * head_cols
    sides = width // lane
    in_rows = attn_in.shape[1]
    out_rows = attn_out.shape[1]
    small = jnp.concatenate([gains, router], axis=0).astype(low)
    small_block = jnp.pad(small, ((0, 16 - small.shape[0]), (0, lane - in_rows)))
    in_block = (
        attn_in.astype(low).reshape(3, 2, in_rows, head_cols).transpose(0, 2, 1, 3).reshape(3 * in_rows, lane)
    )

    def sideways(rows):
        return rows.reshape(-1, sides, lane).transpose(1, 0, 2).reshape(-1, lane)

    out_block = sideways(attn_out.astype(low).reshape(2 * out_rows, width))
    pack_one = jnp.concatenate([in_block, out_block, small_block], axis=0)
    got_one = lax.all_gather(pack_one, "dp", axis=0, tiled=False)
    aligned = in_rows % 16 == 0 and out_rows % 8 == 0 and light_out.shape[0] % 16 == 0
    if aligned:
        w_in, w_out, vectors = kernel_call(
            unpack_body,
            [
                in_vmem((6, width, head_cols), low),
                in_vmem((2, data_size * out_rows, width), low),
                in_vmem((8, width), wide),
            ],
            [],
            (got_one,),
            weight=5,
        )
    else:
        w_in = (
            got_one[:, : 3 * in_rows]
            .reshape(data_size, 3, in_rows, 2, head_cols)
            .transpose(1, 3, 0, 2, 4)
            .reshape(6, width, head_cols)
        )
        at = 3 * in_rows
        w_out = (
            got_one[:, at : at + out_block.shape[0]]
            .reshape(data_size, sides, 2, out_rows, lane)
            .transpose(2, 0, 3, 1, 4)
            .reshape(2, data_size * out_rows, width)
        )
        at = at + out_block.shape[0]
        vectors = got_one[:, at : at + 8, :in_rows].transpose(1, 0, 2).reshape(8, width).astype(wide)

    def blocked(weight):
        lead, rows, cols = weight.shape
        return weight.reshape(lead, rows, cols // CHUNK, CHUNK).transpose(0, 2, 1, 3).reshape(-1, rows, CHUNK)

    def unblocked(blocks, lead):
        count, rows, _ = blocks.shape
        return blocks.reshape(lead, count // lead, rows, CHUNK).transpose(0, 2, 1, 3).reshape(lead, rows, -1)

    light_hidden = light_in.shape[2]
    heavy_hidden = heavy_in.shape[2]
    blocks = [blocked(w.astype(low)) for w in (light_in, light_out[None], heavy_in, heavy_out[None])]
    block_rows = [b.shape[0] * b.shape[1] for b in blocks]
    pack_two = jnp.concatenate([b.reshape(-1, CHUNK) for b in blocks], axis=0)
    w_ffn = lax.all_gather(after(pack_two, got_one, rows_far), "dp", axis=0, tiled=False)
    if not aligned:
        pieces = []
        at = 0
        for block in blocks:
            size = block.shape[0] * block.shape[1]
            pieces.append(
                w_ffn[:, at : at + size]
                .reshape((data_size,) + block.shape)
                .transpose(1, 0, 2, 3)
                .reshape(-1, CHUNK)
            )
            at = at + size
        w_ffn = jnp.concatenate(pieces, axis=0)[None]

    attn_in, attn_out, light_in, light_out, heavy_in, heavy_out, gains, router = (
        lax.optimization_barrier(
            (got_one, attn_in, attn_out, light_in, light_out, heavy_in, heavy_out, gains, router)
        )[1:]
    )

    local_spot = model_index * data_size + data_index
    ffn_list = ffn_matrices(light_hidden, heavy_hidden, width)
    ffn_weights = (light_in, light_out, heavy_in, heavy_out)
    ffn_moments = (
        (row_light_in, col_light_in),
        (row_light_out, col_light_out),
        (row_heavy_in, col_heavy_in),
        (row_heavy_out, col_heavy_out),
    )
    attn_list = attn_matrices(head_cols, width)
    attn_weights = (attn_in, attn_out)
    attn_moments = ((row_attn_in, col_attn_in), (row_attn_out, col_attn_out))

    def moments_of(matrices, weights, moments):
        row_old, col_old, row_mine, col_mine = [], [], [], []
        for array, weight in enumerate(weights):
            rows, cols = moments[array]
            tall = [m.tall for m in matrices if m.array == array][0]
            lead = rows.size // rows.shape[-1]
            rows, cols = rows.reshape(lead, -1), cols.reshape(lead, -1)
            size, span = weight.shape[-2:]
            spot = data_index if tall else local_spot
            my_rows = lax.dynamic_slice_in_dim(rows, spot * size, size, 1)
            row_mine.append(jnp.pad(my_rows, ((0, 0), (0, 128 - size)), constant_values=1.0))
            col_mine.append(lax.dynamic_slice_in_dim(cols, model_index * span, span, 1) if tall else cols)
            row_old.append(rows)
            col_old.append(cols)
        return row_old, col_old, row_mine, col_mine

    ffn_here, attn_here, w_ffn = lax.optimization_barrier(
        (
            moments_of(ffn_list, ffn_weights, ffn_moments),
            moments_of(attn_list, attn_weights, attn_moments),
            w_ffn,
        )
    )

    turns = (jnp.arange(micro_count) % 2)[:, None]
    segment_ids = segments[None, :] * turns
    seg_padded = jnp.pad(segment_ids, ((0, 0), (RADIUS, RADIUS)), constant_values=-1)
    seg_local = lax.dynamic_slice_in_dim(segment_ids, data_index * tok_local, tok_local, axis=1)
    seg_extended = lax.dynamic_slice_in_dim(
        seg_padded, data_index * tok_local, tok_local + 2 * RADIUS, axis=1
    ).reshape(micro_count, -1, 1, BLOCK)

    def picked(ids, spots):
        hit = spots[..., :, None] == jnp.arange(tok_local)
        return jnp.sum(jnp.where(hit, ids[..., None, :], 0), axis=-1)

    key_seg = picked(
        segment_ids.reshape(micro_count, data_size, tok_local),
        key_blocks.reshape(micro_count, data_size, routed_local),
    ).reshape(micro_count, -1)
    query_seg = picked(seg_local, route_query)
    key_list = key_local.reshape(micro_count, -1)

    query_col, query_row = route_query[:, :, None], route_query[:, None, :]
    key_col, key_row = key_list[:, :, None], own_keys.reshape(micro_count, 1, routed_local)
    ffn_col, ffn_row = route_ffn[:, :, None], route_ffn[:, None, :]
    segs = (seg_local[:, :, None], seg_extended, query_seg[:, :, None], key_seg[:, None, :])

    micros = range(micro_count)
    token_parts = [Pick(tokens, m) for m in micros]
    cot_parts = [Pick(cotangent, m) for m in micros]
    projected = kernel_call(
        project_body,
        [
            in_vmem((tok_local, width), low),
            in_vmem((tok_local, head_cols), low),
            in_vmem((tok_local, head_cols), low),
            in_vmem((tok_local, head_cols), low),
            in_vmem((routed_local, head_cols), low),
            in_vmem((routed_local, 1), wide),
            in_vmem((routed_local, width), wide),
            in_vmem((routed_local, width), wide),
            in_vmem((routed_local, width), low),
        ]
        * micro_count,
        [pltpu.VMEM((tok_local, width), low)],
        (vectors, w_in) + sum(((token_parts[m], query_col[m], key_col[m]) for m in micros), ()),
        managed=True,
            weight=12,
    )
    normed_low, light_q, light_k, light_v, heavy_q, score_q, rows_q, rows_k, rows_q_low = (
        projected[i::9] for i in range(9)
    )

    up = [(i, i + 1) for i in range(data_size - 1)]
    down = [(i + 1, i) for i in range(data_size - 1)]
    tails = jnp.stack([jnp.stack([k[tok_local - RADIUS :], v[tok_local - RADIUS :]]) for k, v in zip(light_k, light_v)])
    heads = jnp.stack([jnp.stack([k[:RADIUS], v[:RADIUS]]) for k, v in zip(light_k, light_v)])
    halo_prev = lax.ppermute(tails, "dp", up)
    halo_next = lax.ppermute(heads, "dp", down)

    split = (data_size, model_size, quarter)
    span = min(data_size, 8)

    def split_spec(cols):
        return pl.BlockSpec((span, model_size, quarter, cols), lambda i: (i, 0, 0, 0))

    keyed = pl.pallas_call(
        keys_body,
        grid=(data_size // span,),
        out_shape=[
            in_vmem(split + (width,), low),
            in_vmem(split + (head_cols,), low),
            in_vmem(split + (head_cols,), low),
            in_vmem(split + (1,), wide),
        ]
        * micro_count,
        in_specs=[pl.BlockSpec((span, micro_count, quarter, width), lambda i: (i, 0, 0, 0))] * 4
        + [
            pl.BlockSpec((8, width), lambda i: (0, 0)),
            pl.BlockSpec((6, width, head_cols), lambda i: (0, 0, 0)),
        ],
        out_specs=[split_spec(width), split_spec(head_cols), split_spec(head_cols), split_spec(1)] * micro_count,
        compiler_params=pltpu.CompilerParams(vmem_limit_bytes=VMEM_BYTES),
        cost_estimate=pl.CostEstimate(flops=6 * 1_150_000_000, bytes_accessed=1_000_000, transcendentals=0),
    )(key_rows, rows_core, rows_far, rows_both, vectors, w_in)
    key_normed, heavy_k, heavy_v, score_k = (
        [a.reshape(routed_all, -1) for a in keyed[i::4]] for i in range(4)
    )

    def mp_first(keep, send, *earlier):
        got = lax.ppermute(after(send, *earlier), "mp", core_pairs)
        return (keep.astype(wide) + got.astype(wide)).astype(low)

    def mp_second(mine):
        return mine, lax.ppermute(mine, "mp", far_pairs)

    def mp_third(moved, *held):
        mine, near = moved
        near = after(near, *held)
        done = (mine.astype(wide) + near.astype(wide)).astype(low)
        return done, lax.ppermute(done, "mp", core_pairs)

    extended = pltpu.VMEM((tok_local + 2 * RADIUS, head_cols), low)
    row_shape = (tok_local, width)
    half_shape = (tok_local // 2, width)

    def all_picks(arrays, m):
        return tuple(a[m] for a in arrays)

    attended = []
    attn_moved = []
    held, earlier = (), ()
    for m in micros:
        outs = kernel_call(
            attend_body,
            [
                in_vmem(half_shape, low),
                in_vmem(half_shape, low),
                in_vmem((tok_local, head_cols), low),
                in_vmem((routed_local, head_cols), low),
                in_vmem((routed_local, width), wide),
            ],
            [extended, extended, pltpu.VMEM((routed_local, width), low)],
            (core_flag,)
            + all_picks((light_q, light_k, light_v, halo_prev, halo_next, heavy_q, heavy_k, heavy_v, score_q), m)
            + (after(w_out, *held),)
            + all_picks((query_row,) + segs, m),
            scalars=1,
            managed=False,
            weight=11,
        )
        attended.append(outs)
        begun = mp_first(outs[0], outs[1], *earlier)
        attn_moved.append(mp_second(begun))
        held, earlier = (begun,), (attn_moved[m][1],)

    fed = []
    grad_moved = []
    split = data_size if aligned else 1
    total_rows = ffn_bases(width, light_hidden, heavy_hidden)[1]
    own = [
        (row_shape, low),
        ((tok_local, light_hidden), low),
        ((2, tok_local, light_hidden), low),
        ((routed_local, width), low),
        ((routed_local, heavy_hidden), low),
        ((2, routed_local, heavy_hidden), low),
        ((routed_local, width), low),
    ]
    for m in micros:
        beside = attended[m + 1][0] if m + 1 < micro_count else fed[m - 1][1]
        ffn_outs = [
            in_vmem(row_shape, low),
            in_vmem(half_shape, low),
            in_vmem(half_shape, low),
            in_vmem(half_shape, low),
            in_vmem(half_shape, low),
            in_vmem((1, width), wide),
        ]
        scratch = [
            pltpu.VMEM(row_shape, low),
            pltpu.VMEM((routed_local, width), low),
            pltpu.VMEM((routed_local, width), low),
        ]
        kept = ()
        if m + 1 < micro_count:
            ffn_outs = ffn_outs + [in_vmem(*o) for o in own]
        else:
            ffn_outs = ffn_outs + [in_vmem((split, total_rows // split, CHUNK), low)]
            scratch = [
                *(pltpu.VMEM(*o) for o in own),
                pltpu.VMEM((width, micro_count * tok_local), low),
                pltpu.VMEM((width, micro_count * routed_local), low),
                *scratch,
            ]
            for i in range(m):
                kept = kept + tuple(fed[i][6:13]) + (cot_parts[i],)
        outs = kernel_call(
            functools.partial(ffn_body, m if m + 1 == micro_count else 0),
            ffn_outs,
            scratch,
            (core_flag,)
            + mp_third(attn_moved[m], beside)
            + (token_parts[m], cot_parts[m], after(vectors, *held), ffn_col[m], ffn_row[m], w_ffn)
            + kept,
            scalars=1,
            managed=True,
            weight=17 if m + 1 < micro_count else 23,
        )
        fed.append(outs)
        begun = mp_first(outs[3], outs[4], *earlier)
        grad_moved.append(mp_second(begun))
        held, earlier = (begun,), (grad_moved[m][1],)
    pack_ffn = fed[-1][6]
    if not aligned:
        pieces = []
        at = 0
        for block in blocks:
            size = block.shape[0] * block.shape[1] * data_size
            pieces.append(
                pack_ffn[0, at : at + size]
                .reshape(block.shape[0], data_size, block.shape[1], CHUNK)
                .transpose(1, 0, 2, 3)
                .reshape(data_size, -1, CHUNK)
            )
            at = at + size
        pack_ffn = jnp.concatenate(pieces, axis=1)
    sum_ffn = lax.psum_scatter(pack_ffn.reshape(-1, CHUNK), "dp", scatter_dimension=0, tiled=True)

    y_moved = []
    backs = []
    edges = jnp.zeros((2, 1, 2, RADIUS, head_cols), low)
    y_begun = [mp_first(fed[m][1], fed[m][2]) for m in micros]
    for m in micros:
        outs = kernel_call(
            functools.partial(attend_back_body, m),
            [
                in_vmem(row_shape, low),
                in_vmem((1, width), wide),
                in_vmem((tok_local, head_cols), low),
                in_vmem((2, tok_local, head_cols), low),
                in_vmem((2, 2 * RADIUS, head_cols), wide),
                in_vmem((2, m + 1, 2, RADIUS, head_cols), low),
                in_vmem((routed_local, head_cols), low),
                in_vmem((data_size, routed_local, 2 * head_cols), low),
                in_vmem((routed_all, head_cols), low),
                in_vmem((routed_local, width), low),
                in_vmem((routed_local, 1), wide),
            ],
            [
                extended,
                extended,
                pltpu.VMEM((tok_local, head_cols), low),
                pltpu.VMEM((tok_local + 2 * RADIUS, head_cols), wide),
                pltpu.VMEM((tok_local + 2 * RADIUS, head_cols), wide),
                pltpu.VMEM((min(routed_all, KEYS), head_cols), wide),
                pltpu.VMEM((min(routed_all, KEYS), head_cols), wide),
            ],
            (core_flag,)
            + mp_third(grad_moved[m], pack_ffn if m == 0 else backs[m - 1][0])
            + (fed[m][0], cot_parts[m], after(vectors, pack_ffn, y_begun[m]))
            + all_picks(
                (light_q, light_k, light_v, halo_prev, halo_next, heavy_q, heavy_k, heavy_v, score_k, score_q), m
            )
            + (attended[m][4], w_out)
            + all_picks((query_col,) + segs, m)
            + (edges,),
            scalars=1,
            managed=True,
            weight=22,
        )
        edges = outs[5]
        backs.append(outs)
        y_moved.append(mp_second(after(y_begun[m], outs[0], *earlier)))
        earlier = (y_moved[m][1],)
    held = (y_moved[0][1],)

    from_prev = lax.ppermute(edges[0], "dp", up)
    from_next = lax.ppermute(edges[1], "dp", down)

    last = []
    last_moved = []
    for m in micros:
        outs = backs[m]
        made = kernel_call(
            project_back_body,
            [
                in_vmem(half_shape, low),
                in_vmem(half_shape, low),
                in_vmem((2, tok_local, head_cols), low),
                in_vmem((1, width), wide),
                in_vmem((1, width), wide),
            ],
            [pltpu.VMEM((routed_local, width), low)],
            (core_flag, outs[2], outs[3], outs[4], from_prev[m], from_next[m], outs[6], outs[10], rows_q[m])
            + (after(vectors, *held), w_in, query_row[m], normed_low[m]),
            scalars=1,
            managed=False,
            weight=8,
        )
        last.append(made)
        if m + 1 < micro_count:
            begun = mp_first(made[0], made[1])
            last_moved.append(mp_second(after(begun, *earlier)))
            held, earlier = (), (last_moved[m][1],)

    attn_rows = 3 * in_rows + 2 * out_rows * sides
    groups = []
    for m in micros:
        outs = backs[m]
        groups.append(
            (after(outs[2], *(moved[1] for moved in y_moved)), last[m][2], outs[6], outs[7], outs[8], attended[m][2], outs[0], attended[m][3], outs[9])
            + (normed_low[m], rows_q_low[m], key_normed[m])
        )
    if aligned:
        (pack_attn,) = kernel_call(
            attn_grads_body,
            [in_vmem((data_size, attn_rows + micro_count * routed_local, lane), low)],
            [
                pltpu.VMEM((width, micro_count * tok_local), low),
                pltpu.VMEM((width, micro_count * routed_all), low),
            ],
            sum(groups, ()),
            managed=True,
            weight=12,
        )
    else:
        totals = [0.0] * 8
        for m, group in enumerate(groups):
            grad_k = group[3].reshape(routed_all, -1)[:, :head_cols]
            pairs = (
                (normed_low[m], group[0]), (normed_low[m], group[1][0]), (normed_low[m], group[1][1]),
                (rows_q_low[m], group[2]), (key_normed[m], grad_k), (key_normed[m], group[4]),
                (group[5], group[6]), (group[7], group[8]),
            )
            totals = [total + tn(left, right) for total, (left, right) in zip(totals, pairs)]
        grad_in = jnp.stack(totals[:6]).astype(low)
        grad_out = jnp.stack(totals[6:]).astype(low)
        pack_attn = jnp.concatenate(
            [
                grad_in.reshape(3, 2, data_size, in_rows, head_cols)
                .transpose(2, 0, 3, 1, 4)
                .reshape(data_size, 3 * in_rows, lane),
                grad_out.reshape(2, data_size, out_rows, sides, lane)
                .transpose(1, 3, 0, 2, 4)
                .reshape(data_size, -1, lane),
            ]
            + [backs[m][7] for m in micros],
            axis=1,
        )
    sum_attn = lax.psum_scatter(
        after(pack_attn.reshape(-1, lane), sum_ffn), "dp", scatter_dimension=0, tiled=True
    )

    device_count = data_size * model_size

    def all_parts(values):
        sent = jnp.broadcast_to(values[None], (device_count,) + values.shape)
        return lax.all_to_all(sent, ("dp", "mp"), 0, 0, tiled=True)

    place = jnp.stack([data_index, model_index]).astype(jnp.int32)

    def unpack_ffn(sources, grads):
        if len(sources) > 1:
            for source, grad in zip(sources, grads):
                grad[...] = source[...]
            return
        (ref,) = sources
        at = 0
        for grad, lead in zip(grads, (2, 0, 2, 0)):
            rows, cols = grad.shape[-2:]
            for l in range(max(lead, 1)):
                for j in range(cols // CHUNK):
                    value = ref[at : at + rows, :].astype(wide)
                    spot = slice(j * CHUNK, (j + 1) * CHUNK)
                    if lead:
                        grad[l, :, spot] = value
                    else:
                        grad[:, spot] = value
                    at = at + rows

    def unpack_attn(sources, grads):
        if len(sources) > 1:
            for source, grad in zip(sources, grads):
                grad[...] = source[...]
            return
        total = sources[0][: 3 * in_rows + 2 * out_rows * sides, :].astype(wide)
        for j in range(3):
            pair = total[j * in_rows : (j + 1) * in_rows]
            grads[0][2 * j] = pair[:, :head_cols]
            grads[0][2 * j + 1] = pair[:, head_cols:]
        for j in range(sides):
            at = 3 * in_rows + 2 * j * out_rows
            for m in range(2):
                grads[1][m, :, j * lane : (j + 1) * lane] = total[at + m * out_rows : at + (m + 1) * out_rows]

    def first_sums(matrices, unpack, sources, sums_shape, weights):
        n = len(weights)
        sums_out = kernel_call(
            functools.partial(sums_body, matrices, unpack, n),
            [in_vmem(w.shape, wide) for w in weights] + [in_vmem(sums_shape, wide)],
            [],
            tuple(sources) + tuple(weights),
            weight=4,
        )
        rows, cols = sums_shape
        sent = jnp.broadcast_to(sums_out[n].astype(low)[None], (device_count, rows, cols))
        got = lax.all_to_all(sent, ("dp", "mp"), 0, 0, tiled=True)
        return sums_out, got

    def optimize(matrices, sums_out, parts, weights, moments, moments_here, vectors_in):
        n = len(weights)
        grads = tuple(sums_out[:n])
        row_old, col_old, row_mine, col_mine = moments_here
        vector_count = len(vectors_in)
        made = kernel_call(
            functools.partial(moments_body, matrices, n, vector_count, data_size, model_size),
            [in_vmem(w.shape, wide) for w in weights]
            + [in_vmem(r.shape, wide) for r in row_old]
            + [in_vmem(c.shape, wide) for c in col_old]
            + [in_vmem(v[0].shape, wide) for v in vectors_in for _ in range(3)]
            + [in_vmem((8, 128), wide)],
            [],
            (place, parts)
            + grads
            + tuple(row_old)
            + tuple(col_old)
            + tuple(row_mine)
            + tuple(col_mine)
            + sum(vectors_in, ()),
            scalars=1,
            weight=5,
        )
        updates, row_new, col_new = made[:n], made[n : 2 * n], made[2 * n : 3 * n]
        vector_made = made[3 * n : -1]
        counts = [
            weights[m.array].shape[-2] * weights[m.array].shape[-1] * device_count for m in matrices
        ] + [width for v in vectors_in for _ in range(v[0].shape[0])]
        all_weights = tuple(weights) + tuple(v[1] for v in vectors_in)

        def finish(aux):
            news = kernel_call(
                functools.partial(weights_body, matrices, counts, n, vector_count),
                [in_vmem(w.shape, wide) for w in all_weights],
                [],
                (aux,) + all_weights + tuple(updates) + tuple(vector_made[1::3]),
                weight=4,
            )
            results = []
            for array in range(n):
                rows, cols = moments[array]
                results.append(
                    [grads[array], row_new[array].reshape(rows.shape), col_new[array].reshape(cols.shape), news[array]]
                )
            for i in range(vector_count):
                results.append([vector_made[3 * i + 2], vector_made[3 * i], news[n + i]])
            return results

        return made[-1], finish

    if aligned:
        ffn_sources = (sum_ffn,)
    else:
        ffn_sources = []
        at = 0
        for weight, block, size in zip((light_in, light_out, heavy_in, heavy_out), blocks, block_rows):
            lead = weight.size // (weight.shape[-1] * weight.shape[-2])
            ffn_sources.append(
                unblocked(sum_ffn[at : at + size].reshape(block.shape), lead).reshape(weight.shape).astype(wide)
            )
            at = at + size
    ffn_made, ffn_parts = first_sums(
        ffn_list, unpack_ffn, ffn_sources, (8, light_hidden + width), ffn_weights
    )
    ffn_sums = ffn_made[-1]
    begun = mp_first(last[-1][0], last[-1][1], pack_attn)
    last_moved.append(mp_second(after(begun, ffn_sums, *earlier)))
    ffn_aux, ffn_finish = optimize(
        ffn_list,
        ffn_made,
        ffn_parts,
        ffn_weights,
        ffn_moments,
        ffn_here,
        (),
    )
    ffn_got = all_parts(ffn_aux)
    ffn_results = ffn_finish(ffn_got)

    key_half = (micro_count * routed_local // 2, width)
    chunks = tok_local // CHUNK
    smem = pl.BlockSpec(memory_space=pltpu.SMEM)
    by_chunk = pl.BlockSpec((CHUNK, width), lambda i: (i, 0))
    by_half = pl.BlockSpec((CHUNK, width), lambda i: (i % (chunks // 2), 0))
    both_out = pl.BlockSpec((micro_count, CHUNK, width), lambda i: (0, i, 0))

    def fixed(shape):
        return pl.BlockSpec(shape, lambda i: (0,) * len(shape))

    def streamed(body, in_specs, out_specs, outs, scratch, args, weight):
        return pl.pallas_call(
            functools.partial(body, chunks),
            grid=(chunks,),
            in_specs=in_specs,
            out_specs=out_specs,
            out_shape=outs,
            scratch_shapes=scratch,
            compiler_params=pltpu.CompilerParams(vmem_limit_bytes=VMEM_BYTES),
            cost_estimate=pl.CostEstimate(flops=weight * 1_150_000_000, bytes_accessed=1_000_000, transcendentals=0),
        )(*args)

    join_args = (core_flag,)
    for m in micros:
        join_args = join_args + (fed[m][0],) + mp_third(y_moved[m], pack_attn, ffn_sums)
    (mixed,) = streamed(
        join_body,
        [smem] + [by_chunk, by_half, by_half] * micro_count,
        [both_out],
        [in_vmem(tokens.shape, low)],
        [],
        join_args,
        6,
    )
    if aligned:
        attn_sources = ()
    else:
        own_sums = sum_attn[:attn_rows].astype(wide)
        attn_sources = (
            own_sums[: 3 * in_rows]
            .reshape(3, in_rows, 2, head_cols)
            .transpose(0, 2, 1, 3)
            .reshape(6, in_rows, head_cols),
            own_sums[3 * in_rows :]
            .reshape(sides, 2, out_rows, lane)
            .transpose(1, 2, 0, 3)
            .reshape(2, out_rows, width),
        )
    key_keep, key_send, grad_attn_in, grad_attn_out, sum_blocks = kernel_call(
        functools.partial(owners_body, micro_count, attn_list, unpack_attn),
        [
            in_vmem(key_half, low),
            in_vmem(key_half, low),
            in_vmem(attn_in.shape, wide),
            in_vmem(attn_out.shape, wide),
            in_vmem((data_size, 8, VECTORS_AT + 128), low),
        ],
        [
            pltpu.VMEM((routed_local, width), low),
            pltpu.VMEM((micro_count * routed_local, width), low),
            pltpu.VMEM((8, VECTORS_AT + 128), wide),
        ],
        (core_flag, sum_attn, after(vectors, mixed, ffn_results[0][3]), w_in)
        + tuple(rows_k)
        + tuple(last[m][4] for m in micros)
        + tuple(backs[m][1] for m in micros)
        + tuple(last[m][3] for m in micros)
        + tuple(fed[m][5] for m in micros)
        + attn_weights
        + attn_sources,
        scalars=1,
        weight=6,
    )
    attn_parts = lax.all_to_all(
        jnp.broadcast_to(
            sum_blocks[:, None], (data_size, model_size) + sum_blocks.shape[1:]
        ).reshape((device_count,) + sum_blocks.shape[1:]),
        ("dp", "mp"),
        0,
        0,
        tiled=True,
    )
    key_begun = mp_first(key_keep, key_send)
    key_moved = mp_second(key_begun)
    pieces = mp_third(key_moved) + (after(vectors, ffn_aux),)
    for m in micros:
        pieces = pieces + mp_third(last_moved[m], ffn_sums if m + 1 < micro_count else ffn_aux)
        pieces = pieces + (backs[m][0], key_row[m])
    (grad_tokens,) = streamed(
        finish_body,
        [smem, fixed(key_half), fixed(key_half), fixed((8, width))]
        + [by_half, by_half, by_chunk, fixed((1, routed_local))] * micro_count
        + [both_out],
        [both_out],
        [in_vmem(tokens.shape, wide)],
        [pltpu.VMEM((micro_count * routed_local, width), low)],
        (core_flag,) + pieces + (tokens,),
        8,
    )
    attn_aux, attn_finish = optimize(
        attn_list,
        (grad_attn_in, grad_attn_out),
        attn_parts,
        attn_weights,
        attn_moments,
        attn_here,
        ((second_gains, gains), (second_router, router)),
    )
    attn_results = attn_finish(all_parts(attn_aux))
    results = [mixed, grad_tokens]
    for result in attn_results[:2] + ffn_results + attn_results[2:]:
        results.extend(result)
    return tuple(results)


def solution(mesh):
    placed = (
        P(None, "dp", None),
        P(None, "dp", None),
        P(),
        P(None, "dp"),
        P(),
        P(None, "dp"),
        P(None, "dp", "mp"),
        P(None, ("mp", "dp"), None),
        P(None, "dp", "mp"),
        P(("mp", "dp"), None),
        P(None, "dp", "mp"),
        P(("mp", "dp"), None),
        P(None, "dp"),
        P(None, "dp"),
        P(),
        P(),
        P(),
        P(),
        P(),
        P(),
        P(),
        P(),
        P(),
        P(),
        P(),
        P(),
        P(None, "dp"),
        P(None, "dp"),
    )
    return jax.shard_map(
        shards,
        mesh=mesh,
        in_specs=placed,
        out_specs=(
            P(None, "dp", None),
            P(None, "dp", None),
            P(None, "dp", "mp"),
            P(),
            P(),
            P(None, "dp", "mp"),
            P(None, ("mp", "dp"), None),
            P(),
            P(),
            P(None, ("mp", "dp"), None),
            P(None, "dp", "mp"),
            P(),
            P(),
            P(None, "dp", "mp"),
            P(("mp", "dp"), None),
            P(),
            P(),
            P(("mp", "dp"), None),
            P(None, "dp", "mp"),
            P(),
            P(),
            P(None, "dp", "mp"),
            P(("mp", "dp"), None),
            P(),
            P(),
            P(("mp", "dp"), None),
            P(None, "dp"),
            P(None, "dp"),
            P(None, "dp"),
            P(None, "dp"),
            P(None, "dp"),
            P(None, "dp"),
        ),
        check_vma=False,
    )
```

```python
import functools
import math

import jax
import jax.numpy as jnp
from jax import lax
from jax.experimental import pallas as pl
from jax.experimental.pallas import tpu as pltpu
from jax.sharding import PartitionSpec as P

D = 768
LH = 8
LDH = 96
HH = 12
HDH = 64
WIN = 128
STEP = 10

norm_eps = 1e-06
tiny_square = 1e-30
scale_floor = 0.001
clip_level = 1.0
step_rate = 0.5
masked_score = -1e30
gelu_scale = math.sqrt(2.0 / math.pi)
gelu_cubic = 0.044715

low = jnp.bfloat16
wide = jnp.float32
CHUNK = 256
BLOCK = 128
RADIUS = WIN // 2
KEYS = 1024
VECTORS_AT = 512
SUM_LANES = 640
STREAM = 256
VMEM_BYTES = 60 * 1024 * 1024
LARGE = 200 * 1024


def nn(left, right):
    return lax.dot_general(left, right, (((1,), (0,)), ((), ())), preferred_element_type=wide)


def nt(left, right):
    return lax.dot_general(left, right, (((1,), (1,)), ((), ())), preferred_element_type=wide)


def tn(left, right):
    return lax.dot_general(left, right, (((0,), (0,)), ((), ())), preferred_element_type=wide)


def sigmoid(logit):
    return 1.0 / (1.0 + jnp.exp(-logit))


def gelu_pair(gate):
    squared = gate * gate
    bent = jnp.tanh(gelu_scale * gate * (1.0 + gelu_cubic * squared))
    half = 0.5 * (1.0 + bent)
    value = gate * half
    slope = half + 0.5 * gate * (1.0 - bent * bent) * gelu_scale * (1.0 + 3.0 * gelu_cubic * squared)
    return value, slope


def picks_rows(idx_col, count):
    spots = lax.broadcasted_iota(jnp.int32, (idx_col.shape[0], count), 1)
    return (spots == idx_col).astype(low)


def picks_cols(idx_row, start, count):
    spots = lax.broadcasted_iota(jnp.int32, (count, idx_row.shape[1]), 0) + start
    return (spots == idx_row).astype(low)


def head_mask(width, size, head):
    spot = lax.broadcasted_iota(jnp.int32, (1, width), 1)
    return ((spot >= head * size) & (spot < (head + 1) * size)).astype(low)


def softmax_parts(scores, allowed):
    masked = jnp.where(allowed, scores, masked_score)
    top = jnp.max(masked, axis=-1, keepdims=True)
    grown = jnp.exp(masked - top)
    return grown * (1.0 / jnp.sum(grown, axis=-1, keepdims=True))


def inverse_rms(values):
    return lax.rsqrt(jnp.mean(values * values, axis=-1, keepdims=True) + norm_eps)


def norm_back(values, gain_row, upstream):
    inverse = inverse_rms(values)
    unit = values * inverse
    scaled = upstream * gain_row
    pulled = inverse * (scaled - unit * jnp.mean(scaled * unit, axis=-1, keepdims=True))
    return pulled, jnp.sum(upstream * unit, axis=0, keepdims=True)


def in_vmem(shape, dtype):
    return jax.ShapeDtypeStruct(shape, dtype)


def vmem_bytes(shape, dtype):
    size = jnp.dtype(dtype).itemsize
    shape = (1,) * (2 - len(shape)) + tuple(shape)
    rows, cols = -(-shape[-2] // (32 // size)) * (32 // size), -(-shape[-1] // 128) * 128
    return math.prod(shape[:-2]) * rows * cols * size


class Transfers:
    def __init__(self, ins, outs, sems):
        self.ins = {id(held): (far, held) for far, held in ins}
        self.outs = {id(held): (far, held) for far, held in outs}
        self.sems, self.used = sems, 0
        self.begun, self.finished, self.going = {}, set(), []

    def copy(self, source, target):
        made = pltpu.make_async_copy(source, target, self.sems.at[self.used])
        self.used += 1
        made.start()
        return made

    def begin(self, *refs):
        for ref in refs:
            if id(ref) in self.ins and id(ref) not in self.begun:
                self.begun[id(ref)] = self.copy(*self.ins[id(ref)])

    def need(self, *refs):
        self.begin(*refs)
        for ref in refs:
            if id(ref) in self.ins and id(ref) not in self.finished:
                self.begun[id(ref)].wait()
                self.finished.add(id(ref))

    def done(self, ref, part=None):
        if id(ref) not in self.outs:
            return
        far, held = self.outs[id(ref)]
        self.finished.add(id(ref))
        if part is None:
            self.going.append(self.copy(held, far))
        else:
            self.going.append(self.copy(held.at[part], far.at[part]))

    def close(self):
        for far, held in self.ins.values():
            self.need(held)
        for far, held in self.outs.values():
            if id(held) not in self.finished:
                self.done(held)
        for made in self.going:
            made.wait()


class Pick:
    def __init__(self, array, index):
        self.array, self.index = array, index
        self.shape, self.dtype = array.shape[1:], array.dtype


def kernel_call(body, outs, scratch, args, scalars=0, weight=10, managed=False, parts=4):
    vmem = pl.BlockSpec(memory_space=pltpu.VMEM)
    smem = pl.BlockSpec(memory_space=pltpu.SMEM)
    far = pl.BlockSpec(memory_space=pl.ANY)

    def large(x):
        return managed and vmem_bytes(x.shape, x.dtype) >= LARGE

    picked = {i: arg.index for i, arg in enumerate(args) if isinstance(arg, Pick)}
    ins = [i for i in range(scalars, len(args)) if large(args[i])]
    assert all(i in ins for i in picked)
    ends = [i for i in range(len(outs)) if large(outs[i])]
    held = [pltpu.VMEM(args[i].shape, args[i].dtype) for i in ins]
    held = held + [pltpu.VMEM(outs[i].shape, outs[i].dtype) for i in ends]
    sems = [pltpu.SemaphoreType.DMA((len(held) + parts,))] if managed else []

    def run(*refs):
        refs = list(refs)
        count = len(args) + len(outs)
        operands, results = refs[: len(args)], refs[len(args) : count]
        kept = refs[count : count + len(held)]
        rest = refs[count + len(held) :]
        if managed:
            rest, sem = rest[:-1], rest[-1]
            pairs_in, pairs_out = [], []
            for i, ref in zip(ins, kept):
                pairs_in.append((operands[i].at[picked[i]] if i in picked else operands[i], ref))
                operands[i] = ref
            for i, ref in zip(ends, kept[len(ins) :]):
                pairs_out.append((results[i], ref))
                results[i] = ref
            moves = Transfers(pairs_in, pairs_out, sem)
            body(moves, *operands, *results, *rest)
            moves.close()
        else:
            body(*operands, *results, *rest)

    return pl.pallas_call(
        run,
        out_shape=outs,
        in_specs=[smem] * scalars + [far if large(x) else vmem for x in args[scalars:]],
        out_specs=[far if large(x) else vmem for x in outs],
        scratch_shapes=held + list(scratch) + sems,
        compiler_params=pltpu.CompilerParams(vmem_limit_bytes=VMEM_BYTES),
        cost_estimate=pl.CostEstimate(
            flops=weight * 1_150_000_000, bytes_accessed=1_000_000, transcendentals=0
        ),
    )(*(arg.array if isinstance(arg, Pick) else arg for arg in args))


def mp_total(core, mine_ref, other_ref, chunk, per_half, size=CHUNK):
    rows = pl.ds(pl.multiple_of((chunk % per_half) * size, size), size)
    flag = ((chunk // per_half) == core).astype(wide)
    return mine_ref[rows, :].astype(wide) * flag + other_ref[rows, :].astype(wide) * (1.0 - flag)


def mp_store(core, keep_ref, send_ref, chunk, per_half, size, value):
    rows = pl.ds(pl.multiple_of((chunk % per_half) * size, size), size)
    kept = (chunk // per_half) == core

    @pl.when(kept)
    def _():
        keep_ref[rows, :] = value

    @pl.when(jnp.logical_not(kept))
    def _():
        send_ref[rows, :] = value


def pack_body(in_ref, out_ref, gain_ref, route_ref, pack_ref):
    in_rows = in_ref.shape[1]
    lane = pack_ref.shape[1]
    for j in range(3):
        pair = jnp.concatenate([in_ref[2 * j], in_ref[2 * j + 1]], axis=1)
        pack_ref[j * in_rows : (j + 1) * in_rows, :] = pair.astype(low)
    both = jnp.concatenate([out_ref[0], out_ref[1]], axis=0).astype(low)
    base = 3 * in_rows
    for j in range(out_ref.shape[2] // lane):
        pack_ref[base : base + both.shape[0], :] = both[:, j * lane : (j + 1) * lane]
        base = base + both.shape[0]
    rows = jnp.concatenate([gain_ref[...], route_ref[...]], axis=0)
    rows = jnp.concatenate([rows, jnp.zeros((16 - rows.shape[0], in_rows), wide)], axis=0)
    rows = jnp.concatenate([rows, jnp.zeros((16, lane - in_rows), wide)], axis=1)
    pack_ref[base : base + 16, :] = rows.astype(low)


def unpack_body(got_ref, w_in_ref, w_out_ref, vec_ref):
    count, _, lane = got_ref.shape
    in_rows = w_in_ref.shape[1] // count
    head_cols = w_in_ref.shape[2]
    for j in range(3):
        pair = got_ref[:, j * in_rows : (j + 1) * in_rows, :].reshape(count * in_rows, lane)
        w_in_ref[2 * j] = pair[:, :head_cols]
        w_in_ref[2 * j + 1] = pair[:, head_cols:]
    base = 3 * in_rows
    out_rows = w_out_ref.shape[1] // count
    sides = w_out_ref.shape[2] // lane
    for j in range(sides):
        cols = slice(j * lane, (j + 1) * lane)
        blocks = [
            got_ref[d, base + j * 2 * out_rows : base + (j + 1) * 2 * out_rows, :].astype(wide)
            for d in range(count)
        ]
        for s in range(2):
            w_out_ref[s, :, cols] = jnp.concatenate(
                [b[s * out_rows : (s + 1) * out_rows] for b in blocks], axis=0
            ).astype(low)
    base = base + 2 * out_rows * sides
    vec_ref[...] = jnp.concatenate(
        [got_ref[d, base : base + 16, :].astype(wide)[:8, :in_rows] for d in range(count)], axis=1
    )


def block_of(ref, base, index, full):
    count = ref.shape[0]
    rows = full // count
    return ref[:, row_span(base // count + index * rows, rows), :].reshape(full, CHUNK)


def row_span(start, size):
    if isinstance(start, int):
        return slice(start, start + size)
    return pl.ds(pl.multiple_of(start, math.gcd(size, 128)), size)


def col_span(index):
    return pl.ds(pl.multiple_of(index * CHUNK, CHUNK), CHUNK)


def part_of(ref, base, index, full, piece):
    count = ref.shape[0]
    rows = full // count
    at = base // count + index * rows
    if rows <= CHUNK:
        span = CHUNK // rows
        return ref[pl.ds(piece * span, span), at : at + rows, :].reshape(CHUNK, CHUNK)
    return ref[0, row_span(at + piece * CHUNK, CHUNK), :]


def ffn_bases(width, light, heavy):
    sides = width // CHUNK
    light_in = 2 * (light // CHUNK) * width
    light_out = sides * light
    heavy_in = 2 * (heavy // CHUNK) * width
    bases = [0, light_in, light_in + light_out, light_in + light_out + heavy_in]
    return bases, bases[3] + sides * heavy


def project_body(moves, vec_ref, w_ref, *refs):
    low_ref = refs[-1]
    micros = (len(refs) - 1) // 12
    inputs, outputs = refs[: 3 * micros], refs[3 * micros : -1]
    for m in range(micros):
        moves.begin(inputs[3 * m])
        moves.begin(w_ref)
    for m in range(micros):
        tok_ref, qcol_ref, kcol_ref = inputs[3 * m : 3 * m + 3]
        n1b_ref, q_ref, k_ref, v_ref, hq_ref, sq_ref, nq_ref, nk_ref, qrows_ref = outputs[9 * m : 9 * m + 9]
        count = tok_ref.shape[0]
        moves.need(tok_ref, w_ref)

        def step(c, carry):
            rows = pl.ds(pl.multiple_of(c * CHUNK, CHUNK), CHUNK)
            values = tok_ref[rows, :].astype(wide)
            normed = values * inverse_rms(values) * vec_ref[0:1, :]
            high = normed.astype(low)
            n1b_ref[rows, :] = high
            low_ref[rows, :] = (normed - high.astype(wide)).astype(low)
            q_ref[rows, :] = nn(high, w_ref[0]).astype(low)
            k_ref[rows, :] = nn(high, w_ref[1]).astype(low)
            v_ref[rows, :] = nn(high, w_ref[2]).astype(low)
            return carry

        lax.fori_loop(0, count // CHUNK, step, 0)
        for ref in (k_ref, v_ref, q_ref, n1b_ref):
            moves.done(ref)
        picks = picks_rows(qcol_ref[...], count)
        query_rows = nn(picks, n1b_ref[...])
        query_wide = query_rows + nn(picks, low_ref[...])
        qrows_ref[...] = query_rows.astype(low)
        nq_ref[...] = query_wide
        hq_ref[...] = nn(query_rows.astype(low), w_ref[3]).astype(low)
        sq_ref[...] = sigmoid(jnp.sum(query_wide * vec_ref[2:3, :], axis=-1, keepdims=True))
        picks = picks_rows(kcol_ref[...], count)
        nk_ref[...] = nn(picks, n1b_ref[...]) + nn(picks, low_ref[...])
        for ref in (qrows_ref, nq_ref, nk_ref):
            moves.done(ref)


def keys_body(o_ref, a_ref, b_ref, c_ref, vec_ref, w_ref, *outs):
    blocks, micros, part, width = o_ref.shape
    for m in range(micros):
        n_ref, k_ref, v_ref, sk_ref = outs[4 * m : 4 * m + 4]
        for p, ref in enumerate((o_ref, a_ref, b_ref, c_ref)):
            values = ref[:, m].reshape(blocks * part, width).astype(wide)
            normed = values * inverse_rms(values) * vec_ref[0:1, :]
            high = normed.astype(low)
            score = sigmoid(jnp.sum(normed * vec_ref[3:4, :], axis=-1, keepdims=True))
            n_ref[:, p] = high.reshape(blocks, part, width)
            sk_ref[:, p] = score.reshape(blocks, part, 1)
            k_ref[:, p] = nn(high, w_ref[4]).astype(low).reshape(blocks, part, -1)
            v_ref[:, p] = (nn(high, w_ref[5]) * score).astype(low).reshape(blocks, part, -1)


def fill_extended(ext_ref, prev, inner, after):
    count = inner.shape[0]
    ext_ref[0:RADIUS, :] = prev
    ext_ref[RADIUS : RADIUS + count, :] = inner
    ext_ref[RADIUS + count :, :] = after


def near_mask(seg_q, seg_k):
    shape = (BLOCK, 2 * BLOCK)
    gap = lax.broadcasted_iota(jnp.int32, shape, 1) - lax.broadcasted_iota(jnp.int32, shape, 0)
    return (gap >= 0) & (gap <= 2 * RADIUS) & (seg_q == seg_k)


def attend_body(
    core_ref, q_ref, k_ref, v_ref, prev_ref, after_ref, hq_ref, hk_ref, hv_ref, sq_ref, wo_ref,
    qrow_ref, segq_ref, segk_ref, hsegq_ref, hsegk_ref,
    keep_ref, send_ref, lmix_ref, hmix_ref, hproj_ref,
    kx_ref, vx_ref, rows_ref,
):
    count, width = q_ref.shape
    light_heads = width // LDH
    heavy_heads = width // HDH
    allowed = hsegq_ref[...] == hsegk_ref[...]
    mix = jnp.zeros((hq_ref.shape[0], width), wide)
    for h in range(heavy_heads):
        mask = head_mask(width, HDH, h)
        probs = softmax_parts(nt(hq_ref[...], hk_ref[...] * mask) * (1.0 / math.sqrt(HDH)), allowed)
        mix = mix + nn(probs.astype(low), hv_ref[...] * mask)
    mix_low = mix.astype(low)
    hmix_ref[...] = mix_low
    proj = nn(mix_low, wo_ref[1])
    hproj_ref[...] = proj
    rows_ref[...] = (sq_ref[...] * proj).astype(low)
    fill_extended(kx_ref, prev_ref[0], k_ref[...], after_ref[0])
    fill_extended(vx_ref, prev_ref[1], v_ref[...], after_ref[1])

    def step(b, carry):
        rows = pl.ds(pl.multiple_of(b * BLOCK, BLOCK), BLOCK)
        keys = pl.ds(pl.multiple_of(b * BLOCK, BLOCK), 2 * BLOCK)
        seg_k = jnp.concatenate([segk_ref[b], segk_ref[b + 1]], axis=1)
        near = near_mask(segq_ref[rows, :], seg_k)
        queries = q_ref[rows, :]
        block_keys = kx_ref[keys, :]
        block_values = vx_ref[keys, :]
        total = jnp.zeros((BLOCK, width), wide)
        for h in range(light_heads):
            mask = head_mask(width, LDH, h)
            probs = softmax_parts(nt(queries, block_keys * mask) * (1.0 / math.sqrt(LDH)), near)
            total = total + nn(probs.astype(low), block_values * mask)
        total_low = total.astype(low)
        lmix_ref[rows, :] = total_low
        spread = picks_cols(qrow_ref[...], b * BLOCK, BLOCK)
        part = (nn(total_low, wo_ref[0]) + nn(spread, rows_ref[...])).astype(low)
        mp_store(core_ref[0], keep_ref, send_ref, b, count // BLOCK // 2, BLOCK, part)
        return carry

    lax.fori_loop(0, count // BLOCK, step, 0)


def ffn_body(last, *refs):
    moves, core_ref, mine_ref, other_ref, tok_ref, cot_ref, vec_ref, fcol_ref, frow_ref, w_ref = refs[:10]
    low_ref, out_rows_ref, grad_rows_ref = refs[-3:]
    if last:
        earlier = [refs[10 + 8 * m : 18 + 8 * m] for m in range(last)]
        middle_ref, ykeep_ref, ysend_ref, gkeep_ref, gsend_ref, router_ref, pack_ref = refs[10 + 8 * last : 17 + 8 * last]
        own = refs[17 + 8 * last : 24 + 8 * last]
        turned_ref, turned_rows_ref = refs[24 + 8 * last : 26 + 8 * last]
    else:
        earlier = []
        middle_ref, ykeep_ref, ysend_ref, gkeep_ref, gsend_ref, router_ref = refs[10:16]
        own = refs[16:23]
    n2b_ref, hidden_ref, dgu_ref, frows_ref, hhid_ref, dhgu_ref, dhout_ref = own
    count, width = tok_ref.shape
    chunks = count // CHUNK
    core = core_ref[0]
    light = hidden_ref.shape[1]
    heavy = hhid_ref.shape[1]
    sides = width // CHUNK
    bases, _ = ffn_bases(width, light, heavy)
    moves.begin(mine_ref, other_ref, tok_ref)
    moves.begin(w_ref, cot_ref)
    for group in earlier:
        moves.begin(*group)
    moves.need(mine_ref, other_ref, tok_ref)

    def heavy_in(s, j):
        return block_of(w_ref, bases[2], s * (heavy // CHUNK) + j, width)

    def heavy_out(t, j):
        return part_of(w_ref, bases[3], t, heavy, j)

    def light_in(s):
        return block_of(w_ref, bases[0], s, width)

    def light_out(t):
        return block_of(w_ref, bases[1], t, light)

    def enter(c, carry):
        rows = pl.ds(pl.multiple_of(c * CHUNK, CHUNK), CHUNK)
        middle = tok_ref[rows, :].astype(wide) + mp_total(core, mine_ref, other_ref, c, chunks // 2)
        middle_ref[rows, :] = middle.astype(low)
        normed = middle * inverse_rms(middle) * vec_ref[1:2, :]
        high = normed.astype(low)
        n2b_ref[rows, :] = high
        low_ref[rows, :] = (normed - high.astype(wide)).astype(low)
        return carry

    lax.fori_loop(0, chunks, enter, 0)
    moves.done(middle_ref)
    moves.done(n2b_ref)
    moves.need(w_ref, cot_ref)
    picks = picks_rows(fcol_ref[...], count)
    rows_high = nn(picks, n2b_ref[...])
    rows_wide = rows_high + nn(picks, low_ref[...])
    rows_low = rows_high.astype(low)
    frows_ref[...] = rows_low
    score = sigmoid(jnp.sum(rows_wide * vec_ref[4:5, :], axis=-1, keepdims=True))
    cot_rows = nn(picks, cot_ref[...])
    grad_out = (score * cot_rows).astype(low)
    dhout_ref[...] = grad_out
    out_rows = [jnp.zeros((rows_low.shape[0], CHUNK), wide) for _ in range(sides)]
    grad_rows = jnp.zeros(rows_low.shape, wide)
    for j in range(heavy // CHUNK):
        cols = slice(j * CHUNK, (j + 1) * CHUNK)
        gate = nn(rows_low, heavy_in(0, j))
        up = nn(rows_low, heavy_in(1, j))
        value, slope = gelu_pair(gate)
        hid = (value * up).astype(low)
        hhid_ref[:, cols] = hid
        grad_hid = jnp.zeros_like(gate)
        for t in range(sides):
            piece = heavy_out(t, j)
            out_rows[t] = out_rows[t] + nn(hid, piece)
            grad_hid = grad_hid + nt(grad_out[:, t * CHUNK : (t + 1) * CHUNK], piece)
        grad_gate = (grad_hid * up * slope).astype(low)
        grad_up = (grad_hid * value).astype(low)
        dhgu_ref[0, :, cols] = grad_gate
        dhgu_ref[1, :, cols] = grad_up
        grad_rows = grad_rows + nt(grad_gate, heavy_in(0, j)) + nt(grad_up, heavy_in(1, j))
    out_rows = jnp.concatenate(out_rows, axis=1)
    logit = jnp.sum(cot_rows * out_rows, axis=-1, keepdims=True) * score * (1.0 - score)
    router_ref[...] = jnp.sum(logit * rows_wide, axis=0, keepdims=True)
    out_rows_ref[...] = (score * out_rows).astype(low)
    grad_rows_ref[...] = (grad_rows + logit * vec_ref[4:5, :]).astype(low)
    for ref in (frows_ref, hhid_ref, dhgu_ref, dhout_ref):
        moves.done(ref)

    def light_rows(c, carry):
        rows = pl.ds(pl.multiple_of(c * CHUNK, CHUNK), CHUNK)
        normed = n2b_ref[rows, :]
        gate = nn(normed, light_in(0))
        up = nn(normed, light_in(1))
        value, slope = gelu_pair(gate)
        hid = (value * up).astype(low)
        hidden_ref[rows, :] = hid
        spread = picks_cols(frow_ref[...], c * CHUNK, CHUNK)
        spread_out = nn(spread, out_rows_ref[...])
        grad_hid = jnp.zeros_like(gate)
        outs = []
        for t in range(sides):
            cols = slice(t * CHUNK, (t + 1) * CHUNK)
            outs.append((nn(hid, light_out(t)) + spread_out[:, cols]).astype(low))
            grad_hid = grad_hid + nt(cot_ref[rows, cols], light_out(t))
        grad_gate = (grad_hid * up * slope).astype(low)
        grad_up = (grad_hid * value).astype(low)
        dgu_ref[0, rows, :] = grad_gate
        dgu_ref[1, rows, :] = grad_up
        grad = nt(grad_gate, light_in(0)) + nt(grad_up, light_in(1)) + nn(spread, grad_rows_ref[...])
        mp_store(core, ykeep_ref, ysend_ref, c, chunks // 2, CHUNK, jnp.concatenate(outs, axis=1))
        mp_store(core, gkeep_ref, gsend_ref, c, chunks // 2, CHUNK, grad.astype(low))
        return carry

    lax.fori_loop(0, chunks, light_rows, 0)
    for ref in (gsend_ref, gkeep_ref, ysend_ref, ykeep_ref):
        moves.done(ref)
    if not last:
        return

    split = pack_ref.shape[0]

    def put(base, index, value):
        rows = value.shape[0] // split
        at = base // split + index * rows
        pack_ref[:, at : at + rows, :] = value.astype(low).reshape(split, rows, CHUNK)

    def sent(base, end):
        moves.done(pack_ref, (slice(None), slice(base // split, end // split)))

    for group in earlier:
        moves.need(*group)
    groups = earlier + [own + (cot_ref,)]
    routed = frows_ref.shape[0]
    for m, group in enumerate(groups):
        turned_ref[:, m * count : (m + 1) * count] = group[0][...].T
        turned_rows_ref[:, m * routed : (m + 1) * routed] = group[3][...].T
    pieces = heavy // CHUNK
    for s in range(2):
        for j in range(pieces):
            total = jnp.zeros((width, CHUNK), wide)
            for m, group in enumerate(groups):
                total = total + nn(
                    turned_rows_ref[:, m * routed : (m + 1) * routed],
                    group[5][s, :, j * CHUNK : (j + 1) * CHUNK],
                )
            put(bases[2], s * pieces + j, total)
    sent(bases[2], bases[3])
    for t in range(sides):
        cols = slice(t * CHUNK, (t + 1) * CHUNK)
        total = jnp.zeros((heavy, CHUNK), wide)
        for group in groups:
            total = total + tn(group[4][...], group[6][:, cols])
        put(bases[3], t, total)
    sent(bases[3], split * pack_ref.shape[1])
    for s in range(2):
        total = jnp.zeros((width, CHUNK), wide)
        for m, group in enumerate(groups):
            total = total + nn(turned_ref[:, m * count : (m + 1) * count], group[2][s])
        put(bases[0], s, total)
    total = jnp.zeros((light, width), wide)
    for group in groups:
        total = total + tn(group[1][...], group[7][...])
    for t in range(sides):
        put(bases[1], t, total[:, t * CHUNK : (t + 1) * CHUNK])
    sent(0, bases[2])


def attend_back_body(
    mine, moves, core_ref, mine_ref, other_ref, middle_ref, cot_ref, vec_ref,
    q_ref, k_ref, v_ref, prev_ref, after_ref, hq_ref, hk_ref, hv_ref, sk_ref, sq_ref, hproj_ref, wo_ref,
    qcol_ref, segq_ref, segk_ref, hsegq_ref, hsegk_ref, earlier_edges_ref,
    agl_ref, gain_ref, dq_ref, inner_ref, rims_ref, edges_ref, dhq_ref, spread_ref, draw_ref,
    dproj_ref, logit_ref,
    kx_ref, vx_ref, dmix_ref, dkx_ref, dvx_ref, dk_ref, dv_ref,
):
    count, width = q_ref.shape
    chunks = count // CHUNK
    light_heads = width // LDH
    heavy_heads = width // HDH
    core = core_ref[0]
    moves.begin(mine_ref, other_ref, middle_ref, cot_ref, wo_ref)
    moves.begin(hk_ref, hv_ref, sk_ref, hproj_ref, k_ref, v_ref, q_ref, segq_ref)
    moves.need(mine_ref, other_ref, middle_ref, cot_ref, wo_ref)
    gain_ref[...] = jnp.zeros_like(gain_ref)

    def enter(c, carry):
        rows = pl.ds(pl.multiple_of(c * CHUNK, CHUNK), CHUNK)
        upstream = mp_total(core, mine_ref, other_ref, c, chunks // 2)
        pulled, gain = norm_back(middle_ref[rows, :].astype(wide), vec_ref[1:2, :], upstream)
        gain_ref[...] += gain
        grad_low = (cot_ref[rows, :].astype(wide) + pulled).astype(low)
        agl_ref[rows, :] = grad_low
        dmix_ref[rows, :] = nt(grad_low, wo_ref[0]).astype(low)
        return carry

    lax.fori_loop(0, chunks, enter, 0)

    moves.done(agl_ref)
    moves.need(hk_ref, hv_ref, sk_ref, hproj_ref)
    picks = picks_rows(qcol_ref[...], count)
    grad_rows = nn(picks, agl_ref[...])
    score = sq_ref[...]
    dproj = (score * grad_rows).astype(low)
    dproj_ref[...] = dproj
    logit_ref[...] = (
        jnp.sum(grad_rows * hproj_ref[...], axis=-1, keepdims=True) * score * (1.0 - score)
    )
    dmix = nt(dproj, wo_ref[1]).astype(low)
    scale = 1.0 / math.sqrt(HDH)
    key_count = hk_ref.shape[0]
    if key_count <= KEYS:
        dk_ref[...] = jnp.zeros_like(dk_ref)
        dv_ref[...] = jnp.zeros_like(dv_ref)

        def one_head(h, dq):
            allowed = hsegq_ref[...] == hsegk_ref[...]
            mask = head_mask(width, HDH, h)
            keys = hk_ref[...] * mask
            probs = softmax_parts(nt(hq_ref[...], keys) * scale, allowed)
            grad_soft = nt(dmix, hv_ref[...] * mask)
            centre = jnp.sum(probs * grad_soft, axis=-1, keepdims=True)
            grad_scores = (probs * (grad_soft - centre)).astype(low)
            dk_ref[...] += tn(grad_scores, hq_ref[...] * mask)
            dv_ref[...] += tn(probs.astype(low), dmix * mask)
            return dq + nn(grad_scores, keys)

        dq = lax.fori_loop(0, heavy_heads, one_head, jnp.zeros((hq_ref.shape[0], width), wide))
        dk, dv = dk_ref[...], dv_ref[...]
        both = jnp.concatenate([(dk * scale).astype(low), dv.astype(low)], axis=1)
        spread_ref[...] = both.reshape(spread_ref.shape)
        draw_ref[...] = (dv * sk_ref[...]).astype(low)
    else:
        pieces = key_count // KEYS

        def piece_of(c, mask):
            spots = pl.ds(pl.multiple_of(c * KEYS, KEYS), KEYS)
            allowed = hsegq_ref[...] == hsegk_ref[:, spots]
            keys = hk_ref[spots, :] * mask
            scores = jnp.where(allowed, nt(hq_ref[...], keys) * scale, masked_score)
            return spots, keys, scores, nt(dmix, hv_ref[spots, :] * mask)

        blank = jnp.zeros((hq_ref.shape[0], 1), wide)
        stats = []
        for h in range(heavy_heads):
            mask = head_mask(width, HDH, h)

            def find_top(c, top):
                return jnp.maximum(top, jnp.max(piece_of(c, mask)[2], axis=-1, keepdims=True))

            top = lax.fori_loop(0, pieces, find_top, blank + masked_score)

            def add_up(c, sums):
                _, _, scores, grad_soft = piece_of(c, mask)
                grown = jnp.exp(scores - top)
                return (
                    sums[0] + jnp.sum(grown, axis=-1, keepdims=True),
                    sums[1] + jnp.sum(grown * grad_soft, axis=-1, keepdims=True),
                )

            total, moment = lax.fori_loop(0, pieces, add_up, (blank, blank))
            stats.append((mask, top, 1.0 / total, moment / total))

        def pull(c, dq):
            dk = jnp.zeros((KEYS, width), wide)
            dv = jnp.zeros((KEYS, width), wide)
            for mask, top, inverse, centre in stats:
                spots, keys, scores, grad_soft = piece_of(c, mask)
                probs = jnp.exp(scores - top) * inverse
                grad_scores = (probs * (grad_soft - centre)).astype(low)
                dq = dq + nn(grad_scores, keys)
                dk = dk + tn(grad_scores, hq_ref[...] * mask)
                dv = dv + tn(probs.astype(low), dmix * mask)
            owners = KEYS // spread_ref.shape[1]
            both = jnp.concatenate([(dk * scale).astype(low), dv.astype(low)], axis=1)
            spread_ref[pl.ds(c * owners, owners)] = both.reshape((owners,) + spread_ref.shape[1:])
            draw_ref[spots, :] = (dv * sk_ref[spots, :]).astype(low)
            return dq

        dq = lax.fori_loop(0, pieces, pull, jnp.zeros((hq_ref.shape[0], width), wide))
    dhq_ref[...] = (dq * scale).astype(low)
    moves.need(k_ref, v_ref, q_ref, segq_ref)
    if mine > 0:
        edges_ref[:, :mine] = earlier_edges_ref[...]
    for ref in (spread_ref, draw_ref, dproj_ref):
        moves.done(ref)
    fill_extended(kx_ref, prev_ref[0], k_ref[...], after_ref[0])
    fill_extended(vx_ref, prev_ref[1], v_ref[...], after_ref[1])
    dkx_ref[...] = jnp.zeros_like(dkx_ref)
    dvx_ref[...] = jnp.zeros_like(dvx_ref)
    light_scale = 1.0 / math.sqrt(LDH)

    def step(b, carry):
        rows = pl.ds(pl.multiple_of(b * BLOCK, BLOCK), BLOCK)
        spans = pl.ds(pl.multiple_of(b * BLOCK, BLOCK), 2 * BLOCK)
        seg_k = jnp.concatenate([segk_ref[b], segk_ref[b + 1]], axis=1)
        near = near_mask(segq_ref[rows, :], seg_k)
        queries = q_ref[rows, :]
        block_keys = kx_ref[spans, :]
        block_values = vx_ref[spans, :]
        mix = dmix_ref[rows, :]
        grad_q = jnp.zeros((BLOCK, width), wide)
        grad_k = jnp.zeros((2 * BLOCK, width), wide)
        grad_v = jnp.zeros((2 * BLOCK, width), wide)
        for h in range(light_heads):
            mask = head_mask(width, LDH, h)
            keys = block_keys * mask
            probs = softmax_parts(nt(queries, keys) * light_scale, near)
            grad_soft = nt(mix, block_values * mask)
            centre = jnp.sum(probs * grad_soft, axis=-1, keepdims=True)
            grad_scores = (probs * (grad_soft - centre)).astype(low)
            grad_q = grad_q + nn(grad_scores, keys)
            grad_k = grad_k + tn(grad_scores, queries * mask)
            grad_v = grad_v + tn(probs.astype(low), mix * mask)
        dq_ref[rows, :] = (grad_q * light_scale).astype(low)
        dkx_ref[spans, :] += grad_k * light_scale
        dvx_ref[spans, :] += grad_v
        return carry

    lax.fori_loop(0, count // BLOCK, step, 0)
    for s, ref in enumerate((dkx_ref, dvx_ref)):
        inner_ref[s] = ref[RADIUS : RADIUS + count, :].astype(low)
        rims_ref[s, :RADIUS, :] = ref[RADIUS : 2 * RADIUS, :]
        rims_ref[s, RADIUS:, :] = ref[count : RADIUS + count, :]
        edges_ref[0, mine, s] = ref[RADIUS + count :, :].astype(low)
        edges_ref[1, mine, s] = ref[:RADIUS, :].astype(low)


def project_back_body(
    core_ref, dq_ref, inner_ref, rims_ref, prev_ref, after_ref, dhq_ref, logit_ref, nq_ref, vec_ref, w_ref, qrow_ref,
    normed_ref,
    keep_ref, send_ref, dkv_ref, router_ref, gain_ref,
    rows_ref,
):
    count, width = dq_ref.shape
    for s in range(2):
        dkv_ref[s, RADIUS : count - RADIUS, :] = inner_ref[s, RADIUS : count - RADIUS, :]
        dkv_ref[s, :RADIUS, :] = (rims_ref[s, :RADIUS, :] + prev_ref[s].astype(wide)).astype(low)
        dkv_ref[s, count - RADIUS :, :] = (rims_ref[s, RADIUS:, :] + after_ref[s].astype(wide)).astype(low)
    query_logit = logit_ref[...]
    router_ref[...] = jnp.sum(query_logit * nq_ref[...], axis=0, keepdims=True)
    rows_ref[...] = (nt(dhq_ref[...], w_ref[3]) + query_logit * vec_ref[2:3, :]).astype(low)

    def step(c, carry):
        rows = pl.ds(pl.multiple_of(c * CHUNK, CHUNK), CHUNK)
        part = (
            nt(dq_ref[rows, :], w_ref[0])
            + nt(dkv_ref[0, rows, :], w_ref[1])
            + nt(dkv_ref[1, rows, :], w_ref[2])
            + nn(picks_cols(qrow_ref[...], c * CHUNK, CHUNK), rows_ref[...])
        )
        gain_ref[...] += jnp.sum(part * normed_ref[rows, :].astype(wide), axis=0, keepdims=True)
        mp_store(core_ref[0], keep_ref, send_ref, c, count // CHUNK // 2, CHUNK, part.astype(low))
        return carry

    gain_ref[...] = jnp.zeros_like(gain_ref)
    lax.fori_loop(0, count // CHUNK, step, 0)
    gain_ref[...] = gain_ref[...] / vec_ref[0:1, :]


def owners_body(micros, matrices, unpack, place_ref, owned_ref, vec_ref, w_ref, *refs):
    at = 5 * micros
    nk_refs, vectors = refs[:micros], refs[micros:at]
    gain_ones, gain_twos, queries = (vectors[i * micros : (i + 1) * micros] for i in range(3))
    ffns = vectors[3 * micros :]
    weights = refs[at : at + 2]
    sources, results, sums_ref = refs[at + 2 : -8], refs[-8:-1], refs[-1]
    keep_ref, send_ref = results[:2]
    grads = results[2:4]
    split_ref, turn_ref, rows_ref = results[4:]
    routed = nk_refs[0].shape[0]
    width = w_ref.shape[2]
    parts = place_ref.shape[0] - 1
    part = routed // parts
    inverse_gain = 1.0 / vec_ref[0:1, :]
    router_key = jnp.zeros((1, vec_ref.shape[1]), wide)
    gain_one = jnp.zeros((1, vec_ref.shape[1]), wide)
    for m in range(micros):
        start = owned_ref.shape[0] - (micros - m) * routed
        owned = owned_ref[start : start + routed, :]
        grad_k = owned[:, :width]
        grad_v = owned[:, width:].astype(wide)
        key_wide = nk_refs[m][...]
        raw = nn(key_wide.astype(low), w_ref[5])
        score = sigmoid(jnp.sum(key_wide * vec_ref[3:4, :], axis=-1, keepdims=True))
        logit = jnp.sum(grad_v * raw, axis=-1, keepdims=True) * score * (1.0 - score)
        router_key = router_key + jnp.sum(logit * key_wide, axis=0, keepdims=True)
        rows = nt(grad_k, w_ref[4]) + nt((grad_v * score).astype(low), w_ref[5]) + logit * vec_ref[3:4, :]
        gain_one = gain_one + jnp.sum(rows * key_wide, axis=0, keepdims=True) * inverse_gain
        turn_ref[...] = rows.astype(low)
        for p in range(parts):
            spot = pl.multiple_of(place_ref[1 + p] * part, part)
            rows_ref[m * routed + p * part : m * routed + (p + 1) * part, :] = turn_ref[pl.ds(spot, part), :]
    half = rows_ref.shape[0] // 2
    for c in range(2):
        mp_store(place_ref[0], keep_ref, send_ref, c, 1, half, rows_ref[c * half : (c + 1) * half, :])

    def added(refs):
        total = refs[0][...]
        for ref in refs[1:]:
            total = total + ref[...]
        return total

    gain_one = gain_one + added(gain_ones)
    lines = (gain_one, added(gain_twos) * (1.0 / parts), added(queries), router_key, added(ffns))
    unpack(sources if sources else (owned_ref,), grads)
    sums_ref[...] = jnp.zeros_like(sums_ref)
    write_sums(matrices, grads, weights, sums_ref)
    count = split_ref.shape[0] // parts
    size = gain_one.shape[1] // count
    for d in range(count):
        for i, line in enumerate(lines):
            sums_ref[i : i + 1, VECTORS_AT : VECTORS_AT + size] = line[:, d * size : (d + 1) * size]
        split_ref[d * parts : (d + 1) * parts] = jnp.broadcast_to(
            sums_ref[...].astype(low)[None], (parts,) + sums_ref.shape
        )


def finish_body(chunks, core_ref, kmine_ref, kother_ref, vec_ref, *refs):
    micros = (len(refs) - 3) // 4
    groups = [refs[4 * m : 4 * m + 4] for m in range(micros)]
    tok_ref, out_ref, keys_ref = refs[4 * micros :]
    routed = groups[0][3].shape[1]
    core = core_ref[0]
    chunk = pl.program_id(0)

    @pl.when(chunk == 0)
    def _():
        half = keys_ref.shape[0] // 2
        for c in range(2):
            keys_ref[c * half : (c + 1) * half, :] = mp_total(core, kmine_ref, kother_ref, c, 1, half).astype(low)

    flag = (chunk // (chunks // 2) == core).astype(wide)
    for m in range(micros):
        mine_ref, other_ref, grad_ref, krow_ref = groups[m]
        upstream = mine_ref[...].astype(wide) * flag + other_ref[...].astype(wide) * (1.0 - flag)
        spread = picks_cols(krow_ref[...], chunk * STREAM, STREAM)
        upstream = upstream + nn(spread, keys_ref[m * routed : (m + 1) * routed, :])
        pulled, _ = norm_back(tok_ref[m].astype(wide), vec_ref[0:1, :], upstream)
        out_ref[m] = grad_ref[...].astype(wide) + pulled


def join_body(chunks, core_ref, *refs):
    out_ref = refs[-1]
    flag = (pl.program_id(0) // (chunks // 2) == core_ref[0]).astype(wide)
    for m in range(out_ref.shape[0]):
        middle_ref, mine_ref, other_ref = refs[3 * m : 3 * m + 3]
        total = mine_ref[...].astype(wide) * flag + other_ref[...].astype(wide) * (1.0 - flag)
        out_ref[m] = (middle_ref[...].astype(wide) + total).astype(low)


def attn_grads_body(moves, *refs):
    out_ref, turned_ref, other_ref = refs[-3:]
    micros = len(refs) // 12
    groups = [refs[12 * m : 12 * m + 12] for m in range(micros)]
    tokens, width = groups[0][9].shape
    keys = groups[0][11].shape[0]
    for group in groups:
        moves.begin(group[9], group[0], group[1], group[10])
    for group in groups:
        moves.begin(group[11], group[3], group[4], group[5], group[6], group[7], group[8])
    for group in groups:
        moves.need(group[9], group[0], group[1], group[10])
    grads = []
    for m in range(micros):
        turned_ref[:, m * tokens : (m + 1) * tokens] = groups[m][9][...].T
    for s in range(3):
        total = 0.0
        for m, group in enumerate(groups):
            grad = group[0][...] if s == 0 else group[1][s - 1]
            total = total + nn(turned_ref[:, m * tokens : (m + 1) * tokens], grad)
        grads.append(total)
    total = 0.0
    for m, group in enumerate(groups):
        total = total + tn(group[10][...], group[2][...])
    grads.append(total)
    for group in groups:
        moves.need(*group)
    for m in range(micros):
        other_ref[:, m * keys : (m + 1) * keys] = groups[m][11][...].T
    for s in (3, 4):
        total = 0.0
        for m, group in enumerate(groups):
            if s == 3:
                grad = group[s][...].reshape(keys, -1)[:, : group[4].shape[1]]
            else:
                grad = group[s][...]
            total = total + nn(other_ref[:, m * keys : (m + 1) * keys], grad)
        grads.append(total)
    out_grads = []
    for mix, grad in ((5, 6), (7, 8)):
        total = 0.0
        for group in groups:
            total = total + tn(group[mix][...], group[grad][...])
        out_grads.append(total)
    count, _, lane = out_ref.shape
    in_rows = width // count
    for j in range(3):
        pair = jnp.concatenate([grads[2 * j], grads[2 * j + 1]], axis=1).astype(low)
        out_ref[:, j * in_rows : (j + 1) * in_rows, :] = pair.reshape(count, in_rows, lane)
    out_rows = out_grads[0].shape[0] // count
    own = groups[0][3].shape[1]
    for m, group in enumerate(groups):
        at = out_ref.shape[1] - (micros - m) * own
        out_ref[:, at : at + own, :] = group[3][...]
    for d in range(count):
        rows = slice(d * out_rows, (d + 1) * out_rows)
        both = jnp.concatenate([g[rows] for g in out_grads], axis=0).astype(low)
        for j in range(width // lane):
            at = 3 * in_rows + j * 2 * out_rows
            out_ref[d, at : at + 2 * out_rows, :] = both[:, j * lane : (j + 1) * lane]


class Matrix:
    def __init__(self, array, lead, tall, cols_at, rows_at, weight_at):
        self.array, self.lead, self.tall = array, lead, tall
        self.cols_at, self.rows_at, self.weight_at = cols_at, rows_at, weight_at

    def read(self, refs):
        ref = refs[self.array]
        return ref[...] if self.lead is None else ref[self.lead]

    def write(self, refs, value):
        if self.lead is None:
            refs[self.array][...] = value
        else:
            refs[self.array][self.lead] = value

    def line(self):
        lead = 0 if self.lead is None else self.lead
        return slice(lead, lead + 1)


def ffn_matrices(light, heavy, width):
    cut = SUM_LANES
    rest = heavy - cut
    tail = width - cut
    return [
        Matrix(0, 0, True, [(4, rest, light)], (6, 2 * tail), (7, 3 * 128)),
        Matrix(0, 1, True, [(5, rest, light)], (6, 2 * tail + 128), (7, 3 * 128 + 1)),
        Matrix(1, None, False, [(2, 0, cut), (6, 0, tail)], (6, 2 * tail + 256), (7, 3 * 128 + 2)),
        Matrix(2, 0, True, [(0, 0, cut), (4, 0, rest)], (7, 0), (7, 3 * 128 + 3)),
        Matrix(2, 1, True, [(1, 0, cut), (5, 0, rest)], (7, 128), (7, 3 * 128 + 4)),
        Matrix(3, None, False, [(3, 0, cut), (6, tail, tail)], (7, 256), (7, 3 * 128 + 5)),
    ]


def attn_matrices(cols, width):
    listed = [
        Matrix(0, i, True, [(i, 0, cols)], (6 + i // 4, 128 * (i % 4)), (i, 224)) for i in range(6)
    ]
    piece = width // 3
    for s in range(2):
        spots = [(3 * s + j, 256, piece) for j in range(3)]
        listed.append(Matrix(1, s, False, spots, (7, 256 + 128 * s), (s, 232)))
    return listed


def total_of(values):
    return jnp.sum(jnp.sum(values, axis=1, keepdims=True), axis=0, keepdims=True)


def sums_body(matrices, unpack, array_count, *refs):
    weights = refs[-2 * array_count - 1 : -array_count - 1]
    grads, sums_ref = refs[-array_count - 1 : -1], refs[-1]
    unpack(refs[: -2 * array_count - 1], grads)
    sums_ref[...] = jnp.zeros_like(sums_ref)
    write_sums(matrices, grads, weights, sums_ref)


def write_sums(matrices, grads, weights, sums_ref):
    for matrix in matrices:
        square = matrix.read(grads)
        square = square * square + tiny_square
        cols = jnp.sum(square, axis=0, keepdims=True)
        at = 0
        for row, lane, size in matrix.cols_at:
            sums_ref[row : row + 1, lane : lane + size] = cols[:, at : at + size]
            at = at + size
        rows = lax.dot_general(
            jnp.ones((8, square.shape[1]), wide),
            square,
            (((1,), (1,)), ((), ())),
            precision=lax.Precision.HIGHEST,
            preferred_element_type=wide,
        )
        row, lane = matrix.rows_at
        sums_ref[row : row + 1, lane : lane + square.shape[0]] = rows[0:1]
        weight = matrix.read(weights)
        row, lane = matrix.weight_at
        sums_ref[row : row + 1, lane : lane + 1] = total_of(weight * weight)


def lane_row(values):
    spots = lax.broadcasted_iota(jnp.int32, (1, 128), 1)
    row = jnp.zeros((1, 128), wide)
    for place, value in enumerate(values):
        row = row + jnp.where(spots == place, value, 0.0)
    return row


def moments_body(matrices, array_count, vector_count, data_size, model_size, place_ref, parts_ref, *refs):
    keep = 1.0 - STEP ** (-0.8)
    n = array_count
    grads, row_old, col_old, row_mine, col_mine = (refs[i * n : (i + 1) * n] for i in range(5))
    at = 5 * n
    vector_in = refs[at : at + 2 * vector_count]
    at = at + 2 * vector_count
    updates, row_new, col_new = (refs[at + i * n : at + (i + 1) * n] for i in range(3))
    at = at + 3 * n
    vector_out = refs[at : at + 3 * vector_count]
    aux_ref = refs[-1]
    d, k = place_ref[0], place_ref[1]
    devices = data_size * model_size

    def part(index):
        return parts_ref[index].astype(wide)

    whole = part(0)
    for i in range(1, devices):
        whole = whole + part(i)
    by_model = []
    for j in range(model_size):
        total = part(j)
        for i in range(1, data_size):
            total = total + part(i * model_size + j)
        by_model.append(total)
    by_data = []
    for i in range(data_size):
        total = part(i * model_size)
        for j in range(1, model_size):
            total = total + part(i * model_size + j)
        by_data.append(total)
    my_cols = part(k)
    for i in range(1, data_size):
        my_cols = my_cols + part(i * model_size + k)
    my_rows = part(d * model_size)
    for j in range(1, model_size):
        my_rows = my_rows + part(d * model_size + j)
    mine = part(d * model_size + k)

    def cols_of(sums, matrix):
        pieces = [sums[row : row + 1, lane : lane + size] for row, lane, size in matrix.cols_at]
        return pieces[0] if len(pieces) == 1 else jnp.concatenate(pieces, axis=1)

    lines, extents = [], []
    for matrix in matrices:
        grad_rows, grad_cols = matrix.read(grads).shape
        row_total = grad_rows * data_size * (1 if matrix.tall else model_size)
        col_total = grad_cols * (model_size if matrix.tall else 1)
        extents.append((row_total, col_total))
        row, lane = matrix.rows_at
        source = my_rows if matrix.tall else mine
        old = row_mine[matrix.array][matrix.line(), :]
        lines.append(keep * old + (1.0 - keep) / col_total * source[row : row + 1, lane : lane + 128])
    while len(lines) < 8:
        lines.append(jnp.zeros((1, 128), wide))
    columns = jnp.concatenate(lines, axis=0).T
    update_sums, weight_sums = [], []
    for place, (matrix, (row_total, col_total)) in enumerate(zip(matrices, extents)):
        grad = matrix.read(grads)
        row, lane = matrix.rows_at
        size = grad.shape[0]
        old_rows = row_old[matrix.array][matrix.line(), :]
        old_cols = col_old[matrix.array][matrix.line(), :]
        mean = keep * jnp.mean(old_rows, axis=1, keepdims=True) + (1.0 - keep) / (
            row_total * col_total
        ) * jnp.sum(whole[row : row + 1, lane : lane + 128], axis=1, keepdims=True)
        if matrix.tall:
            cols = keep * col_mine[matrix.array][matrix.line(), :] + (1.0 - keep) / row_total * cols_of(my_cols, matrix)
            all_cols = jnp.concatenate([cols_of(sums, matrix) for sums in by_model], axis=1)
            all_rows = jnp.concatenate([sums[row : row + 1, lane : lane + size] for sums in by_data], axis=1)
            new_cols = keep * old_cols + (1.0 - keep) / row_total * all_cols
        else:
            cols = keep * old_cols + (1.0 - keep) / row_total * cols_of(whole, matrix)
            all_rows = jnp.concatenate(
                [
                    part(i * model_size + j)[row : row + 1, lane : lane + size]
                    for j in range(model_size)
                    for i in range(data_size)
                ],
                axis=1,
            )
            new_cols = cols
        row_new[matrix.array][matrix.line(), :] = keep * old_rows + (1.0 - keep) / col_total * all_rows
        col_new[matrix.array][matrix.line(), :] = new_cols
        update = grad * lax.rsqrt(columns[:size, place : place + 1] * (cols / mean))
        matrix.write(updates, update)
        update_sums.append(total_of(update * update))
        row, lane = matrix.weight_at
        weight_sums.append(whole[row : row + 1, lane : lane + 1] * (1.0 / devices))
    line_at = 0
    for i in range(vector_count):
        old_ref, weight_ref = vector_in[2 * i : 2 * i + 2]
        lines, size = old_ref.shape
        grad = whole[line_at : line_at + lines, VECTORS_AT : VECTORS_AT + size]
        line_at = line_at + lines
        vector_out[3 * i + 2][...] = grad
        moment = keep * old_ref[...] + (1.0 - keep) * (grad * grad + tiny_square)
        update = grad * lax.rsqrt(moment)
        vector_out[3 * i][...] = moment
        vector_out[3 * i + 1][...] = update
        for r in range(grad.shape[0]):
            line = update[r : r + 1]
            update_sums.append(total_of(line * line) * (1.0 / model_size))
            line = weight_ref[r : r + 1, :]
            weight_sums.append(total_of(line * line) * (1.0 / model_size))
    lines = jnp.concatenate([lane_row(update_sums), lane_row(weight_sums), jnp.zeros((6, 128), wide)], axis=0)
    aux_ref[...] = jnp.broadcast_to(lines[None], aux_ref.shape)


def step_size(update_sum, weight_sum, count):
    rms_weight = jnp.sqrt(weight_sum * (1.0 / count))
    rms_update = jnp.sqrt(update_sum * (1.0 / count))
    return step_rate * jnp.maximum(scale_floor, rms_weight) / jnp.maximum(1.0, rms_update / clip_level)


def weights_body(matrices, counts, array_count, vector_count, aux_ref, *refs):
    n = array_count + vector_count
    weights, updates, news = refs[:n], refs[n : 2 * n], refs[2 * n :]
    sums = aux_ref[0]
    for i in range(1, aux_ref.shape[0]):
        sums = sums + aux_ref[i]

    def step(place):
        spot = slice(place, place + 1)
        return step_size(sums[0:1, spot], sums[1:2, spot], counts[place])

    for place, matrix in enumerate(matrices):
        matrix.write(news, matrix.read(weights) - step(place) * matrix.read(updates))
    place = len(matrices)
    for i in range(array_count, n):
        for r in range(weights[i].shape[0]):
            row = slice(r, r + 1)
            news[i][row, :] = weights[i][row, :] - step(place) * updates[i][row, :]
            place = place + 1


def after(value, *others):
    return lax.optimization_barrier((value,) + others)[0]


def shards(
    tokens,
    cotangent,
    segments,
    route_query,
    route_key,
    route_ffn,
    attn_in,
    attn_out,
    light_in,
    light_out,
    heavy_in,
    heavy_out,
    gains,
    router,
    row_attn_in,
    col_attn_in,
    row_attn_out,
    col_attn_out,
    row_light_in,
    col_light_in,
    row_light_out,
    col_light_out,
    row_heavy_in,
    col_heavy_in,
    row_heavy_out,
    col_heavy_out,
    second_gains,
    second_router,
):
    data_size = lax.axis_size("dp")
    model_size = lax.axis_size("mp")
    data_index = lax.axis_index("dp")
    model_index = lax.axis_index("mp")
    core = model_index % 2
    order = jnp.arange(model_size) ^ model_index
    core_flag = jnp.concatenate([core.reshape(1), order]).astype(jnp.int32)
    core_pairs = [(i, i ^ 1) for i in range(model_size)]
    far_pairs = [(i, i ^ 2) for i in range(model_size)]
    micro_count, tok_local, width = tokens.shape
    routed_local = route_query.shape[1]
    routed_all = route_key.shape[1]
    quarter = routed_local // model_size
    head_cols = attn_in.shape[2]
    in_rows = attn_in.shape[1]

    key_blocks = route_key.reshape(micro_count, data_size, model_size, quarter)
    own_keys = lax.dynamic_slice_in_dim(key_blocks, data_index, 1, axis=1)
    key_blocks = jnp.take(key_blocks, order, axis=2)
    key_local = lax.dynamic_slice_in_dim(key_blocks, data_index, 1, axis=1)[:, 0]
    my_quarter = key_local[:, 0]
    picks = (my_quarter[:, :, None] == jnp.arange(tok_local)[None, None, :]).astype(low)
    my_rows = jnp.einsum("mrt,mtd->mrd", picks, tokens, preferred_element_type=wide).astype(low)

    def to_all(rows):
        sent = jnp.broadcast_to(rows[None], (data_size,) + rows.shape)
        return lax.all_to_all(sent, "dp", 0, 0, tiled=True)

    key_rows = to_all(my_rows).reshape(data_size, micro_count, quarter, width)
    rows_core = lax.ppermute(key_rows, "mp", core_pairs)
    rows_far = lax.ppermute(key_rows, "mp", far_pairs)
    rows_both = lax.ppermute(rows_far, "mp", core_pairs)

    lane = 2 * head_cols
    sides = width // lane
    in_rows = attn_in.shape[1]
    out_rows = attn_out.shape[1]
    aligned = in_rows % 16 == 0 and out_rows % 8 == 0 and light_out.shape[0] % 16 == 0
    if aligned:
        (pack_one,) = kernel_call(
            pack_body,
            [in_vmem((3 * in_rows + 2 * out_rows * sides + 16, lane), low)],
            [],
            (attn_in, attn_out, gains, router),
            weight=3,
        )
    else:
        small = jnp.concatenate([gains, router], axis=0).astype(low)
        small_block = jnp.pad(small, ((0, 16 - small.shape[0]), (0, lane - in_rows)))
        in_block = (
            attn_in.astype(low).reshape(3, 2, in_rows, head_cols).transpose(0, 2, 1, 3).reshape(3 * in_rows, lane)
        )

        def sideways(rows):
            return rows.reshape(-1, sides, lane).transpose(1, 0, 2).reshape(-1, lane)

        out_block = sideways(attn_out.astype(low).reshape(2 * out_rows, width))
        pack_one = jnp.concatenate([in_block, out_block, small_block], axis=0)
    got_one = lax.all_gather(pack_one, "dp", axis=0, tiled=False)

    light_hidden = light_in.shape[2]
    heavy_hidden = heavy_in.shape[2]
    local_spot = model_index * data_size + data_index
    ffn_list = ffn_matrices(light_hidden, heavy_hidden, width)
    ffn_weights = (light_in, light_out, heavy_in, heavy_out)
    ffn_moments = (
        (row_light_in, col_light_in),
        (row_light_out, col_light_out),
        (row_heavy_in, col_heavy_in),
        (row_heavy_out, col_heavy_out),
    )
    attn_list = attn_matrices(head_cols, width)
    attn_weights = (attn_in, attn_out)
    attn_moments = ((row_attn_in, col_attn_in), (row_attn_out, col_attn_out))

    def moments_of(matrices, weights, moments):
        row_old, col_old, row_mine, col_mine = [], [], [], []
        for array, weight in enumerate(weights):
            rows, cols = moments[array]
            tall = [m.tall for m in matrices if m.array == array][0]
            lead = rows.size // rows.shape[-1]
            rows, cols = rows.reshape(lead, -1), cols.reshape(lead, -1)
            size, span = weight.shape[-2:]
            spot = data_index if tall else local_spot
            my_rows = lax.dynamic_slice_in_dim(rows, spot * size, size, 1)
            row_mine.append(jnp.pad(my_rows, ((0, 0), (0, 128 - size)), constant_values=1.0))
            col_mine.append(lax.dynamic_slice_in_dim(cols, model_index * span, span, 1) if tall else cols)
            row_old.append(rows)
            col_old.append(cols)
        return row_old, col_old, row_mine, col_mine

    ffn_here, attn_here, got_one = lax.optimization_barrier(
        (
            moments_of(ffn_list, ffn_weights, ffn_moments),
            moments_of(attn_list, attn_weights, attn_moments),
            got_one,
        )
    )

    if aligned:
        w_in, w_out, vectors = kernel_call(
            unpack_body,
            [
                in_vmem((6, width, head_cols), low),
                in_vmem((2, data_size * out_rows, width), low),
                in_vmem((8, width), wide),
            ],
            [],
            (got_one,),
            weight=5,
        )
    else:
        w_in = (
            got_one[:, : 3 * in_rows]
            .reshape(data_size, 3, in_rows, 2, head_cols)
            .transpose(1, 3, 0, 2, 4)
            .reshape(6, width, head_cols)
        )
        at = 3 * in_rows
        w_out = (
            got_one[:, at : at + out_block.shape[0]]
            .reshape(data_size, sides, 2, out_rows, lane)
            .transpose(2, 0, 3, 1, 4)
            .reshape(2, data_size * out_rows, width)
        )
        at = at + out_block.shape[0]
        vectors = got_one[:, at : at + 8, :in_rows].transpose(1, 0, 2).reshape(8, width).astype(wide)

    def blocked(weight):
        lead, rows, cols = weight.shape
        return weight.reshape(lead, rows, cols // CHUNK, CHUNK).transpose(0, 2, 1, 3).reshape(-1, rows, CHUNK)

    def unblocked(blocks, lead):
        count, rows, _ = blocks.shape
        return blocks.reshape(lead, count // lead, rows, CHUNK).transpose(0, 2, 1, 3).reshape(lead, rows, -1)

    light_hidden = light_in.shape[2]
    heavy_hidden = heavy_in.shape[2]
    blocks = [blocked(w.astype(low)) for w in (light_in, light_out[None], heavy_in, heavy_out[None])]
    block_rows = [b.shape[0] * b.shape[1] for b in blocks]
    pack_two = jnp.concatenate([b.reshape(-1, CHUNK) for b in blocks], axis=0)
    w_ffn = lax.all_gather(after(pack_two, got_one, rows_far), "dp", axis=0, tiled=False)
    if not aligned:
        pieces = []
        at = 0
        for block in blocks:
            size = block.shape[0] * block.shape[1]
            pieces.append(
                w_ffn[:, at : at + size]
                .reshape((data_size,) + block.shape)
                .transpose(1, 0, 2, 3)
                .reshape(-1, CHUNK)
            )
            at = at + size
        w_ffn = jnp.concatenate(pieces, axis=0)[None]

    attn_in, attn_out, light_in, light_out, heavy_in, heavy_out, gains, router = (
        lax.optimization_barrier(
            (got_one, attn_in, attn_out, light_in, light_out, heavy_in, heavy_out, gains, router)
        )[1:]
    )

    turns = (jnp.arange(micro_count) % 2)[:, None]
    segment_ids = segments[None, :] * turns
    seg_padded = jnp.pad(segment_ids, ((0, 0), (RADIUS, RADIUS)), constant_values=-1)
    seg_local = lax.dynamic_slice_in_dim(segment_ids, data_index * tok_local, tok_local, axis=1)
    seg_extended = lax.dynamic_slice_in_dim(
        seg_padded, data_index * tok_local, tok_local + 2 * RADIUS, axis=1
    ).reshape(micro_count, -1, 1, BLOCK)

    def picked(ids, spots):
        hit = spots[..., :, None] == jnp.arange(tok_local)
        return jnp.sum(jnp.where(hit, ids[..., None, :], 0), axis=-1)

    key_seg = picked(
        segment_ids.reshape(micro_count, data_size, tok_local),
        key_blocks.reshape(micro_count, data_size, routed_local),
    ).reshape(micro_count, -1)
    query_seg = picked(seg_local, route_query)
    key_list = key_local.reshape(micro_count, -1)

    query_col, query_row = route_query[:, :, None], route_query[:, None, :]
    key_col, key_row = key_list[:, :, None], own_keys.reshape(micro_count, 1, routed_local)
    ffn_col, ffn_row = route_ffn[:, :, None], route_ffn[:, None, :]
    segs = (seg_local[:, :, None], seg_extended, query_seg[:, :, None], key_seg[:, None, :])

    micros = range(micro_count)
    token_parts = [Pick(tokens, m) for m in micros]
    cot_parts = [Pick(cotangent, m) for m in micros]
    projected = kernel_call(
        project_body,
        [
            in_vmem((tok_local, width), low),
            in_vmem((tok_local, head_cols), low),
            in_vmem((tok_local, head_cols), low),
            in_vmem((tok_local, head_cols), low),
            in_vmem((routed_local, head_cols), low),
            in_vmem((routed_local, 1), wide),
            in_vmem((routed_local, width), wide),
            in_vmem((routed_local, width), wide),
            in_vmem((routed_local, width), low),
        ]
        * micro_count,
        [pltpu.VMEM((tok_local, width), low)],
        (vectors, w_in) + sum(((token_parts[m], query_col[m], key_col[m]) for m in micros), ()),
        managed=True,
            weight=12,
    )
    normed_low, light_q, light_k, light_v, heavy_q, score_q, rows_q, rows_k, rows_q_low = (
        projected[i::9] for i in range(9)
    )

    up = [(i, i + 1) for i in range(data_size - 1)]
    down = [(i + 1, i) for i in range(data_size - 1)]
    tails = jnp.stack([jnp.stack([k[tok_local - RADIUS :], v[tok_local - RADIUS :]]) for k, v in zip(light_k, light_v)])
    heads = jnp.stack([jnp.stack([k[:RADIUS], v[:RADIUS]]) for k, v in zip(light_k, light_v)])
    halo_prev = lax.ppermute(tails, "dp", up)
    halo_next = lax.ppermute(heads, "dp", down)

    split = (data_size, model_size, quarter)
    span = min(data_size, 8)

    def split_spec(cols):
        return pl.BlockSpec((span, model_size, quarter, cols), lambda i: (i, 0, 0, 0))

    keyed = pl.pallas_call(
        keys_body,
        grid=(data_size // span,),
        out_shape=[
            in_vmem(split + (width,), low),
            in_vmem(split + (head_cols,), low),
            in_vmem(split + (head_cols,), low),
            in_vmem(split + (1,), wide),
        ]
        * micro_count,
        in_specs=[pl.BlockSpec((span, micro_count, quarter, width), lambda i: (i, 0, 0, 0))] * 4
        + [
            pl.BlockSpec((8, width), lambda i: (0, 0)),
            pl.BlockSpec((6, width, head_cols), lambda i: (0, 0, 0)),
        ],
        out_specs=[split_spec(width), split_spec(head_cols), split_spec(head_cols), split_spec(1)] * micro_count,
        compiler_params=pltpu.CompilerParams(vmem_limit_bytes=VMEM_BYTES),
        cost_estimate=pl.CostEstimate(flops=6 * 1_150_000_000, bytes_accessed=1_000_000, transcendentals=0),
    )(key_rows, rows_core, rows_far, rows_both, vectors, w_in)
    key_normed, heavy_k, heavy_v, score_k = (
        [a.reshape(routed_all, -1) for a in keyed[i::4]] for i in range(4)
    )

    def mp_first(keep, send, *earlier):
        got = lax.ppermute(after(send, *earlier), "mp", core_pairs)
        return (keep.astype(wide) + got.astype(wide)).astype(low)

    def mp_second(mine):
        return mine, lax.ppermute(mine, "mp", far_pairs)

    def mp_third(moved, *held):
        mine, near = moved
        near = after(near, *held)
        done = (mine.astype(wide) + near.astype(wide)).astype(low)
        return done, lax.ppermute(done, "mp", core_pairs)

    extended = pltpu.VMEM((tok_local + 2 * RADIUS, head_cols), low)
    row_shape = (tok_local, width)
    half_shape = (tok_local // 2, width)

    def all_picks(arrays, m):
        return tuple(a[m] for a in arrays)

    attended = []
    attn_moved = []
    held, earlier = (), ()
    for m in micros:
        outs = kernel_call(
            attend_body,
            [
                in_vmem(half_shape, low),
                in_vmem(half_shape, low),
                in_vmem((tok_local, head_cols), low),
                in_vmem((routed_local, head_cols), low),
                in_vmem((routed_local, width), wide),
            ],
            [extended, extended, pltpu.VMEM((routed_local, width), low)],
            (core_flag,)
            + all_picks((light_q, light_k, light_v, halo_prev, halo_next, heavy_q, heavy_k, heavy_v, score_q), m)
            + (after(w_out, *held),)
            + all_picks((query_row,) + segs, m),
            scalars=1,
            managed=False,
            weight=11,
        )
        attended.append(outs)
        begun = mp_first(outs[0], outs[1], *earlier)
        attn_moved.append(mp_second(begun))
        held, earlier = (begun,), (attn_moved[m][1],)

    fed = []
    grad_moved = []
    split = data_size if aligned else 1
    total_rows = ffn_bases(width, light_hidden, heavy_hidden)[1]
    own = [
        (row_shape, low),
        ((tok_local, light_hidden), low),
        ((2, tok_local, light_hidden), low),
        ((routed_local, width), low),
        ((routed_local, heavy_hidden), low),
        ((2, routed_local, heavy_hidden), low),
        ((routed_local, width), low),
    ]
    for m in micros:
        beside = attended[m + 1][0] if m + 1 < micro_count else fed[m - 1][1]
        ffn_outs = [
            in_vmem(row_shape, low),
            in_vmem(half_shape, low),
            in_vmem(half_shape, low),
            in_vmem(half_shape, low),
            in_vmem(half_shape, low),
            in_vmem((1, width), wide),
        ]
        scratch = [
            pltpu.VMEM(row_shape, low),
            pltpu.VMEM((routed_local, width), low),
            pltpu.VMEM((routed_local, width), low),
        ]
        kept = ()
        if m + 1 < micro_count:
            ffn_outs = ffn_outs + [in_vmem(*o) for o in own]
        else:
            ffn_outs = ffn_outs + [in_vmem((split, total_rows // split, CHUNK), low)]
            scratch = [
                *(pltpu.VMEM(*o) for o in own),
                pltpu.VMEM((width, micro_count * tok_local), low),
                pltpu.VMEM((width, micro_count * routed_local), low),
                *scratch,
            ]
            for i in range(m):
                kept = kept + tuple(fed[i][6:13]) + (cot_parts[i],)
        outs = kernel_call(
            functools.partial(ffn_body, m if m + 1 == micro_count else 0),
            ffn_outs,
            scratch,
            (core_flag,)
            + mp_third(attn_moved[m], beside)
            + (token_parts[m], cot_parts[m], after(vectors, *held), ffn_col[m], ffn_row[m], w_ffn)
            + kept,
            scalars=1,
            managed=True,
            weight=17 if m + 1 < micro_count else 23,
        )
        fed.append(outs)
        begun = mp_first(outs[3], outs[4], *earlier)
        grad_moved.append(mp_second(begun))
        held, earlier = (begun,), (grad_moved[m][1],)
    pack_ffn = fed[-1][6]
    if not aligned:
        pieces = []
        at = 0
        for block in blocks:
            size = block.shape[0] * block.shape[1] * data_size
            pieces.append(
                pack_ffn[0, at : at + size]
                .reshape(block.shape[0], data_size, block.shape[1], CHUNK)
                .transpose(1, 0, 2, 3)
                .reshape(data_size, -1, CHUNK)
            )
            at = at + size
        pack_ffn = jnp.concatenate(pieces, axis=1)
    sum_ffn = lax.psum_scatter(pack_ffn.reshape(-1, CHUNK), "dp", scatter_dimension=0, tiled=True)

    y_moved = []
    backs = []
    edges = jnp.zeros((2, 1, 2, RADIUS, head_cols), low)
    y_begun = [mp_first(fed[m][1], fed[m][2]) for m in micros]
    for m in micros:
        outs = kernel_call(
            functools.partial(attend_back_body, m),
            [
                in_vmem(row_shape, low),
                in_vmem((1, width), wide),
                in_vmem((tok_local, head_cols), low),
                in_vmem((2, tok_local, head_cols), low),
                in_vmem((2, 2 * RADIUS, head_cols), wide),
                in_vmem((2, m + 1, 2, RADIUS, head_cols), low),
                in_vmem((routed_local, head_cols), low),
                in_vmem((data_size, routed_local, 2 * head_cols), low),
                in_vmem((routed_all, head_cols), low),
                in_vmem((routed_local, width), low),
                in_vmem((routed_local, 1), wide),
            ],
            [
                extended,
                extended,
                pltpu.VMEM((tok_local, head_cols), low),
                pltpu.VMEM((tok_local + 2 * RADIUS, head_cols), wide),
                pltpu.VMEM((tok_local + 2 * RADIUS, head_cols), wide),
                pltpu.VMEM((min(routed_all, KEYS), head_cols), wide),
                pltpu.VMEM((min(routed_all, KEYS), head_cols), wide),
            ],
            (core_flag,)
            + mp_third(grad_moved[m], pack_ffn if m == 0 else backs[m - 1][0])
            + (fed[m][0], cot_parts[m], after(vectors, pack_ffn, y_begun[m]))
            + all_picks(
                (light_q, light_k, light_v, halo_prev, halo_next, heavy_q, heavy_k, heavy_v, score_k, score_q), m
            )
            + (attended[m][4], w_out)
            + all_picks((query_col,) + segs, m)
            + (edges,),
            scalars=1,
            managed=True,
            weight=22,
        )
        edges = outs[5]
        backs.append(outs)
        y_moved.append(mp_second(after(y_begun[m], outs[0], *earlier)))
        earlier = (y_moved[m][1],)
    held = (y_moved[0][1],)

    from_prev = lax.ppermute(edges[0], "dp", up)
    from_next = lax.ppermute(edges[1], "dp", down)

    last = []
    last_moved = []
    for m in micros:
        outs = backs[m]
        made = kernel_call(
            project_back_body,
            [
                in_vmem(half_shape, low),
                in_vmem(half_shape, low),
                in_vmem((2, tok_local, head_cols), low),
                in_vmem((1, width), wide),
                in_vmem((1, width), wide),
            ],
            [pltpu.VMEM((routed_local, width), low)],
            (core_flag, outs[2], outs[3], outs[4], from_prev[m], from_next[m], outs[6], outs[10], rows_q[m])
            + (after(vectors, *held), w_in, query_row[m], normed_low[m]),
            scalars=1,
            managed=False,
            weight=8,
        )
        last.append(made)
        if m + 1 < micro_count:
            begun = mp_first(made[0], made[1])
            last_moved.append(mp_second(after(begun, *earlier)))
            held, earlier = (), (last_moved[m][1],)

    attn_rows = 3 * in_rows + 2 * out_rows * sides
    groups = []
    for m in micros:
        outs = backs[m]
        groups.append(
            (after(outs[2], *(moved[1] for moved in y_moved)), last[m][2], outs[6], outs[7], outs[8], attended[m][2], outs[0], attended[m][3], outs[9])
            + (normed_low[m], rows_q_low[m], key_normed[m])
        )
    if aligned:
        (pack_attn,) = kernel_call(
            attn_grads_body,
            [in_vmem((data_size, attn_rows + micro_count * routed_local, lane), low)],
            [
                pltpu.VMEM((width, micro_count * tok_local), low),
                pltpu.VMEM((width, micro_count * routed_all), low),
            ],
            sum(groups, ()),
            managed=True,
            weight=12,
        )
    else:
        totals = [0.0] * 8
        for m, group in enumerate(groups):
            grad_k = group[3].reshape(routed_all, -1)[:, :head_cols]
            pairs = (
                (normed_low[m], group[0]), (normed_low[m], group[1][0]), (normed_low[m], group[1][1]),
                (rows_q_low[m], group[2]), (key_normed[m], grad_k), (key_normed[m], group[4]),
                (group[5], group[6]), (group[7], group[8]),
            )
            totals = [total + tn(left, right) for total, (left, right) in zip(totals, pairs)]
        grad_in = jnp.stack(totals[:6]).astype(low)
        grad_out = jnp.stack(totals[6:]).astype(low)
        pack_attn = jnp.concatenate(
            [
                grad_in.reshape(3, 2, data_size, in_rows, head_cols)
                .transpose(2, 0, 3, 1, 4)
                .reshape(data_size, 3 * in_rows, lane),
                grad_out.reshape(2, data_size, out_rows, sides, lane)
                .transpose(1, 3, 0, 2, 4)
                .reshape(data_size, -1, lane),
            ]
            + [backs[m][7] for m in micros],
            axis=1,
        )
    sum_attn = lax.psum_scatter(
        after(pack_attn.reshape(-1, lane), sum_ffn), "dp", scatter_dimension=0, tiled=True
    )

    device_count = data_size * model_size

    def exchanged(blocks):
        return lax.all_to_all(blocks, ("dp", "mp"), 0, 0, tiled=True)

    place = jnp.stack([data_index, model_index]).astype(jnp.int32)

    def unpack_ffn(sources, grads):
        if len(sources) > 1:
            for source, grad in zip(sources, grads):
                grad[...] = source[...]
            return
        (ref,) = sources
        at = 0
        for grad, lead in zip(grads, (2, 0, 2, 0)):
            rows, cols = grad.shape[-2:]
            for l in range(max(lead, 1)):
                for j in range(cols // CHUNK):
                    value = ref[at : at + rows, :].astype(wide)
                    spot = slice(j * CHUNK, (j + 1) * CHUNK)
                    if lead:
                        grad[l, :, spot] = value
                    else:
                        grad[:, spot] = value
                    at = at + rows

    def unpack_attn(sources, grads):
        if len(sources) > 1:
            for source, grad in zip(sources, grads):
                grad[...] = source[...]
            return
        total = sources[0][: 3 * in_rows + 2 * out_rows * sides, :].astype(wide)
        for j in range(3):
            pair = total[j * in_rows : (j + 1) * in_rows]
            grads[0][2 * j] = pair[:, :head_cols]
            grads[0][2 * j + 1] = pair[:, head_cols:]
        for j in range(sides):
            at = 3 * in_rows + 2 * j * out_rows
            for m in range(2):
                grads[1][m, :, j * lane : (j + 1) * lane] = total[at + m * out_rows : at + (m + 1) * out_rows]

    def first_sums(matrices, unpack, sources, sums_shape, weights):
        n = len(weights)
        sums_out = kernel_call(
            functools.partial(sums_body, matrices, unpack, n),
            [in_vmem(w.shape, wide) for w in weights] + [in_vmem(sums_shape, wide)],
            [],
            tuple(sources) + tuple(weights),
            weight=4,
        )
        rows, cols = sums_shape
        sent = jnp.broadcast_to(sums_out[n].astype(low)[None], (device_count, rows, cols))
        got = lax.all_to_all(sent, ("dp", "mp"), 0, 0, tiled=True)
        return sums_out, got

    def optimize(matrices, sums_out, parts, weights, moments, moments_here, vectors_in):
        n = len(weights)
        grads = tuple(sums_out[:n])
        row_old, col_old, row_mine, col_mine = moments_here
        vector_count = len(vectors_in)
        made = kernel_call(
            functools.partial(moments_body, matrices, n, vector_count, data_size, model_size),
            [in_vmem(w.shape, wide) for w in weights]
            + [in_vmem(r.shape, wide) for r in row_old]
            + [in_vmem(c.shape, wide) for c in col_old]
            + [in_vmem(v[0].shape, wide) for v in vectors_in for _ in range(3)]
            + [in_vmem((device_count, 8, 128), wide)],
            [],
            (place, parts)
            + grads
            + tuple(row_old)
            + tuple(col_old)
            + tuple(row_mine)
            + tuple(col_mine)
            + sum(vectors_in, ()),
            scalars=1,
            weight=5,
        )
        updates, row_new, col_new = made[:n], made[n : 2 * n], made[2 * n : 3 * n]
        vector_made = made[3 * n : -1]
        counts = [
            weights[m.array].shape[-2] * weights[m.array].shape[-1] * device_count for m in matrices
        ] + [width for v in vectors_in for _ in range(v[0].shape[0])]
        all_weights = tuple(weights) + tuple(v[1] for v in vectors_in)

        def finish(aux):
            news = kernel_call(
                functools.partial(weights_body, matrices, counts, n, vector_count),
                [in_vmem(w.shape, wide) for w in all_weights],
                [],
                (aux,) + all_weights + tuple(updates) + tuple(vector_made[1::3]),
                weight=4,
            )
            results = []
            for array in range(n):
                rows, cols = moments[array]
                results.append(
                    [grads[array], row_new[array].reshape(rows.shape), col_new[array].reshape(cols.shape), news[array]]
                )
            for i in range(vector_count):
                results.append([vector_made[3 * i + 2], vector_made[3 * i], news[n + i]])
            return results

        return made[-1], finish

    if aligned:
        ffn_sources = (sum_ffn,)
    else:
        ffn_sources = []
        at = 0
        for weight, block, size in zip((light_in, light_out, heavy_in, heavy_out), blocks, block_rows):
            lead = weight.size // (weight.shape[-1] * weight.shape[-2])
            ffn_sources.append(
                unblocked(sum_ffn[at : at + size].reshape(block.shape), lead).reshape(weight.shape).astype(wide)
            )
            at = at + size
    ffn_made, ffn_parts = first_sums(
        ffn_list, unpack_ffn, ffn_sources, (8, SUM_LANES), ffn_weights
    )
    ffn_sums = ffn_made[-1]
    begun = mp_first(last[-1][0], last[-1][1], pack_attn)
    last_moved.append(mp_second(after(begun, ffn_sums, *earlier)))
    ffn_aux, ffn_finish = optimize(
        ffn_list,
        ffn_made,
        ffn_parts,
        ffn_weights,
        ffn_moments,
        ffn_here,
        (),
    )
    ffn_got = exchanged(ffn_aux)
    ffn_results = ffn_finish(ffn_got)

    key_half = (micro_count * routed_local // 2, width)
    chunks = tok_local // STREAM
    smem = pl.BlockSpec(memory_space=pltpu.SMEM)
    by_chunk = pl.BlockSpec((STREAM, width), lambda i: (i, 0))
    by_half = pl.BlockSpec((STREAM, width), lambda i: (i % (chunks // 2), 0))
    both_out = pl.BlockSpec((micro_count, STREAM, width), lambda i: (0, i, 0))

    def fixed(shape):
        return pl.BlockSpec(shape, lambda i: (0,) * len(shape))

    def streamed(body, in_specs, out_specs, outs, scratch, args, weight):
        return pl.pallas_call(
            functools.partial(body, chunks),
            grid=(chunks,),
            in_specs=in_specs,
            out_specs=out_specs,
            out_shape=outs,
            scratch_shapes=scratch,
            compiler_params=pltpu.CompilerParams(vmem_limit_bytes=VMEM_BYTES),
            cost_estimate=pl.CostEstimate(flops=weight * 1_150_000_000, bytes_accessed=1_000_000, transcendentals=0),
        )(*args)

    join_args = (core_flag,)
    for m in micros:
        join_args = join_args + (fed[m][0],) + mp_third(y_moved[m], pack_attn, ffn_sums)
    (mixed,) = streamed(
        join_body,
        [smem] + [by_chunk, by_half, by_half] * micro_count,
        [both_out],
        [in_vmem(tokens.shape, low)],
        [],
        join_args,
        6,
    )
    if aligned:
        attn_sources = ()
    else:
        own_sums = sum_attn[:attn_rows].astype(wide)
        attn_sources = (
            own_sums[: 3 * in_rows]
            .reshape(3, in_rows, 2, head_cols)
            .transpose(0, 2, 1, 3)
            .reshape(6, in_rows, head_cols),
            own_sums[3 * in_rows :]
            .reshape(sides, 2, out_rows, lane)
            .transpose(1, 2, 0, 3)
            .reshape(2, out_rows, width),
        )
    key_keep, key_send, grad_attn_in, grad_attn_out, sum_blocks = kernel_call(
        functools.partial(owners_body, micro_count, attn_list, unpack_attn),
        [
            in_vmem(key_half, low),
            in_vmem(key_half, low),
            in_vmem(attn_in.shape, wide),
            in_vmem(attn_out.shape, wide),
            in_vmem((device_count, 8, VECTORS_AT + 128), low),
        ],
        [
            pltpu.VMEM((routed_local, width), low),
            pltpu.VMEM((micro_count * routed_local, width), low),
            pltpu.VMEM((8, VECTORS_AT + 128), wide),
        ],
        (core_flag, sum_attn, after(vectors, mixed, ffn_results[0][3]), w_in)
        + tuple(rows_k)
        + tuple(last[m][4] for m in micros)
        + tuple(backs[m][1] for m in micros)
        + tuple(last[m][3] for m in micros)
        + tuple(fed[m][5] for m in micros)
        + attn_weights
        + attn_sources,
        scalars=1,
        weight=6,
    )
    attn_parts = exchanged(sum_blocks)
    key_begun = mp_first(key_keep, key_send)
    key_moved = mp_second(key_begun)
    pieces = mp_third(key_moved) + (after(vectors, ffn_aux),)
    for m in micros:
        pieces = pieces + mp_third(last_moved[m], ffn_sums if m + 1 < micro_count else ffn_aux)
        pieces = pieces + (backs[m][0], key_row[m])
    (grad_tokens,) = streamed(
        finish_body,
        [smem, fixed(key_half), fixed(key_half), fixed((8, width))]
        + [by_half, by_half, by_chunk, fixed((1, routed_local))] * micro_count
        + [both_out],
        [both_out],
        [in_vmem(tokens.shape, wide)],
        [pltpu.VMEM((micro_count * routed_local, width), low)],
        (core_flag,) + pieces + (tokens,),
        8,
    )
    attn_aux, attn_finish = optimize(
        attn_list,
        (grad_attn_in, grad_attn_out),
        attn_parts,
        attn_weights,
        attn_moments,
        attn_here,
        ((second_gains, gains), (second_router, router)),
    )
    attn_results = attn_finish(exchanged(attn_aux))
    results = [mixed, grad_tokens]
    for result in attn_results[:2] + ffn_results + attn_results[2:]:
        results.extend(result)
    return tuple(results)


def solution(mesh):
    placed = (
        P(None, "dp", None),
        P(None, "dp", None),
        P(),
        P(None, "dp"),
        P(),
        P(None, "dp"),
        P(None, "dp", "mp"),
        P(None, ("mp", "dp"), None),
        P(None, "dp", "mp"),
        P(("mp", "dp"), None),
        P(None, "dp", "mp"),
        P(("mp", "dp"), None),
        P(None, "dp"),
        P(None, "dp"),
        P(),
        P(),
        P(),
        P(),
        P(),
        P(),
        P(),
        P(),
        P(),
        P(),
        P(),
        P(),
        P(None, "dp"),
        P(None, "dp"),
    )
    return jax.shard_map(
        shards,
        mesh=mesh,
        in_specs=placed,
        out_specs=(
            P(None, "dp", None),
            P(None, "dp", None),
            P(None, "dp", "mp"),
            P(),
            P(),
            P(None, "dp", "mp"),
            P(None, ("mp", "dp"), None),
            P(),
            P(),
            P(None, ("mp", "dp"), None),
            P(None, "dp", "mp"),
            P(),
            P(),
            P(None, "dp", "mp"),
            P(("mp", "dp"), None),
            P(),
            P(),
            P(("mp", "dp"), None),
            P(None, "dp", "mp"),
            P(),
            P(),
            P(None, "dp", "mp"),
            P(("mp", "dp"), None),
            P(),
            P(),
            P(("mp", "dp"), None),
            P(None, "dp"),
            P(None, "dp"),
            P(None, "dp"),
            P(None, "dp"),
            P(None, "dp"),
            P(None, "dp"),
        ),
        check_vma=False,
    )
```

```python
import functools
import math

import jax
import jax.numpy as jnp
from jax import lax
from jax.experimental import pallas as pl
from jax.experimental.pallas import tpu as pltpu
from jax.sharding import PartitionSpec as P

D = 768
LH = 8
LDH = 96
HH = 12
HDH = 64
WIN = 128
STEP = 10

norm_eps = 1e-06
tiny_square = 1e-30
scale_floor = 0.001
clip_level = 1.0
step_rate = 0.5
masked_score = -1e30
gelu_scale = math.sqrt(2.0 / math.pi)
gelu_cubic = 0.044715

low = jnp.bfloat16
wide = jnp.float32
CHUNK = 256
BLOCK = 128
RADIUS = WIN // 2
KEYS = 1024
VECTORS_AT = 512
SUM_LANES = 640
STREAM = 256
VMEM_BYTES = 60 * 1024 * 1024
LARGE = 200 * 1024


def nn(left, right):
    return lax.dot_general(left, right, (((1,), (0,)), ((), ())), preferred_element_type=wide)


def nt(left, right):
    return lax.dot_general(left, right, (((1,), (1,)), ((), ())), preferred_element_type=wide)


def tn(left, right):
    return lax.dot_general(left, right, (((0,), (0,)), ((), ())), preferred_element_type=wide)


def sigmoid(logit):
    return 1.0 / (1.0 + jnp.exp(-logit))


def gelu_pair(gate):
    squared = gate * gate
    bent = jnp.tanh(gelu_scale * gate * (1.0 + gelu_cubic * squared))
    half = 0.5 * (1.0 + bent)
    value = gate * half
    slope = half + 0.5 * gate * (1.0 - bent * bent) * gelu_scale * (1.0 + 3.0 * gelu_cubic * squared)
    return value, slope


def picks_rows(idx_col, count):
    spots = lax.broadcasted_iota(jnp.int32, (idx_col.shape[0], count), 1)
    return (spots == idx_col).astype(low)


def picks_cols(idx_row, start, count):
    spots = lax.broadcasted_iota(jnp.int32, (count, idx_row.shape[1]), 0) + start
    return (spots == idx_row).astype(low)


def head_mask(width, size, head):
    spot = lax.broadcasted_iota(jnp.int32, (1, width), 1)
    return ((spot >= head * size) & (spot < (head + 1) * size)).astype(low)


def softmax_parts(scores, allowed):
    masked = jnp.where(allowed, scores, masked_score)
    top = jnp.max(masked, axis=-1, keepdims=True)
    grown = jnp.exp(masked - top)
    return grown * (1.0 / jnp.sum(grown, axis=-1, keepdims=True))


def inverse_rms(values):
    return lax.rsqrt(jnp.mean(values * values, axis=-1, keepdims=True) + norm_eps)


def norm_back(values, gain_row, upstream):
    inverse = inverse_rms(values)
    unit = values * inverse
    scaled = upstream * gain_row
    pulled = inverse * (scaled - unit * jnp.mean(scaled * unit, axis=-1, keepdims=True))
    return pulled, jnp.sum(upstream * unit, axis=0, keepdims=True)


def in_vmem(shape, dtype):
    return jax.ShapeDtypeStruct(shape, dtype)


def vmem_bytes(shape, dtype):
    size = jnp.dtype(dtype).itemsize
    shape = (1,) * (2 - len(shape)) + tuple(shape)
    rows, cols = -(-shape[-2] // (32 // size)) * (32 // size), -(-shape[-1] // 128) * 128
    return math.prod(shape[:-2]) * rows * cols * size


class Transfers:
    def __init__(self, ins, outs, sems):
        self.ins = {id(held): (far, held) for far, held in ins}
        self.outs = {id(held): (far, held) for far, held in outs}
        self.sems, self.used = sems, 0
        self.begun, self.finished, self.going = {}, set(), []

    def copy(self, source, target):
        made = pltpu.make_async_copy(source, target, self.sems.at[self.used])
        self.used += 1
        made.start()
        return made

    def begin(self, *refs):
        for ref in refs:
            if id(ref) in self.ins and id(ref) not in self.begun:
                self.begun[id(ref)] = self.copy(*self.ins[id(ref)])

    def need(self, *refs):
        self.begin(*refs)
        for ref in refs:
            if id(ref) in self.ins and id(ref) not in self.finished:
                self.begun[id(ref)].wait()
                self.finished.add(id(ref))

    def done(self, ref, part=None):
        if id(ref) not in self.outs:
            return
        far, held = self.outs[id(ref)]
        self.finished.add(id(ref))
        if part is None:
            self.going.append(self.copy(held, far))
        else:
            self.going.append(self.copy(held.at[part], far.at[part]))

    def close(self):
        for far, held in self.ins.values():
            self.need(held)
        for far, held in self.outs.values():
            if id(held) not in self.finished:
                self.done(held)
        for made in self.going:
            made.wait()


class Pick:
    def __init__(self, array, index):
        self.array, self.index = array, index
        self.shape, self.dtype = array.shape[1:], array.dtype


def kernel_call(body, outs, scratch, args, scalars=0, weight=10, managed=False, parts=4):
    vmem = pl.BlockSpec(memory_space=pltpu.VMEM)
    smem = pl.BlockSpec(memory_space=pltpu.SMEM)
    far = pl.BlockSpec(memory_space=pl.ANY)

    def large(x):
        return managed and vmem_bytes(x.shape, x.dtype) >= LARGE

    picked = {i: arg.index for i, arg in enumerate(args) if isinstance(arg, Pick)}
    ins = [i for i in range(scalars, len(args)) if large(args[i])]
    assert all(i in ins for i in picked)
    ends = [i for i in range(len(outs)) if large(outs[i])]
    held = [pltpu.VMEM(args[i].shape, args[i].dtype) for i in ins]
    held = held + [pltpu.VMEM(outs[i].shape, outs[i].dtype) for i in ends]
    sems = [pltpu.SemaphoreType.DMA((len(held) + parts,))] if managed else []

    def run(*refs):
        refs = list(refs)
        count = len(args) + len(outs)
        operands, results = refs[: len(args)], refs[len(args) : count]
        kept = refs[count : count + len(held)]
        rest = refs[count + len(held) :]
        if managed:
            rest, sem = rest[:-1], rest[-1]
            pairs_in, pairs_out = [], []
            for i, ref in zip(ins, kept):
                pairs_in.append((operands[i].at[picked[i]] if i in picked else operands[i], ref))
                operands[i] = ref
            for i, ref in zip(ends, kept[len(ins) :]):
                pairs_out.append((results[i], ref))
                results[i] = ref
            moves = Transfers(pairs_in, pairs_out, sem)
            body(moves, *operands, *results, *rest)
            moves.close()
        else:
            body(*operands, *results, *rest)

    return pl.pallas_call(
        run,
        out_shape=outs,
        in_specs=[smem] * scalars + [far if large(x) else vmem for x in args[scalars:]],
        out_specs=[far if large(x) else vmem for x in outs],
        scratch_shapes=held + list(scratch) + sems,
        compiler_params=pltpu.CompilerParams(vmem_limit_bytes=VMEM_BYTES),
        cost_estimate=pl.CostEstimate(
            flops=weight * 1_150_000_000, bytes_accessed=1_000_000, transcendentals=0
        ),
    )(*(arg.array if isinstance(arg, Pick) else arg for arg in args))


def mp_total(core, mine_ref, other_ref, chunk, per_half, size=CHUNK):
    rows = pl.ds(pl.multiple_of((chunk % per_half) * size, size), size)
    flag = ((chunk // per_half) == core).astype(wide)
    return mine_ref[rows, :].astype(wide) * flag + other_ref[rows, :].astype(wide) * (1.0 - flag)


def mp_store(core, keep_ref, send_ref, chunk, per_half, size, value):
    rows = pl.ds(pl.multiple_of((chunk % per_half) * size, size), size)
    kept = (chunk // per_half) == core

    @pl.when(kept)
    def _():
        keep_ref[rows, :] = value

    @pl.when(jnp.logical_not(kept))
    def _():
        send_ref[rows, :] = value


def pack_body(in_ref, out_ref, gain_ref, route_ref, pack_ref):
    in_rows = in_ref.shape[1]
    lane = pack_ref.shape[1]
    for j in range(3):
        pair = jnp.concatenate([in_ref[2 * j], in_ref[2 * j + 1]], axis=1)
        pack_ref[j * in_rows : (j + 1) * in_rows, :] = pair.astype(low)
    both = jnp.concatenate([out_ref[0], out_ref[1]], axis=0).astype(low)
    base = 3 * in_rows
    for j in range(out_ref.shape[2] // lane):
        pack_ref[base : base + both.shape[0], :] = both[:, j * lane : (j + 1) * lane]
        base = base + both.shape[0]
    rows = jnp.concatenate([gain_ref[...], route_ref[...]], axis=0)
    rows = jnp.concatenate([rows, jnp.zeros((16 - rows.shape[0], in_rows), wide)], axis=0)
    rows = jnp.concatenate([rows, jnp.zeros((16, lane - in_rows), wide)], axis=1)
    pack_ref[base : base + 16, :] = rows.astype(low)


def unpack_body(got_ref, w_in_ref, w_out_ref, vec_ref):
    count, _, lane = got_ref.shape
    in_rows = w_in_ref.shape[1] // count
    head_cols = w_in_ref.shape[2]
    for j in range(3):
        pair = got_ref[:, j * in_rows : (j + 1) * in_rows, :].reshape(count * in_rows, lane)
        w_in_ref[2 * j] = pair[:, :head_cols]
        w_in_ref[2 * j + 1] = pair[:, head_cols:]
    base = 3 * in_rows
    out_rows = w_out_ref.shape[1] // count
    sides = w_out_ref.shape[2] // lane
    for j in range(sides):
        cols = slice(j * lane, (j + 1) * lane)
        blocks = [
            got_ref[d, base + j * 2 * out_rows : base + (j + 1) * 2 * out_rows, :].astype(wide)
            for d in range(count)
        ]
        for s in range(2):
            w_out_ref[s, :, cols] = jnp.concatenate(
                [b[s * out_rows : (s + 1) * out_rows] for b in blocks], axis=0
            ).astype(low)
    base = base + 2 * out_rows * sides
    vec_ref[...] = jnp.concatenate(
        [got_ref[d, base : base + 16, :].astype(wide)[:8, :in_rows] for d in range(count)], axis=1
    )


def block_of(ref, base, index, full):
    count = ref.shape[0]
    rows = full // count
    return ref[:, row_span(base // count + index * rows, rows), :].reshape(full, CHUNK)


def row_span(start, size):
    if isinstance(start, int):
        return slice(start, start + size)
    return pl.ds(pl.multiple_of(start, math.gcd(size, 128)), size)


def col_span(index):
    return pl.ds(pl.multiple_of(index * CHUNK, CHUNK), CHUNK)


def part_of(ref, base, index, full, piece):
    count = ref.shape[0]
    rows = full // count
    at = base // count + index * rows
    if rows <= CHUNK:
        span = CHUNK // rows
        return ref[pl.ds(piece * span, span), at : at + rows, :].reshape(CHUNK, CHUNK)
    return ref[0, row_span(at + piece * CHUNK, CHUNK), :]


def ffn_bases(width, light, heavy):
    sides = width // CHUNK
    light_in = 2 * (light // CHUNK) * width
    light_out = sides * light
    heavy_in = 2 * (heavy // CHUNK) * width
    bases = [0, light_in, light_in + light_out, light_in + light_out + heavy_in]
    return bases, bases[3] + sides * heavy


def project_body(moves, vec_ref, w_ref, *refs):
    low_ref = refs[-1]
    micros = (len(refs) - 1) // 12
    inputs, outputs = refs[: 3 * micros], refs[3 * micros : -1]
    for m in range(micros):
        moves.begin(inputs[3 * m])
        moves.begin(w_ref)
    for m in range(micros):
        tok_ref, qcol_ref, kcol_ref = inputs[3 * m : 3 * m + 3]
        n1b_ref, q_ref, k_ref, v_ref, hq_ref, sq_ref, nq_ref, nk_ref, qrows_ref = outputs[9 * m : 9 * m + 9]
        count = tok_ref.shape[0]
        moves.need(tok_ref, w_ref)

        def step(c, carry):
            rows = pl.ds(pl.multiple_of(c * CHUNK, CHUNK), CHUNK)
            values = tok_ref[rows, :].astype(wide)
            normed = values * inverse_rms(values) * vec_ref[0:1, :]
            high = normed.astype(low)
            n1b_ref[rows, :] = high
            low_ref[rows, :] = (normed - high.astype(wide)).astype(low)
            q_ref[rows, :] = nn(high, w_ref[0]).astype(low)
            k_ref[rows, :] = nn(high, w_ref[1]).astype(low)
            v_ref[rows, :] = nn(high, w_ref[2]).astype(low)
            return carry

        lax.fori_loop(0, count // CHUNK, step, 0)
        for ref in (k_ref, v_ref, q_ref, n1b_ref):
            moves.done(ref)
        picks = picks_rows(qcol_ref[...], count)
        query_rows = nn(picks, n1b_ref[...])
        query_wide = query_rows + nn(picks, low_ref[...])
        qrows_ref[...] = query_rows.astype(low)
        nq_ref[...] = query_wide
        hq_ref[...] = nn(query_rows.astype(low), w_ref[3]).astype(low)
        sq_ref[...] = sigmoid(jnp.sum(query_wide * vec_ref[2:3, :], axis=-1, keepdims=True))
        picks = picks_rows(kcol_ref[...], count)
        nk_ref[...] = nn(picks, n1b_ref[...]) + nn(picks, low_ref[...])
        for ref in (qrows_ref, nq_ref, nk_ref):
            moves.done(ref)


def keys_body(o_ref, a_ref, b_ref, c_ref, vec_ref, w_ref, *outs):
    blocks, micros, part, width = o_ref.shape
    for m in range(micros):
        n_ref, k_ref, v_ref, sk_ref = outs[4 * m : 4 * m + 4]
        for p, ref in enumerate((o_ref, a_ref, b_ref, c_ref)):
            values = ref[:, m].reshape(blocks * part, width).astype(wide)
            normed = values * inverse_rms(values) * vec_ref[0:1, :]
            high = normed.astype(low)
            score = sigmoid(jnp.sum(normed * vec_ref[3:4, :], axis=-1, keepdims=True))
            n_ref[:, p] = high.reshape(blocks, part, width)
            sk_ref[:, p] = score.reshape(blocks, part, 1)
            k_ref[:, p] = nn(high, w_ref[4]).astype(low).reshape(blocks, part, -1)
            v_ref[:, p] = (nn(high, w_ref[5]) * score).astype(low).reshape(blocks, part, -1)


def fill_extended(ext_ref, prev, inner, after):
    count = inner.shape[0]
    ext_ref[0:RADIUS, :] = prev
    ext_ref[RADIUS : RADIUS + count, :] = inner
    ext_ref[RADIUS + count :, :] = after


def near_mask(seg_q, seg_k):
    shape = (BLOCK, 2 * BLOCK)
    gap = lax.broadcasted_iota(jnp.int32, shape, 1) - lax.broadcasted_iota(jnp.int32, shape, 0)
    return (gap >= 0) & (gap <= 2 * RADIUS) & (seg_q == seg_k)


def attend_body(
    core_ref, q_ref, k_ref, v_ref, prev_ref, after_ref, hq_ref, hk_ref, hv_ref, sq_ref, wo_ref,
    qrow_ref, segq_ref, segk_ref, hsegq_ref, hsegk_ref,
    keep_ref, send_ref, lmix_ref, hmix_ref, hproj_ref,
    kx_ref, vx_ref, rows_ref,
):
    count, width = q_ref.shape
    light_heads = width // LDH
    heavy_heads = width // HDH
    allowed = hsegq_ref[...] == hsegk_ref[...]
    mix = jnp.zeros((hq_ref.shape[0], width), wide)
    for h in range(heavy_heads):
        mask = head_mask(width, HDH, h)
        probs = softmax_parts(nt(hq_ref[...], hk_ref[...] * mask) * (1.0 / math.sqrt(HDH)), allowed)
        mix = mix + nn(probs.astype(low), hv_ref[...] * mask)
    mix_low = mix.astype(low)
    hmix_ref[...] = mix_low
    proj = nn(mix_low, wo_ref[1])
    hproj_ref[...] = proj
    rows_ref[...] = (sq_ref[...] * proj).astype(low)
    fill_extended(kx_ref, prev_ref[0], k_ref[...], after_ref[0])
    fill_extended(vx_ref, prev_ref[1], v_ref[...], after_ref[1])

    def step(b, carry):
        rows = pl.ds(pl.multiple_of(b * BLOCK, BLOCK), BLOCK)
        keys = pl.ds(pl.multiple_of(b * BLOCK, BLOCK), 2 * BLOCK)
        seg_k = jnp.concatenate([segk_ref[b], segk_ref[b + 1]], axis=1)
        near = near_mask(segq_ref[rows, :], seg_k)
        queries = q_ref[rows, :]
        block_keys = kx_ref[keys, :]
        block_values = vx_ref[keys, :]
        total = jnp.zeros((BLOCK, width), wide)
        for h in range(light_heads):
            mask = head_mask(width, LDH, h)
            probs = softmax_parts(nt(queries, block_keys * mask) * (1.0 / math.sqrt(LDH)), near)
            total = total + nn(probs.astype(low), block_values * mask)
        total_low = total.astype(low)
        lmix_ref[rows, :] = total_low
        spread = picks_cols(qrow_ref[...], b * BLOCK, BLOCK)
        part = (nn(total_low, wo_ref[0]) + nn(spread, rows_ref[...])).astype(low)
        mp_store(core_ref[0], keep_ref, send_ref, b, count // BLOCK // 2, BLOCK, part)
        return carry

    lax.fori_loop(0, count // BLOCK, step, 0)


def ffn_body(last, *refs):
    moves, core_ref, mine_ref, other_ref, tok_ref, cot_ref, vec_ref, fcol_ref, frow_ref, w_ref = refs[:10]
    low_ref, out_rows_ref, grad_rows_ref = refs[-3:]
    if last:
        earlier = [refs[10 + 8 * m : 18 + 8 * m] for m in range(last)]
        middle_ref, ykeep_ref, ysend_ref, gkeep_ref, gsend_ref, router_ref, pack_ref = refs[10 + 8 * last : 17 + 8 * last]
        own = refs[17 + 8 * last : 24 + 8 * last]
        turned_ref, turned_rows_ref = refs[24 + 8 * last : 26 + 8 * last]
    else:
        earlier = []
        middle_ref, ykeep_ref, ysend_ref, gkeep_ref, gsend_ref, router_ref = refs[10:16]
        own = refs[16:23]
    n2b_ref, hidden_ref, dgu_ref, frows_ref, hhid_ref, dhgu_ref, dhout_ref = own
    count, width = tok_ref.shape
    chunks = count // CHUNK
    core = core_ref[0]
    light = hidden_ref.shape[1]
    heavy = hhid_ref.shape[1]
    sides = width // CHUNK
    bases, _ = ffn_bases(width, light, heavy)
    moves.begin(mine_ref, other_ref, tok_ref)
    moves.begin(w_ref, cot_ref)
    for group in earlier:
        moves.begin(*group)
    moves.need(mine_ref, other_ref, tok_ref)

    def heavy_in(s, j):
        return block_of(w_ref, bases[2], s * (heavy // CHUNK) + j, width)

    def heavy_out(t, j):
        return part_of(w_ref, bases[3], t, heavy, j)

    def light_in(s):
        return block_of(w_ref, bases[0], s, width)

    def light_out(t):
        return block_of(w_ref, bases[1], t, light)

    def enter(c, carry):
        rows = pl.ds(pl.multiple_of(c * CHUNK, CHUNK), CHUNK)
        middle = tok_ref[rows, :].astype(wide) + mp_total(core, mine_ref, other_ref, c, chunks // 2)
        middle_ref[rows, :] = middle.astype(low)
        normed = middle * inverse_rms(middle) * vec_ref[1:2, :]
        high = normed.astype(low)
        n2b_ref[rows, :] = high
        low_ref[rows, :] = (normed - high.astype(wide)).astype(low)
        return carry

    lax.fori_loop(0, chunks, enter, 0)
    moves.done(middle_ref)
    moves.done(n2b_ref)
    moves.need(w_ref, cot_ref)
    picks = picks_rows(fcol_ref[...], count)
    rows_high = nn(picks, n2b_ref[...])
    rows_wide = rows_high + nn(picks, low_ref[...])
    rows_low = rows_high.astype(low)
    frows_ref[...] = rows_low
    score = sigmoid(jnp.sum(rows_wide * vec_ref[4:5, :], axis=-1, keepdims=True))
    cot_rows = nn(picks, cot_ref[...])
    grad_out = (score * cot_rows).astype(low)
    dhout_ref[...] = grad_out
    out_rows = [jnp.zeros((rows_low.shape[0], CHUNK), wide) for _ in range(sides)]
    grad_rows = jnp.zeros(rows_low.shape, wide)
    for j in range(heavy // CHUNK):
        cols = slice(j * CHUNK, (j + 1) * CHUNK)
        gate = nn(rows_low, heavy_in(0, j))
        up = nn(rows_low, heavy_in(1, j))
        value, slope = gelu_pair(gate)
        hid = (value * up).astype(low)
        hhid_ref[:, cols] = hid
        grad_hid = jnp.zeros_like(gate)
        for t in range(sides):
            piece = heavy_out(t, j)
            out_rows[t] = out_rows[t] + nn(hid, piece)
            grad_hid = grad_hid + nt(grad_out[:, t * CHUNK : (t + 1) * CHUNK], piece)
        grad_gate = (grad_hid * up * slope).astype(low)
        grad_up = (grad_hid * value).astype(low)
        dhgu_ref[0, :, cols] = grad_gate
        dhgu_ref[1, :, cols] = grad_up
        grad_rows = grad_rows + nt(grad_gate, heavy_in(0, j)) + nt(grad_up, heavy_in(1, j))
    out_rows = jnp.concatenate(out_rows, axis=1)
    logit = jnp.sum(cot_rows * out_rows, axis=-1, keepdims=True) * score * (1.0 - score)
    router_ref[...] = jnp.sum(logit * rows_wide, axis=0, keepdims=True)
    out_rows_ref[...] = (score * out_rows).astype(low)
    grad_rows_ref[...] = (grad_rows + logit * vec_ref[4:5, :]).astype(low)
    for ref in (frows_ref, hhid_ref, dhgu_ref, dhout_ref):
        moves.done(ref)

    def light_rows(c, carry):
        rows = pl.ds(pl.multiple_of(c * CHUNK, CHUNK), CHUNK)
        normed = n2b_ref[rows, :]
        gate = nn(normed, light_in(0))
        up = nn(normed, light_in(1))
        value, slope = gelu_pair(gate)
        hid = (value * up).astype(low)
        hidden_ref[rows, :] = hid
        spread = picks_cols(frow_ref[...], c * CHUNK, CHUNK)
        spread_out = nn(spread, out_rows_ref[...])
        grad_hid = jnp.zeros_like(gate)
        outs = []
        for t in range(sides):
            cols = slice(t * CHUNK, (t + 1) * CHUNK)
            outs.append((nn(hid, light_out(t)) + spread_out[:, cols]).astype(low))
            grad_hid = grad_hid + nt(cot_ref[rows, cols], light_out(t))
        grad_gate = (grad_hid * up * slope).astype(low)
        grad_up = (grad_hid * value).astype(low)
        dgu_ref[0, rows, :] = grad_gate
        dgu_ref[1, rows, :] = grad_up
        grad = nt(grad_gate, light_in(0)) + nt(grad_up, light_in(1)) + nn(spread, grad_rows_ref[...])
        mp_store(core, ykeep_ref, ysend_ref, c, chunks // 2, CHUNK, jnp.concatenate(outs, axis=1))
        mp_store(core, gkeep_ref, gsend_ref, c, chunks // 2, CHUNK, grad.astype(low))
        return carry

    lax.fori_loop(0, chunks, light_rows, 0)
    for ref in (gsend_ref, gkeep_ref, ysend_ref, ykeep_ref):
        moves.done(ref)
    if not last:
        return

    split = pack_ref.shape[0]

    def put(base, index, value):
        rows = value.shape[0] // split
        at = base // split + index * rows
        pack_ref[:, at : at + rows, :] = value.astype(low).reshape(split, rows, CHUNK)

    def sent(base, end):
        moves.done(pack_ref, (slice(None), slice(base // split, end // split)))

    for group in earlier:
        moves.need(*group)
    groups = earlier + [own + (cot_ref,)]
    routed = frows_ref.shape[0]
    for m, group in enumerate(groups):
        turned_ref[:, m * count : (m + 1) * count] = group[0][...].T
        turned_rows_ref[:, m * routed : (m + 1) * routed] = group[3][...].T
    pieces = heavy // CHUNK
    for s in range(2):
        for j in range(pieces):
            total = jnp.zeros((width, CHUNK), wide)
            for m, group in enumerate(groups):
                total = total + nn(
                    turned_rows_ref[:, m * routed : (m + 1) * routed],
                    group[5][s, :, j * CHUNK : (j + 1) * CHUNK],
                )
            put(bases[2], s * pieces + j, total)
    sent(bases[2], bases[3])
    for t in range(sides):
        cols = slice(t * CHUNK, (t + 1) * CHUNK)
        total = jnp.zeros((heavy, CHUNK), wide)
        for group in groups:
            total = total + tn(group[4][...], group[6][:, cols])
        put(bases[3], t, total)
    sent(bases[3], split * pack_ref.shape[1])
    for s in range(2):
        total = jnp.zeros((width, CHUNK), wide)
        for m, group in enumerate(groups):
            total = total + nn(turned_ref[:, m * count : (m + 1) * count], group[2][s])
        put(bases[0], s, total)
    total = jnp.zeros((light, width), wide)
    for group in groups:
        total = total + tn(group[1][...], group[7][...])
    for t in range(sides):
        put(bases[1], t, total[:, t * CHUNK : (t + 1) * CHUNK])
    sent(0, bases[2])


def attend_back_body(
    mine, moves, core_ref, mine_ref, other_ref, middle_ref, cot_ref, vec_ref,
    q_ref, k_ref, v_ref, prev_ref, after_ref, hq_ref, hk_ref, hv_ref, sk_ref, sq_ref, hproj_ref, wo_ref,
    qcol_ref, segq_ref, segk_ref, hsegq_ref, hsegk_ref, earlier_edges_ref,
    agl_ref, gain_ref, dq_ref, inner_ref, rims_ref, edges_ref, dhq_ref, spread_ref, draw_ref,
    dproj_ref, logit_ref,
    kx_ref, vx_ref, dmix_ref, dkx_ref, dvx_ref, dk_ref, dv_ref,
):
    count, width = q_ref.shape
    chunks = count // CHUNK
    light_heads = width // LDH
    heavy_heads = width // HDH
    core = core_ref[0]
    moves.begin(mine_ref, other_ref, middle_ref, cot_ref, wo_ref)
    moves.begin(hk_ref, hv_ref, sk_ref, hproj_ref, k_ref, v_ref, q_ref, segq_ref)
    moves.need(mine_ref, other_ref, middle_ref, cot_ref, wo_ref)
    gain_ref[...] = jnp.zeros_like(gain_ref)

    def enter(c, carry):
        rows = pl.ds(pl.multiple_of(c * CHUNK, CHUNK), CHUNK)
        upstream = mp_total(core, mine_ref, other_ref, c, chunks // 2)
        pulled, gain = norm_back(middle_ref[rows, :].astype(wide), vec_ref[1:2, :], upstream)
        gain_ref[...] += gain
        grad_low = (cot_ref[rows, :].astype(wide) + pulled).astype(low)
        agl_ref[rows, :] = grad_low
        dmix_ref[rows, :] = nt(grad_low, wo_ref[0]).astype(low)
        return carry

    lax.fori_loop(0, chunks, enter, 0)

    moves.done(agl_ref)
    moves.need(hk_ref, hv_ref, sk_ref, hproj_ref)
    picks = picks_rows(qcol_ref[...], count)
    grad_rows = nn(picks, agl_ref[...])
    score = sq_ref[...]
    dproj = (score * grad_rows).astype(low)
    dproj_ref[...] = dproj
    logit_ref[...] = (
        jnp.sum(grad_rows * hproj_ref[...], axis=-1, keepdims=True) * score * (1.0 - score)
    )
    dmix = nt(dproj, wo_ref[1]).astype(low)
    scale = 1.0 / math.sqrt(HDH)
    key_count = hk_ref.shape[0]
    if key_count <= KEYS:
        dk_ref[...] = jnp.zeros_like(dk_ref)
        dv_ref[...] = jnp.zeros_like(dv_ref)

        def one_head(h, dq):
            allowed = hsegq_ref[...] == hsegk_ref[...]
            mask = head_mask(width, HDH, h)
            keys = hk_ref[...] * mask
            probs = softmax_parts(nt(hq_ref[...], keys) * scale, allowed)
            grad_soft = nt(dmix, hv_ref[...] * mask)
            centre = jnp.sum(probs * grad_soft, axis=-1, keepdims=True)
            grad_scores = (probs * (grad_soft - centre)).astype(low)
            dk_ref[...] += tn(grad_scores, hq_ref[...] * mask)
            dv_ref[...] += tn(probs.astype(low), dmix * mask)
            return dq + nn(grad_scores, keys)

        dq = lax.fori_loop(0, heavy_heads, one_head, jnp.zeros((hq_ref.shape[0], width), wide))
        dk, dv = dk_ref[...], dv_ref[...]
        both = jnp.concatenate([(dk * scale).astype(low), dv.astype(low)], axis=1)
        spread_ref[...] = both.reshape(spread_ref.shape)
        draw_ref[...] = (dv * sk_ref[...]).astype(low)
    else:
        pieces = key_count // KEYS

        def piece_of(c, mask):
            spots = pl.ds(pl.multiple_of(c * KEYS, KEYS), KEYS)
            allowed = hsegq_ref[...] == hsegk_ref[:, spots]
            keys = hk_ref[spots, :] * mask
            scores = jnp.where(allowed, nt(hq_ref[...], keys) * scale, masked_score)
            return spots, keys, scores, nt(dmix, hv_ref[spots, :] * mask)

        blank = jnp.zeros((hq_ref.shape[0], 1), wide)
        stats = []
        for h in range(heavy_heads):
            mask = head_mask(width, HDH, h)

            def find_top(c, top):
                return jnp.maximum(top, jnp.max(piece_of(c, mask)[2], axis=-1, keepdims=True))

            top = lax.fori_loop(0, pieces, find_top, blank + masked_score)

            def add_up(c, sums):
                _, _, scores, grad_soft = piece_of(c, mask)
                grown = jnp.exp(scores - top)
                return (
                    sums[0] + jnp.sum(grown, axis=-1, keepdims=True),
                    sums[1] + jnp.sum(grown * grad_soft, axis=-1, keepdims=True),
                )

            total, moment = lax.fori_loop(0, pieces, add_up, (blank, blank))
            stats.append((mask, top, 1.0 / total, moment / total))

        def pull(c, dq):
            dk = jnp.zeros((KEYS, width), wide)
            dv = jnp.zeros((KEYS, width), wide)
            for mask, top, inverse, centre in stats:
                spots, keys, scores, grad_soft = piece_of(c, mask)
                probs = jnp.exp(scores - top) * inverse
                grad_scores = (probs * (grad_soft - centre)).astype(low)
                dq = dq + nn(grad_scores, keys)
                dk = dk + tn(grad_scores, hq_ref[...] * mask)
                dv = dv + tn(probs.astype(low), dmix * mask)
            owners = KEYS // spread_ref.shape[1]
            both = jnp.concatenate([(dk * scale).astype(low), dv.astype(low)], axis=1)
            spread_ref[pl.ds(c * owners, owners)] = both.reshape((owners,) + spread_ref.shape[1:])
            draw_ref[spots, :] = (dv * sk_ref[spots, :]).astype(low)
            return dq

        dq = lax.fori_loop(0, pieces, pull, jnp.zeros((hq_ref.shape[0], width), wide))
    dhq_ref[...] = (dq * scale).astype(low)
    moves.need(k_ref, v_ref, q_ref, segq_ref)
    if mine > 0:
        edges_ref[:, :mine] = earlier_edges_ref[...]
    for ref in (spread_ref, draw_ref, dproj_ref):
        moves.done(ref)
    fill_extended(kx_ref, prev_ref[0], k_ref[...], after_ref[0])
    fill_extended(vx_ref, prev_ref[1], v_ref[...], after_ref[1])
    dkx_ref[...] = jnp.zeros_like(dkx_ref)
    dvx_ref[...] = jnp.zeros_like(dvx_ref)
    light_scale = 1.0 / math.sqrt(LDH)

    def step(b, carry):
        rows = pl.ds(pl.multiple_of(b * BLOCK, BLOCK), BLOCK)
        spans = pl.ds(pl.multiple_of(b * BLOCK, BLOCK), 2 * BLOCK)
        seg_k = jnp.concatenate([segk_ref[b], segk_ref[b + 1]], axis=1)
        near = near_mask(segq_ref[rows, :], seg_k)
        queries = q_ref[rows, :]
        block_keys = kx_ref[spans, :]
        block_values = vx_ref[spans, :]
        mix = dmix_ref[rows, :]
        grad_q = jnp.zeros((BLOCK, width), wide)
        grad_k = jnp.zeros((2 * BLOCK, width), wide)
        grad_v = jnp.zeros((2 * BLOCK, width), wide)
        for h in range(light_heads):
            mask = head_mask(width, LDH, h)
            keys = block_keys * mask
            probs = softmax_parts(nt(queries, keys) * light_scale, near)
            grad_soft = nt(mix, block_values * mask)
            centre = jnp.sum(probs * grad_soft, axis=-1, keepdims=True)
            grad_scores = (probs * (grad_soft - centre)).astype(low)
            grad_q = grad_q + nn(grad_scores, keys)
            grad_k = grad_k + tn(grad_scores, queries * mask)
            grad_v = grad_v + tn(probs.astype(low), mix * mask)
        dq_ref[rows, :] = (grad_q * light_scale).astype(low)
        dkx_ref[spans, :] += grad_k * light_scale
        dvx_ref[spans, :] += grad_v
        return carry

    lax.fori_loop(0, count // BLOCK, step, 0)
    for s, ref in enumerate((dkx_ref, dvx_ref)):
        inner_ref[s] = ref[RADIUS : RADIUS + count, :].astype(low)
        rims_ref[s, :RADIUS, :] = ref[RADIUS : 2 * RADIUS, :]
        rims_ref[s, RADIUS:, :] = ref[count : RADIUS + count, :]
        edges_ref[0, mine, s] = ref[RADIUS + count :, :].astype(low)
        edges_ref[1, mine, s] = ref[:RADIUS, :].astype(low)


def project_back_body(
    core_ref, dq_ref, inner_ref, rims_ref, prev_ref, after_ref, dhq_ref, logit_ref, nq_ref, vec_ref, w_ref, qrow_ref,
    normed_ref,
    keep_ref, send_ref, dkv_ref, router_ref, gain_ref,
    rows_ref,
):
    count, width = dq_ref.shape
    for s in range(2):
        dkv_ref[s, RADIUS : count - RADIUS, :] = inner_ref[s, RADIUS : count - RADIUS, :]
        dkv_ref[s, :RADIUS, :] = (rims_ref[s, :RADIUS, :] + prev_ref[s].astype(wide)).astype(low)
        dkv_ref[s, count - RADIUS :, :] = (rims_ref[s, RADIUS:, :] + after_ref[s].astype(wide)).astype(low)
    query_logit = logit_ref[...]
    router_ref[...] = jnp.sum(query_logit * nq_ref[...], axis=0, keepdims=True)
    rows_ref[...] = (nt(dhq_ref[...], w_ref[3]) + query_logit * vec_ref[2:3, :]).astype(low)

    def step(c, carry):
        rows = pl.ds(pl.multiple_of(c * CHUNK, CHUNK), CHUNK)
        part = (
            nt(dq_ref[rows, :], w_ref[0])
            + nt(dkv_ref[0, rows, :], w_ref[1])
            + nt(dkv_ref[1, rows, :], w_ref[2])
            + nn(picks_cols(qrow_ref[...], c * CHUNK, CHUNK), rows_ref[...])
        )
        gain_ref[...] += jnp.sum(part * normed_ref[rows, :].astype(wide), axis=0, keepdims=True)
        mp_store(core_ref[0], keep_ref, send_ref, c, count // CHUNK // 2, CHUNK, part.astype(low))
        return carry

    gain_ref[...] = jnp.zeros_like(gain_ref)
    lax.fori_loop(0, count // CHUNK, step, 0)
    gain_ref[...] = gain_ref[...] / vec_ref[0:1, :]


def keys_back_body(micros, place_ref, owned_ref, vec_ref, w_ref, *refs):
    keep_ref, send_ref, split_ref, turn_ref, rows_ref = refs[-5:]
    nk_refs, lines_in = refs[:micros], refs[micros:-5]
    gain_ones, gain_twos, queries, ffns = (lines_in[i * micros : (i + 1) * micros] for i in range(4))
    routed = nk_refs[0].shape[0]
    width = w_ref.shape[2]
    parts = place_ref.shape[0] - 1
    part = routed // parts
    inverse_gain = 1.0 / vec_ref[0:1, :]
    router_key = jnp.zeros((1, vec_ref.shape[1]), wide)
    gain_one = jnp.zeros((1, vec_ref.shape[1]), wide)
    for m in range(micros):
        start = owned_ref.shape[0] - (micros - m) * routed
        owned = owned_ref[start : start + routed, :]
        grad_k = owned[:, :width]
        grad_v = owned[:, width:].astype(wide)
        key_wide = nk_refs[m][...]
        raw = nn(key_wide.astype(low), w_ref[5])
        score = sigmoid(jnp.sum(key_wide * vec_ref[3:4, :], axis=-1, keepdims=True))
        logit = jnp.sum(grad_v * raw, axis=-1, keepdims=True) * score * (1.0 - score)
        router_key = router_key + jnp.sum(logit * key_wide, axis=0, keepdims=True)
        rows = nt(grad_k, w_ref[4]) + nt((grad_v * score).astype(low), w_ref[5]) + logit * vec_ref[3:4, :]
        gain_one = gain_one + jnp.sum(rows * key_wide, axis=0, keepdims=True) * inverse_gain
        turn_ref[...] = rows.astype(low)
        for p in range(parts):
            spot = pl.multiple_of(place_ref[1 + p] * part, part)
            rows_ref[m * routed + p * part : m * routed + (p + 1) * part, :] = turn_ref[pl.ds(spot, part), :]
    half = rows_ref.shape[0] // 2
    for c in range(2):
        mp_store(place_ref[0], keep_ref, send_ref, c, 1, half, rows_ref[c * half : (c + 1) * half, :])

    def added(refs):
        total = refs[0][...]
        for ref in refs[1:]:
            total = total + ref[...]
        return total

    gain_one = gain_one + added(gain_ones)
    lines = (gain_one, added(gain_twos) * (1.0 / parts), added(queries), router_key, added(ffns))
    split_ref[...] = jnp.zeros_like(split_ref)
    count = split_ref.shape[0]
    size = gain_one.shape[1] // count
    for d in range(count):
        for i, line in enumerate(lines):
            split_ref[d, i : i + 1, :size] = line[:, d * size : (d + 1) * size]


def owners_body(matrices, unpack, sum_ref, lines_ref, *refs):
    weights, sources, grads, split_ref, sums_ref = refs[:2], refs[2:-4], refs[-4:-2], refs[-2], refs[-1]
    unpack(sources if sources else (sum_ref,), grads)
    sums_ref[...] = jnp.zeros_like(sums_ref)
    write_sums(matrices, grads, weights, sums_ref)
    count = lines_ref.shape[0]
    parts = split_ref.shape[0] // count
    for d in range(count):
        sums_ref[:, VECTORS_AT:] = lines_ref[d]
        split_ref[d * parts : (d + 1) * parts] = jnp.broadcast_to(
            sums_ref[...].astype(low)[None], (parts,) + sums_ref.shape
        )


def finish_body(chunks, core_ref, kmine_ref, kother_ref, vec_ref, *refs):
    micros = (len(refs) - 3) // 4
    groups = [refs[4 * m : 4 * m + 4] for m in range(micros)]
    tok_ref, out_ref, keys_ref = refs[4 * micros :]
    routed = groups[0][3].shape[1]
    core = core_ref[0]
    chunk = pl.program_id(0)

    @pl.when(chunk == 0)
    def _():
        half = keys_ref.shape[0] // 2
        for c in range(2):
            keys_ref[c * half : (c + 1) * half, :] = mp_total(core, kmine_ref, kother_ref, c, 1, half).astype(low)

    flag = (chunk // (chunks // 2) == core).astype(wide)
    for m in range(micros):
        mine_ref, other_ref, grad_ref, krow_ref = groups[m]
        upstream = mine_ref[...].astype(wide) * flag + other_ref[...].astype(wide) * (1.0 - flag)
        spread = picks_cols(krow_ref[...], chunk * STREAM, STREAM)
        upstream = upstream + nn(spread, keys_ref[m * routed : (m + 1) * routed, :])
        pulled, _ = norm_back(tok_ref[m].astype(wide), vec_ref[0:1, :], upstream)
        out_ref[m] = grad_ref[...].astype(wide) + pulled


def join_body(chunks, core_ref, *refs):
    out_ref = refs[-1]
    flag = (pl.program_id(0) // (chunks // 2) == core_ref[0]).astype(wide)
    for m in range(out_ref.shape[0]):
        middle_ref, mine_ref, other_ref = refs[3 * m : 3 * m + 3]
        total = mine_ref[...].astype(wide) * flag + other_ref[...].astype(wide) * (1.0 - flag)
        out_ref[m] = (middle_ref[...].astype(wide) + total).astype(low)


def attn_grads_body(moves, *refs):
    out_ref, turned_ref, other_ref = refs[-3:]
    micros = len(refs) // 12
    groups = [refs[12 * m : 12 * m + 12] for m in range(micros)]
    tokens, width = groups[0][9].shape
    keys = groups[0][11].shape[0]
    for group in groups:
        moves.begin(group[9], group[0], group[1], group[10])
    for group in groups:
        moves.begin(group[11], group[3], group[4], group[5], group[6], group[7], group[8])
    for group in groups:
        moves.need(group[9], group[0], group[1], group[10])
    grads = []
    for m in range(micros):
        turned_ref[:, m * tokens : (m + 1) * tokens] = groups[m][9][...].T
    for s in range(3):
        total = 0.0
        for m, group in enumerate(groups):
            grad = group[0][...] if s == 0 else group[1][s - 1]
            total = total + nn(turned_ref[:, m * tokens : (m + 1) * tokens], grad)
        grads.append(total)
    total = 0.0
    for m, group in enumerate(groups):
        total = total + tn(group[10][...], group[2][...])
    grads.append(total)
    for group in groups:
        moves.need(*group)
    for m in range(micros):
        other_ref[:, m * keys : (m + 1) * keys] = groups[m][11][...].T
    for s in (3, 4):
        total = 0.0
        for m, group in enumerate(groups):
            if s == 3:
                grad = group[s][...].reshape(keys, -1)[:, : group[4].shape[1]]
            else:
                grad = group[s][...]
            total = total + nn(other_ref[:, m * keys : (m + 1) * keys], grad)
        grads.append(total)
    out_grads = []
    for mix, grad in ((5, 6), (7, 8)):
        total = 0.0
        for group in groups:
            total = total + tn(group[mix][...], group[grad][...])
        out_grads.append(total)
    count, _, lane = out_ref.shape
    in_rows = width // count
    for j in range(3):
        pair = jnp.concatenate([grads[2 * j], grads[2 * j + 1]], axis=1).astype(low)
        out_ref[:, j * in_rows : (j + 1) * in_rows, :] = pair.reshape(count, in_rows, lane)
    out_rows = out_grads[0].shape[0] // count
    own = groups[0][3].shape[1]
    for m, group in enumerate(groups):
        at = out_ref.shape[1] - (micros - m) * own
        out_ref[:, at : at + own, :] = group[3][...]
    for d in range(count):
        rows = slice(d * out_rows, (d + 1) * out_rows)
        both = jnp.concatenate([g[rows] for g in out_grads], axis=0).astype(low)
        for j in range(width // lane):
            at = 3 * in_rows + j * 2 * out_rows
            out_ref[d, at : at + 2 * out_rows, :] = both[:, j * lane : (j + 1) * lane]


class Matrix:
    def __init__(self, array, lead, tall, cols_at, rows_at, weight_at):
        self.array, self.lead, self.tall = array, lead, tall
        self.cols_at, self.rows_at, self.weight_at = cols_at, rows_at, weight_at

    def read(self, refs):
        ref = refs[self.array]
        return ref[...] if self.lead is None else ref[self.lead]

    def write(self, refs, value):
        if self.lead is None:
            refs[self.array][...] = value
        else:
            refs[self.array][self.lead] = value

    def line(self):
        lead = 0 if self.lead is None else self.lead
        return slice(lead, lead + 1)


def ffn_matrices(light, heavy, width):
    cut = SUM_LANES
    rest = heavy - cut
    tail = width - cut
    return [
        Matrix(0, 0, True, [(4, rest, light)], (6, 2 * tail), (7, 3 * 128)),
        Matrix(0, 1, True, [(5, rest, light)], (6, 2 * tail + 128), (7, 3 * 128 + 1)),
        Matrix(1, None, False, [(2, 0, cut), (6, 0, tail)], (6, 2 * tail + 256), (7, 3 * 128 + 2)),
        Matrix(2, 0, True, [(0, 0, cut), (4, 0, rest)], (7, 0), (7, 3 * 128 + 3)),
        Matrix(2, 1, True, [(1, 0, cut), (5, 0, rest)], (7, 128), (7, 3 * 128 + 4)),
        Matrix(3, None, False, [(3, 0, cut), (6, tail, tail)], (7, 256), (7, 3 * 128 + 5)),
    ]


def attn_matrices(cols, width):
    listed = [
        Matrix(0, i, True, [(i, 0, cols)], (6 + i // 4, 128 * (i % 4)), (i, 224)) for i in range(6)
    ]
    piece = width // 3
    for s in range(2):
        spots = [(3 * s + j, 256, piece) for j in range(3)]
        listed.append(Matrix(1, s, False, spots, (7, 256 + 128 * s), (s, 232)))
    return listed


def total_of(values):
    return jnp.sum(jnp.sum(values, axis=1, keepdims=True), axis=0, keepdims=True)


def sums_body(matrices, unpack, array_count, *refs):
    weights = refs[-2 * array_count - 1 : -array_count - 1]
    grads, sums_ref = refs[-array_count - 1 : -1], refs[-1]
    unpack(refs[: -2 * array_count - 1], grads)
    sums_ref[...] = jnp.zeros_like(sums_ref)
    write_sums(matrices, grads, weights, sums_ref)


def write_sums(matrices, grads, weights, sums_ref):
    for matrix in matrices:
        square = matrix.read(grads)
        square = square * square + tiny_square
        cols = jnp.sum(square, axis=0, keepdims=True)
        at = 0
        for row, lane, size in matrix.cols_at:
            sums_ref[row : row + 1, lane : lane + size] = cols[:, at : at + size]
            at = at + size
        rows = lax.dot_general(
            jnp.ones((8, square.shape[1]), wide),
            square,
            (((1,), (1,)), ((), ())),
            precision=lax.Precision.HIGHEST,
            preferred_element_type=wide,
        )
        row, lane = matrix.rows_at
        sums_ref[row : row + 1, lane : lane + square.shape[0]] = rows[0:1]
        weight = matrix.read(weights)
        row, lane = matrix.weight_at
        sums_ref[row : row + 1, lane : lane + 1] = total_of(weight * weight)


def lane_row(values):
    spots = lax.broadcasted_iota(jnp.int32, (1, 128), 1)
    row = jnp.zeros((1, 128), wide)
    for place, value in enumerate(values):
        row = row + jnp.where(spots == place, value, 0.0)
    return row


def moments_body(matrices, array_count, vector_count, data_size, model_size, place_ref, parts_ref, *refs):
    keep = 1.0 - STEP ** (-0.8)
    n = array_count
    grads, row_old, col_old, row_mine, col_mine = (refs[i * n : (i + 1) * n] for i in range(5))
    at = 5 * n
    vector_in = refs[at : at + 2 * vector_count]
    at = at + 2 * vector_count
    updates, row_new, col_new = (refs[at + i * n : at + (i + 1) * n] for i in range(3))
    at = at + 3 * n
    vector_out = refs[at : at + 3 * vector_count]
    aux_ref = refs[-1]
    d, k = place_ref[0], place_ref[1]
    devices = data_size * model_size

    def part(index):
        return parts_ref[index].astype(wide)

    whole = part(0)
    for i in range(1, devices):
        whole = whole + part(i)
    by_model = []
    for j in range(model_size):
        total = part(j)
        for i in range(1, data_size):
            total = total + part(i * model_size + j)
        by_model.append(total)
    by_data = []
    for i in range(data_size):
        total = part(i * model_size)
        for j in range(1, model_size):
            total = total + part(i * model_size + j)
        by_data.append(total)
    my_cols = part(k)
    for i in range(1, data_size):
        my_cols = my_cols + part(i * model_size + k)
    my_rows = part(d * model_size)
    for j in range(1, model_size):
        my_rows = my_rows + part(d * model_size + j)
    mine = part(d * model_size + k)

    def cols_of(sums, matrix):
        pieces = [sums[row : row + 1, lane : lane + size] for row, lane, size in matrix.cols_at]
        return pieces[0] if len(pieces) == 1 else jnp.concatenate(pieces, axis=1)

    lines, extents = [], []
    for matrix in matrices:
        grad_rows, grad_cols = matrix.read(grads).shape
        row_total = grad_rows * data_size * (1 if matrix.tall else model_size)
        col_total = grad_cols * (model_size if matrix.tall else 1)
        extents.append((row_total, col_total))
        row, lane = matrix.rows_at
        source = my_rows if matrix.tall else mine
        old = row_mine[matrix.array][matrix.line(), :]
        lines.append(keep * old + (1.0 - keep) / col_total * source[row : row + 1, lane : lane + 128])
    while len(lines) < 8:
        lines.append(jnp.zeros((1, 128), wide))
    columns = jnp.concatenate(lines, axis=0).T
    update_sums, weight_sums = [], []
    for place, (matrix, (row_total, col_total)) in enumerate(zip(matrices, extents)):
        grad = matrix.read(grads)
        row, lane = matrix.rows_at
        size = grad.shape[0]
        old_rows = row_old[matrix.array][matrix.line(), :]
        old_cols = col_old[matrix.array][matrix.line(), :]
        mean = keep * jnp.mean(old_rows, axis=1, keepdims=True) + (1.0 - keep) / (
            row_total * col_total
        ) * jnp.sum(whole[row : row + 1, lane : lane + 128], axis=1, keepdims=True)
        if matrix.tall:
            cols = keep * col_mine[matrix.array][matrix.line(), :] + (1.0 - keep) / row_total * cols_of(my_cols, matrix)
            all_cols = jnp.concatenate([cols_of(sums, matrix) for sums in by_model], axis=1)
            all_rows = jnp.concatenate([sums[row : row + 1, lane : lane + size] for sums in by_data], axis=1)
            new_cols = keep * old_cols + (1.0 - keep) / row_total * all_cols
        else:
            cols = keep * old_cols + (1.0 - keep) / row_total * cols_of(whole, matrix)
            all_rows = jnp.concatenate(
                [
                    part(i * model_size + j)[row : row + 1, lane : lane + size]
                    for j in range(model_size)
                    for i in range(data_size)
                ],
                axis=1,
            )
            new_cols = cols
        row_new[matrix.array][matrix.line(), :] = keep * old_rows + (1.0 - keep) / col_total * all_rows
        col_new[matrix.array][matrix.line(), :] = new_cols
        update = grad * lax.rsqrt(columns[:size, place : place + 1] * (cols / mean))
        matrix.write(updates, update)
        update_sums.append(total_of(update * update))
        row, lane = matrix.weight_at
        weight_sums.append(whole[row : row + 1, lane : lane + 1] * (1.0 / devices))
    line_at = 0
    for i in range(vector_count):
        old_ref, weight_ref = vector_in[2 * i : 2 * i + 2]
        lines, size = old_ref.shape
        grad = whole[line_at : line_at + lines, VECTORS_AT : VECTORS_AT + size]
        line_at = line_at + lines
        vector_out[3 * i + 2][...] = grad
        moment = keep * old_ref[...] + (1.0 - keep) * (grad * grad + tiny_square)
        update = grad * lax.rsqrt(moment)
        vector_out[3 * i][...] = moment
        vector_out[3 * i + 1][...] = update
        for r in range(grad.shape[0]):
            line = update[r : r + 1]
            update_sums.append(total_of(line * line) * (1.0 / model_size))
            line = weight_ref[r : r + 1, :]
            weight_sums.append(total_of(line * line) * (1.0 / model_size))
    lines = jnp.concatenate([lane_row(update_sums), lane_row(weight_sums), jnp.zeros((6, 128), wide)], axis=0)
    aux_ref[...] = jnp.broadcast_to(lines[None], aux_ref.shape)


def step_size(update_sum, weight_sum, count):
    rms_weight = jnp.sqrt(weight_sum * (1.0 / count))
    rms_update = jnp.sqrt(update_sum * (1.0 / count))
    return step_rate * jnp.maximum(scale_floor, rms_weight) / jnp.maximum(1.0, rms_update / clip_level)


def weights_body(matrices, counts, array_count, vector_count, aux_ref, *refs):
    n = array_count + vector_count
    weights, updates, news = refs[:n], refs[n : 2 * n], refs[2 * n :]
    sums = aux_ref[0]
    for i in range(1, aux_ref.shape[0]):
        sums = sums + aux_ref[i]

    def step(place):
        spot = slice(place, place + 1)
        return step_size(sums[0:1, spot], sums[1:2, spot], counts[place])

    for place, matrix in enumerate(matrices):
        matrix.write(news, matrix.read(weights) - step(place) * matrix.read(updates))
    place = len(matrices)
    for i in range(array_count, n):
        for r in range(weights[i].shape[0]):
            row = slice(r, r + 1)
            news[i][row, :] = weights[i][row, :] - step(place) * updates[i][row, :]
            place = place + 1


def after(value, *others):
    return lax.optimization_barrier((value,) + others)[0]


def shards(
    tokens,
    cotangent,
    segments,
    route_query,
    route_key,
    route_ffn,
    attn_in,
    attn_out,
    light_in,
    light_out,
    heavy_in,
    heavy_out,
    gains,
    router,
    row_attn_in,
    col_attn_in,
    row_attn_out,
    col_attn_out,
    row_light_in,
    col_light_in,
    row_light_out,
    col_light_out,
    row_heavy_in,
    col_heavy_in,
    row_heavy_out,
    col_heavy_out,
    second_gains,
    second_router,
):
    data_size = lax.axis_size("dp")
    model_size = lax.axis_size("mp")
    data_index = lax.axis_index("dp")
    model_index = lax.axis_index("mp")
    core = model_index % 2
    order = jnp.arange(model_size) ^ model_index
    core_flag = jnp.concatenate([core.reshape(1), order]).astype(jnp.int32)
    core_pairs = [(i, i ^ 1) for i in range(model_size)]
    far_pairs = [(i, i ^ 2) for i in range(model_size)]
    micro_count, tok_local, width = tokens.shape
    routed_local = route_query.shape[1]
    routed_all = route_key.shape[1]
    quarter = routed_local // model_size
    head_cols = attn_in.shape[2]
    in_rows = attn_in.shape[1]

    key_blocks = route_key.reshape(micro_count, data_size, model_size, quarter)
    own_keys = lax.dynamic_slice_in_dim(key_blocks, data_index, 1, axis=1)
    key_blocks = jnp.take(key_blocks, order, axis=2)
    key_local = lax.dynamic_slice_in_dim(key_blocks, data_index, 1, axis=1)[:, 0]
    my_quarter = key_local[:, 0]
    picks = (my_quarter[:, :, None] == jnp.arange(tok_local)[None, None, :]).astype(low)
    my_rows = jnp.einsum("mrt,mtd->mrd", picks, tokens, preferred_element_type=wide).astype(low)

    def to_all(rows):
        sent = jnp.broadcast_to(rows[None], (data_size,) + rows.shape)
        return lax.all_to_all(sent, "dp", 0, 0, tiled=True)

    key_rows = to_all(my_rows).reshape(data_size, micro_count, quarter, width)
    rows_core = lax.ppermute(key_rows, "mp", core_pairs)
    rows_far = lax.ppermute(key_rows, "mp", far_pairs)
    rows_both = lax.ppermute(rows_far, "mp", core_pairs)

    lane = 2 * head_cols
    sides = width // lane
    in_rows = attn_in.shape[1]
    out_rows = attn_out.shape[1]
    aligned = in_rows % 16 == 0 and out_rows % 8 == 0 and light_out.shape[0] % 16 == 0
    if aligned:
        (pack_one,) = kernel_call(
            pack_body,
            [in_vmem((3 * in_rows + 2 * out_rows * sides + 16, lane), low)],
            [],
            (attn_in, attn_out, gains, router),
            weight=3,
        )
    else:
        small = jnp.concatenate([gains, router], axis=0).astype(low)
        small_block = jnp.pad(small, ((0, 16 - small.shape[0]), (0, lane - in_rows)))
        in_block = (
            attn_in.astype(low).reshape(3, 2, in_rows, head_cols).transpose(0, 2, 1, 3).reshape(3 * in_rows, lane)
        )

        def sideways(rows):
            return rows.reshape(-1, sides, lane).transpose(1, 0, 2).reshape(-1, lane)

        out_block = sideways(attn_out.astype(low).reshape(2 * out_rows, width))
        pack_one = jnp.concatenate([in_block, out_block, small_block], axis=0)
    got_one = lax.all_gather(pack_one, "dp", axis=0, tiled=False)

    light_hidden = light_in.shape[2]
    heavy_hidden = heavy_in.shape[2]
    local_spot = model_index * data_size + data_index
    ffn_list = ffn_matrices(light_hidden, heavy_hidden, width)
    ffn_weights = (light_in, light_out, heavy_in, heavy_out)
    ffn_moments = (
        (row_light_in, col_light_in),
        (row_light_out, col_light_out),
        (row_heavy_in, col_heavy_in),
        (row_heavy_out, col_heavy_out),
    )
    attn_list = attn_matrices(head_cols, width)
    attn_weights = (attn_in, attn_out)
    attn_moments = ((row_attn_in, col_attn_in), (row_attn_out, col_attn_out))

    def moments_of(matrices, weights, moments):
        row_old, col_old, row_mine, col_mine = [], [], [], []
        for array, weight in enumerate(weights):
            rows, cols = moments[array]
            tall = [m.tall for m in matrices if m.array == array][0]
            lead = rows.size // rows.shape[-1]
            rows, cols = rows.reshape(lead, -1), cols.reshape(lead, -1)
            size, span = weight.shape[-2:]
            spot = data_index if tall else local_spot
            my_rows = lax.dynamic_slice_in_dim(rows, spot * size, size, 1)
            row_mine.append(jnp.pad(my_rows, ((0, 0), (0, 128 - size)), constant_values=1.0))
            col_mine.append(lax.dynamic_slice_in_dim(cols, model_index * span, span, 1) if tall else cols)
            row_old.append(rows)
            col_old.append(cols)
        return row_old, col_old, row_mine, col_mine

    ffn_here, attn_here, got_one = lax.optimization_barrier(
        (
            moments_of(ffn_list, ffn_weights, ffn_moments),
            moments_of(attn_list, attn_weights, attn_moments),
            got_one,
        )
    )

    if aligned:
        w_in, w_out, vectors = kernel_call(
            unpack_body,
            [
                in_vmem((6, width, head_cols), low),
                in_vmem((2, data_size * out_rows, width), low),
                in_vmem((8, width), wide),
            ],
            [],
            (got_one,),
            weight=5,
        )
    else:
        w_in = (
            got_one[:, : 3 * in_rows]
            .reshape(data_size, 3, in_rows, 2, head_cols)
            .transpose(1, 3, 0, 2, 4)
            .reshape(6, width, head_cols)
        )
        at = 3 * in_rows
        w_out = (
            got_one[:, at : at + out_block.shape[0]]
            .reshape(data_size, sides, 2, out_rows, lane)
            .transpose(2, 0, 3, 1, 4)
            .reshape(2, data_size * out_rows, width)
        )
        at = at + out_block.shape[0]
        vectors = got_one[:, at : at + 8, :in_rows].transpose(1, 0, 2).reshape(8, width).astype(wide)

    def blocked(weight):
        lead, rows, cols = weight.shape
        return weight.reshape(lead, rows, cols // CHUNK, CHUNK).transpose(0, 2, 1, 3).reshape(-1, rows, CHUNK)

    def unblocked(blocks, lead):
        count, rows, _ = blocks.shape
        return blocks.reshape(lead, count // lead, rows, CHUNK).transpose(0, 2, 1, 3).reshape(lead, rows, -1)

    light_hidden = light_in.shape[2]
    heavy_hidden = heavy_in.shape[2]
    blocks = [blocked(w.astype(low)) for w in (light_in, light_out[None], heavy_in, heavy_out[None])]
    block_rows = [b.shape[0] * b.shape[1] for b in blocks]
    pack_two = jnp.concatenate([b.reshape(-1, CHUNK) for b in blocks], axis=0)
    w_ffn = lax.all_gather(after(pack_two, got_one, rows_far), "dp", axis=0, tiled=False)
    if not aligned:
        pieces = []
        at = 0
        for block in blocks:
            size = block.shape[0] * block.shape[1]
            pieces.append(
                w_ffn[:, at : at + size]
                .reshape((data_size,) + block.shape)
                .transpose(1, 0, 2, 3)
                .reshape(-1, CHUNK)
            )
            at = at + size
        w_ffn = jnp.concatenate(pieces, axis=0)[None]

    attn_in, attn_out, light_in, light_out, heavy_in, heavy_out, gains, router = (
        lax.optimization_barrier(
            (got_one, attn_in, attn_out, light_in, light_out, heavy_in, heavy_out, gains, router)
        )[1:]
    )

    turns = (jnp.arange(micro_count) % 2)[:, None]
    segment_ids = segments[None, :] * turns
    seg_padded = jnp.pad(segment_ids, ((0, 0), (RADIUS, RADIUS)), constant_values=-1)
    seg_local = lax.dynamic_slice_in_dim(segment_ids, data_index * tok_local, tok_local, axis=1)
    seg_extended = lax.dynamic_slice_in_dim(
        seg_padded, data_index * tok_local, tok_local + 2 * RADIUS, axis=1
    ).reshape(micro_count, -1, 1, BLOCK)

    def picked(ids, spots):
        hit = spots[..., :, None] == jnp.arange(tok_local)
        return jnp.sum(jnp.where(hit, ids[..., None, :], 0), axis=-1)

    key_seg = picked(
        segment_ids.reshape(micro_count, data_size, tok_local),
        key_blocks.reshape(micro_count, data_size, routed_local),
    ).reshape(micro_count, -1)
    query_seg = picked(seg_local, route_query)
    key_list = key_local.reshape(micro_count, -1)

    query_col, query_row = route_query[:, :, None], route_query[:, None, :]
    key_col, key_row = key_list[:, :, None], own_keys.reshape(micro_count, 1, routed_local)
    ffn_col, ffn_row = route_ffn[:, :, None], route_ffn[:, None, :]
    segs = (seg_local[:, :, None], seg_extended, query_seg[:, :, None], key_seg[:, None, :])

    micros = range(micro_count)
    token_parts = [Pick(tokens, m) for m in micros]
    cot_parts = [Pick(cotangent, m) for m in micros]
    projected = kernel_call(
        project_body,
        [
            in_vmem((tok_local, width), low),
            in_vmem((tok_local, head_cols), low),
            in_vmem((tok_local, head_cols), low),
            in_vmem((tok_local, head_cols), low),
            in_vmem((routed_local, head_cols), low),
            in_vmem((routed_local, 1), wide),
            in_vmem((routed_local, width), wide),
            in_vmem((routed_local, width), wide),
            in_vmem((routed_local, width), low),
        ]
        * micro_count,
        [pltpu.VMEM((tok_local, width), low)],
        (vectors, w_in) + sum(((token_parts[m], query_col[m], key_col[m]) for m in micros), ()),
        managed=True,
            weight=12,
    )
    normed_low, light_q, light_k, light_v, heavy_q, score_q, rows_q, rows_k, rows_q_low = (
        projected[i::9] for i in range(9)
    )

    up = [(i, i + 1) for i in range(data_size - 1)]
    down = [(i + 1, i) for i in range(data_size - 1)]
    tails = jnp.stack([jnp.stack([k[tok_local - RADIUS :], v[tok_local - RADIUS :]]) for k, v in zip(light_k, light_v)])
    heads = jnp.stack([jnp.stack([k[:RADIUS], v[:RADIUS]]) for k, v in zip(light_k, light_v)])
    halo_prev = lax.ppermute(tails, "dp", up)
    halo_next = lax.ppermute(heads, "dp", down)

    split = (data_size, model_size, quarter)
    span = min(data_size, 8)

    def split_spec(cols):
        return pl.BlockSpec((span, model_size, quarter, cols), lambda i: (i, 0, 0, 0))

    keyed = pl.pallas_call(
        keys_body,
        grid=(data_size // span,),
        out_shape=[
            in_vmem(split + (width,), low),
            in_vmem(split + (head_cols,), low),
            in_vmem(split + (head_cols,), low),
            in_vmem(split + (1,), wide),
        ]
        * micro_count,
        in_specs=[pl.BlockSpec((span, micro_count, quarter, width), lambda i: (i, 0, 0, 0))] * 4
        + [
            pl.BlockSpec((8, width), lambda i: (0, 0)),
            pl.BlockSpec((6, width, head_cols), lambda i: (0, 0, 0)),
        ],
        out_specs=[split_spec(width), split_spec(head_cols), split_spec(head_cols), split_spec(1)] * micro_count,
        compiler_params=pltpu.CompilerParams(vmem_limit_bytes=VMEM_BYTES),
        cost_estimate=pl.CostEstimate(flops=6 * 1_150_000_000, bytes_accessed=1_000_000, transcendentals=0),
    )(key_rows, rows_core, rows_far, rows_both, vectors, w_in)
    key_normed, heavy_k, heavy_v, score_k = (
        [a.reshape(routed_all, -1) for a in keyed[i::4]] for i in range(4)
    )

    def mp_first(keep, send, *earlier):
        got = lax.ppermute(after(send, *earlier), "mp", core_pairs)
        return (keep.astype(wide) + got.astype(wide)).astype(low)

    def mp_second(mine):
        return mine, lax.ppermute(mine, "mp", far_pairs)

    def mp_third(moved, *held):
        mine, near = moved
        near = after(near, *held)
        done = (mine.astype(wide) + near.astype(wide)).astype(low)
        return done, lax.ppermute(done, "mp", core_pairs)

    extended = pltpu.VMEM((tok_local + 2 * RADIUS, head_cols), low)
    row_shape = (tok_local, width)
    half_shape = (tok_local // 2, width)

    def all_picks(arrays, m):
        return tuple(a[m] for a in arrays)

    attended = []
    attn_moved = []
    held, earlier = (), ()
    for m in micros:
        outs = kernel_call(
            attend_body,
            [
                in_vmem(half_shape, low),
                in_vmem(half_shape, low),
                in_vmem((tok_local, head_cols), low),
                in_vmem((routed_local, head_cols), low),
                in_vmem((routed_local, width), wide),
            ],
            [extended, extended, pltpu.VMEM((routed_local, width), low)],
            (core_flag,)
            + all_picks((light_q, light_k, light_v, halo_prev, halo_next, heavy_q, heavy_k, heavy_v, score_q), m)
            + (after(w_out, *held),)
            + all_picks((query_row,) + segs, m),
            scalars=1,
            managed=False,
            weight=11,
        )
        attended.append(outs)
        begun = mp_first(outs[0], outs[1], *earlier)
        attn_moved.append(mp_second(begun))
        held, earlier = (begun,), (attn_moved[m][1],)

    fed = []
    grad_moved = []
    split = data_size if aligned else 1
    total_rows = ffn_bases(width, light_hidden, heavy_hidden)[1]
    own = [
        (row_shape, low),
        ((tok_local, light_hidden), low),
        ((2, tok_local, light_hidden), low),
        ((routed_local, width), low),
        ((routed_local, heavy_hidden), low),
        ((2, routed_local, heavy_hidden), low),
        ((routed_local, width), low),
    ]
    for m in micros:
        beside = attended[m + 1][0] if m + 1 < micro_count else fed[m - 1][1]
        ffn_outs = [
            in_vmem(row_shape, low),
            in_vmem(half_shape, low),
            in_vmem(half_shape, low),
            in_vmem(half_shape, low),
            in_vmem(half_shape, low),
            in_vmem((1, width), wide),
        ]
        scratch = [
            pltpu.VMEM(row_shape, low),
            pltpu.VMEM((routed_local, width), low),
            pltpu.VMEM((routed_local, width), low),
        ]
        kept = ()
        if m + 1 < micro_count:
            ffn_outs = ffn_outs + [in_vmem(*o) for o in own]
        else:
            ffn_outs = ffn_outs + [in_vmem((split, total_rows // split, CHUNK), low)]
            scratch = [
                *(pltpu.VMEM(*o) for o in own),
                pltpu.VMEM((width, micro_count * tok_local), low),
                pltpu.VMEM((width, micro_count * routed_local), low),
                *scratch,
            ]
            for i in range(m):
                kept = kept + tuple(fed[i][6:13]) + (cot_parts[i],)
        outs = kernel_call(
            functools.partial(ffn_body, m if m + 1 == micro_count else 0),
            ffn_outs,
            scratch,
            (core_flag,)
            + mp_third(attn_moved[m], beside)
            + (token_parts[m], cot_parts[m], after(vectors, *held), ffn_col[m], ffn_row[m], w_ffn)
            + kept,
            scalars=1,
            managed=True,
            weight=17 if m + 1 < micro_count else 23,
        )
        fed.append(outs)
        begun = mp_first(outs[3], outs[4], *earlier)
        grad_moved.append(mp_second(begun))
        held, earlier = (begun,), (grad_moved[m][1],)
    pack_ffn = fed[-1][6]
    if not aligned:
        pieces = []
        at = 0
        for block in blocks:
            size = block.shape[0] * block.shape[1] * data_size
            pieces.append(
                pack_ffn[0, at : at + size]
                .reshape(block.shape[0], data_size, block.shape[1], CHUNK)
                .transpose(1, 0, 2, 3)
                .reshape(data_size, -1, CHUNK)
            )
            at = at + size
        pack_ffn = jnp.concatenate(pieces, axis=1)
    sum_ffn = lax.psum_scatter(pack_ffn.reshape(-1, CHUNK), "dp", scatter_dimension=0, tiled=True)

    y_moved = []
    backs = []
    edges = jnp.zeros((2, 1, 2, RADIUS, head_cols), low)
    y_begun = [mp_first(fed[m][1], fed[m][2]) for m in micros]
    for m in micros:
        outs = kernel_call(
            functools.partial(attend_back_body, m),
            [
                in_vmem(row_shape, low),
                in_vmem((1, width), wide),
                in_vmem((tok_local, head_cols), low),
                in_vmem((2, tok_local, head_cols), low),
                in_vmem((2, 2 * RADIUS, head_cols), wide),
                in_vmem((2, m + 1, 2, RADIUS, head_cols), low),
                in_vmem((routed_local, head_cols), low),
                in_vmem((data_size, routed_local, 2 * head_cols), low),
                in_vmem((routed_all, head_cols), low),
                in_vmem((routed_local, width), low),
                in_vmem((routed_local, 1), wide),
            ],
            [
                extended,
                extended,
                pltpu.VMEM((tok_local, head_cols), low),
                pltpu.VMEM((tok_local + 2 * RADIUS, head_cols), wide),
                pltpu.VMEM((tok_local + 2 * RADIUS, head_cols), wide),
                pltpu.VMEM((min(routed_all, KEYS), head_cols), wide),
                pltpu.VMEM((min(routed_all, KEYS), head_cols), wide),
            ],
            (core_flag,)
            + mp_third(grad_moved[m], pack_ffn if m == 0 else backs[m - 1][0])
            + (fed[m][0], cot_parts[m], after(vectors, pack_ffn, y_begun[m]))
            + all_picks(
                (light_q, light_k, light_v, halo_prev, halo_next, heavy_q, heavy_k, heavy_v, score_k, score_q), m
            )
            + (attended[m][4], w_out)
            + all_picks((query_col,) + segs, m)
            + (edges,),
            scalars=1,
            managed=True,
            weight=22,
        )
        edges = outs[5]
        backs.append(outs)
        y_moved.append(mp_second(after(y_begun[m], outs[0], *earlier)))
        earlier = (y_moved[m][1],)
    held = (y_moved[0][1],)

    from_prev = lax.ppermute(edges[0], "dp", up)
    from_next = lax.ppermute(edges[1], "dp", down)

    last = []
    last_moved = []
    for m in micros:
        outs = backs[m]
        made = kernel_call(
            project_back_body,
            [
                in_vmem(half_shape, low),
                in_vmem(half_shape, low),
                in_vmem((2, tok_local, head_cols), low),
                in_vmem((1, width), wide),
                in_vmem((1, width), wide),
            ],
            [pltpu.VMEM((routed_local, width), low)],
            (core_flag, outs[2], outs[3], outs[4], from_prev[m], from_next[m], outs[6], outs[10], rows_q[m])
            + (after(vectors, *held), w_in, query_row[m], normed_low[m]),
            scalars=1,
            managed=False,
            weight=8,
        )
        last.append(made)
        if m + 1 < micro_count:
            begun = mp_first(made[0], made[1])
            last_moved.append(mp_second(after(begun, *earlier)))
            held, earlier = (), (last_moved[m][1],)

    attn_rows = 3 * in_rows + 2 * out_rows * sides
    groups = []
    for m in micros:
        outs = backs[m]
        groups.append(
            (after(outs[2], *(moved[1] for moved in y_moved)), last[m][2], outs[6], outs[7], outs[8], attended[m][2], outs[0], attended[m][3], outs[9])
            + (normed_low[m], rows_q_low[m], key_normed[m])
        )
    if aligned:
        (pack_attn,) = kernel_call(
            attn_grads_body,
            [in_vmem((data_size, attn_rows + micro_count * routed_local, lane), low)],
            [
                pltpu.VMEM((width, micro_count * tok_local), low),
                pltpu.VMEM((width, micro_count * routed_all), low),
            ],
            sum(groups, ()),
            managed=True,
            weight=12,
        )
    else:
        totals = [0.0] * 8
        for m, group in enumerate(groups):
            grad_k = group[3].reshape(routed_all, -1)[:, :head_cols]
            pairs = (
                (normed_low[m], group[0]), (normed_low[m], group[1][0]), (normed_low[m], group[1][1]),
                (rows_q_low[m], group[2]), (key_normed[m], grad_k), (key_normed[m], group[4]),
                (group[5], group[6]), (group[7], group[8]),
            )
            totals = [total + tn(left, right) for total, (left, right) in zip(totals, pairs)]
        grad_in = jnp.stack(totals[:6]).astype(low)
        grad_out = jnp.stack(totals[6:]).astype(low)
        pack_attn = jnp.concatenate(
            [
                grad_in.reshape(3, 2, data_size, in_rows, head_cols)
                .transpose(2, 0, 3, 1, 4)
                .reshape(data_size, 3 * in_rows, lane),
                grad_out.reshape(2, data_size, out_rows, sides, lane)
                .transpose(1, 3, 0, 2, 4)
                .reshape(data_size, -1, lane),
            ]
            + [backs[m][7] for m in micros],
            axis=1,
        )
    sum_attn = lax.psum_scatter(
        after(pack_attn.reshape(-1, lane), sum_ffn), "dp", scatter_dimension=0, tiled=True
    )

    device_count = data_size * model_size

    def exchanged(blocks):
        return lax.all_to_all(blocks, ("dp", "mp"), 0, 0, tiled=True)

    place = jnp.stack([data_index, model_index]).astype(jnp.int32)

    def unpack_ffn(sources, grads):
        if len(sources) > 1:
            for source, grad in zip(sources, grads):
                grad[...] = source[...]
            return
        (ref,) = sources
        at = 0
        for grad, lead in zip(grads, (2, 0, 2, 0)):
            rows, cols = grad.shape[-2:]
            for l in range(max(lead, 1)):
                for j in range(cols // CHUNK):
                    value = ref[at : at + rows, :].astype(wide)
                    spot = slice(j * CHUNK, (j + 1) * CHUNK)
                    if lead:
                        grad[l, :, spot] = value
                    else:
                        grad[:, spot] = value
                    at = at + rows

    def unpack_attn(sources, grads):
        if len(sources) > 1:
            for source, grad in zip(sources, grads):
                grad[...] = source[...]
            return
        total = sources[0][: 3 * in_rows + 2 * out_rows * sides, :].astype(wide)
        for j in range(3):
            pair = total[j * in_rows : (j + 1) * in_rows]
            grads[0][2 * j] = pair[:, :head_cols]
            grads[0][2 * j + 1] = pair[:, head_cols:]
        for j in range(sides):
            at = 3 * in_rows + 2 * j * out_rows
            for m in range(2):
                grads[1][m, :, j * lane : (j + 1) * lane] = total[at + m * out_rows : at + (m + 1) * out_rows]

    def first_sums(matrices, unpack, sources, sums_shape, weights):
        n = len(weights)
        sums_out = kernel_call(
            functools.partial(sums_body, matrices, unpack, n),
            [in_vmem(w.shape, wide) for w in weights] + [in_vmem(sums_shape, wide)],
            [],
            tuple(sources) + tuple(weights),
            weight=4,
        )
        rows, cols = sums_shape
        sent = jnp.broadcast_to(sums_out[n].astype(low)[None], (device_count, rows, cols))
        got = lax.all_to_all(sent, ("dp", "mp"), 0, 0, tiled=True)
        return sums_out, got

    def optimize(matrices, sums_out, parts, weights, moments, moments_here, vectors_in):
        n = len(weights)
        grads = tuple(sums_out[:n])
        row_old, col_old, row_mine, col_mine = moments_here
        vector_count = len(vectors_in)
        made = kernel_call(
            functools.partial(moments_body, matrices, n, vector_count, data_size, model_size),
            [in_vmem(w.shape, wide) for w in weights]
            + [in_vmem(r.shape, wide) for r in row_old]
            + [in_vmem(c.shape, wide) for c in col_old]
            + [in_vmem(v[0].shape, wide) for v in vectors_in for _ in range(3)]
            + [in_vmem((device_count, 8, 128), wide)],
            [],
            (place, parts)
            + grads
            + tuple(row_old)
            + tuple(col_old)
            + tuple(row_mine)
            + tuple(col_mine)
            + sum(vectors_in, ()),
            scalars=1,
            weight=5,
        )
        updates, row_new, col_new = made[:n], made[n : 2 * n], made[2 * n : 3 * n]
        vector_made = made[3 * n : -1]
        counts = [
            weights[m.array].shape[-2] * weights[m.array].shape[-1] * device_count for m in matrices
        ] + [width for v in vectors_in for _ in range(v[0].shape[0])]
        all_weights = tuple(weights) + tuple(v[1] for v in vectors_in)

        def finish(aux):
            news = kernel_call(
                functools.partial(weights_body, matrices, counts, n, vector_count),
                [in_vmem(w.shape, wide) for w in all_weights],
                [],
                (aux,) + all_weights + tuple(updates) + tuple(vector_made[1::3]),
                weight=4,
            )
            results = []
            for array in range(n):
                rows, cols = moments[array]
                results.append(
                    [grads[array], row_new[array].reshape(rows.shape), col_new[array].reshape(cols.shape), news[array]]
                )
            for i in range(vector_count):
                results.append([vector_made[3 * i + 2], vector_made[3 * i], news[n + i]])
            return results

        return made[-1], finish

    if aligned:
        ffn_sources = (sum_ffn,)
    else:
        ffn_sources = []
        at = 0
        for weight, block, size in zip((light_in, light_out, heavy_in, heavy_out), blocks, block_rows):
            lead = weight.size // (weight.shape[-1] * weight.shape[-2])
            ffn_sources.append(
                unblocked(sum_ffn[at : at + size].reshape(block.shape), lead).reshape(weight.shape).astype(wide)
            )
            at = at + size
    ffn_made, ffn_parts = first_sums(
        ffn_list, unpack_ffn, ffn_sources, (8, SUM_LANES), ffn_weights
    )
    ffn_sums = ffn_made[-1]
    begun = mp_first(last[-1][0], last[-1][1], pack_attn)
    last_moved.append(mp_second(after(begun, ffn_sums, *earlier)))
    ffn_aux, ffn_finish = optimize(
        ffn_list,
        ffn_made,
        ffn_parts,
        ffn_weights,
        ffn_moments,
        ffn_here,
        (),
    )
    ffn_got = exchanged(ffn_aux)
    ffn_results = ffn_finish(ffn_got)

    key_half = (micro_count * routed_local // 2, width)
    chunks = tok_local // STREAM
    smem = pl.BlockSpec(memory_space=pltpu.SMEM)
    by_chunk = pl.BlockSpec((STREAM, width), lambda i: (i, 0))
    by_half = pl.BlockSpec((STREAM, width), lambda i: (i % (chunks // 2), 0))
    both_out = pl.BlockSpec((micro_count, STREAM, width), lambda i: (0, i, 0))

    def fixed(shape):
        return pl.BlockSpec(shape, lambda i: (0,) * len(shape))

    def streamed(body, in_specs, out_specs, outs, scratch, args, weight):
        return pl.pallas_call(
            functools.partial(body, chunks),
            grid=(chunks,),
            in_specs=in_specs,
            out_specs=out_specs,
            out_shape=outs,
            scratch_shapes=scratch,
            compiler_params=pltpu.CompilerParams(vmem_limit_bytes=VMEM_BYTES),
            cost_estimate=pl.CostEstimate(flops=weight * 1_150_000_000, bytes_accessed=1_000_000, transcendentals=0),
        )(*args)

    join_args = (core_flag,)
    for m in micros:
        join_args = join_args + (fed[m][0],) + mp_third(y_moved[m], pack_attn, ffn_sums)
    (mixed,) = streamed(
        join_body,
        [smem] + [by_chunk, by_half, by_half] * micro_count,
        [both_out],
        [in_vmem(tokens.shape, low)],
        [],
        join_args,
        6,
    )
    if aligned:
        attn_sources = ()
    else:
        own_sums = sum_attn[:attn_rows].astype(wide)
        attn_sources = (
            own_sums[: 3 * in_rows]
            .reshape(3, in_rows, 2, head_cols)
            .transpose(0, 2, 1, 3)
            .reshape(6, in_rows, head_cols),
            own_sums[3 * in_rows :]
            .reshape(sides, 2, out_rows, lane)
            .transpose(1, 2, 0, 3)
            .reshape(2, out_rows, width),
        )
    key_keep, key_send, vector_lines = kernel_call(
        functools.partial(keys_back_body, micro_count),
        [in_vmem(key_half, low), in_vmem(key_half, low), in_vmem((data_size, 8, 128), wide)],
        [pltpu.VMEM((routed_local, width), low), pltpu.VMEM((micro_count * routed_local, width), low)],
        (core_flag, sum_attn, after(vectors, mixed, ffn_results[0][3]), w_in)
        + tuple(rows_k)
        + tuple(last[m][4] for m in micros)
        + tuple(backs[m][1] for m in micros)
        + tuple(last[m][3] for m in micros)
        + tuple(fed[m][5] for m in micros),
        scalars=1,
        weight=3,
    )
    grad_attn_in, grad_attn_out, sum_blocks = kernel_call(
        functools.partial(owners_body, attn_list, unpack_attn),
        [
            in_vmem(attn_in.shape, wide),
            in_vmem(attn_out.shape, wide),
            in_vmem((device_count, 8, VECTORS_AT + 128), low),
        ],
        [pltpu.VMEM((8, VECTORS_AT + 128), wide)],
        (sum_attn, vector_lines) + attn_weights + attn_sources,
        weight=3,
    )
    key_begun = mp_first(key_keep, key_send)
    attn_parts = exchanged(after(sum_blocks, key_begun))
    key_moved = mp_second(key_begun)
    pieces = mp_third(key_moved) + (after(vectors, ffn_aux),)
    for m in micros:
        pieces = pieces + mp_third(last_moved[m], ffn_sums if m + 1 < micro_count else ffn_aux)
        pieces = pieces + (backs[m][0], key_row[m])
    (grad_tokens,) = streamed(
        finish_body,
        [smem, fixed(key_half), fixed(key_half), fixed((8, width))]
        + [by_half, by_half, by_chunk, fixed((1, routed_local))] * micro_count
        + [both_out],
        [both_out],
        [in_vmem(tokens.shape, wide)],
        [pltpu.VMEM((micro_count * routed_local, width), low)],
        (core_flag,) + pieces + (tokens,),
        8,
    )
    attn_aux, attn_finish = optimize(
        attn_list,
        (grad_attn_in, grad_attn_out),
        attn_parts,
        attn_weights,
        attn_moments,
        attn_here,
        ((second_gains, gains), (second_router, router)),
    )
    attn_results = attn_finish(exchanged(attn_aux))
    results = [mixed, grad_tokens]
    for result in attn_results[:2] + ffn_results + attn_results[2:]:
        results.extend(result)
    return tuple(results)


def solution(mesh):
    placed = (
        P(None, "dp", None),
        P(None, "dp", None),
        P(),
        P(None, "dp"),
        P(),
        P(None, "dp"),
        P(None, "dp", "mp"),
        P(None, ("mp", "dp"), None),
        P(None, "dp", "mp"),
        P(("mp", "dp"), None),
        P(None, "dp", "mp"),
        P(("mp", "dp"), None),
        P(None, "dp"),
        P(None, "dp"),
        P(),
        P(),
        P(),
        P(),
        P(),
        P(),
        P(),
        P(),
        P(),
        P(),
        P(),
        P(),
        P(None, "dp"),
        P(None, "dp"),
    )
    return jax.shard_map(
        shards,
        mesh=mesh,
        in_specs=placed,
        out_specs=(
            P(None, "dp", None),
            P(None, "dp", None),
            P(None, "dp", "mp"),
            P(),
            P(),
            P(None, "dp", "mp"),
            P(None, ("mp", "dp"), None),
            P(),
            P(),
            P(None, ("mp", "dp"), None),
            P(None, "dp", "mp"),
            P(),
            P(),
            P(None, "dp", "mp"),
            P(("mp", "dp"), None),
            P(),
            P(),
            P(("mp", "dp"), None),
            P(None, "dp", "mp"),
            P(),
            P(),
            P(None, "dp", "mp"),
            P(("mp", "dp"), None),
            P(),
            P(),
            P(("mp", "dp"), None),
            P(None, "dp"),
            P(None, "dp"),
            P(None, "dp"),
            P(None, "dp"),
            P(None, "dp"),
            P(None, "dp"),
        ),
        check_vma=False,
    )
```
